32 devices in a mesh: seq: 4 (over x, core), head: 8 (over z, y).
Axes of the slice: x: 2, y: 2, z: 4, core: 2. Of those that a mesh axis runs over, the one named last changes fastest.
Arguments:
- qk_in: bfloat16 [4, 4096, 2, 2048], P(None, 'seq', None, 'head'), may hold values from -6 to 6
- v_in: bfloat16 [4, 4096, 4096], P(None, 'seq', 'head'), may hold values from -6 to 6
- gate_z: bfloat16 [4, 4096, 4096], P(None, 'seq', 'head'), may hold values from -6 to 6
- conv_qk: bfloat16 [4, 2, 2048], P(None, None, 'head'), may hold values from -3 to 3
- conv_v: bfloat16 [4, 4096], P(None, 'head'), may hold values from -3 to 3
- log_decay: float32 [4, 32, 4096], P(None, 'head', 'seq'), may hold values from -0.7 to 0
- write_gain: float32 [4, 32, 4096], P(None, 'head', 'seq'), may hold values from 0 to 1
- norm_gain: float32 [128], replicated, may hold values from 0.5 to 1.5
- prompt_lengths: int32 [4], replicated, may hold values from 1 to 4096, 10240 in all
- placement: int32 [4, 8], P('seq'), may hold values from 0 to 3
Outputs:
- attended: bfloat16 [4, 4096, 4096], P(None, 'seq', 'head')
- rollout_state: float32 [4, 8, 32, 128, 128], P('seq', 'head')
The draws below stay inside these ranges and needn't reach their ends.
Inputs may be any that keep to these rules, and one draw needn't show every extreme that they name: `prompt_lengths`: the largest length is exactly 4096; the lengths sum to 10240. Device (s, r) serves prompt placement[s, r]; the values 0 and 3 each occur at least once.
All inputs are finite; a program needn't handle non-finite values.
Results may differ from the reference program's by a relative error of at most 0.02.
Values may be sent and summed in bfloat16 or wider, within the bound.
No kernel may reach another device: no remote copies, remote signals or barrier semaphores. Data moves between devices by JAX's collectives and lax.ppermute only.
A program may use at most 128 MiB of HBM per device.

```python
import math
import jax
import jax.numpy as jnp
import numpy as np
from jax import lax

VALUE_HEAD_COUNT = 32
HK = 16
DK = 128
DV = 128
CONV = 4
SPAN = 64
PROMPT_COUNT = 4
TOK_DEV = 1024
PROMPT_LENGTH = 4096
N_SEQ = 4
N_HEAD = 8


def head_speed(key, fast_share):
    marks = jax.random.uniform(jax.random.fold_in(key, 77), (PROMPT_COUNT, VALUE_HEAD_COUNT, 1), jnp.float32)
    return (marks < fast_share).astype(jnp.float32)


def draw_log_decay(key, part):
    fast_mask = head_speed(key, 0.5)
    key = jax.random.fold_in(key, 1)
    random_subkeys = jax.random.split(key, 6)
    quick_rate = jax.random.uniform(random_subkeys[0], (PROMPT_COUNT, VALUE_HEAD_COUNT, 1), jnp.float32, 1.0 / 50.0, 1.0 / 30.0)
    slow_rate = 0.15 / PROMPT_LENGTH * jnp.exp(jax.random.uniform(random_subkeys[1], (PROMPT_COUNT, VALUE_HEAD_COUNT, 1), jnp.float32, -0.7, 0.7))
    base_rate = jnp.where(fast_mask > 0.5, quick_rate, slow_rate)
    roughness = jax.random.uniform(random_subkeys[2], (PROMPT_COUNT, VALUE_HEAD_COUNT, PROMPT_LENGTH), jnp.float32, 0.4, 1.6)
    segments = jnp.exp(jax.random.uniform(random_subkeys[3], (PROMPT_COUNT, VALUE_HEAD_COUNT, PROMPT_LENGTH // TOK_DEV, 1), jnp.float32, -0.7, 0.7))
    segments = jnp.broadcast_to(segments, (PROMPT_COUNT, VALUE_HEAD_COUNT, PROMPT_LENGTH // TOK_DEV, TOK_DEV)).reshape(PROMPT_COUNT, VALUE_HEAD_COUNT, PROMPT_LENGTH)
    smoothing_factor = -base_rate * roughness * segments
    spike_mask = jax.random.uniform(random_subkeys[4], (PROMPT_COUNT, VALUE_HEAD_COUNT, PROMPT_LENGTH), jnp.float32) < 2.0 / PROMPT_LENGTH
    spike_removal = jax.random.uniform(random_subkeys[5], (PROMPT_COUNT, VALUE_HEAD_COUNT, PROMPT_LENGTH), jnp.float32, -0.69, -0.23)
    return jnp.where(spike_mask, spike_removal, smoothing_factor)


def draw_write_gain(key, part):
    fast_mask = head_speed(key, 0.5)
    key = jax.random.fold_in(key, 2)
    random_subkeys = jax.random.split(key, 2)
    quick_beta = jax.random.uniform(random_subkeys[0], (PROMPT_COUNT, VALUE_HEAD_COUNT, PROMPT_LENGTH), jnp.float32, 0.2, 0.95)
    slow_scale = min(0.5, 32.0 / PROMPT_LENGTH)
    slow_beta = slow_scale * jax.random.uniform(random_subkeys[1], (PROMPT_COUNT, VALUE_HEAD_COUNT, PROMPT_LENGTH), jnp.float32, 0.4, 1.6)
    return jnp.where(fast_mask > 0.5, quick_beta, slow_beta)


def with_ends(values, rng, smallest, high):
    shape = values.shape
    place = [jax.random.randint(jax.random.fold_in(rng, axis), (), 0, shape[axis]) for axis in range(len(shape))]
    values = values.at[tuple(place)].set(smallest)
    longest = shape.index(max(shape))
    place[longest] = (place[longest] + 1) % shape[longest]
    return values.at[tuple(place)].set(high)


def block_levels(stream_key, extent, pieces, smallest, top_value):
    loudness = 1.0
    for axis_at, shards_of in pieces:
        heights = jax.random.uniform(jax.random.fold_in(jax.random.fold_in(stream_key, 6), axis_at), (shards_of,), jnp.float32, smallest / len(pieces), top_value / len(pieces))
        loudness = loudness * jnp.repeat(jnp.exp(heights), extent[axis_at] // shards_of).reshape((-1,) + (1,) * (len(extent) - 1 - axis_at))
    return loudness


def rank_bounds(amount, skew):
    loads = [(1 << 20) // math.isqrt(rank ** skew) + 1 for rank in range(1, amount + 1)]
    scale = 1 + sum(loads) // (1 << 30)
    return np.cumsum(np.array([max(1, weight // scale) for weight in loads]))


def ranked_ids(rng, shape, amount, skew):
    grid = rank_bounds(amount, skew)
    lot = jax.random.randint(jax.random.fold_in(rng, 1), shape, 0, int(grid[amount - 1]))
    standing = jnp.searchsorted(jnp.asarray(grid, jnp.int32), lot, side="right")
    return jax.random.permutation(jax.random.fold_in(rng, 2), amount)[standing].astype(jnp.int32)


def profile(count, total, bound, slope):
    weights = [(1 << 20) // math.isqrt(rank ** slope) + 1 for rank in range(2, count + 1)]
    rest, given = total - bound - (count - 1), [1] * (count - 1)
    while rest > 0:
        free = [i for i in range(count - 1) if given[i] < bound]
        whole, left = sum([weights[i] for i in free]), rest
        for i in free:
            extra = min(bound - given[i], max(1, left * weights[i] // whole), rest)
            given[i] = given[i] + extra
            rest = rest - extra
    return np.array([bound] + given)


def ragged(stream_key, count, total, most, slope):
    if count == 2:
        one = jax.random.randint(stream_key, (), max(1, total - most), min(most, total - 1) + 1)
        return jnp.stack([one, total - one])
    tallies = jnp.asarray(profile(count, total, most, slope), jnp.int32)
    twos = (count - 1) // 2
    donor, sink = tallies[1:1 + 2 * twos:2], tallies[2:2 + 2 * twos:2]
    slack = jnp.minimum(donor - 1, most - sink)
    shifted = jax.random.randint(jax.random.fold_in(stream_key, 1), (twos,), 0, 1 << 20) % (slack + 1)
    tallies = tallies.at[1:1 + 2 * twos:2].set(donor - shifted).at[2:2 + 2 * twos:2].set(sink + shifted)
    return tallies[jax.random.permutation(jax.random.fold_in(stream_key, 2), count)]


def bell_draw(stream_key, shape, scale, limit, cuts=(), kind=jnp.bfloat16):
    values = jax.random.normal(stream_key, shape, jnp.float32) * scale
    if len(cuts) > 0:
        values = block_levels(stream_key, shape, cuts, -0.22, 0.18) * values
    return jnp.clip(values, min=-limit, max=limit).astype(kind)


def setup_inputs(seed: int = 0) -> dict:
    key_list = jax.random.split(jax.random.key(seed), 11)
    return {
        "qk_in": bell_draw(key_list[0], (PROMPT_COUNT, PROMPT_LENGTH, 2, HK * DK), 1.0, 6.0, ((1, 4), (3, 8))),
        "v_in": bell_draw(key_list[1], (PROMPT_COUNT, PROMPT_LENGTH, VALUE_HEAD_COUNT * DV), 1.0, 6.0, ((1, 4), (2, 8))),
        "gate_z": bell_draw(key_list[2], (PROMPT_COUNT, PROMPT_LENGTH, VALUE_HEAD_COUNT * DV), 1.0, 6.0, ((1, 4), (2, 8))),
        "conv_qk": bell_draw(key_list[3], (CONV, 2, HK * DK), CONV ** -0.5, 3.0, ((2, 8),)),
        "conv_v": bell_draw(key_list[4], (CONV, VALUE_HEAD_COUNT * DV), CONV ** -0.5, 3.0, ((1, 8),)),
        "log_decay": draw_log_decay(jax.random.fold_in(key_list[10], 71), 0),
        "write_gain": draw_write_gain(jax.random.fold_in(key_list[10], 71), 0),
        "norm_gain": jnp.clip(1.0 + 0.1 * jax.random.normal(key_list[7], (DV,), jnp.float32), 0.5, 1.5),
        "prompt_lengths": ragged(key_list[8], PROMPT_COUNT, PROMPT_COUNT * PROMPT_LENGTH * 5 // 8, PROMPT_LENGTH, 1).astype(jnp.int32),
        "placement": with_ends(ranked_ids(key_list[9], (N_SEQ, N_HEAD), PROMPT_COUNT, 2), jax.random.fold_in(key_list[9], 3), 0, PROMPT_COUNT - 1).astype(jnp.int32),
    }


TOP_PRECISION = lax.Precision.HIGHEST
EPSILON = 1e-06

def unit_lower_inverse(strict):
    length = strict.shape[-1]
    identity_matrix = jnp.eye(length, dtype=jnp.float32)
    power_term = -strict
    result = identity_matrix + power_term
    for section_index in range(1, length.bit_length() - 1):
        power_term = jnp.matmul(power_term, power_term, precision=TOP_PRECISION)
        result = result + jnp.matmul(result, power_term, precision=TOP_PRECISION)
    return result

def causal_conv(previous, current, conv_weight):
    joined = jnp.concatenate([previous, current], axis=1).astype(jnp.float32)
    length = current.shape[1]
    taps_count = conv_weight.shape[0]
    tap_weights = conv_weight.astype(jnp.float32)
    summed = joined[:, 0:length] * tap_weights[0]
    for offset in range(1, taps_count):
        summed = summed + joined[:, offset:offset + length] * tap_weights[offset]
    return jax.nn.silu(summed)

def unit_rows(row_block):
    return row_block / jnp.sqrt(lax.optimization_barrier(jnp.sum(row_block * row_block, axis=-1, keepdims=True)) + EPSILON)

def wide(tensor):
    return tensor.astype(jnp.float32)

def reference(qk_in, v_in, gate_z, conv_qk, conv_v, log_decay, write_gain, norm_gain, prompt_lengths, placement):
    group_size = VALUE_HEAD_COUNT // HK
    blocks = PROMPT_LENGTH // SPAN
    positions = jnp.arange(PROMPT_LENGTH, dtype=jnp.int32)
    lower_incl = jnp.tril(jnp.ones((SPAN, SPAN), dtype=bool))
    lower_strict = jnp.tril(jnp.ones((SPAN, SPAN), dtype=bool), -1)

    def advance(present_state, inputs):
        block_queries, key_block, value_block, gate_block, gain_block = inputs
        running_total = jnp.cumsum(gate_block, axis=-1)
        spread = running_total[:, :, None] - running_total[:, None, :]
        decay_ratio = jnp.where(lower_incl, jnp.exp(jnp.where(lower_incl, spread, 0.0)), 0.0)
        key_key = jnp.einsum('hik,hjk->hij', wide(key_block), wide(key_block), precision=TOP_PRECISION)
        query_key = jnp.einsum('hik,hjk->hij', wide(block_queries), wide(key_block), precision=TOP_PRECISION)
        strict = jnp.where(lower_strict, gain_block[:, :, None] * decay_ratio * key_key, 0.0)
        inverse = unit_lower_inverse(strict).astype(jnp.bfloat16)
        faded_state = jnp.exp(running_total)
        scaled_keys = (wide(key_block) * (gain_block * faded_state)[:, :, None]).astype(jnp.bfloat16)
        scaled_values = (wide(value_block) * gain_block[:, :, None]).astype(jnp.bfloat16)
        w_rows = jnp.einsum('hij,hjk->hik', wide(inverse), wide(scaled_keys), precision=TOP_PRECISION).astype(jnp.bfloat16)
        u_rows = jnp.einsum('hij,hjv->hiv', wide(inverse), wide(scaled_values), precision=TOP_PRECISION).astype(jnp.bfloat16)
        start = present_state.astype(jnp.bfloat16)
        fresh = (wide(u_rows) - jnp.einsum('xtc,xcy->xty', wide(w_rows), wide(start), precision=TOP_PRECISION)).astype(jnp.bfloat16)
        scores = (decay_ratio * query_key).astype(jnp.bfloat16)
        state_contribution = jnp.einsum('xtc,xcy->xty', wide(block_queries), wide(start), precision=TOP_PRECISION) * faded_state[:, :, None]
        outputs = state_contribution + jnp.einsum('hij,hjv->hiv', wide(scores), wide(fresh), precision=TOP_PRECISION)
        trailing_keys = (wide(key_block) * jnp.exp(running_total[:, -1:] - running_total)[:, :, None]).astype(jnp.bfloat16)
        following_state = jnp.exp(running_total[:, -1])[:, None, None] * present_state + jnp.einsum('sjb,sjf->sbf', wide(trailing_keys), wide(fresh), precision=TOP_PRECISION)
        return (following_state, outputs)

    def blocked(tensor):
        return jnp.transpose(tensor.reshape(blocks, SPAN, VALUE_HEAD_COUNT, tensor.shape[-1]), (0, 2, 1, 3))

    def blocked_gate(tensor):
        return jnp.transpose(tensor.reshape(VALUE_HEAD_COUNT, blocks, SPAN), (1, 0, 2))

    def one_prompt(inputs):
        qk_raw, v_raw, z_raw, log_row, gain_row, length = inputs
        is_valid = positions < length
        zeros_qk = jnp.zeros((1, CONV - 1, 2, HK * DK), jnp.bfloat16)
        zeros_v = jnp.zeros((1, CONV - 1, VALUE_HEAD_COUNT * DV), jnp.bfloat16)
        qk_mixed = causal_conv(zeros_qk, qk_raw[None], conv_qk)[0]
        v_mixed = causal_conv(zeros_v, v_raw[None], conv_v)[0].astype(jnp.bfloat16)
        queries = jnp.repeat(unit_rows(qk_mixed[:, 0].reshape(PROMPT_LENGTH, HK, DK)).astype(jnp.bfloat16), group_size, axis=1)
        keys_all = jnp.repeat(unit_rows(qk_mixed[:, 1].reshape(PROMPT_LENGTH, HK, DK)).astype(jnp.bfloat16), group_size, axis=1)
        values = v_mixed.reshape(PROMPT_LENGTH, VALUE_HEAD_COUNT, DV)
        log_gate = jnp.where(is_valid[None, :], log_row, 0.0)
        gain_rows = jnp.where(is_valid[None, :], gain_row, 0.0)
        zero_state = jnp.zeros((VALUE_HEAD_COUNT, DK, DV), jnp.float32)
        final_state, outputs = lax.scan(advance, zero_state, (blocked(queries), blocked(keys_all), blocked(values), blocked_gate(log_gate), blocked_gate(gain_rows)))
        raw_out = jnp.transpose(outputs, (0, 2, 1, 3)).reshape(PROMPT_LENGTH, VALUE_HEAD_COUNT, DV)
        scaled = raw_out * lax.rsqrt(lax.optimization_barrier(jnp.mean(raw_out * raw_out, axis=-1, keepdims=True)) + EPSILON)
        gated = scaled * norm_gain * jax.nn.silu(z_raw.astype(jnp.float32).reshape(PROMPT_LENGTH, VALUE_HEAD_COUNT, DV))
        attended = jnp.where(is_valid[:, None, None], gated, 0.0).reshape(PROMPT_LENGTH, VALUE_HEAD_COUNT * DV).astype(jnp.bfloat16)
        return (attended, final_state)
    attended, finals = lax.map(one_prompt, (qk_in, v_in, gate_z, log_decay, write_gain, prompt_lengths))
    rollout = jnp.take(finals, placement, axis=0)
    return (attended, rollout)
```

```python
import functools

import jax
import jax.numpy as jnp
from jax import lax
from jax.experimental import pallas as pl
from jax.experimental.pallas import tpu as pltpu
from jax.sharding import PartitionSpec as P

DK = 128
DV = 128
CONV = 4
BLOCK = 128
TINY = 16
EPSILON = 1e-06
VMEM_BYTES = 56 * 1024 * 1024
F32 = jnp.float32
BF16 = jnp.bfloat16


def dot(a, b):
    return lax.dot_general(a, b, (((1,), (0,)), ((), ())), preferred_element_type=F32)


def silu(x):
    half = 0.5 * x
    return half + half * jnp.tanh(half)


def load_padded(pad_ref, halo_ref, raw_ref):
    pad_ref[0:8, :] = halo_ref[0]
    pad_ref[8:, :] = raw_ref[0].astype(F32)


def conv_block(pad_ref, taps_ref, c):
    total = None
    for i in range(CONV):
        rows = pad_ref[8 - CONV + 1 + i + c * BLOCK : 8 - CONV + 1 + i + (c + 1) * BLOCK, :]
        term = rows * taps_ref[i : i + 1, :]
        total = term if total is None else total + term
    return silu(total)


def unit_rows(x):
    return x * lax.rsqrt(jnp.sum(x * x, axis=-1, keepdims=True) + EPSILON)


def gate_rows(log_ref, gain_ref, used, group, chunks):
    rows = group * chunks
    row = lax.broadcasted_iota(jnp.int32, (rows, BLOCK), 0)
    lane = lax.broadcasted_iota(jnp.int32, (rows, BLOCK), 1)
    valid = (row % chunks) * BLOCK + lane < used
    cum = jnp.where(valid, log_ref[0, 0], 0.0)
    gain = jnp.where(valid, gain_ref[0, 0], 0.0)
    shift = 1
    while shift < BLOCK:
        cum = cum + jnp.where(lane >= shift, pltpu.roll(cum, shift, 1), 0.0)
        shift *= 2
    return cum, gain


def columns_of(parts):
    rows = sum(part.shape[0] for part in parts)
    parts = list(parts) + [jnp.zeros((BLOCK - rows, BLOCK), F32)]
    return jnp.concatenate(parts, axis=0).T


def prepare_kernel(
    groups, group, chunks,
    used_ref, k_ref, v_ref, k_halo_ref, v_halo_ref, k_taps_ref, v_taps_ref, log_ref, gain_ref,
    kn_ref, wu_ref, start_ref, state_ref, trans_ref,
    k_pad, v_pad, m_scr, b_scr, fade_scr, st_scr, a_scr, x_scr,
):
    step = pl.program_id(0)
    prompt = jnp.minimum(step, groups - 1) * used_ref.shape[0] // groups
    used = used_ref[prompt]
    units = [(h, c) for c in range(chunks) for h in range(group)]

    @pl.when(jnp.logical_and(step < groups, used <= 0))
    def _():
        kn_ref[...] = jnp.zeros_like(kn_ref)
        wu_ref[...] = jnp.zeros_like(wu_ref)
        fade_scr[step] = jnp.ones((group * chunks, BLOCK), F32)
        for h, c in units:
            m_scr[c, step * group + h] = jnp.zeros((DK, DK), BF16)
            b_scr[c, step * group + h] = jnp.zeros((DK, DV), F32)

    @pl.when(jnp.logical_and(step < groups, used > 0))
    def _():
        load_padded(k_pad, k_halo_ref, k_ref)
        load_padded(v_pad, v_halo_ref, v_ref)
        cum, gain = gate_rows(log_ref, gain_ref, used, group, chunks)
        faded = jnp.exp(cum)
        rows = group * chunks
        columns = columns_of([cum, gain, gain * faded])
        last = cum[:, BLOCK - 1 : BLOCK]
        fade_scr[step] = jnp.broadcast_to(jnp.exp(last), (rows, BLOCK))
        tail = jnp.exp(last - cum)

        row = lax.broadcasted_iota(jnp.int32, (BLOCK, BLOCK), 0)
        lane = lax.broadcasted_iota(jnp.int32, (BLOCK, BLOCK), 1)
        below = row > lane
        small_row = lax.broadcasted_iota(jnp.int32, (TINY, BLOCK), 0)
        small_lane = lax.broadcasted_iota(jnp.int32, (TINY, BLOCK), 1)
        part_of = small_lane // TINY
        tiny_eye = jnp.where(small_row == small_lane % TINY, 1.0, 0.0).astype(F32)

        keys = []
        for c in range(chunks):
            kc = unit_rows(conv_block(k_pad, k_taps_ref, c)).astype(BF16)
            kn_ref[0, c * BLOCK : (c + 1) * BLOCK, :] = kc
            keys.append(kc)
        turned = [kc.T for kc in keys]

        compact = {}
        for c in range(chunks):
            kk = dot(keys[c], turned[c])
            for h in range(group):
                r = h * chunks + c
                ratio = jnp.exp(columns[:, r : r + 1] - cum[r : r + 1, :])
                strict = jnp.where(below, columns[:, rows + r : rows + r + 1] * ratio * kk, 0.0)
                a_scr[r] = strict.astype(BF16)
                tiny = strict[0:TINY]
                for b in range(1, BLOCK // TINY):
                    tiny = jnp.where(part_of == b, strict[b * TINY : (b + 1) * TINY], tiny)
                compact[r] = tiny

        solved = {r: tiny_eye for r in compact}
        for j in range(TINY - 1):
            pick = part_of * TINY + j
            for r in solved:
                factor = jnp.take_along_axis(compact[r], pick, axis=1, mode="promise_in_bounds")
                solved[r] = solved[r] - factor * solved[r][j : j + 1, :]
        for r in solved:
            for b in range(BLOCK // TINY):
                x_scr[r, b * TINY : (b + 1) * TINY, :] = jnp.where(
                    part_of == b, solved[r], 0.0
                ).astype(BF16)

        size = TINY
        while size < BLOCK:
            odd = [s for s in range(size, BLOCK, 2 * size)]
            half_lane = lax.broadcasted_iota(jnp.int32, (BLOCK // 2, BLOCK), 1)
            half_row = lax.broadcasted_iota(jnp.int32, (BLOCK // 2, BLOCK), 0)
            left = half_lane // size == 2 * (half_row // size)
            moved = {}
            for h, c in units:
                r = h * chunks + c
                lower = jnp.concatenate([a_scr[r, s : s + size, :] for s in odd], axis=0)
                lower = jnp.where(left, lower, jnp.zeros_like(lower))
                moved[r] = dot(lower, x_scr[r]).astype(BF16)
            for h, c in units:
                r = h * chunks + c
                spread = []
                for n in range(len(odd)):
                    spread.append(jnp.zeros((size, BLOCK), BF16))
                    spread.append(moved[r][n * size : (n + 1) * size])
                own = jnp.concatenate([x_scr[r, s : s + size, :] for s in odd], axis=0)
                update = own.astype(F32) - dot(own, jnp.concatenate(spread, axis=0))
                update = update.astype(BF16)
                for n, s in enumerate(odd):
                    x_scr[r, s : s + size, :] = update[n * size : (n + 1) * size]
            size *= 2

        for c in range(chunks):
            vc = conv_block(v_pad, v_taps_ref, c).astype(BF16).astype(F32)
            kc = keys[c].astype(F32)
            for h in range(group):
                r = h * chunks + c
                gain_col = columns[:, rows + r : rows + r + 1]
                fade_col = columns[:, 2 * rows + r : 2 * rows + r + 1]
                right = jnp.concatenate(
                    [(kc * fade_col).astype(BF16), (vc[:, h * DV : (h + 1) * DV] * gain_col).astype(BF16)],
                    axis=1,
                )
                wu = dot(x_scr[r], right).astype(BF16)
                wu_ref[0, r] = wu
        for c in range(chunks):
            for h in range(group):
                r = h * chunks + c
                scaled = (turned[c].astype(F32) * tail[r : r + 1, :]).astype(BF16)
                both = dot(scaled, wu_ref[0, r])
                m_scr[c, step * group + h] = (-both[:, :DK]).astype(BF16)
                b_scr[c, step * group + h] = both[:, DK:]

    @pl.when(step >= groups)
    def _():
        c = step - groups
        chains = groups * group

        @pl.when(c == 0)
        def _():
            row = lax.broadcasted_iota(jnp.int32, (DK, DV + DK), 0)
            lane = lax.broadcasted_iota(jnp.int32, (DK, DV + DK), 1)
            first = jnp.where(lane == row + DV, 1.0, 0.0).astype(F32)
            for n in range(chains):
                st_scr[n] = first

        for n in range(chains):
            now = st_scr[n]
            now_b = now.astype(BF16)
            start_ref[0, n] = now_b
            fade = fade_scr[n // group, pl.ds((n % group) * chunks + c, 1), :]
            moved = dot(m_scr[c, n], now_b)
            state = now[:, :DV] * fade + moved[:, :DV] + b_scr[c, n]
            trans = now[:, DV:] * fade + moved[:, DV:]
            st_scr[n, :, :DV] = state
            st_scr[n, :, DV:] = trans
            state_ref[n] = state.astype(BF16)
            trans_ref[n] = trans.astype(BF16)


def prepare(used, k_raw, v_in, k_halo, v_halo, k_taps, v_taps, log_rows, gain_rows):
    prompts, tok = k_raw.shape[:2]
    key_heads = k_raw.shape[2] // DK
    value_heads = v_in.shape[2] // DV
    group = value_heads // key_heads
    groups = prompts * key_heads
    chunks = tok // BLOCK
    chains = groups * group
    rows = group * chunks
    wide = group * DV

    def at(i):
        n = jnp.minimum(i, groups - 1)
        return n // key_heads, n % key_heads

    def rows_of(i, used):
        p, h = at(i)
        return (p, 0, h)

    def taps_of(i, used):
        return (0, at(i)[1])

    def gates_of(i, used):
        p, h = at(i)
        return (p, h, 0, 0)

    return pl.pallas_call(
        functools.partial(prepare_kernel, groups, group, chunks),
        grid_spec=pltpu.PrefetchScalarGridSpec(
            num_scalar_prefetch=1,
            grid=(groups + chunks,),
            in_specs=[
                pl.BlockSpec((1, tok, DK), rows_of),
                pl.BlockSpec((1, tok, wide), rows_of),
                pl.BlockSpec((1, 8, DK), rows_of),
                pl.BlockSpec((1, 8, wide), rows_of),
                pl.BlockSpec((CONV, DK), taps_of),
                pl.BlockSpec((CONV, wide), taps_of),
                pl.BlockSpec((1, 1, rows, BLOCK), gates_of),
                pl.BlockSpec((1, 1, rows, BLOCK), gates_of),
            ],
            out_specs=[
                pl.BlockSpec((1, tok, DK), rows_of),
                pl.BlockSpec((1, rows, BLOCK, DK + DV), lambda i, used: (jnp.minimum(i, groups - 1), 0, 0, 0)),
                pl.BlockSpec((1, chains, DK, DV + DK), lambda i, used: (jnp.maximum(i - groups, 0), 0, 0, 0)),
                pl.BlockSpec((chains, DK, DV), lambda i, used: (0, 0, 0)),
                pl.BlockSpec((chains, DK, DK), lambda i, used: (0, 0, 0)),
            ],
            scratch_shapes=[
                pltpu.VMEM((tok + 8, DK), F32),
                pltpu.VMEM((tok + 8, wide), F32),
                pltpu.VMEM((chunks, chains, DK, DK), BF16),
                pltpu.VMEM((chunks, chains, DK, DV), F32),
                pltpu.VMEM((groups, rows, BLOCK), F32),
                pltpu.VMEM((chains, DK, DV + DK), F32),
                pltpu.VMEM((rows, BLOCK, BLOCK), BF16),
                pltpu.VMEM((rows, BLOCK, BLOCK), BF16),
            ],
        ),
        out_shape=[
            jax.ShapeDtypeStruct((prompts, tok, key_heads * DK), BF16),
            jax.ShapeDtypeStruct((groups, rows, BLOCK, DK + DV), BF16),
            jax.ShapeDtypeStruct((chunks, chains, DK, DV + DK), BF16),
            jax.ShapeDtypeStruct((chains, DK, DV), BF16),
            jax.ShapeDtypeStruct((chains, DK, DK), BF16),
        ],
        compiler_params=pltpu.CompilerParams(vmem_limit_bytes=VMEM_BYTES),
        name="prepare",
    )(used, k_raw, v_in, k_halo, v_halo, k_taps, v_taps, log_rows, gain_rows)


def outputs_kernel(
    groups, group, chunks,
    used_ref, q_ref, q_halo_ref, q_taps_ref, kn_ref, wu_ref, start_ref, log_ref, gain_ref,
    own_ref, map_ref,
    q_pad,
):
    step = pl.program_id(0)
    used = used_ref[step * used_ref.shape[0] // groups]

    @pl.when(used <= 0)
    def _():
        own_ref[...] = jnp.zeros_like(own_ref)
        map_ref[...] = jnp.zeros_like(map_ref)

    @pl.when(used > 0)
    def _():
        load_padded(q_pad, q_halo_ref, q_ref)
        cum, gain = gate_rows(log_ref, gain_ref, used, group, chunks)
        rows = group * chunks
        columns = columns_of([cum, jnp.exp(cum)])
        row = lax.broadcasted_iota(jnp.int32, (BLOCK, BLOCK), 0)
        lane = lax.broadcasted_iota(jnp.int32, (BLOCK, BLOCK), 1)
        upto = row >= lane
        for c in range(chunks):
            span = slice(c * BLOCK, (c + 1) * BLOCK)
            qc = unit_rows(conv_block(q_pad, q_taps_ref, c)).astype(BF16)
            qk = dot(qc, kn_ref[0, span, :].T)
            q_wide = qc.astype(F32)
            for h in range(group):
                r = h * chunks + c
                ratio = jnp.exp(columns[:, r : r + 1] - cum[r : r + 1, :])
                scores = jnp.where(upto, ratio * qk, 0.0).astype(BF16)
                both = dot(scores, wu_ref[0, r])
                seen = (q_wide * columns[:, rows + r : rows + r + 1] - both[:, :DK]).astype(BF16)
                out = dot(seen, start_ref[c, h])
                cols = slice(h * DV, (h + 1) * DV)
                own_ref[0, span, cols] = (out[:, :DV] + both[:, DK:]).astype(BF16)
                map_ref[0, span, cols] = out[:, DV:].astype(BF16)


def local_outputs(used, q_raw, q_halo, q_taps, kn, wu, starts, log_rows, gain_rows):
    prompts, tok = q_raw.shape[:2]
    key_heads = q_raw.shape[2] // DK
    groups, rows = wu.shape[:2]
    chunks = tok // BLOCK
    group = rows // chunks
    wide = group * DV
    value_heads = key_heads * group

    def rows_of(i, used):
        return (i // key_heads, 0, i % key_heads)

    def gates_of(i, used):
        return (i // key_heads, i % key_heads, 0, 0)

    return pl.pallas_call(
        functools.partial(outputs_kernel, groups, group, chunks),
        grid_spec=pltpu.PrefetchScalarGridSpec(
            num_scalar_prefetch=1,
            grid=(groups,),
            in_specs=[
                pl.BlockSpec((1, tok, DK), rows_of),
                pl.BlockSpec((1, 8, DK), rows_of),
                pl.BlockSpec((CONV, DK), lambda i, used: (0, i % key_heads)),
                pl.BlockSpec((1, tok, DK), rows_of),
                pl.BlockSpec((1, rows, BLOCK, DK + DV), lambda i, used: (i, 0, 0, 0)),
                pl.BlockSpec((chunks, group, DK, DV + DK), lambda i, used: (0, i, 0, 0)),
                pl.BlockSpec((1, 1, rows, BLOCK), gates_of),
                pl.BlockSpec((1, 1, rows, BLOCK), gates_of),
            ],
            out_specs=[
                pl.BlockSpec((1, tok, wide), rows_of),
                pl.BlockSpec((1, tok, wide), rows_of),
            ],
            scratch_shapes=[pltpu.VMEM((tok + 8, DK), F32)],
        ),
        out_shape=[
            jax.ShapeDtypeStruct((prompts, tok, value_heads * DV), BF16),
            jax.ShapeDtypeStruct((prompts, tok, value_heads * DV), BF16),
        ],
        compiler_params=pltpu.CompilerParams(vmem_limit_bytes=VMEM_BYTES),
        name="local_outputs",
    )(used, q_raw, q_halo, q_taps, kn, wu, starts, log_rows, gain_rows)


def gate_kernel(groups, group, chunks, used_ref, own_ref, map_ref, enter_ref, z_ref, norm_ref, out_ref):
    step = pl.program_id(0)
    used = used_ref[step * used_ref.shape[0] // groups]

    @pl.when(used <= 0)
    def _():
        out_ref[...] = jnp.zeros_like(out_ref)

    @pl.when(used > 0)
    def _():
        row = lax.broadcasted_iota(jnp.int32, (BLOCK, DV), 0)
        norm_gain = norm_ref[...]
        for c in range(chunks):
            span = slice(c * BLOCK, (c + 1) * BLOCK)
            valid = row + c * BLOCK < used
            for h in range(group):
                cols = slice(h * DV, (h + 1) * DV)
                raw = own_ref[0, span, cols].astype(F32) + dot(map_ref[0, span, cols], enter_ref[h])
                mean = jnp.sum(raw * raw, axis=-1, keepdims=True) * (1.0 / DV)
                gated = raw * lax.rsqrt(mean + EPSILON) * norm_gain * silu(z_ref[0, span, cols].astype(F32))
                out_ref[0, span, cols] = jnp.where(valid, gated, 0.0).astype(BF16)


def gate(used, own, maps, enter, gate_z, norm_gain, key_heads):
    prompts, tok, width = own.shape
    value_heads = width // DV
    group = value_heads // key_heads
    groups = prompts * key_heads
    wide = group * DV

    def rows_of(i, used):
        return (i // key_heads, 0, i % key_heads)

    return pl.pallas_call(
        functools.partial(gate_kernel, groups, group, tok // BLOCK),
        grid_spec=pltpu.PrefetchScalarGridSpec(
            num_scalar_prefetch=1,
            grid=(groups,),
            in_specs=[
                pl.BlockSpec((1, tok, wide), rows_of),
                pl.BlockSpec((1, tok, wide), rows_of),
                pl.BlockSpec((group, DK, DV), lambda i, used: (i, 0, 0)),
                pl.BlockSpec((1, tok, wide), rows_of),
                pl.BlockSpec((1, DV), lambda i, used: (0, 0)),
            ],
            out_specs=pl.BlockSpec((1, tok, wide), rows_of),
        ),
        out_shape=jax.ShapeDtypeStruct((prompts, tok, width), BF16),
        compiler_params=pltpu.CompilerParams(vmem_limit_bytes=VMEM_BYTES),
        name="gate",
    )(used, own, maps, enter, gate_z, norm_gain.reshape(1, DV))


def apply_map(trans, state):
    return jnp.einsum("nij,njv->niv", trans, state, preferred_element_type=F32)


def pair_swap(block):
    count = lax.axis_size("seq")
    return lax.ppermute(block, "seq", [(i, i ^ 1) for i in range(count)])


def from_chip_behind(block, distance, skip_first):
    count = lax.axis_size("seq")
    chips = count // 2
    route = [
        (i, ((i // 2 + distance) % chips) * 2 + i % 2)
        for i in range(count)
        if not (skip_first and i < 2)
    ]
    return lax.ppermute(block, "seq", route)


def across_seq(state, trans):
    chips = lax.axis_size("seq") // 2
    core = lax.axis_index("seq") % 2
    chip = lax.axis_index("seq") // 2
    odd = core == 1
    half = state.shape[0] // 2
    state_other, trans_other = pair_swap(state), pair_swap(trans)
    state_early = jnp.where(odd, state_other, state)
    state_late = jnp.where(odd, state, state_other)
    trans_early = jnp.where(odd, trans_other, trans)
    trans_late = jnp.where(odd, trans, trans_other)

    def mine(x):
        return lax.dynamic_slice_in_dim(x, core * half, half, 0)

    chip_state = (apply_map(mine(trans_late), mine(state_early)) + mine(state_late).astype(F32)).astype(BF16)
    chip_trans = apply_map(mine(trans_late), mine(trans_early)).astype(BF16)
    states, transes = [chip_state], [chip_trans]
    for k in range(1, chips):
        states.append(from_chip_behind(chip_state, k, False))
        transes.append(from_chip_behind(chip_trans, k, True))

    def of_chip(parts, j):
        value = parts[0]
        for k in range(1, chips):
            value = jnp.where((chip - k) % chips == j, parts[k], value)
        return value

    entering = jnp.zeros_like(chip_state)
    running = of_chip(states, 0).astype(F32)
    for j in range(1, chips):
        running_b = running.astype(BF16)
        entering = jnp.where(chip == j, running_b, entering)
        running = apply_map(of_chip(transes, j), running_b) + of_chip(states, j).astype(F32)
    both = jnp.stack([entering, running.astype(BF16)])
    other = pair_swap(both)
    both = jnp.concatenate([jnp.where(odd, other, both), jnp.where(odd, both, other)], axis=1)
    chip_enter, final = both[0], both[1]
    second = (apply_map(trans_early, chip_enter) + state_early.astype(F32)).astype(BF16)
    return jnp.where(odd, second, chip_enter), final


def shards(
    qk_in, v_in, gate_z, conv_qk, conv_v, log_decay, write_gain, norm_gain, prompt_lengths, placement,
):
    prompts, tok = qk_in.shape[:2]
    key_width = qk_in.shape[3]
    key_heads = key_width // DK
    value_heads = v_in.shape[2] // DV
    group = value_heads // key_heads
    chunks = tok // BLOCK
    rim = CONV - 1
    seq_count = lax.axis_size("seq")
    head_count = lax.axis_size("head")

    tails = jnp.concatenate(
        [qk_in[:, tok - rim :].reshape(prompts, rim, 2 * key_width), v_in[:, tok - rim :]], axis=2
    )
    arrived = lax.ppermute(tails, "seq", [(i, i + 1) for i in range(seq_count - 1)])
    halo = jnp.pad(arrived.astype(F32), ((0, 0), (8 - rim, 0), (0, 0)))
    q_halo = halo[:, :, :key_width]
    k_halo = halo[:, :, key_width : 2 * key_width]
    v_halo = halo[:, :, 2 * key_width :]
    taps = conv_qk.astype(F32)
    used = prompt_lengths - lax.axis_index("seq") * tok

    def by_block(x):
        return x.reshape(prompts, key_heads, group * chunks, BLOCK)

    log_rows, gain_rows = by_block(log_decay), by_block(write_gain)
    kn, wu, starts, state, trans = prepare(
        used, qk_in[:, :, 1], v_in, k_halo, v_halo, taps[:, 1], conv_v.astype(F32), log_rows, gain_rows
    )
    enter, final = across_seq(state, trans)
    own, maps = local_outputs(
        used, qk_in[:, :, 0], q_halo, taps[:, 0], kn, wu, starts, log_rows, gain_rows
    )
    attended = gate(used, own, maps, enter, gate_z, norm_gain, key_heads)
    final = final.reshape(prompts, value_heads, DK, DV)
    outgoing = jnp.take(final, placement[0], axis=0)
    rollout = lax.all_to_all(outgoing, "head", 0, 0).astype(F32)
    return attended, rollout.reshape(1, 1, head_count * value_heads, DK, DV)


def solution(mesh):
    return jax.shard_map(
        shards,
        mesh=mesh,
        in_specs=(
            P(None, "seq", None, "head"),
            P(None, "seq", "head"),
            P(None, "seq", "head"),
            P(None, None, "head"),
            P(None, "head"),
            P(None, "head", "seq"),
            P(None, "head", "seq"),
            P(),
            P(),
            P("seq", None),
        ),
        out_specs=(P(None, "seq", "head"), P("seq", "head", None, None, None)),
        check_vma=False,
    )
```

```python
import functools

import jax
import jax.numpy as jnp
from jax import lax
from jax.experimental import pallas as pl
from jax.experimental.pallas import tpu as pltpu
from jax.sharding import PartitionSpec as P

DK = 128
DV = 128
CONV = 4
BLOCK = 128
TINY = 16
EDGE = 8
EPSILON = 1e-06
VMEM_BYTES = 56 * 1024 * 1024
F32 = jnp.float32
BF16 = jnp.bfloat16


def dot(a, b):
    return lax.dot_general(a, b, (((1,), (0,)), ((), ())), preferred_element_type=F32)


def silu(x):
    half = 0.5 * x
    return half + half * jnp.tanh(half)


def load_padded(pad_ref, halo, raw_ref):
    rim = halo.shape[0]
    pad_ref[0:rim, :] = halo
    pad_ref[rim:, :] = raw_ref[0].astype(F32)


def mixed_rows(pad_ref, taps, rim, first, step, c):
    total = None
    for i in range(CONV):
        start = rim + first + step * (c * BLOCK + i - (CONV - 1))
        stride = None if step == 1 else step
        term = pad_ref[pl.ds(start, BLOCK, stride), :] * taps[i]
        total = term if total is None else total + term
    return silu(total)


def unit_rows(x):
    return x * lax.rsqrt(jnp.sum(x * x, axis=-1, keepdims=True) + EPSILON)


def heads_rows(ref, head, group):
    every = ref[0]
    rows = every[:group]
    for n in range(1, every.shape[0] // group):
        rows = jnp.where(head == n, every[n * group : (n + 1) * group], rows)
    return rows


def gates_of_heads(log_ref, gain_ref, used, head, group):
    log = heads_rows(log_ref, head, group)
    lane = lax.broadcasted_iota(jnp.int32, log.shape, 1)
    valid = lane < used
    cum = jnp.where(valid, log, 0.0)
    gain = jnp.where(valid, heads_rows(gain_ref, head, group), 0.0)
    shift = 1
    while shift < BLOCK:
        cum = cum + jnp.where(lane % BLOCK >= shift, pltpu.roll(cum, shift, 1), 0.0)
        shift *= 2
    return cum, gain


def as_columns(rows, chunks):
    parts = [rows[:, c * BLOCK : (c + 1) * BLOCK] for c in range(chunks)]
    short = BLOCK - 8 * chunks
    if short:
        parts.append(jnp.zeros((short, BLOCK), F32))
    return jnp.concatenate(parts, axis=0).T


def prepare_kernel(
    groups, group, chunks, key_heads,
    length_ref, qk_ref, v_ref, halo_ref, qk_taps_ref, v_taps_ref, log_ref, gain_ref,
    kn_ref, wu_ref, start_ref, state_ref, trans_ref,
    qk_pad, v_pad, halo_scr, taps_scr, m_scr, b_scr, fade_scr, st_scr, a_scr, x_scr,
):
    step = pl.program_id(0)
    now = jnp.minimum(step, groups - 1)
    prompt, head = now // key_heads, now % key_heads
    used = length_ref[prompt] - lax.axis_index("seq") * (chunks * BLOCK)
    units = [(h, c) for c in range(chunks) for h in range(group)]

    @pl.when(jnp.logical_and(step < groups, used <= 0))
    def _():
        kn_ref[...] = jnp.zeros_like(kn_ref)
        wu_ref[...] = jnp.zeros_like(wu_ref)
        for h, c in units:
            fade_scr[c, pl.ds(step * group + h, 1), :] = jnp.ones((1, BLOCK), F32)
            m_scr[c, step * group + h] = jnp.zeros((DK, DK), BF16)
            b_scr[c, step * group + h] = jnp.zeros((DK, DV), F32)

    @pl.when(jnp.logical_and(step < groups, used > 0))
    def _():
        @pl.when(head == 0)
        def _():
            halo = halo_ref[0].astype(F32)
            halo_scr[...] = halo
            taps_scr[...] = qk_taps_ref[...].astype(F32)
            load_padded(qk_pad, halo[: 2 * EDGE], qk_ref)

        v_pad[EDGE:, :] = v_ref[0].astype(F32)
        for i in range(CONV - 1):
            for h in range(group):
                source = 2 * EDGE + i * key_heads * group + head * group + h
                v_pad[EDGE - CONV + 1 + i : EDGE - CONV + 2 + i, h * DV : (h + 1) * DV] = halo_scr[
                    pl.ds(source, 1), :
                ]
        k_taps = [taps_scr[pl.ds(i * 2 * key_heads + 2 * head + 1, 1), :] for i in range(CONV)]
        v_all_taps = v_taps_ref[...].astype(F32)
        v_taps = [v_all_taps[i : i + 1] for i in range(CONV)]

        cum, gain = gates_of_heads(log_ref, gain_ref, used, head, group)
        faded = jnp.exp(cum)
        columns = as_columns(jnp.concatenate([cum, gain, gain * faded, faded], axis=0), chunks)

        def column(which, h, c):
            n = c * 8 + which * group + h
            return columns[:, n : n + 1]

        row = lax.broadcasted_iota(jnp.int32, (BLOCK, BLOCK), 0)
        lane = lax.broadcasted_iota(jnp.int32, (BLOCK, BLOCK), 1)
        below = row > lane
        small_row = lax.broadcasted_iota(jnp.int32, (TINY, BLOCK), 0)
        small_lane = lax.broadcasted_iota(jnp.int32, (TINY, BLOCK), 1)
        part_of = small_lane // TINY
        tiny_eye = jnp.where(small_row == small_lane % TINY, 1.0, 0.0).astype(F32)

        keys = []
        for c in range(chunks):
            kc = mixed_rows(qk_pad, k_taps, 2 * EDGE, 2 * head + 1, 2 * key_heads, c)
            kc = unit_rows(kc).astype(BF16)
            kn_ref[0, c * BLOCK : (c + 1) * BLOCK, :] = kc
            keys.append(kc)
        turned = [kc.T for kc in keys]

        compact = {}
        for c in range(chunks):
            kk = dot(keys[c], turned[c])
            for h in range(group):
                r = h * chunks + c
                span = slice(c * BLOCK, (c + 1) * BLOCK)
                ratio = jnp.exp(column(0, h, c) - cum[h : h + 1, span])
                strict = jnp.where(below, column(1, h, c) * ratio * kk, 0.0)
                a_scr[r] = strict.astype(BF16)
                tiny = strict[0:TINY]
                for b in range(1, BLOCK // TINY):
                    tiny = jnp.where(part_of == b, strict[b * TINY : (b + 1) * TINY], tiny)
                compact[r] = tiny

        solved = {r: tiny_eye for r in compact}
        for j in range(TINY - 1):
            pick = part_of * TINY + j
            for r in solved:
                factor = jnp.take_along_axis(compact[r], pick, axis=1, mode="promise_in_bounds")
                solved[r] = solved[r] - factor * solved[r][j : j + 1, :]
        for r in solved:
            for b in range(BLOCK // TINY):
                x_scr[r, b * TINY : (b + 1) * TINY, :] = jnp.where(
                    part_of == b, solved[r], 0.0
                ).astype(BF16)

        size = TINY
        while size < BLOCK:
            odd = [s for s in range(size, BLOCK, 2 * size)]
            half_lane = lax.broadcasted_iota(jnp.int32, (BLOCK // 2, BLOCK), 1)
            half_row = lax.broadcasted_iota(jnp.int32, (BLOCK // 2, BLOCK), 0)
            left = half_lane // size == 2 * (half_row // size)
            moved = {}
            for h, c in units:
                r = h * chunks + c
                lower = jnp.concatenate([a_scr[r, s : s + size, :] for s in odd], axis=0)
                lower = jnp.where(left, lower, jnp.zeros_like(lower))
                moved[r] = dot(lower, x_scr[r]).astype(BF16)
            for h, c in units:
                r = h * chunks + c
                spread = []
                for n in range(len(odd)):
                    spread.append(jnp.zeros((size, BLOCK), BF16))
                    spread.append(moved[r][n * size : (n + 1) * size])
                own = jnp.concatenate([x_scr[r, s : s + size, :] for s in odd], axis=0)
                update = own.astype(F32) - dot(own, jnp.concatenate(spread, axis=0))
                update = update.astype(BF16)
                for n, s in enumerate(odd):
                    x_scr[r, s : s + size, :] = update[n * size : (n + 1) * size]
            size *= 2

        for c in range(chunks):
            vc = mixed_rows(v_pad, v_taps, EDGE, 0, 1, c).astype(BF16).astype(F32)
            kc = keys[c].astype(F32)
            for h in range(group):
                r = h * chunks + c
                right = jnp.concatenate(
                    [
                        (kc * column(2, h, c)).astype(BF16),
                        (vc[:, h * DV : (h + 1) * DV] * column(1, h, c)).astype(BF16),
                    ],
                    axis=1,
                )
                wu_ref[0, r] = dot(x_scr[r], right).astype(BF16)
        for c in range(chunks):
            sums = cum[:, c * BLOCK : (c + 1) * BLOCK]
            last = sums[:, BLOCK - 1 : BLOCK]
            tail = jnp.exp(last - sums)
            fade = jnp.broadcast_to(jnp.exp(last), (group, BLOCK))
            for h in range(group):
                r = h * chunks + c
                fade_scr[c, pl.ds(step * group + h, 1), :] = fade[h : h + 1]
                scaled = (turned[c].astype(F32) * tail[h : h + 1, :]).astype(BF16)
                both = dot(scaled, wu_ref[0, r])
                m_scr[c, step * group + h] = (-both[:, :DK]).astype(BF16)
                b_scr[c, step * group + h] = both[:, DK:]

    @pl.when(step >= groups)
    def _():
        c = step - groups
        chains = groups * group

        @pl.when(c == 0)
        def _():
            row = lax.broadcasted_iota(jnp.int32, (DK, DV + DK), 0)
            lane = lax.broadcasted_iota(jnp.int32, (DK, DV + DK), 1)
            first = jnp.where(lane == row + DV, 1.0, 0.0).astype(F32)
            for n in range(chains):
                st_scr[n] = first

        fades = fade_scr[c]
        for low in range(0, chains, 4):
            some = range(low, low + 4)
            narrow = {}
            for n in some:
                narrow[n] = st_scr[n].astype(BF16)
                start_ref[0, n] = narrow[n]
            moved = {n: dot(m_scr[c, n], narrow[n]) for n in some}
            after = {}
            for n in some:
                fade = fades[n : n + 1, :]
                state = st_scr[n, :, :DV] * fade + (moved[n][:, :DV] + b_scr[c, n])
                trans = st_scr[n, :, DV:] * fade + moved[n][:, DV:]
                after[n] = state, trans
            for n in some:
                st_scr[n, :, :DV] = after[n][0]
                st_scr[n, :, DV:] = after[n][1]

        @pl.when(c == chunks - 1)
        def _():
            for n in range(chains):
                state_ref[n] = st_scr[n, :, :DV].astype(BF16)
                trans_ref[n] = st_scr[n, :, DV:].astype(BF16)


def prepare(lengths, qk_rows, v_in, halo, qk_taps, v_taps, log_decay, write_gain, key_heads):
    prompts, tok = v_in.shape[:2]
    value_heads = v_in.shape[2] // DV
    group = value_heads // key_heads
    groups = prompts * key_heads
    chunks = tok // BLOCK
    chains = groups * group
    rows = group * chunks
    wide = group * DV

    def prompt_of(i):
        return jnp.minimum(i, groups - 1) // key_heads

    def head_of(i):
        return jnp.minimum(i, groups - 1) % key_heads

    def rows_of(i, lengths):
        return (prompt_of(i), 0, head_of(i))

    def whole_of(i, lengths):
        return (prompt_of(i), 0, 0)

    return pl.pallas_call(
        functools.partial(prepare_kernel, groups, group, chunks, key_heads),
        grid_spec=pltpu.PrefetchScalarGridSpec(
            num_scalar_prefetch=1,
            grid=(groups + chunks,),
            in_specs=[
                pl.BlockSpec((1,) + qk_rows.shape[1:], whole_of),
                pl.BlockSpec((1, tok, wide), rows_of),
                pl.BlockSpec((1,) + halo.shape[1:], whole_of),
                pl.BlockSpec(qk_taps.shape, lambda i, lengths: (0, 0)),
                pl.BlockSpec((CONV, wide), lambda i, lengths: (0, head_of(i))),
                pl.BlockSpec((1, value_heads, tok), whole_of),
                pl.BlockSpec((1, value_heads, tok), whole_of),
            ],
            out_specs=[
                pl.BlockSpec((1, tok, DK), rows_of),
                pl.BlockSpec((1, rows, BLOCK, DK + DV), lambda i, lengths: (jnp.minimum(i, groups - 1), 0, 0, 0)),
                pl.BlockSpec((1, chains, DK, DV + DK), lambda i, lengths: (jnp.maximum(i - groups, 0), 0, 0, 0)),
                pl.BlockSpec((chains, DK, DV), lambda i, lengths: (0, 0, 0)),
                pl.BlockSpec((chains, DK, DK), lambda i, lengths: (0, 0, 0)),
            ],
            scratch_shapes=[
                pltpu.VMEM((qk_rows.shape[1] + 2 * EDGE, DK), F32),
                pltpu.VMEM((tok + EDGE, wide), F32),
                pltpu.VMEM(halo.shape[1:], F32),
                pltpu.VMEM(qk_taps.shape, F32),
                pltpu.VMEM((chunks, chains, DK, DK), BF16),
                pltpu.VMEM((chunks, chains, DK, DV), F32),
                pltpu.VMEM((chunks, chains, BLOCK), F32),
                pltpu.VMEM((chains, DK, DV + DK), F32),
                pltpu.VMEM((rows, BLOCK, BLOCK), BF16),
                pltpu.VMEM((rows, BLOCK, BLOCK), BF16),
            ],
        ),
        out_shape=[
            jax.ShapeDtypeStruct((prompts, tok, key_heads * DK), BF16),
            jax.ShapeDtypeStruct((groups, rows, BLOCK, DK + DV), BF16),
            jax.ShapeDtypeStruct((chunks, chains, DK, DV + DK), BF16),
            jax.ShapeDtypeStruct((chains, DK, DV), BF16),
            jax.ShapeDtypeStruct((chains, DK, DK), BF16),
        ],
        compiler_params=pltpu.CompilerParams(vmem_limit_bytes=VMEM_BYTES),
        cost_estimate=pl.CostEstimate(flops=40 * 10**9, bytes_accessed=28 * 2**20, transcendentals=10**7),
        name="prepare",
    )(lengths, qk_rows, v_in, halo, qk_taps, v_taps, log_decay, write_gain)


def outputs_kernel(
    groups, group, chunks, key_heads,
    length_ref, qk_ref, halo_ref, qk_taps_ref, kn_ref, wu_ref, start_ref, log_ref, gain_ref,
    own_ref, map_ref,
    qk_pad, taps_scr,
):
    step = pl.program_id(0)
    prompt, head = step // key_heads, step % key_heads
    used = length_ref[prompt] - lax.axis_index("seq") * (chunks * BLOCK)

    @pl.when(used <= 0)
    def _():
        own_ref[...] = jnp.zeros_like(own_ref)
        map_ref[...] = jnp.zeros_like(map_ref)

    @pl.when(used > 0)
    def _():
        @pl.when(head == 0)
        def _():
            taps_scr[...] = qk_taps_ref[...].astype(F32)
            load_padded(qk_pad, halo_ref[0].astype(F32)[: 2 * EDGE], qk_ref)

        q_taps = [taps_scr[pl.ds(i * 2 * key_heads + 2 * head, 1), :] for i in range(CONV)]
        cum, gain = gates_of_heads(log_ref, gain_ref, used, head, group)
        faded = jnp.exp(cum)
        columns = as_columns(jnp.concatenate([cum, faded, gain, gain], axis=0), chunks)

        def column(which, h, c):
            n = c * 8 + which * group + h
            return columns[:, n : n + 1]

        row = lax.broadcasted_iota(jnp.int32, (BLOCK, BLOCK), 0)
        lane = lax.broadcasted_iota(jnp.int32, (BLOCK, BLOCK), 1)
        upto = row >= lane
        for c in range(chunks):
            span = slice(c * BLOCK, (c + 1) * BLOCK)
            qc = mixed_rows(qk_pad, q_taps, 2 * EDGE, 2 * head, 2 * key_heads, c)
            qc = unit_rows(qc).astype(BF16)
            qk = dot(qc, kn_ref[0, span, :].T)
            q_wide = qc.astype(F32)
            for h in range(group):
                r = h * chunks + c
                ratio = jnp.exp(column(0, h, c) - cum[h : h + 1, span])
                scores = jnp.where(upto, ratio * qk, 0.0).astype(BF16)
                both = dot(scores, wu_ref[0, r])
                seen = (q_wide * column(1, h, c) - both[:, :DK]).astype(BF16)
                out = dot(seen, start_ref[c, h])
                cols = slice(h * DV, (h + 1) * DV)
                own_ref[0, span, cols] = (out[:, :DV] + both[:, DK:]).astype(BF16)
                map_ref[0, span, cols] = out[:, DV:].astype(BF16)


def local_outputs(lengths, qk_rows, halo, qk_taps, kn, wu, starts, log_decay, write_gain, key_heads):
    prompts, tok = kn.shape[:2]
    groups, rows = wu.shape[:2]
    chunks = tok // BLOCK
    group = rows // chunks
    wide = group * DV
    value_heads = key_heads * group

    def rows_of(i, lengths):
        return (i // key_heads, 0, i % key_heads)

    def whole_of(i, lengths):
        return (i // key_heads, 0, 0)

    return pl.pallas_call(
        functools.partial(outputs_kernel, groups, group, chunks, key_heads),
        grid_spec=pltpu.PrefetchScalarGridSpec(
            num_scalar_prefetch=1,
            grid=(groups,),
            in_specs=[
                pl.BlockSpec((1,) + qk_rows.shape[1:], whole_of),
                pl.BlockSpec((1,) + halo.shape[1:], whole_of),
                pl.BlockSpec(qk_taps.shape, lambda i, lengths: (0, 0)),
                pl.BlockSpec((1, tok, DK), rows_of),
                pl.BlockSpec((1, rows, BLOCK, DK + DV), lambda i, lengths: (i, 0, 0, 0)),
                pl.BlockSpec((chunks, group, DK, DV + DK), lambda i, lengths: (0, i, 0, 0)),
                pl.BlockSpec((1, value_heads, tok), whole_of),
                pl.BlockSpec((1, value_heads, tok), whole_of),
            ],
            out_specs=[
                pl.BlockSpec((1, tok, wide), rows_of),
                pl.BlockSpec((1, tok, wide), rows_of),
            ],
            scratch_shapes=[
                pltpu.VMEM((qk_rows.shape[1] + 2 * EDGE, DK), F32),
                pltpu.VMEM(qk_taps.shape, F32),
            ],
        ),
        out_shape=[
            jax.ShapeDtypeStruct((prompts, tok, value_heads * DV), BF16),
            jax.ShapeDtypeStruct((prompts, tok, value_heads * DV), BF16),
        ],
        compiler_params=pltpu.CompilerParams(vmem_limit_bytes=VMEM_BYTES),
        cost_estimate=pl.CostEstimate(flops=20 * 10**9, bytes_accessed=28 * 2**20, transcendentals=10**7),
        name="local_outputs",
    )(lengths, qk_rows, halo, qk_taps, kn, wu, starts, log_decay, write_gain)


def gate_kernel(group, chunks, key_heads, length_ref, own_ref, map_ref, enter_ref, z_ref, norm_ref, out_ref):
    used = length_ref[pl.program_id(0) // key_heads] - lax.axis_index("seq") * (chunks * BLOCK)

    @pl.when(used <= 0)
    def _():
        out_ref[...] = jnp.zeros_like(out_ref)

    @pl.when(used > 0)
    def _():
        row = lax.broadcasted_iota(jnp.int32, (BLOCK, DV), 0)
        norm_gain = norm_ref[...]
        for c in range(chunks):
            span = slice(c * BLOCK, (c + 1) * BLOCK)
            valid = row + c * BLOCK < used
            for h in range(group):
                cols = slice(h * DV, (h + 1) * DV)
                raw = own_ref[0, span, cols].astype(F32) + dot(map_ref[0, span, cols], enter_ref[h])
                mean = jnp.sum(raw * raw, axis=-1, keepdims=True) * (1.0 / DV)
                gated = raw * lax.rsqrt(mean + EPSILON) * norm_gain * silu(z_ref[0, span, cols].astype(F32))
                out_ref[0, span, cols] = jnp.where(valid, gated, 0.0).astype(BF16)


def gate(lengths, own, maps, enter, gate_z, norm_gain, key_heads):
    prompts, tok, width = own.shape
    value_heads = width // DV
    group = value_heads // key_heads
    groups = prompts * key_heads
    wide = group * DV

    def rows_of(i, lengths):
        return (i // key_heads, 0, i % key_heads)

    return pl.pallas_call(
        functools.partial(gate_kernel, group, tok // BLOCK, key_heads),
        grid_spec=pltpu.PrefetchScalarGridSpec(
            num_scalar_prefetch=1,
            grid=(groups,),
            in_specs=[
                pl.BlockSpec((1, tok, wide), rows_of),
                pl.BlockSpec((1, tok, wide), rows_of),
                pl.BlockSpec((group, DK, DV), lambda i, lengths: (i, 0, 0)),
                pl.BlockSpec((1, tok, wide), rows_of),
                pl.BlockSpec((1, DV), lambda i, lengths: (0, 0)),
            ],
            out_specs=pl.BlockSpec((1, tok, wide), rows_of),
        ),
        out_shape=jax.ShapeDtypeStruct((prompts, tok, width), BF16),
        compiler_params=pltpu.CompilerParams(vmem_limit_bytes=VMEM_BYTES),
        cost_estimate=pl.CostEstimate(flops=10 * 10**9, bytes_accessed=16 * 2**20, transcendentals=10**7),
        name="gate",
    )(lengths, own, maps, enter, gate_z, norm_gain.reshape(1, DV))


def apply_map(trans, state):
    return jnp.einsum("nij,njv->niv", trans, state, preferred_element_type=F32)


def pair_swap(block):
    count = lax.axis_size("seq")
    return lax.ppermute(block, "seq", [(i, i ^ 1) for i in range(count)])


def from_chip_behind(block, distance, skip_first):
    count = lax.axis_size("seq")
    chips = count // 2
    route = [
        (i, ((i // 2 + distance) % chips) * 2 + i % 2)
        for i in range(count)
        if not (skip_first and i < 2)
    ]
    return lax.ppermute(block, "seq", route)


def across_seq(state, trans, meanwhile):
    chips = lax.axis_size("seq") // 2
    core = lax.axis_index("seq") % 2
    chip = lax.axis_index("seq") // 2
    odd = core == 1
    half = state.shape[0] // 2
    state_other, trans_other = pair_swap(state), pair_swap(trans)
    state_early = jnp.where(odd, state_other, state)
    state_late = jnp.where(odd, state, state_other)
    trans_early = jnp.where(odd, trans_other, trans)
    trans_late = jnp.where(odd, trans, trans_other)

    def mine(x):
        return lax.dynamic_slice_in_dim(x, core * half, half, 0)

    chip_state = (apply_map(mine(trans_late), mine(state_early)) + mine(state_late).astype(F32)).astype(BF16)
    chip_trans = apply_map(mine(trans_late), mine(trans_early)).astype(BF16)
    states, transes = [chip_state], [chip_trans]
    for k in range(1, chips):
        states.append(from_chip_behind(chip_state, k, False))
        transes.append(from_chip_behind(chip_trans, k, True))
    beside = meanwhile(chip_state, chip_trans)
    states, transes, beside = lax.optimization_barrier((states, transes, beside))

    def of_chip(parts, j):
        value = parts[0]
        for k in range(1, chips):
            value = jnp.where((chip - k) % chips == j, parts[k], value)
        return value

    entering = jnp.zeros_like(chip_state)
    running = of_chip(states, 0).astype(F32)
    for j in range(1, chips):
        running_b = running.astype(BF16)
        entering = jnp.where(chip == j, running_b, entering)
        running = apply_map(of_chip(transes, j), running_b) + of_chip(states, j).astype(F32)
    both = jnp.stack([entering, running.astype(BF16)])
    other = pair_swap(both)
    both = jnp.concatenate([jnp.where(odd, other, both), jnp.where(odd, both, other)], axis=1)
    chip_enter, final = both[0], both[1]
    second = (apply_map(trans_early, chip_enter) + state_early.astype(F32)).astype(BF16)
    return jnp.where(odd, second, chip_enter), final, beside


def shards(
    qk_in, v_in, gate_z, conv_qk, conv_v, log_decay, write_gain, norm_gain, prompt_lengths, placement,
):
    prompts, tok = qk_in.shape[:2]
    key_heads = qk_in.shape[3] // DK
    value_heads = v_in.shape[2] // DV
    rim = CONV - 1
    seq_count = lax.axis_size("seq")
    head_count = lax.axis_size("head")

    def by_head(x):
        x = x.reshape(x.shape[0], x.shape[1], 2, key_heads, DK)
        return jnp.transpose(x, (0, 1, 3, 2, 4)).reshape(x.shape[0], -1, DK)

    qk_rows = by_head(qk_in)
    qk_taps = by_head(conv_qk[None])[0]
    qk_tail = qk_rows[:, (tok - rim) * 2 * key_heads :]
    v_tail = v_in[:, tok - rim :].reshape(prompts, rim * value_heads, DV)
    front = 2 * EDGE - qk_tail.shape[1]
    back = 2 * EDGE - v_tail.shape[1]
    tails = jnp.concatenate(
        [
            jnp.zeros((prompts, front, DK), BF16),
            qk_tail,
            v_tail,
            jnp.zeros((prompts, back, DK), BF16),
        ],
        axis=1,
    )
    halo = lax.ppermute(tails, "seq", [(i, i + 1) for i in range(seq_count - 1)])
    kn, wu, starts, state, trans = prepare(
        prompt_lengths, qk_rows, v_in, halo, qk_taps, conv_v, log_decay, write_gain, key_heads
    )

    def meanwhile(*ready):
        rows = lax.optimization_barrier((qk_rows, ready))[0]
        return local_outputs(
            prompt_lengths, rows, halo, qk_taps, kn, wu, starts, log_decay, write_gain, key_heads
        )

    enter, final, (own, maps) = across_seq(state, trans, meanwhile)
    attended = gate(prompt_lengths, own, maps, enter, gate_z, norm_gain, key_heads)
    final = final.reshape(prompts, value_heads, DK, DV)
    outgoing = jnp.take(final, placement[0], axis=0)
    rollout = lax.all_to_all(outgoing, "head", 0, 0).astype(F32)
    return attended, rollout.reshape(1, 1, head_count * value_heads, DK, DV)


def solution(mesh):
    return jax.shard_map(
        shards,
        mesh=mesh,
        in_specs=(
            P(None, "seq", None, "head"),
            P(None, "seq", "head"),
            P(None, "seq", "head"),
            P(None, None, "head"),
            P(None, "head"),
            P(None, "head", "seq"),
            P(None, "head", "seq"),
            P(),
            P(),
            P("seq", None),
        ),
        out_specs=(P(None, "seq", "head"), P("seq", "head", None, None, None)),
        check_vma=False,
    )
```

```python
import functools

import jax
import jax.numpy as jnp
from jax import lax
from jax.experimental import pallas as pl
from jax.experimental.pallas import tpu as pltpu
from jax.sharding import PartitionSpec as P

DK = 128
DV = 128
CONV = 4
BLOCK = 128
TINY = 16
EDGE = 8
EPSILON = 1e-06
VMEM_BYTES = 20 * 1024 * 1024
F32 = jnp.float32
BF16 = jnp.bfloat16


def dot(a, b):
    return lax.dot_general(a, b, (((1,), (0,)), ((), ())), preferred_element_type=F32)


def silu(x):
    half = 0.5 * x
    return half + half * jnp.tanh(half)


def load_padded(pad_ref, halo, raw_ref):
    rim = halo.shape[0]
    pad_ref[0:rim, :] = halo
    pad_ref[rim:, :] = raw_ref[0].astype(F32)


def mixed_rows(pad_ref, taps, rim, first, step, c):
    total = None
    for i in range(CONV):
        start = rim + first + step * (c * BLOCK + i - (CONV - 1))
        stride = None if step == 1 else step
        term = pad_ref[pl.ds(start, BLOCK, stride), :] * taps[i]
        total = term if total is None else total + term
    return silu(total)


def unit_rows(x):
    return x * lax.rsqrt(jnp.sum(x * x, axis=-1, keepdims=True) + EPSILON)


def heads_rows(ref, head, group):
    every = ref[0]
    rows = every[:group]
    for n in range(1, every.shape[0] // group):
        rows = jnp.where(head == n, every[n * group : (n + 1) * group], rows)
    return rows


def gates_of_heads(log_ref, gain_ref, used, head, group):
    log = heads_rows(log_ref, head, group)
    lane = lax.broadcasted_iota(jnp.int32, log.shape, 1)
    valid = lane < used
    cum = jnp.where(valid, log, 0.0)
    gain = jnp.where(valid, heads_rows(gain_ref, head, group), 0.0)
    shift = 1
    while shift < BLOCK:
        cum = cum + jnp.where(lane % BLOCK >= shift, pltpu.roll(cum, shift, 1), 0.0)
        shift *= 2
    return cum, gain


def as_columns(rows, chunks):
    parts = [rows[:, c * BLOCK : (c + 1) * BLOCK] for c in range(chunks)]
    short = BLOCK - 8 * chunks
    if short:
        parts.append(jnp.zeros((short, BLOCK), F32))
    return jnp.concatenate(parts, axis=0).T


def prepare_kernel(
    first, count, head, group, chunks, key_heads,
    length_ref, qk_ref, v_ref, halo_ref, qk_taps_ref, v_taps_ref, log_ref, gain_ref, after_ref,
    kn_ref, wu_ref, start_ref, state_ref, trans_ref,
    qk_pad, v_pad, halo_scr, m_scr, b_scr, fade_scr, st_scr, a_scr, x_scr,
):
    step = pl.program_id(0)
    used = length_ref[first + jnp.minimum(step, count - 1)] - lax.axis_index("seq") * (chunks * BLOCK)
    units = [(h, c) for c in range(chunks) for h in range(group)]
    slot = step % 2
    live = jnp.logical_and(step < count, used > 0)

    def begin():
        row = lax.broadcasted_iota(jnp.int32, (DK, DV + DK), 0)
        lane = lax.broadcasted_iota(jnp.int32, (DK, DV + DK), 1)
        for h in range(group):
            st_scr[h] = jnp.where(lane == row + DV, 1.0, 0.0).astype(F32)

    def advance(c):
        narrow, moved = [], []
        for h in range(group):
            narrow.append(st_scr[h].astype(BF16))
            start_ref[0, c, h] = narrow[h]
        for h in range(group):
            moved.append(dot(m_scr[1 - slot, c, h], narrow[h]))
        for h in range(group):
            fade = fade_scr[1 - slot, c, h : h + 1, :]
            state = st_scr[h, :, :DV] * fade + (moved[h][:, :DV] + b_scr[1 - slot, c, h])
            trans = st_scr[h, :, DV:] * fade + moved[h][:, DV:]
            if c < chunks - 1:
                st_scr[h, :, :DV] = state
                st_scr[h, :, DV:] = trans
            else:
                state_ref[h] = state.astype(BF16)
                trans_ref[h] = trans.astype(BF16)

    todo = [begin] + [functools.partial(advance, c) for c in range(chunks)]

    def run(n):
        for _ in range(min(n, len(todo))):
            todo.pop(0)()

    @pl.when(jnp.logical_not(live))
    def _():
        @pl.when(step > 0)
        def _():
            begin()
            for c in range(chunks):
                advance(c)

        @pl.when(step < count)
        def _():
            kn_ref[...] = jnp.zeros_like(kn_ref)
            wu_ref[...] = jnp.zeros_like(wu_ref)
            fade_scr[slot] = jnp.ones(fade_scr.shape[1:], F32)
            m_scr[slot] = jnp.zeros(m_scr.shape[1:], BF16)
            b_scr[slot] = jnp.zeros(b_scr.shape[1:], F32)

    @pl.when(live)
    def _():
        halo = halo_ref[0].astype(F32)
        halo_scr[...] = halo
        load_padded(qk_pad, halo[: 2 * EDGE], qk_ref)
        v_pad[EDGE:, :] = v_ref[0].astype(F32)
        for i in range(CONV - 1):
            for h in range(group):
                source = 2 * EDGE + (i * key_heads + head) * group + h
                v_pad[EDGE - CONV + 1 + i : EDGE - CONV + 2 + i, h * DV : (h + 1) * DV] = halo_scr[
                    source : source + 1, :
                ]
        all_taps = qk_taps_ref[...].astype(F32)
        k_taps = [all_taps[n : n + 1] for n in range(2 * head + 1, all_taps.shape[0], 2 * key_heads)]
        v_all_taps = v_taps_ref[...].astype(F32)
        v_taps = [v_all_taps[i : i + 1] for i in range(CONV)]
        run(1)

        cum, gain = gates_of_heads(log_ref, gain_ref, used, head, group)
        faded = jnp.exp(cum)
        columns = as_columns(jnp.concatenate([cum, gain, gain * faded, faded], axis=0), chunks)

        def column(which, h, c):
            n = c * 8 + which * group + h
            return columns[:, n : n + 1]

        row = lax.broadcasted_iota(jnp.int32, (BLOCK, BLOCK), 0)
        lane = lax.broadcasted_iota(jnp.int32, (BLOCK, BLOCK), 1)
        below = row > lane
        small_row = lax.broadcasted_iota(jnp.int32, (TINY, BLOCK), 0)
        small_lane = lax.broadcasted_iota(jnp.int32, (TINY, BLOCK), 1)
        part_of = small_lane // TINY
        tiny_eye = jnp.where(small_row == small_lane % TINY, 1.0, 0.0).astype(F32)

        keys = []
        for c in range(chunks):
            kc = mixed_rows(qk_pad, k_taps, 2 * EDGE, 2 * head + 1, 2 * key_heads, c)
            kc = unit_rows(kc).astype(BF16)
            kn_ref[0, c * BLOCK : (c + 1) * BLOCK, :] = kc
            keys.append(kc)
        turned = [kc.T for kc in keys]
        run(1)

        compact = {}
        for c in range(chunks):
            kk = dot(keys[c], turned[c])
            for h in range(group):
                r = h * chunks + c
                span = slice(c * BLOCK, (c + 1) * BLOCK)
                ratio = jnp.exp(column(0, h, c) - cum[h : h + 1, span])
                strict = jnp.where(below, column(1, h, c) * ratio * kk, 0.0)
                a_scr[r] = strict.astype(BF16)
                tiny = strict[0:TINY]
                for b in range(1, BLOCK // TINY):
                    tiny = jnp.where(part_of == b, strict[b * TINY : (b + 1) * TINY], tiny)
                compact[r] = tiny

        run(1)
        solved = {r: tiny_eye for r in compact}
        for j in range(TINY - 1):
            pick = part_of * TINY + j
            for r in solved:
                factor = jnp.take_along_axis(compact[r], pick, axis=1, mode="promise_in_bounds")
                solved[r] = solved[r] - factor * solved[r][j : j + 1, :]
        for r in solved:
            for b in range(BLOCK // TINY):
                x_scr[r, b * TINY : (b + 1) * TINY, :] = jnp.where(
                    part_of == b, solved[r], 0.0
                ).astype(BF16)

        run(1)
        size = TINY
        while size < BLOCK:
            odd = [s for s in range(size, BLOCK, 2 * size)]
            half_lane = lax.broadcasted_iota(jnp.int32, (BLOCK // 2, BLOCK), 1)
            half_row = lax.broadcasted_iota(jnp.int32, (BLOCK // 2, BLOCK), 0)
            left = half_lane // size == 2 * (half_row // size)
            moved = {}
            for h, c in units:
                r = h * chunks + c
                lower = jnp.concatenate([a_scr[r, s : s + size, :] for s in odd], axis=0)
                lower = jnp.where(left, lower, jnp.zeros_like(lower))
                moved[r] = dot(lower, x_scr[r]).astype(BF16)
            for h, c in units:
                r = h * chunks + c
                spread = []
                for n in range(len(odd)):
                    spread.append(jnp.zeros((size, BLOCK), BF16))
                    spread.append(moved[r][n * size : (n + 1) * size])
                own = jnp.concatenate([x_scr[r, s : s + size, :] for s in odd], axis=0)
                update = own.astype(F32) - dot(own, jnp.concatenate(spread, axis=0))
                update = update.astype(BF16)
                for n, s in enumerate(odd):
                    x_scr[r, s : s + size, :] = update[n * size : (n + 1) * size]
            run(1)
            size *= 2

        for c in range(chunks):
            vc = mixed_rows(v_pad, v_taps, EDGE, 0, 1, c).astype(BF16).astype(F32)
            kc = keys[c].astype(F32)
            for h in range(group):
                r = h * chunks + c
                right = jnp.concatenate(
                    [
                        (kc * column(2, h, c)).astype(BF16),
                        (vc[:, h * DV : (h + 1) * DV] * column(1, h, c)).astype(BF16),
                    ],
                    axis=1,
                )
                wu_ref[0, r] = dot(x_scr[r], right).astype(BF16)
            if c == chunks // 2:
                run(1)
        run(len(todo))
        for c in range(chunks):
            sums = cum[:, c * BLOCK : (c + 1) * BLOCK]
            last = sums[:, BLOCK - 1 : BLOCK]
            tail = jnp.exp(last - sums)
            fade = jnp.broadcast_to(jnp.exp(last), (group, BLOCK))
            for h in range(group):
                r = h * chunks + c
                fade_scr[slot, c, h : h + 1, :] = fade[h : h + 1]
                scaled = (turned[c].astype(F32) * tail[h : h + 1, :]).astype(BF16)
                both = dot(scaled, wu_ref[0, r])
                m_scr[slot, c, h] = (-both[:, :DK]).astype(BF16)
                b_scr[slot, c, h] = both[:, DK:]


def prepare(job, lengths, qk_rows, v_in, halo, qk_taps, v_taps, log_decay, write_gain, key_heads, after):
    head, first, count = job
    tok = v_in.shape[1]
    value_heads = v_in.shape[2] // DV
    group = value_heads // key_heads
    chunks = tok // BLOCK
    rows = group * chunks
    wide = group * DV

    def now(i):
        return jnp.minimum(i, count - 1)

    def before(i):
        return jnp.maximum(i - 1, 0)

    def whole_of(i, lengths):
        return (first + now(i), 0, 0)

    return pl.pallas_call(
        functools.partial(prepare_kernel, first, count, head, group, chunks, key_heads),
        grid_spec=pltpu.PrefetchScalarGridSpec(
            num_scalar_prefetch=1,
            grid=(count + 1,),
            in_specs=[
                pl.BlockSpec((1,) + qk_rows.shape[1:], whole_of),
                pl.BlockSpec((1, tok, wide), lambda i, lengths: (first + now(i), 0, head)),
                pl.BlockSpec((1,) + halo.shape[1:], whole_of),
                pl.BlockSpec(qk_taps.shape, lambda i, lengths: (0, 0)),
                pl.BlockSpec((CONV, wide), lambda i, lengths: (0, head)),
                pl.BlockSpec((1, value_heads, tok), whole_of),
                pl.BlockSpec((1, value_heads, tok), whole_of),
                pl.BlockSpec(memory_space=pl.ANY),
            ],
            out_specs=[
                pl.BlockSpec((1, tok, DK), lambda i, lengths: (now(i), 0, 0)),
                pl.BlockSpec((1, rows, BLOCK, DK + DV), lambda i, lengths: (now(i), 0, 0, 0)),
                pl.BlockSpec((1, chunks, group, DK, DV + DK), lambda i, lengths: (before(i), 0, 0, 0, 0)),
                pl.BlockSpec((group, DK, DV), lambda i, lengths: (before(i), 0, 0)),
                pl.BlockSpec((group, DK, DK), lambda i, lengths: (before(i), 0, 0)),
            ],
            scratch_shapes=[
                pltpu.VMEM((qk_rows.shape[1] + 2 * EDGE, DK), F32),
                pltpu.VMEM((tok + EDGE, wide), F32),
                pltpu.VMEM(halo.shape[1:], F32),
                pltpu.VMEM((2, chunks, group, DK, DK), BF16),
                pltpu.VMEM((2, chunks, group, DK, DV), F32),
                pltpu.VMEM((2, chunks, group, BLOCK), F32),
                pltpu.VMEM((group, DK, DV + DK), F32),
                pltpu.VMEM((rows, BLOCK, BLOCK), BF16),
                pltpu.VMEM((rows, BLOCK, BLOCK), BF16),
            ],
        ),
        out_shape=[
            jax.ShapeDtypeStruct((count, tok, DK), BF16),
            jax.ShapeDtypeStruct((count, rows, BLOCK, DK + DV), BF16),
            jax.ShapeDtypeStruct((count, chunks, group, DK, DV + DK), BF16),
            jax.ShapeDtypeStruct((count * group, DK, DV), BF16),
            jax.ShapeDtypeStruct((count * group, DK, DK), BF16),
        ],
        compiler_params=pltpu.CompilerParams(vmem_limit_bytes=VMEM_BYTES),
        cost_estimate=pl.CostEstimate(flops=5 * 10**9 * count, bytes_accessed=4 * 2**20 * count, transcendentals=10**6),
        name="prepare",
    )(lengths, qk_rows, v_in, halo, qk_taps, v_taps, log_decay, write_gain, after)


def outputs_kernel(
    first, head, group, chunks, key_heads,
    length_ref, qk_ref, halo_ref, qk_taps_ref, kn_ref, wu_ref, start_ref, log_ref, gain_ref,
    enter_ref, z_ref, norm_ref, held_ref, after_ref,
    out_ref,
    qk_pad,
):
    used = length_ref[first + pl.program_id(0)] - lax.axis_index("seq") * (chunks * BLOCK)

    @pl.when(used <= 0)
    def _():
        out_ref[...] = jnp.zeros_like(out_ref)

    @pl.when(used > 0)
    def _():
        load_padded(qk_pad, halo_ref[0].astype(F32)[: 2 * EDGE], qk_ref)
        all_taps = qk_taps_ref[...].astype(F32)
        q_taps = [all_taps[n : n + 1] for n in range(2 * head, all_taps.shape[0], 2 * key_heads)]
        cum, gain = gates_of_heads(log_ref, gain_ref, used, head, group)
        faded = jnp.exp(cum)
        columns = as_columns(jnp.concatenate([cum, faded, gain, gain], axis=0), chunks)

        def column(which, h, c):
            n = c * 8 + which * group + h
            return columns[:, n : n + 1]

        row = lax.broadcasted_iota(jnp.int32, (BLOCK, BLOCK), 0)
        lane = lax.broadcasted_iota(jnp.int32, (BLOCK, BLOCK), 1)
        upto = row >= lane
        norm_gain = norm_ref[...]
        for c in range(chunks):
            span = slice(c * BLOCK, (c + 1) * BLOCK)
            qc = mixed_rows(qk_pad, q_taps, 2 * EDGE, 2 * head, 2 * key_heads, c)
            qc = unit_rows(qc).astype(BF16)
            qk = dot(qc, kn_ref[0, span, :].T)
            q_wide = qc.astype(F32)
            valid = row + c * BLOCK < used
            for h in range(group):
                r = h * chunks + c
                cols = slice(h * DV, (h + 1) * DV)
                first_state = dot(start_ref[0, c, h, :, DV:], enter_ref[h])
                first_state = (first_state + start_ref[0, c, h, :, :DV].astype(F32)).astype(BF16)
                ratio = jnp.exp(column(0, h, c) - cum[h : h + 1, span])
                scores = jnp.where(upto, ratio * qk, 0.0).astype(BF16)
                both = dot(scores, wu_ref[0, r])
                seen = (q_wide * column(1, h, c) - both[:, :DK]).astype(BF16)
                raw = dot(seen, first_state) + both[:, DK:]
                mean = jnp.sum(raw * raw, axis=-1, keepdims=True) * (1.0 / DV)
                gated = raw * lax.rsqrt(mean + EPSILON) * norm_gain * silu(z_ref[0, span, cols].astype(F32))
                out_ref[0, span, cols] = jnp.where(valid, gated, 0.0).astype(BF16)


def outputs(
    job, piece, lengths, qk_rows, halo, qk_taps, kn, wu, starts, log_decay, write_gain, enter, gate_z, norm_gain,
    key_heads, held, after,
):
    head, first, _ = job
    begin, count = piece
    prompts, tok, width = gate_z.shape
    rows = wu.shape[1]
    chunks = tok // BLOCK
    group = rows // chunks
    wide = group * DV
    value_heads = key_heads * group
    shift = begin - first

    def whole_of(i, lengths):
        return (begin + i, 0, 0)

    def wide_of(i, lengths):
        return (begin + i, 0, head)

    empty = held is None
    return pl.pallas_call(
        functools.partial(outputs_kernel, begin, head, group, chunks, key_heads),
        grid_spec=pltpu.PrefetchScalarGridSpec(
            num_scalar_prefetch=1,
            grid=(count,),
            in_specs=[
                pl.BlockSpec((1,) + qk_rows.shape[1:], whole_of),
                pl.BlockSpec((1,) + halo.shape[1:], whole_of),
                pl.BlockSpec(qk_taps.shape, lambda i, lengths: (0, 0)),
                pl.BlockSpec((1, tok, DK), lambda i, lengths: (shift + i, 0, 0)),
                pl.BlockSpec((1, rows, BLOCK, DK + DV), lambda i, lengths: (shift + i, 0, 0, 0)),
                pl.BlockSpec((1, chunks, group, DK, DV + DK), lambda i, lengths: (shift + i, 0, 0, 0, 0)),
                pl.BlockSpec((1, value_heads, tok), whole_of),
                pl.BlockSpec((1, value_heads, tok), whole_of),
                pl.BlockSpec((group, DK, DV), lambda i, lengths: (shift + i, 0, 0)),
                pl.BlockSpec((1, tok, wide), wide_of),
                pl.BlockSpec((1, DV), lambda i, lengths: (0, 0)),
                pl.BlockSpec(memory_space=pl.ANY),
                pl.BlockSpec(memory_space=pl.ANY),
            ],
            out_specs=pl.BlockSpec((1, tok, wide), wide_of),
            scratch_shapes=[pltpu.VMEM((qk_rows.shape[1] + 2 * EDGE, DK), F32)],
        ),
        out_shape=jax.ShapeDtypeStruct((prompts, tok, width), BF16),
        input_output_aliases={} if empty else {12: 0},
        compiler_params=pltpu.CompilerParams(vmem_limit_bytes=VMEM_BYTES),
        cost_estimate=pl.CostEstimate(flops=3 * 10**9 * count, bytes_accessed=4 * 2**20 * count, transcendentals=10**6),
        name="outputs",
    )(
        lengths, qk_rows, halo, qk_taps, kn, wu, starts, log_decay, write_gain, enter, gate_z,
        norm_gain.reshape(1, DV), after if empty else held, lengths if after is held else after,
    )


def own_chip():
    seq = lax.axis_index("seq")
    return seq // 2, seq % 2 == 1


def early_late(own, other, odd):
    return jnp.where(odd, other, own), jnp.where(odd, own, other)


def compose_maps(ins, outs):
    state_ref, trans_ref, state_other_ref, trans_other_ref = ins
    _, odd = own_chip()
    for n in range(state_ref.shape[0]):
        state_early, state_late = early_late(state_ref[n], state_other_ref[n], odd)
        trans_early, trans_late = early_late(trans_ref[n], trans_other_ref[n], odd)
        both = dot(trans_late, jnp.concatenate([state_early, trans_early], axis=1))
        outs[0][n] = (both[:, :DV] + state_late.astype(F32)).astype(BF16)
        outs[1][n] = both[:, DV:].astype(BF16)


def close_maps(chips, ins, outs):
    state_ref, trans_ref, state_other_ref, trans_other_ref = ins[:4]
    states, transes = ins[4 : 4 + chips], ins[4 + chips :]
    chip, odd = own_chip()

    def of_chip(refs, j, n):
        value = refs[0][n]
        for k in range(1, chips):
            value = jnp.where((chip + chips - k) % chips == j, refs[k][n], value)
        return value

    for n in range(state_ref.shape[0]):
        running = of_chip(states, 0, n)
        entering = jnp.zeros_like(running)
        for j in range(1, chips):
            entering = jnp.where(chip == j, running, entering)
            running = dot(of_chip(transes, j, n), running) + of_chip(states, j, n).astype(F32)
            running = running.astype(BF16)
        state_early, _ = early_late(state_ref[n], state_other_ref[n], odd)
        trans_early, _ = early_late(trans_ref[n], trans_other_ref[n], odd)
        second = (dot(trans_early, entering) + state_early.astype(F32)).astype(BF16)
        outs[0][n] = jnp.where(odd, second, entering)
        outs[1][n] = running


def choose_finals(group, placement_ref, finals, outs):
    refs = [(ref, n) for ref in finals for n in range(ref.shape[0] // group)]
    for r in range(placement_ref.shape[1]):
        prompt = placement_ref[0, r]
        for p, (ref, n) in enumerate(refs):
            @pl.when(prompt == p)
            def _(ref=ref, n=n):
                outs[0][r] = ref[n * group : (n + 1) * group]


def state_step(placement, group, compose, close, earlier, after):
    operands, shapes = [placement], []
    steps = []
    if compose is not None:
        steps.append(("compose", len(operands), len(compose), len(shapes)))
        operands += compose
        shapes += [compose[0], compose[1]]
    if close is not None:
        steps.append(("close", len(operands), len(close), len(shapes)))
        operands += close
        shapes += [close[0], close[0]]
        if earlier is not None:
            steps.append(("choose", len(operands), len(earlier), len(shapes)))
            operands += earlier
            shapes.append(jax.ShapeDtypeStruct((placement.shape[1], group, DK, DV), BF16))
    out_shape = [jax.ShapeDtypeStruct(x.shape, x.dtype) for x in shapes]

    def kernel(*refs):
        ins, outs = refs[: len(operands)], refs[len(operands) + 1 :]
        closed = None
        for kind, at, size, to in steps:
            part = ins[at : at + size]
            if kind == "compose":
                compose_maps(part, outs[to : to + 2])
            elif kind == "close":
                close_maps((size - 4) // 2, part, outs[to : to + 2])
                closed = outs[to + 1]
            else:
                choose_finals(group, ins[0], list(part) + [closed], outs[to:])

    vmem = pl.BlockSpec(memory_space=pltpu.VMEM)
    return pl.pallas_call(
        kernel,
        in_specs=[pl.BlockSpec(memory_space=pltpu.SMEM)]
        + [vmem] * (len(operands) - 1)
        + [pl.BlockSpec(memory_space=pl.ANY)],
        out_specs=[vmem] * len(out_shape),
        out_shape=out_shape,
        compiler_params=pltpu.CompilerParams(vmem_limit_bytes=VMEM_BYTES),
        cost_estimate=pl.CostEstimate(flops=10**9, bytes_accessed=2**20, transcendentals=0),
        name="state_step",
    )(*operands, after)


def deliver(parts):
    count, group = parts[0].shape[:2]

    def kernel(*refs):
        for n, ref in enumerate(refs[:-1]):
            refs[-1][0, n * group : (n + 1) * group] = ref[0].astype(F32)

    return pl.pallas_call(
        kernel,
        grid=(count,),
        in_specs=[pl.BlockSpec((1, group, DK, DV), lambda i: (i, 0, 0, 0))] * len(parts),
        out_specs=pl.BlockSpec((1, group * len(parts), DK, DV), lambda i: (i, 0, 0, 0)),
        out_shape=jax.ShapeDtypeStruct((count, group * len(parts), DK, DV), F32),
        compiler_params=pltpu.CompilerParams(vmem_limit_bytes=VMEM_BYTES),
        name="deliver",
    )(*parts)


def pair_swap(block):
    count = lax.axis_size("seq")
    return lax.ppermute(block, "seq", [(i, i ^ 1) for i in range(count)])


def from_chip_behind(block, distance, skip_first):
    count = lax.axis_size("seq")
    chips = count // 2
    route = [
        (i, ((i // 2 + distance) % chips) * 2 + i % 2)
        for i in range(count)
        if not (skip_first and i < 2)
    ]
    return lax.ppermute(block, "seq", route)


def shards(
    qk_in, v_in, gate_z, conv_qk, conv_v, log_decay, write_gain, norm_gain, prompt_lengths, placement,
):
    prompts, tok = qk_in.shape[:2]
    key_heads = qk_in.shape[3] // DK
    value_heads = v_in.shape[2] // DV
    rim = CONV - 1
    seq_count = lax.axis_size("seq")
    head_count = lax.axis_size("head")

    def by_head(x):
        x = x.reshape(x.shape[0], x.shape[1], 2, key_heads, DK)
        return jnp.transpose(x, (0, 1, 3, 2, 4)).reshape(x.shape[0], -1, DK)

    qk_rows = by_head(qk_in)
    qk_taps = by_head(conv_qk[None])[0]
    qk_tail = qk_rows[:, (tok - rim) * 2 * key_heads :]
    v_tail = v_in[:, tok - rim :].reshape(prompts, rim * value_heads, DV)
    front = 2 * EDGE - qk_tail.shape[1]
    back = 2 * EDGE - v_tail.shape[1]
    tails = jnp.concatenate(
        [
            jnp.zeros((prompts, front, DK), BF16),
            qk_tail,
            v_tail,
            jnp.zeros((prompts, back, DK), BF16),
        ],
        axis=1,
    )
    halo = lax.ppermute(tails, "seq", [(i, i + 1) for i in range(seq_count - 1)])
    group = value_heads // key_heads
    chips = seq_count // 2
    half = prompts // 2
    jobs = [(head, 0, prompts) for head in range(key_heads - 1)]
    jobs += [(key_heads - 1, 0, half), (key_heads - 1, half, prompts - half)]
    total = len(jobs)

    made, maps, chip_maps, entered, finals, sent = {}, {}, {}, {}, {}, {}
    waiting = []
    attended = None
    last = v_in

    def emit(attended, last):
        job, piece = waiting.pop(0)
        kn, wu, starts = made[job]
        attended = outputs(
            jobs[job], piece, prompt_lengths, qk_rows, halo, qk_taps, kn, wu, starts, log_decay, write_gain,
            entered[job], gate_z, norm_gain, key_heads, attended, last,
        )
        return attended, attended

    for t in range(total + 2):
        if t < total:
            kn, wu, starts, state, trans = prepare(
                jobs[t], prompt_lengths, qk_rows, v_in, halo, qk_taps, conv_v, log_decay, write_gain, key_heads, last
            )
            made[t] = kn, wu, starts
            maps[t] = [state, trans, pair_swap(state), pair_swap(trans)]
            last = state
        elif waiting:
            attended, last = emit(attended, last)
        compose = maps[t - 1] if 0 <= t - 1 < total else None
        close, earlier = None, None
        if 0 <= t - 2 < total:
            close = maps[t - 2] + chip_maps[t - 2]
            head = jobs[t - 2][0]
            if t - 2 == max(n for n in range(total) if jobs[n][0] == head):
                earlier = [finals[n] for n in range(t - 2) if jobs[n][0] == head]
        if compose is None and close is None:
            continue
        results = state_step(placement, group, compose, close, earlier, last)
        last = results[0]
        if compose is not None:
            state, trans = results[:2]
            results = results[2:]
            states, transes = [state], [trans]
            for k in range(1, chips):
                states.append(from_chip_behind(state, k, False))
                transes.append(from_chip_behind(trans, k, True))
            chip_maps[t - 1] = states + transes
        if close is not None:
            entered[t - 2], finals[t - 2] = results[:2]
            if earlier is not None:
                sent[jobs[t - 2][0]] = lax.all_to_all(results[2], "head", 0, 0)
            _, begin, count = jobs[t - 2]
            while count > 0:
                waiting.append((t - 2, (begin, min(half, count))))
                begin, count = begin + half, count - half
    while waiting:
        attended, last = emit(attended, last)
    rollout = deliver([sent[head] for head in range(key_heads)])
    return attended, rollout.reshape(1, 1, head_count * value_heads, DK, DV)


def solution(mesh):
    return jax.shard_map(
        shards,
        mesh=mesh,
        in_specs=(
            P(None, "seq", None, "head"),
            P(None, "seq", "head"),
            P(None, "seq", "head"),
            P(None, None, "head"),
            P(None, "head"),
            P(None, "head", "seq"),
            P(None, "head", "seq"),
            P(),
            P(),
            P("seq", None),
        ),
        out_specs=(P(None, "seq", "head"), P("seq", "head", None, None, None)),
        check_vma=False,
    )
```

```python
import functools

import jax
import jax.numpy as jnp
from jax import lax
from jax.experimental import pallas as pl
from jax.experimental.pallas import tpu as pltpu
from jax.sharding import PartitionSpec as P

DK = 128
DV = 128
CONV = 4
BLOCK = 128
TINY = 16
EDGE = 8
HALF = BLOCK // 2
EPSILON = 1e-06
VMEM_BYTES = 56 * 1024 * 1024
F32 = jnp.float32
BF16 = jnp.bfloat16


def dot(a, b):
    return lax.dot_general(a, b, (((1,), (0,)), ((), ())), preferred_element_type=F32)


def silu(x):
    half = 0.5 * x
    return half + half * jnp.tanh(half)


def mixed_rows(pad_ref, taps, c, columns):
    total = None
    for i in range(CONV):
        start = EDGE - (CONV - 1) + i + c * BLOCK
        term = pad_ref[start : start + BLOCK, columns] * taps[i]
        total = term if total is None else total + term
    return silu(total)


def unit_rows(x):
    return x * lax.rsqrt(jnp.sum(x * x, axis=-1, keepdims=True) + EPSILON)


def heads_rows(ref, head, group):
    every = ref[0]
    rows = every[:group]
    for n in range(1, every.shape[0] // group):
        rows = jnp.where(head == n, every[n * group : (n + 1) * group], rows)
    return rows


def gates_of_heads(log_ref, gain_ref, used, head, group):
    log = heads_rows(log_ref, head, group)
    lane = lax.broadcasted_iota(jnp.int32, log.shape, 1)
    valid = lane < used
    cum = jnp.where(valid, log, 0.0)
    gain = jnp.where(valid, heads_rows(gain_ref, head, group), 0.0)
    shift = 1
    while shift < BLOCK:
        cum = cum + jnp.where(lane % BLOCK >= shift, pltpu.roll(cum, shift, 1), 0.0)
        shift *= 2
    return cum, gain


def as_columns(rows, chunks):
    parts = [rows[:, c * BLOCK : (c + 1) * BLOCK] for c in range(chunks)]
    short = BLOCK - 8 * chunks
    if short:
        parts.append(jnp.zeros((short, BLOCK), F32))
    return jnp.concatenate(parts, axis=0).T


def mix(qk_ref, halo_ref, taps_ref, qn_ref, kn_ref, raw_scr, dense_scr, key_heads, chunks):
    kinds = 2 * key_heads
    tok = chunks * BLOCK
    halo = halo_ref[0].astype(F32)
    taps = taps_ref[...].astype(F32)
    raw_scr[...] = qk_ref[0].astype(F32)
    for kind in range(kinds):
        columns = slice(kind * DK, (kind + 1) * DK)
        for i in range(1, CONV):
            source = 2 * EDGE - i * kinds + kind
            dense_scr[EDGE - i : EDGE - i + 1, columns] = halo[source : source + 1]
        dense_scr[EDGE:, columns] = raw_scr[pl.ds(kind, tok, kinds), :]
    for c in range(chunks):
        span = slice(c * BLOCK, (c + 1) * BLOCK)
        for kind in range(kinds):
            own = [taps[n : n + 1] for n in range(kind, taps.shape[0], kinds)]
            rows = unit_rows(mixed_rows(dense_scr, own, c, slice(kind * DK, (kind + 1) * DK)))
            to_ref = kn_ref if kind % 2 else qn_ref
            to_ref[0, span, kind // 2 * DK : (kind // 2 + 1) * DK] = rows.astype(BF16)


def prepare_kernel(first, count, head, group, chunks, key_heads, mixes, *refs):
    length_ref, v_ref, halo_ref, v_taps_ref, log_ref, gain_ref, after_ref = refs[:7]
    refs = refs[7:]
    if mixes:
        qk_ref, qk_taps_ref, wu_ref, start_ref, map_ref, qn_ref, kn_ref = refs[:7]
        v_pad, m_scr, b_scr, fade_scr, st_scr, a_scr, x_scr, raw_scr, dense_scr = refs[7:]
        key_columns = slice(head * DK, (head + 1) * DK)
    else:
        kn_ref, wu_ref, start_ref, map_ref = refs[:4]
        v_pad, m_scr, b_scr, fade_scr, st_scr, a_scr, x_scr = refs[4:]
        key_columns = slice(0, DK)
    step = pl.program_id(0)
    used = length_ref[first + jnp.minimum(step, count - 1)] - lax.axis_index("seq") * (chunks * BLOCK)
    units = [(h, c) for c in range(chunks) for h in range(group)]
    slot = step % 2
    live = jnp.logical_and(step < count, used > 0)

    def begin():
        row = lax.broadcasted_iota(jnp.int32, (DK, DV + DK), 0)
        lane = lax.broadcasted_iota(jnp.int32, (DK, DV + DK), 1)
        for h in range(group):
            st_scr[h] = jnp.where(lane == row + DV, 1.0, 0.0).astype(F32)

    def advance(c):
        narrow, moved = [], []
        for h in range(group):
            narrow.append(st_scr[h].astype(BF16))
            start_ref[0, h, c * DK : (c + 1) * DK, :] = narrow[h]
        for h in range(group):
            moved.append(dot(m_scr[1 - slot, c, h], narrow[h]))
        for h in range(group):
            fade = fade_scr[1 - slot, c, h : h + 1, :]
            state = st_scr[h, :, :DV] * fade + (moved[h][:, :DV] + b_scr[1 - slot, c, h])
            trans = st_scr[h, :, DV:] * fade + moved[h][:, DV:]
            if c < chunks - 1:
                st_scr[h, :, :DV] = state
                st_scr[h, :, DV:] = trans
            else:
                map_ref[h, :, :DV] = state.astype(BF16)
                map_ref[h, :, DV:] = trans.astype(BF16)

    todo = [begin] + [functools.partial(advance, c) for c in range(chunks)]

    def run(n):
        for _ in range(min(n, len(todo))):
            todo.pop(0)()

    @pl.when(jnp.logical_not(live))
    def _():
        @pl.when(step > 0)
        def _():
            begin()
            for c in range(chunks):
                advance(c)

        @pl.when(step < count)
        def _():
            if mixes:
                qn_ref[...] = jnp.zeros_like(qn_ref)
                kn_ref[...] = jnp.zeros_like(kn_ref)
            wu_ref[...] = jnp.zeros_like(wu_ref)
            fade_scr[slot] = jnp.ones(fade_scr.shape[1:], F32)
            m_scr[slot] = jnp.zeros(m_scr.shape[1:], BF16)
            b_scr[slot] = jnp.zeros(b_scr.shape[1:], F32)

    @pl.when(live)
    def _():
        if mixes:
            mix(qk_ref, halo_ref, qk_taps_ref, qn_ref, kn_ref, raw_scr, dense_scr, key_heads, chunks)
        halo = halo_ref[0].astype(F32)
        v_pad[EDGE:, :] = v_ref[0].astype(F32)
        for i in range(CONV - 1):
            for h in range(group):
                source = 2 * EDGE + (i * key_heads + head) * group + h
                v_pad[EDGE - CONV + 1 + i : EDGE - CONV + 2 + i, h * DV : (h + 1) * DV] = halo[
                    source : source + 1
                ]
        v_all_taps = v_taps_ref[...].astype(F32)
        v_taps = [v_all_taps[i : i + 1] for i in range(CONV)]
        run(1)

        cum, gain = gates_of_heads(log_ref, gain_ref, used, head, group)
        faded = jnp.exp(cum)
        columns = as_columns(jnp.concatenate([cum, gain, gain * faded, faded], axis=0), chunks)

        def column(which, h, c):
            n = c * 8 + which * group + h
            return columns[:, n : n + 1]

        row = lax.broadcasted_iota(jnp.int32, (BLOCK, BLOCK), 0)
        lane = lax.broadcasted_iota(jnp.int32, (BLOCK, BLOCK), 1)
        below = row > lane
        small_row = lax.broadcasted_iota(jnp.int32, (TINY, BLOCK), 0)
        small_lane = lax.broadcasted_iota(jnp.int32, (TINY, BLOCK), 1)
        part_of = small_lane // TINY
        tiny_eye = jnp.where(small_row == small_lane % TINY, 1.0, 0.0).astype(F32)

        keys = [kn_ref[0, c * BLOCK : (c + 1) * BLOCK, key_columns] for c in range(chunks)]
        turned = [kc.T for kc in keys]
        run(1)

        compact = {}
        for c in range(chunks):
            kk = dot(keys[c], turned[c])
            for h in range(group):
                r = h * chunks + c
                span = slice(c * BLOCK, (c + 1) * BLOCK)
                ratio = jnp.exp(column(0, h, c) - cum[h : h + 1, span])
                strict = jnp.where(below, column(1, h, c) * ratio * kk, 0.0)
                a_scr[r] = strict.astype(BF16)
                tiny = strict[0:TINY]
                for b in range(1, BLOCK // TINY):
                    tiny = jnp.where(part_of == b, strict[b * TINY : (b + 1) * TINY], tiny)
                compact[r] = tiny

        run(1)
        solved = {r: tiny_eye for r in compact}
        for j in range(TINY - 1):
            pick = part_of * TINY + j
            for r in solved:
                factor = jnp.take_along_axis(compact[r], pick, axis=1, mode="promise_in_bounds")
                solved[r] = solved[r] - factor * solved[r][j : j + 1, :]
        for r in solved:
            for b in range(BLOCK // TINY):
                x_scr[r, b * TINY : (b + 1) * TINY, :] = jnp.where(
                    part_of == b, solved[r], 0.0
                ).astype(BF16)

        run(1)
        size = TINY
        while size < HALF:
            odd = [s for s in range(size, BLOCK, 2 * size)]
            half_lane = lax.broadcasted_iota(jnp.int32, (BLOCK // 2, BLOCK), 1)
            half_row = lax.broadcasted_iota(jnp.int32, (BLOCK // 2, BLOCK), 0)
            left = half_lane // size == 2 * (half_row // size)
            moved = {}
            for h, c in units:
                r = h * chunks + c
                lower = jnp.concatenate([a_scr[r, s : s + size, :] for s in odd], axis=0)
                lower = jnp.where(left, lower, jnp.zeros_like(lower))
                moved[r] = dot(lower, x_scr[r]).astype(BF16)
            for h, c in units:
                r = h * chunks + c
                spread = []
                for n in range(len(odd)):
                    spread.append(jnp.zeros((size, BLOCK), BF16))
                    spread.append(moved[r][n * size : (n + 1) * size])
                own = jnp.concatenate([x_scr[r, s : s + size, :] for s in odd], axis=0)
                update = own.astype(F32) - dot(own, jnp.concatenate(spread, axis=0))
                update = update.astype(BF16)
                for n, s in enumerate(odd):
                    x_scr[r, s : s + size, :] = update[n * size : (n + 1) * size]
            run(1)
            size *= 2

        for c in range(chunks):
            vc = mixed_rows(v_pad, v_taps, c, slice(0, group * DV)).astype(BF16).astype(F32)
            kc = keys[c].astype(F32)
            for h in range(group):
                r = h * chunks + c
                wu_ref[0, r, :, :DK] = (kc * column(2, h, c)).astype(BF16)
                wu_ref[0, r, :, DK:] = (vc[:, h * DV : (h + 1) * DV] * column(1, h, c)).astype(BF16)
        run(1)
        for h, c in units:
            r = h * chunks + c
            wu_ref[0, r, :HALF] = dot(x_scr[r, :HALF, :HALF], wu_ref[0, r, :HALF]).astype(BF16)
        run(1)
        for h, c in units:
            r = h * chunks + c
            rest = wu_ref[0, r, HALF:].astype(F32) - dot(a_scr[r, HALF:, :HALF], wu_ref[0, r, :HALF])
            wu_ref[0, r, HALF:] = rest.astype(BF16)
        for h, c in units:
            r = h * chunks + c
            wu_ref[0, r, HALF:] = dot(x_scr[r, HALF:, HALF:], wu_ref[0, r, HALF:]).astype(BF16)
        run(len(todo))
        for c in range(chunks):
            sums = cum[:, c * BLOCK : (c + 1) * BLOCK]
            last = sums[:, BLOCK - 1 : BLOCK]
            tail = jnp.exp(last - sums)
            fade = jnp.broadcast_to(jnp.exp(last), (group, BLOCK))
            for h in range(group):
                r = h * chunks + c
                fade_scr[slot, c, h : h + 1, :] = fade[h : h + 1]
                scaled = (turned[c].astype(F32) * tail[h : h + 1, :]).astype(BF16)
                both = dot(scaled, wu_ref[0, r])
                m_scr[slot, c, h] = (-both[:, :DK]).astype(BF16)
                b_scr[slot, c, h] = both[:, DK:]


def prepare(job, lengths, qk_rows, v_in, halo, qk_taps, v_taps, log_decay, write_gain, key_heads, mixed, after):
    head, first, count = job
    tok = v_in.shape[1]
    value_heads = v_in.shape[2] // DV
    group = value_heads // key_heads
    chunks = tok // BLOCK
    rows = group * chunks
    wide = group * DV
    mixes = mixed is None

    def now(i):
        return jnp.minimum(i, count - 1)

    def before(i):
        return jnp.maximum(i - 1, 0)

    def whole_of(i, lengths):
        return (first + now(i), 0, 0)

    operands = [v_in, halo, v_taps, log_decay, write_gain, after]
    in_specs = [
        pl.BlockSpec((1, tok, wide), lambda i, lengths: (first + now(i), 0, head)),
        pl.BlockSpec((1,) + halo.shape[1:], whole_of),
        pl.BlockSpec((CONV, wide), lambda i, lengths: (0, head)),
        pl.BlockSpec((1, value_heads, tok), whole_of),
        pl.BlockSpec((1, value_heads, tok), whole_of),
        pl.BlockSpec(memory_space=pltpu.HBM),
    ]
    out_specs = [
        pl.BlockSpec((1, rows, BLOCK, DK + DV), lambda i, lengths: (now(i), 0, 0, 0)),
        pl.BlockSpec((1, group, chunks * DK, DV + DK), lambda i, lengths: (before(i), 0, 0, 0)),
        pl.BlockSpec((group, DK, DV + DK), lambda i, lengths: (before(i), 0, 0)),
    ]
    out_shape = [
        jax.ShapeDtypeStruct((count, rows, BLOCK, DK + DV), BF16),
        jax.ShapeDtypeStruct((count, group, chunks * DK, DV + DK), BF16),
        jax.ShapeDtypeStruct((count * group, DK, DV + DK), BF16),
    ]
    scratch = [
        pltpu.VMEM((tok + EDGE, wide), F32),
        pltpu.VMEM((2, chunks, group, DK, DK), BF16),
        pltpu.VMEM((2, chunks, group, DK, DV), F32),
        pltpu.VMEM((2, chunks, group, BLOCK), F32),
        pltpu.VMEM((group, DK, DV + DK), F32),
        pltpu.VMEM((rows, BLOCK, BLOCK), BF16),
        pltpu.VMEM((rows, BLOCK, BLOCK), BF16),
    ]
    if mixes:
        operands += [qk_rows, qk_taps]
        in_specs += [
            pl.BlockSpec((1,) + qk_rows.shape[1:], whole_of),
            pl.BlockSpec(qk_taps.shape, lambda i, lengths: (0, 0)),
        ]
        out_specs += [pl.BlockSpec((1, tok, key_heads * DK), lambda i, lengths: (now(i), 0, 0))] * 2
        out_shape += [jax.ShapeDtypeStruct((count, tok, key_heads * DK), BF16)] * 2
        scratch += [
            pltpu.VMEM(qk_rows.shape[1:], F32),
            pltpu.VMEM((tok + EDGE, 2 * key_heads * DK), F32),
        ]
    else:
        operands.append(mixed)
        in_specs.append(pl.BlockSpec((1, tok, DK), lambda i, lengths: (first + now(i), 0, head)))
    return pl.pallas_call(
        functools.partial(prepare_kernel, first, count, head, group, chunks, key_heads, mixes),
        grid_spec=pltpu.PrefetchScalarGridSpec(
            num_scalar_prefetch=1,
            grid=(count + 1,),
            in_specs=in_specs,
            out_specs=out_specs,
            scratch_shapes=scratch,
        ),
        out_shape=out_shape,
        compiler_params=pltpu.CompilerParams(vmem_limit_bytes=VMEM_BYTES),
        cost_estimate=pl.CostEstimate(flops=5 * 10**9 * count, bytes_accessed=4 * 2**20 * count, transcendentals=10**6),
        name="prepare",
    )(lengths, *operands)


def outputs_kernel(
    first, head, group, chunks,
    length_ref, qn_ref, kn_ref, wu_ref, start_ref, log_ref, gain_ref, enter_ref, z_ref, norm_ref, held_ref, after_ref,
    out_ref,
    first_scr, score_scr, raw_scr,
):
    used = length_ref[first + pl.program_id(0)] - lax.axis_index("seq") * (chunks * BLOCK)
    units = [(h, c) for c in range(chunks) for h in range(group)]

    @pl.when(used <= 0)
    def _():
        out_ref[...] = jnp.zeros_like(out_ref)

    @pl.when(used > 0)
    def _():
        cum, gain = gates_of_heads(log_ref, gain_ref, used, head, group)
        faded = jnp.exp(cum)
        columns = as_columns(jnp.concatenate([cum, faded, gain, gain], axis=0), chunks)

        def column(which, h, c):
            n = c * 8 + which * group + h
            return columns[:, n : n + 1]

        row = lax.broadcasted_iota(jnp.int32, (BLOCK, BLOCK), 0)
        lane = lax.broadcasted_iota(jnp.int32, (BLOCK, BLOCK), 1)
        upto = row >= lane
        norm_gain = norm_ref[...]

        def span(c):
            return slice(c * BLOCK, (c + 1) * BLOCK)

        for h in range(group):
            moved = dot(start_ref[0, h, :, DV:], enter_ref[h])
            first_scr[h] = (moved + start_ref[0, h, :, :DV].astype(F32)).astype(BF16)
        for c in range(chunks):
            qk = dot(qn_ref[0, span(c), :], kn_ref[0, span(c), :].T)
            for h in range(group):
                ratio = jnp.exp(column(0, h, c) - cum[h : h + 1, span(c)])
                score_scr[h * chunks + c] = jnp.where(upto, ratio * qk, 0.0).astype(BF16)
        for h, c in units:
            r = h * chunks + c
            both = dot(score_scr[r], wu_ref[0, r])
            seen = qn_ref[0, span(c), :].astype(F32) * column(1, h, c) - both[:, :DK]
            score_scr[r] = seen.astype(BF16)
            raw_scr[r] = both[:, DK:]
        for h, c in units:
            r = h * chunks + c
            raw_scr[r] += dot(score_scr[r], first_scr[h, span(c), :])
        for h, c in units:
            raw = raw_scr[h * chunks + c]
            cols = slice(h * DV, (h + 1) * DV)
            mean = jnp.sum(raw * raw, axis=-1, keepdims=True) * (1.0 / DV)
            gated = raw * lax.rsqrt(mean + EPSILON) * norm_gain * silu(z_ref[0, span(c), cols].astype(F32))
            out_ref[0, span(c), cols] = jnp.where(row + c * BLOCK < used, gated, 0.0).astype(BF16)


def outputs(
    job, piece, lengths, qn, kn, wu, starts, log_decay, write_gain, enter, gate_z, norm_gain, key_heads, held, after,
):
    head, first, _ = job
    begin, count = piece
    prompts, tok, width = gate_z.shape
    rows = wu.shape[1]
    chunks = tok // BLOCK
    group = rows // chunks
    wide = group * DV
    value_heads = key_heads * group
    shift = begin - first
    from_mix = begin if qn.shape[0] == prompts else shift

    def whole_of(i, lengths):
        return (begin + i, 0, 0)

    def wide_of(i, lengths):
        return (begin + i, 0, head)

    def mixed_of(i, lengths):
        return (from_mix + i, 0, head)

    empty = held is None
    return pl.pallas_call(
        functools.partial(outputs_kernel, begin, head, group, chunks),
        grid_spec=pltpu.PrefetchScalarGridSpec(
            num_scalar_prefetch=1,
            grid=(count,),
            in_specs=[
                pl.BlockSpec((1, tok, DK), mixed_of),
                pl.BlockSpec((1, tok, DK), mixed_of),
                pl.BlockSpec((1, rows, BLOCK, DK + DV), lambda i, lengths: (shift + i, 0, 0, 0)),
                pl.BlockSpec((1, group, chunks * DK, DV + DK), lambda i, lengths: (shift + i, 0, 0, 0)),
                pl.BlockSpec((1, value_heads, tok), whole_of),
                pl.BlockSpec((1, value_heads, tok), whole_of),
                pl.BlockSpec((group, DK, DV), lambda i, lengths: (shift + i, 0, 0)),
                pl.BlockSpec((1, tok, wide), wide_of),
                pl.BlockSpec((1, DV), lambda i, lengths: (0, 0)),
                pl.BlockSpec(memory_space=pltpu.HBM),
                pl.BlockSpec(memory_space=pltpu.HBM),
            ],
            out_specs=pl.BlockSpec((1, tok, wide), wide_of),
            scratch_shapes=[
                pltpu.VMEM((group, chunks * DK, DV), BF16),
                pltpu.VMEM((rows, BLOCK, BLOCK), BF16),
                pltpu.VMEM((rows, BLOCK, DV), F32),
            ],
        ),
        out_shape=jax.ShapeDtypeStruct((prompts, tok, width), BF16),
        input_output_aliases={} if empty else {10: 0},
        compiler_params=pltpu.CompilerParams(vmem_limit_bytes=VMEM_BYTES),
        cost_estimate=pl.CostEstimate(flops=3 * 10**9 * count, bytes_accessed=4 * 2**20 * count, transcendentals=10**6),
        name="outputs",
    )(
        lengths, qn, kn, wu, starts, log_decay, write_gain, enter, gate_z,
        norm_gain.reshape(1, DV), after if empty else held, lengths if after is held else after,
    )


def own_chip():
    seq = lax.axis_index("seq")
    return seq // 2, seq % 2 == 1


def early_late(own, other, odd):
    return jnp.where(odd, other, own), jnp.where(odd, own, other)


def compose_maps(ins, outs):
    own_ref, other_ref = ins
    _, odd = own_chip()
    for n in range(own_ref.shape[0]):
        early, late = early_late(own_ref[n], other_ref[n], odd)
        both = dot(late[:, DV:], early)
        outs[0][n, :, :DV] = (both[:, :DV] + late[:, :DV].astype(F32)).astype(BF16)
        outs[0][n, :, DV:] = both[:, DV:].astype(BF16)


def close_maps(ins, outs):
    own_ref, other_ref = ins[:2]
    refs = ins[2:]
    chips = len(refs)
    chip, odd = own_chip()

    def of_chip(j, n):
        value = refs[0][n]
        for k in range(1, chips):
            value = jnp.where((chip + chips - k) % chips == j, refs[k][n], value)
        return value

    for n in range(own_ref.shape[0]):
        running = of_chip(0, n)[:, :DV]
        entering = jnp.zeros_like(running)
        for j in range(1, chips):
            entering = jnp.where(chip == j, running, entering)
            there = of_chip(j, n)
            running = (dot(there[:, DV:], running) + there[:, :DV].astype(F32)).astype(BF16)
        early, _ = early_late(own_ref[n], other_ref[n], odd)
        second = (dot(early[:, DV:], entering) + early[:, :DV].astype(F32)).astype(BF16)
        outs[0][n] = jnp.where(odd, second, entering)
        outs[1][n] = running


def choose_finals(group, placement_ref, finals, outs):
    refs = [(ref, n) for ref in finals for n in range(ref.shape[0] // group)]
    for r in range(placement_ref.shape[1]):
        prompt = placement_ref[0, r]
        for p, (ref, n) in enumerate(refs):
            @pl.when(prompt == p)
            def _(ref=ref, n=n):
                outs[0][r] = ref[n * group : (n + 1) * group]


def state_step(placement, group, compose, close, earlier, after):
    operands, shapes = [placement], []
    steps = []
    if compose is not None:
        steps.append(("compose", len(operands), len(compose), len(shapes)))
        operands += compose
        shapes += [compose[0]]
    if close is not None:
        steps.append(("close", len(operands), len(close), len(shapes)))
        operands += close
        shapes += [jax.ShapeDtypeStruct((close[0].shape[0], DK, DV), BF16)] * 2
        if earlier is not None:
            steps.append(("choose", len(operands), len(earlier), len(shapes)))
            operands += earlier
            shapes.append(jax.ShapeDtypeStruct((placement.shape[1], group, DK, DV), BF16))
    out_shape = [jax.ShapeDtypeStruct(x.shape, x.dtype) for x in shapes]

    def kernel(*refs):
        ins, outs = refs[: len(operands)], refs[len(operands) + 1 :]
        closed = None
        for kind, at, size, to in steps:
            part = ins[at : at + size]
            if kind == "compose":
                compose_maps(part, outs[to : to + 1])
            elif kind == "close":
                close_maps(part, outs[to : to + 2])
                closed = outs[to + 1]
            else:
                choose_finals(group, ins[0], list(part) + [closed], outs[to:])

    vmem = pl.BlockSpec(memory_space=pltpu.VMEM)
    return pl.pallas_call(
        kernel,
        in_specs=[pl.BlockSpec(memory_space=pltpu.SMEM)]
        + [vmem] * (len(operands) - 1)
        + [pl.BlockSpec(memory_space=pltpu.HBM)],
        out_specs=[vmem] * len(out_shape),
        out_shape=out_shape,
        compiler_params=pltpu.CompilerParams(vmem_limit_bytes=VMEM_BYTES),
        cost_estimate=pl.CostEstimate(flops=10**9, bytes_accessed=2**20, transcendentals=0),
        name="state_step",
    )(*operands, after)


def deliver(parts):
    count, group = parts[0].shape[:2]

    def kernel(*refs):
        for n, ref in enumerate(refs[:-1]):
            refs[-1][0, n * group : (n + 1) * group] = ref[0].astype(F32)

    return pl.pallas_call(
        kernel,
        grid=(count,),
        in_specs=[pl.BlockSpec((1, group, DK, DV), lambda i: (i, 0, 0, 0))] * len(parts),
        out_specs=pl.BlockSpec((1, group * len(parts), DK, DV), lambda i: (i, 0, 0, 0)),
        out_shape=jax.ShapeDtypeStruct((count, group * len(parts), DK, DV), F32),
        compiler_params=pltpu.CompilerParams(vmem_limit_bytes=VMEM_BYTES),
        name="deliver",
    )(*parts)


def pair_swap(block):
    count = lax.axis_size("seq")
    return lax.ppermute(block, "seq", [(i, i ^ 1) for i in range(count)])


def from_chip_behind(block, distance):
    count = lax.axis_size("seq")
    chips = count // 2
    route = [(i, ((i // 2 + distance) % chips) * 2 + i % 2) for i in range(count)]
    return lax.ppermute(block, "seq", route)


def shards(
    qk_in, v_in, gate_z, conv_qk, conv_v, log_decay, write_gain, norm_gain, prompt_lengths, placement,
):
    prompts, tok = qk_in.shape[:2]
    key_heads = qk_in.shape[3] // DK
    value_heads = v_in.shape[2] // DV
    rim = CONV - 1
    seq_count = lax.axis_size("seq")
    head_count = lax.axis_size("head")

    def by_head(x):
        x = x.reshape(x.shape[0], x.shape[1], 2, key_heads, DK)
        return jnp.transpose(x, (0, 1, 3, 2, 4)).reshape(x.shape[0], -1, DK)

    qk_rows = by_head(qk_in)
    qk_taps = by_head(conv_qk[None])[0]
    qk_tail = qk_rows[:, (tok - rim) * 2 * key_heads :]
    v_tail = v_in[:, tok - rim :].reshape(prompts, rim * value_heads, DV)
    front = 2 * EDGE - qk_tail.shape[1]
    back = 2 * EDGE - v_tail.shape[1]
    tails = jnp.concatenate(
        [
            jnp.zeros((prompts, front, DK), BF16),
            qk_tail,
            v_tail,
            jnp.zeros((prompts, back, DK), BF16),
        ],
        axis=1,
    )
    halo = lax.ppermute(tails, "seq", [(i, i + 1) for i in range(seq_count - 1)])
    group = value_heads // key_heads
    chips = seq_count // 2
    half = prompts // 2
    jobs = [(head, 0, prompts) for head in range(key_heads - 1)]
    jobs += [(key_heads - 1, 0, half), (key_heads - 1, half, prompts - half)]
    total = len(jobs)

    made, maps, chip_maps, entered, finals, sent = {}, {}, {}, {}, {}, {}
    waiting = []
    attended = None
    last = v_in

    def emit(attended, last):
        job, piece = waiting.pop(0)
        qn, kn, wu, starts = made[job]
        attended = outputs(
            jobs[job], piece, prompt_lengths, qn, kn, wu, starts, log_decay, write_gain,
            entered[job], gate_z, norm_gain, key_heads, attended, last,
        )
        return attended, attended

    for t in range(total + 2):
        if t < total:
            mixed = None if jobs[t][0] == 0 else made[0][:2]
            wu, starts, own_map, *new = prepare(
                jobs[t], prompt_lengths, qk_rows, v_in, halo, qk_taps, conv_v, log_decay, write_gain, key_heads,
                mixed and mixed[1], last,
            )
            made[t] = (*(mixed or new), wu, starts)
            maps[t] = [own_map, pair_swap(own_map)]
            last = own_map
        elif waiting:
            attended, last = emit(attended, last)
        compose = maps[t - 1] if 0 <= t - 1 < total else None
        close, earlier = None, None
        if 0 <= t - 2 < total:
            close = maps[t - 2] + chip_maps[t - 2]
            head = jobs[t - 2][0]
            if t - 2 == max(n for n in range(total) if jobs[n][0] == head):
                earlier = [finals[n] for n in range(t - 2) if jobs[n][0] == head]
        if compose is None and close is None:
            continue
        results = state_step(placement, group, compose, close, earlier, last)
        last = results[0]
        if compose is not None:
            chip_map, results = results[0], results[1:]
            chip_maps[t - 1] = [chip_map] + [from_chip_behind(chip_map, k) for k in range(1, chips)]
        if close is not None:
            entered[t - 2], finals[t - 2] = results[:2]
            if earlier is not None:
                sent[jobs[t - 2][0]] = lax.all_to_all(results[2], "head", 0, 0)
            _, begin, count = jobs[t - 2]
            while count > 0:
                waiting.append((t - 2, (begin, min(half, count))))
                begin, count = begin + half, count - half
    while waiting:
        attended, last = emit(attended, last)
    rollout = deliver([sent[head] for head in range(key_heads)])
    return attended, rollout.reshape(1, 1, head_count * value_heads, DK, DV)


def solution(mesh):
    return jax.shard_map(
        shards,
        mesh=mesh,
        in_specs=(
            P(None, "seq", None, "head"),
            P(None, "seq", "head"),
            P(None, "seq", "head"),
            P(None, None, "head"),
            P(None, "head"),
            P(None, "head", "seq"),
            P(None, "head", "seq"),
            P(),
            P(),
            P("seq", None),
        ),
        out_specs=(P(None, "seq", "head"), P("seq", "head", None, None, None)),
        check_vma=False,
    )
```

```python
import functools

import jax
import jax.numpy as jnp
from jax import lax
from jax.experimental import pallas as pl
from jax.experimental.pallas import tpu as pltpu
from jax.sharding import PartitionSpec as P

DK = 128
DV = 128
CONV = 4
BLOCK = 128
TINY = 16
EDGE = 8
EPSILON = 1e-06
VMEM_BYTES = 40 * 1024 * 1024
SMALL_VMEM_BYTES = 8 * 1024 * 1024
F32 = jnp.float32
BF16 = jnp.bfloat16


def far(x):
    return pltpu.with_memory_space_constraint(x, pltpu.HBM)


def dot(a, b):
    return lax.dot_general(a, b, (((1,), (0,)), ((), ())), preferred_element_type=F32)


def silu(x):
    half = 0.5 * x
    return half + half * jnp.tanh(half)


def mixed_rows(pad_ref, taps, c, columns):
    total = None
    for i in range(CONV):
        start = EDGE - (CONV - 1) + i + c * BLOCK
        term = pad_ref[start : start + BLOCK, columns] * taps[i]
        total = term if total is None else total + term
    return silu(total)


def unit_rows(x):
    return x * lax.rsqrt(jnp.sum(x * x, axis=-1, keepdims=True) + EPSILON)


def heads_rows(ref, head, group):
    every = ref[0]
    rows = every[:group]
    for n in range(1, every.shape[0] // group):
        rows = jnp.where(head == n, every[n * group : (n + 1) * group], rows)
    return rows


def gates_of_heads(log_ref, gain_ref, used, head, group):
    log = heads_rows(log_ref, head, group)
    lane = lax.broadcasted_iota(jnp.int32, log.shape, 1)
    valid = lane < used
    cum = jnp.where(valid, log, 0.0)
    gain = jnp.where(valid, heads_rows(gain_ref, head, group), 0.0)
    shift = 1
    while shift < BLOCK:
        cum = cum + jnp.where(lane % BLOCK >= shift, pltpu.roll(cum, shift, 1), 0.0)
        shift *= 2
    return cum, gain


def block_bases(parts, chunks):
    rows = jnp.concatenate(parts, axis=0)
    short = 7 - rows.shape[0]
    fill = [jnp.zeros((short, rows.shape[1]), F32)] if short else []
    rows = jnp.concatenate([rows] + fill + [jnp.ones((1, rows.shape[1]), F32)], axis=0)
    return [rows[:, c * BLOCK : (c + 1) * BLOCK] for c in range(chunks)]


def spread_squares(base, group, kinds):
    high = base.astype(BF16).astype(F32)
    middle = (base - high).astype(BF16).astype(F32)
    low = base - high - middle
    parts = [high, middle, low]
    row = lax.broadcasted_iota(jnp.int32, (32, BLOCK), 0)
    which = row % 8
    real = row < 24
    stacked = jnp.concatenate(parts + [jnp.zeros_like(high)], axis=0)
    left = jnp.where(jnp.logical_and(which == 7, real), 1.0, stacked).T.astype(BF16)
    blocks = []
    for h in range(group):
        minus = jnp.concatenate([jnp.broadcast_to(-part[h : h + 1], (8, BLOCK)) for part in parts + [low]], axis=0)
        blocks.append(jnp.where(which == h, 1.0, jnp.where(which == 7, minus, 0.0)))
    for n in range(group, group * kinds):
        blocks.append(jnp.where(which == n, 1.0, 0.0).astype(F32))
    every = dot(left, jnp.concatenate(blocks, axis=1).astype(BF16))
    return [every[:, n * BLOCK : (n + 1) * BLOCK] for n in range(group * kinds)]


def mix(qk_ref, halo_ref, taps_ref, qn_ref, kn_ref, raw_scr, dense_scr, key_heads, chunks):
    kinds = 2 * key_heads
    tok = chunks * BLOCK
    halo = halo_ref[0].astype(F32)
    taps = taps_ref[...].astype(F32)
    raw_scr[...] = qk_ref[0].astype(F32)
    for kind in range(kinds):
        columns = slice(kind * DK, (kind + 1) * DK)
        for i in range(1, CONV):
            source = 2 * EDGE - i * kinds + kind
            dense_scr[EDGE - i : EDGE - i + 1, columns] = halo[source : source + 1]
        dense_scr[EDGE:, columns] = raw_scr[pl.ds(kind, tok, kinds), :]
    for c in range(chunks):
        span = slice(c * BLOCK, (c + 1) * BLOCK)
        for kind in range(kinds):
            own = [taps[n : n + 1] for n in range(kind, taps.shape[0], kinds)]
            rows = unit_rows(mixed_rows(dense_scr, own, c, slice(kind * DK, (kind + 1) * DK)))
            to_ref = kn_ref if kind % 2 else qn_ref
            to_ref[0, span, kind // 2 * DK : (kind // 2 + 1) * DK] = rows.astype(BF16)


def prepare_kernel(first, count, head, group, chunks, key_heads, mixes, *refs):
    length_ref, v_ref, halo_ref, v_taps_ref, log_ref, gain_ref, after_ref = refs[:7]
    refs = refs[7:]
    if mixes:
        qk_ref, qk_taps_ref, wu_ref, start_ref, map_ref, qn_ref, kn_ref = refs[:7]
        v_pad, m_scr, b_scr, fade_scr, st_scr, a_scr, x_scr, raw_scr, dense_scr = refs[7:]
        key_columns = slice(head * DK, (head + 1) * DK)
    else:
        kn_ref, wu_ref, start_ref, map_ref = refs[:4]
        v_pad, m_scr, b_scr, fade_scr, st_scr, a_scr, x_scr = refs[4:]
        key_columns = slice(0, DK)
    step = pl.program_id(0)
    used = length_ref[first + jnp.minimum(step, count - 1)] - lax.axis_index("seq") * (chunks * BLOCK)
    units = [(h, c) for c in range(chunks) for h in range(group)]
    slot = step % 2
    live = jnp.logical_and(step < count, used > 0)

    def begin():
        row = lax.broadcasted_iota(jnp.int32, (DK, DV + DK), 0)
        lane = lax.broadcasted_iota(jnp.int32, (DK, DV + DK), 1)
        for h in range(group):
            st_scr[h] = jnp.where(lane == row + DV, 1.0, 0.0).astype(F32)

    def advance(c):
        narrow, moved = [], []
        for h in range(group):
            narrow.append(st_scr[h].astype(BF16))
            start_ref[0, h, c * DK : (c + 1) * DK, :] = narrow[h]
        for h in range(group):
            moved.append(dot(m_scr[1 - slot, c, h], narrow[h]))
        for h in range(group):
            fade = fade_scr[1 - slot, c, h : h + 1, :]
            state = st_scr[h, :, :DV] * fade + (moved[h][:, :DV] + b_scr[1 - slot, c, h])
            trans = st_scr[h, :, DV:] * fade + moved[h][:, DV:]
            if c < chunks - 1:
                st_scr[h, :, :DV] = state
                st_scr[h, :, DV:] = trans
            else:
                map_ref[h, :, :DV] = state.astype(BF16)
                map_ref[h, :, DV:] = trans.astype(BF16)

    todo = [begin] + [functools.partial(advance, c) for c in range(chunks)]

    def run(n):
        for _ in range(min(n, len(todo))):
            todo.pop(0)()

    @pl.when(jnp.logical_not(live))
    def _():
        @pl.when(step > 0)
        def _():
            begin()
            for c in range(chunks):
                advance(c)

        @pl.when(step < count)
        def _():
            if mixes:
                qn_ref[...] = jnp.zeros_like(qn_ref)
                kn_ref[...] = jnp.zeros_like(kn_ref)
            wu_ref[...] = jnp.zeros_like(wu_ref)
            fade_scr[slot] = jnp.ones(fade_scr.shape[1:], F32)
            m_scr[slot] = jnp.zeros(m_scr.shape[1:], BF16)
            b_scr[slot] = jnp.zeros(b_scr.shape[1:], F32)

    @pl.when(live)
    def _():
        if mixes:
            mix(qk_ref, halo_ref, qk_taps_ref, qn_ref, kn_ref, raw_scr, dense_scr, key_heads, chunks)
        halo = halo_ref[0].astype(F32)
        v_pad[EDGE:, :] = v_ref[0].astype(F32)
        for i in range(CONV - 1):
            for h in range(group):
                source = 2 * EDGE + (i * key_heads + head) * group + h
                v_pad[EDGE - CONV + 1 + i : EDGE - CONV + 2 + i, h * DV : (h + 1) * DV] = halo[
                    source : source + 1
                ]
        v_all_taps = v_taps_ref[...].astype(F32)
        v_taps = [v_all_taps[i : i + 1] for i in range(CONV)]
        run(1)

        cum, gain = gates_of_heads(log_ref, gain_ref, used, head, group)
        faded = jnp.exp(cum)
        bases = block_bases([cum, gain, gain * faded], chunks)

        row = lax.broadcasted_iota(jnp.int32, (BLOCK, BLOCK), 0)
        lane = lax.broadcasted_iota(jnp.int32, (BLOCK, BLOCK), 1)
        below = row > lane
        small_row = lax.broadcasted_iota(jnp.int32, (TINY, BLOCK), 0)
        small_lane = lax.broadcasted_iota(jnp.int32, (TINY, BLOCK), 1)
        part_of = small_lane // TINY
        tiny_eye = jnp.where(small_row == small_lane % TINY, 1.0, 0.0).astype(F32)

        keys = [kn_ref[0, c * BLOCK : (c + 1) * BLOCK, key_columns] for c in range(chunks)]
        turned = [kc.T for kc in keys]
        run(1)

        compact = {}
        for c in range(chunks):
            kk = dot(keys[c], turned[c])
            squares = spread_squares(bases[c], group, 3)
            vc = mixed_rows(v_pad, v_taps, c, slice(0, group * DV)).astype(BF16).astype(F32)
            kc = keys[c].astype(F32)
            for h in range(group):
                r = h * chunks + c
                gain_square, fade_square = squares[group + h], squares[2 * group + h]
                wu_ref[0, r, :, :DK] = (kc * fade_square).astype(BF16)
                wu_ref[0, r, :, DK:] = (vc[:, h * DV : (h + 1) * DV] * gain_square).astype(BF16)
                strict = jnp.where(below, gain_square * jnp.exp(squares[h]) * kk, 0.0)
                a_scr[r] = strict.astype(BF16)
                tiny = strict[0:TINY]
                for b in range(1, BLOCK // TINY):
                    tiny = jnp.where(part_of == b, strict[b * TINY : (b + 1) * TINY], tiny)
                compact[r] = tiny

        run(1)
        solved = {r: tiny_eye for r in compact}
        for j in range(TINY - 1):
            pick = part_of * TINY + j
            for r in solved:
                factor = jnp.take_along_axis(compact[r], pick, axis=1, mode="promise_in_bounds")
                solved[r] = solved[r] - factor * solved[r][j : j + 1, :]
        for r in solved:
            for b in range(BLOCK // TINY):
                x_scr[r, b * TINY : (b + 1) * TINY, :] = jnp.where(
                    part_of == b, solved[r], 0.0
                ).astype(BF16)

        run(1)
        size = TINY
        while size < BLOCK:
            odd = [s for s in range(size, BLOCK, 2 * size)]
            half_lane = lax.broadcasted_iota(jnp.int32, (BLOCK // 2, BLOCK), 1)
            half_row = lax.broadcasted_iota(jnp.int32, (BLOCK // 2, BLOCK), 0)
            left = half_lane // size == 2 * (half_row // size)
            moved = {}
            for h, c in units:
                r = h * chunks + c
                lower = jnp.concatenate([a_scr[r, s : s + size, :] for s in odd], axis=0)
                lower = jnp.where(left, lower, jnp.zeros_like(lower))
                moved[r] = dot(lower, x_scr[r]).astype(BF16)
            for h, c in units:
                r = h * chunks + c
                spread = []
                for n in range(len(odd)):
                    spread.append(jnp.zeros((size, BLOCK), BF16))
                    spread.append(moved[r][n * size : (n + 1) * size])
                own = jnp.concatenate([x_scr[r, s : s + size, :] for s in odd], axis=0)
                update = own.astype(F32) - dot(own, jnp.concatenate(spread, axis=0))
                update = update.astype(BF16)
                for n, s in enumerate(odd):
                    x_scr[r, s : s + size, :] = update[n * size : (n + 1) * size]
            run(1)
            size *= 2

        run(1)
        solved_rows = {}
        for h, c in units:
            r = h * chunks + c
            solved_rows[r] = dot(x_scr[r], wu_ref[0, r]).astype(BF16)
            if len(solved_rows) == len(units) // 2:
                run(1)
        for r in solved_rows:
            wu_ref[0, r] = solved_rows[r]
        run(len(todo))
        for c in range(chunks):
            sums = cum[:, c * BLOCK : (c + 1) * BLOCK]
            last = sums[:, BLOCK - 1 : BLOCK]
            tail = jnp.exp(last - sums)
            fade = jnp.broadcast_to(jnp.exp(last), (group, BLOCK))
            for h in range(group):
                r = h * chunks + c
                fade_scr[slot, c, h : h + 1, :] = fade[h : h + 1]
                scaled = (turned[c].astype(F32) * tail[h : h + 1, :]).astype(BF16)
                both = dot(scaled, solved_rows[r])
                m_scr[slot, c, h] = (-both[:, :DK]).astype(BF16)
                b_scr[slot, c, h] = both[:, DK:]


def prepare(job, lengths, qk_rows, v_in, halo, qk_taps, v_taps, log_decay, write_gain, key_heads, mixed, after):
    head, first, count = job
    tok = v_in.shape[1]
    value_heads = v_in.shape[2] // DV
    group = value_heads // key_heads
    chunks = tok // BLOCK
    rows = group * chunks
    wide = group * DV
    mixes = mixed is None

    def now(i):
        return jnp.minimum(i, count - 1)

    def before(i):
        return jnp.maximum(i - 1, 0)

    def whole_of(i, lengths):
        return (first + now(i), 0, 0)

    operands = [far(v_in), halo, far(v_taps), far(log_decay), far(write_gain), far(after)]
    in_specs = [
        pl.BlockSpec((1, tok, wide), lambda i, lengths: (first + now(i), 0, head)),
        pl.BlockSpec((1,) + halo.shape[1:], whole_of),
        pl.BlockSpec((CONV, wide), lambda i, lengths: (0, head)),
        pl.BlockSpec((1, value_heads, tok), whole_of),
        pl.BlockSpec((1, value_heads, tok), whole_of),
        pl.BlockSpec(memory_space=pltpu.HBM),
    ]
    out_specs = [
        pl.BlockSpec((1, rows, BLOCK, DK + DV), lambda i, lengths: (now(i), 0, 0, 0)),
        pl.BlockSpec((1, group, chunks * DK, DV + DK), lambda i, lengths: (before(i), 0, 0, 0)),
        pl.BlockSpec((group, DK, DV + DK), lambda i, lengths: (before(i), 0, 0)),
    ]
    out_shape = [
        pltpu.HBM((count, rows, BLOCK, DK + DV), BF16),
        pltpu.HBM((count, group, chunks * DK, DV + DK), BF16),
        jax.ShapeDtypeStruct((count * group, DK, DV + DK), BF16),
    ]
    scratch = [
        pltpu.VMEM((tok + EDGE, wide), F32),
        pltpu.VMEM((2, chunks, group, DK, DK), BF16),
        pltpu.VMEM((2, chunks, group, DK, DV), F32),
        pltpu.VMEM((2, chunks, group, BLOCK), F32),
        pltpu.VMEM((group, DK, DV + DK), F32),
        pltpu.VMEM((rows, BLOCK, BLOCK), BF16),
        pltpu.VMEM((rows, BLOCK, BLOCK), BF16),
    ]
    if mixes:
        operands += [far(qk_rows), far(qk_taps)]
        in_specs += [
            pl.BlockSpec((1,) + qk_rows.shape[1:], whole_of),
            pl.BlockSpec(qk_taps.shape, lambda i, lengths: (0, 0)),
        ]
        out_specs += [pl.BlockSpec((1, tok, key_heads * DK), lambda i, lengths: (now(i), 0, 0))] * 2
        out_shape += [pltpu.HBM((count, tok, key_heads * DK), BF16)] * 2
        scratch += [
            pltpu.VMEM(qk_rows.shape[1:], F32),
            pltpu.VMEM((tok + EDGE, 2 * key_heads * DK), F32),
        ]
    else:
        operands.append(far(mixed))
        in_specs.append(pl.BlockSpec((1, tok, DK), lambda i, lengths: (first + now(i), 0, head)))
    return pl.pallas_call(
        functools.partial(prepare_kernel, first, count, head, group, chunks, key_heads, mixes),
        grid_spec=pltpu.PrefetchScalarGridSpec(
            num_scalar_prefetch=1,
            grid=(count + 1,),
            in_specs=in_specs,
            out_specs=out_specs,
            scratch_shapes=scratch,
        ),
        out_shape=out_shape,
        compiler_params=pltpu.CompilerParams(vmem_limit_bytes=VMEM_BYTES),
        cost_estimate=pl.CostEstimate(flops=5 * 10**9 * count, bytes_accessed=4 * 2**20 * count, transcendentals=10**6),
        name="prepare",
    )(lengths, *operands)


def outputs_kernel(
    first, head, group, chunks,
    length_ref, qn_ref, kn_ref, wu_ref, start_ref, log_ref, gain_ref, enter_ref, z_ref, norm_ref, held_ref, after_ref,
    out_ref,
    first_scr, score_scr, seen_scr,
):
    used = length_ref[first + pl.program_id(0)] - lax.axis_index("seq") * (chunks * BLOCK)
    units = [(h, c) for c in range(chunks) for h in range(group)]

    @pl.when(used <= 0)
    def _():
        out_ref[...] = jnp.zeros_like(out_ref)

    @pl.when(used > 0)
    def _():
        cum, gain = gates_of_heads(log_ref, gain_ref, used, head, group)
        faded = jnp.exp(cum)
        bases = block_bases([cum, faded], chunks)

        row = lax.broadcasted_iota(jnp.int32, (BLOCK, BLOCK), 0)
        lane = lax.broadcasted_iota(jnp.int32, (BLOCK, BLOCK), 1)
        upto = row >= lane
        norm_gain = norm_ref[...]

        def span(c):
            return slice(c * BLOCK, (c + 1) * BLOCK)

        for h in range(group):
            moved = dot(start_ref[0, h, :, DV:], enter_ref[h])
            first_scr[h] = (moved + start_ref[0, h, :, :DV].astype(F32)).astype(BF16)
        for c in range(chunks):
            qk = dot(qn_ref[0, span(c), :], kn_ref[0, span(c), :].T)
            squares = spread_squares(bases[c], group, 2)
            q_wide = qn_ref[0, span(c), :].astype(F32)
            for h in range(group):
                r = h * chunks + c
                score_scr[r] = jnp.where(upto, jnp.exp(squares[h]) * qk, 0.0).astype(BF16)
                seen_scr[r] = q_wide * squares[group + h]
        both, raws = {}, {}
        for h, c in units:
            r = h * chunks + c
            both[r] = dot(score_scr[r], wu_ref[0, r])
        for h, c in units:
            r = h * chunks + c
            seen = (seen_scr[r] - both[r][:, :DK]).astype(BF16)
            raws[r] = dot(seen, first_scr[h, span(c), :]) + both[r][:, DK:]
        for h, c in units:
            raw = raws[h * chunks + c]
            cols = slice(h * DV, (h + 1) * DV)
            mean = jnp.sum(raw * raw, axis=-1, keepdims=True) * (1.0 / DV)
            gated = raw * lax.rsqrt(mean + EPSILON) * norm_gain * silu(z_ref[0, span(c), cols].astype(F32))
            out_ref[0, span(c), cols] = jnp.where(row + c * BLOCK < used, gated, 0.0).astype(BF16)


def outputs(
    job, piece, lengths, qn, kn, wu, starts, log_decay, write_gain, enter, gate_z, norm_gain, key_heads, held, after,
):
    head, first, _ = job
    begin, count = piece
    prompts, tok, width = gate_z.shape
    rows = wu.shape[1]
    chunks = tok // BLOCK
    group = rows // chunks
    wide = group * DV
    value_heads = key_heads * group
    shift = begin - first
    from_mix = begin if qn.shape[0] == prompts else shift

    def whole_of(i, lengths):
        return (begin + i, 0, 0)

    def wide_of(i, lengths):
        return (begin + i, 0, head)

    def mixed_of(i, lengths):
        return (from_mix + i, 0, head)

    empty = held is None
    return pl.pallas_call(
        functools.partial(outputs_kernel, begin, head, group, chunks),
        grid_spec=pltpu.PrefetchScalarGridSpec(
            num_scalar_prefetch=1,
            grid=(count,),
            in_specs=[
                pl.BlockSpec((1, tok, DK), mixed_of),
                pl.BlockSpec((1, tok, DK), mixed_of),
                pl.BlockSpec((1, rows, BLOCK, DK + DV), lambda i, lengths: (shift + i, 0, 0, 0)),
                pl.BlockSpec((1, group, chunks * DK, DV + DK), lambda i, lengths: (shift + i, 0, 0, 0)),
                pl.BlockSpec((1, value_heads, tok), whole_of),
                pl.BlockSpec((1, value_heads, tok), whole_of),
                pl.BlockSpec((group, DK, DV), lambda i, lengths: (shift + i, 0, 0)),
                pl.BlockSpec((1, tok, wide), wide_of),
                pl.BlockSpec((1, DV), lambda i, lengths: (0, 0)),
                pl.BlockSpec(memory_space=pltpu.HBM),
                pl.BlockSpec(memory_space=pltpu.HBM),
            ],
            out_specs=pl.BlockSpec((1, tok, wide), wide_of),
            scratch_shapes=[
                pltpu.VMEM((group, chunks * DK, DV), BF16),
                pltpu.VMEM((rows, BLOCK, BLOCK), BF16),
                pltpu.VMEM((rows, BLOCK, DV), F32),
            ],
        ),
        out_shape=pltpu.HBM((prompts, tok, width), BF16),
        input_output_aliases={} if empty else {10: 0},
        compiler_params=pltpu.CompilerParams(vmem_limit_bytes=VMEM_BYTES),
        cost_estimate=pl.CostEstimate(flops=3 * 10**9 * count, bytes_accessed=4 * 2**20 * count, transcendentals=10**6),
        name="outputs",
    )(
        lengths, far(qn), far(kn), far(wu), far(starts), far(log_decay), far(write_gain), enter, far(gate_z),
        far(norm_gain.reshape(1, DV)), far(after if empty else held), far(wu if after is held else after),
    )


def own_chip():
    seq = lax.axis_index("seq")
    return seq // 2, seq % 2 == 1


def early_late(own, other, odd):
    return jnp.where(odd, other, own), jnp.where(odd, own, other)


def compose_maps(ins, outs):
    own_ref, other_ref = ins
    _, odd = own_chip()
    for n in range(own_ref.shape[0]):
        early, late = early_late(own_ref[n], other_ref[n], odd)
        both = dot(late[:, DV:], early)
        outs[0][n, :, :DV] = (both[:, :DV] + late[:, :DV].astype(F32)).astype(BF16)
        outs[0][n, :, DV:] = both[:, DV:].astype(BF16)


def close_maps(ins, outs):
    own_ref, other_ref = ins[:2]
    refs = ins[2:]
    chips = len(refs)
    chip, odd = own_chip()

    def of_chip(j, n):
        value = refs[0][n]
        for k in range(1, chips):
            value = jnp.where((chip + chips - k) % chips == j, refs[k][n], value)
        return value

    for n in range(own_ref.shape[0]):
        running = of_chip(0, n)[:, :DV]
        entering = jnp.zeros_like(running)
        for j in range(1, chips):
            entering = jnp.where(chip == j, running, entering)
            there = of_chip(j, n)
            running = (dot(there[:, DV:], running) + there[:, :DV].astype(F32)).astype(BF16)
        early, _ = early_late(own_ref[n], other_ref[n], odd)
        second = (dot(early[:, DV:], entering) + early[:, :DV].astype(F32)).astype(BF16)
        outs[0][n] = jnp.where(odd, second, entering)
        outs[1][n] = running


def choose_finals(group, placement_ref, finals, outs):
    refs = [(ref, n) for ref in finals for n in range(ref.shape[0] // group)]
    for r in range(placement_ref.shape[1]):
        prompt = placement_ref[0, r]
        for p, (ref, n) in enumerate(refs):
            @pl.when(prompt == p)
            def _(ref=ref, n=n):
                outs[0][r] = ref[n * group : (n + 1) * group]


def state_step(placement, group, compose, close, earlier, after):
    operands, shapes = [placement], []
    steps = []
    if compose is not None:
        steps.append(("compose", len(operands), len(compose), len(shapes)))
        operands += compose
        shapes += [compose[0]]
    if close is not None:
        steps.append(("close", len(operands), len(close), len(shapes)))
        operands += close
        shapes += [jax.ShapeDtypeStruct((close[0].shape[0], DK, DV), BF16)] * 2
        if earlier is not None:
            steps.append(("choose", len(operands), len(earlier), len(shapes)))
            operands += earlier
            shapes.append(jax.ShapeDtypeStruct((placement.shape[1], group, DK, DV), BF16))
    out_shape = [jax.ShapeDtypeStruct(x.shape, x.dtype) for x in shapes]

    def kernel(*refs):
        ins, outs = refs[: len(operands)], refs[len(operands) + 1 :]
        closed = None
        for kind, at, size, to in steps:
            part = ins[at : at + size]
            if kind == "compose":
                compose_maps(part, outs[to : to + 1])
            elif kind == "close":
                close_maps(part, outs[to : to + 2])
                closed = outs[to + 1]
            else:
                choose_finals(group, ins[0], list(part) + [closed], outs[to:])

    vmem = pl.BlockSpec(memory_space=pltpu.VMEM)
    return pl.pallas_call(
        kernel,
        in_specs=[pl.BlockSpec(memory_space=pltpu.SMEM)]
        + [vmem] * (len(operands) - 1)
        + [pl.BlockSpec(memory_space=pltpu.HBM)],
        out_specs=[vmem] * len(out_shape),
        out_shape=out_shape,
        compiler_params=pltpu.CompilerParams(vmem_limit_bytes=SMALL_VMEM_BYTES),
        cost_estimate=pl.CostEstimate(flops=10**9, bytes_accessed=2**20, transcendentals=0),
        name="state_step",
    )(*operands, far(after))


def deliver(parts):
    count, group = parts[0].shape[:2]

    def kernel(*refs):
        for n, ref in enumerate(refs[:-1]):
            refs[-1][:, n * group : (n + 1) * group] = ref[...].astype(F32)

    return pl.pallas_call(
        kernel,
        grid=(2,),
        in_specs=[pl.BlockSpec((count // 2, group, DK, DV), lambda i: (i, 0, 0, 0))] * len(parts),
        out_specs=pl.BlockSpec((count // 2, group * len(parts), DK, DV), lambda i: (i, 0, 0, 0)),
        out_shape=jax.ShapeDtypeStruct((count, group * len(parts), DK, DV), F32),
        compiler_params=pltpu.CompilerParams(vmem_limit_bytes=VMEM_BYTES),
        name="deliver",
    )(*parts)


def pair_swap(block):
    count = lax.axis_size("seq")
    return lax.ppermute(block, "seq", [(i, i ^ 1) for i in range(count)])


def from_chip_behind(block, distance):
    count = lax.axis_size("seq")
    chips = count // 2
    route = [(i, ((i // 2 + distance) % chips) * 2 + i % 2) for i in range(count)]
    return lax.ppermute(block, "seq", route)


def shards(
    qk_in, v_in, gate_z, conv_qk, conv_v, log_decay, write_gain, norm_gain, prompt_lengths, placement,
):
    prompts, tok = qk_in.shape[:2]
    key_heads = qk_in.shape[3] // DK
    value_heads = v_in.shape[2] // DV
    rim = CONV - 1
    seq_count = lax.axis_size("seq")
    head_count = lax.axis_size("head")

    def by_head(x):
        x = x.reshape(x.shape[0], x.shape[1], 2, key_heads, DK)
        return jnp.transpose(x, (0, 1, 3, 2, 4)).reshape(x.shape[0], -1, DK)

    qk_rows = by_head(qk_in)
    qk_taps = by_head(conv_qk[None])[0]
    qk_tail = qk_rows[:, (tok - rim) * 2 * key_heads :]
    v_tail = v_in[:, tok - rim :].reshape(prompts, rim * value_heads, DV)
    front = 2 * EDGE - qk_tail.shape[1]
    back = 2 * EDGE - v_tail.shape[1]
    tails = jnp.concatenate(
        [
            jnp.zeros((prompts, front, DK), BF16),
            qk_tail,
            v_tail,
            jnp.zeros((prompts, back, DK), BF16),
        ],
        axis=1,
    )
    halo = lax.ppermute(tails, "seq", [(i, i + 1) for i in range(seq_count - 1)])
    group = value_heads // key_heads
    chips = seq_count // 2
    half = prompts // 2
    jobs = [(head, 0, prompts) for head in range(key_heads - 1)]
    jobs += [(key_heads - 1, 0, half), (key_heads - 1, half, prompts - half)]
    total = len(jobs)

    made, maps, chip_maps, entered, finals, sent = {}, {}, {}, {}, {}, {}
    waiting = []
    attended = None
    last = v_in

    def emit(attended, last):
        job, piece = waiting.pop(0)
        qn, kn, wu, starts = made[job]
        attended = outputs(
            jobs[job], piece, prompt_lengths, qn, kn, wu, starts, log_decay, write_gain,
            entered[job], gate_z, norm_gain, key_heads, attended, last,
        )
        return attended, attended

    for t in range(total + 2):
        if t < total:
            mixed = None if jobs[t][0] == 0 else made[0][:2]
            wu, starts, own_map, *new = prepare(
                jobs[t], prompt_lengths, qk_rows, v_in, halo, qk_taps, conv_v, log_decay, write_gain, key_heads,
                mixed and mixed[1], last,
            )
            made[t] = (*(mixed or new), wu, starts)
            maps[t] = [own_map, pair_swap(own_map)]
            last = own_map
        elif waiting:
            attended, last = emit(attended, last)
        compose = maps[t - 1] if 0 <= t - 1 < total else None
        close, earlier = None, None
        if 0 <= t - 2 < total:
            close = maps[t - 2] + chip_maps[t - 2]
            head = jobs[t - 2][0]
            if t - 2 == max(n for n in range(total) if jobs[n][0] == head):
                earlier = [finals[n] for n in range(t - 2) if jobs[n][0] == head]
        if compose is None and close is None:
            continue
        results = state_step(placement, group, compose, close, earlier, last)
        last = results[0]
        if compose is not None:
            chip_map, results = results[0], results[1:]
            chip_maps[t - 1] = [chip_map] + [from_chip_behind(chip_map, k) for k in range(1, chips)]
        if close is not None:
            entered[t - 2], finals[t - 2] = results[:2]
            if earlier is not None:
                sent[jobs[t - 2][0]] = lax.all_to_all(results[2], "head", 0, 0)
            _, begin, count = jobs[t - 2]
            while count > 0:
                waiting.append((t - 2, (begin, min(half, count))))
                begin, count = begin + half, count - half
    while waiting:
        attended, last = emit(attended, last)
    rollout = deliver([sent[head] for head in range(key_heads)])
    return attended, rollout.reshape(1, 1, head_count * value_heads, DK, DV)


def solution(mesh):
    return jax.shard_map(
        shards,
        mesh=mesh,
        in_specs=(
            P(None, "seq", None, "head"),
            P(None, "seq", "head"),
            P(None, "seq", "head"),
            P(None, None, "head"),
            P(None, "head"),
            P(None, "head", "seq"),
            P(None, "head", "seq"),
            P(),
            P(),
            P("seq", None),
        ),
        out_specs=(P(None, "seq", "head"), P("seq", "head", None, None, None)),
        check_vma=False,
    )
```

```python
import functools

import jax
import jax.numpy as jnp
from jax import lax
from jax.experimental import pallas as pl
from jax.experimental.pallas import tpu as pltpu
from jax.sharding import PartitionSpec as P

DK = 128
DV = 128
CONV = 4
BLOCK = 128
TINY = 16
EDGE = 8
EPSILON = 1e-06
VMEM_BYTES = 40 * 1024 * 1024
SMALL_VMEM_BYTES = 8 * 1024 * 1024
F32 = jnp.float32
BF16 = jnp.bfloat16


def far(x):
    return pltpu.with_memory_space_constraint(x, pltpu.HBM)


def dot(a, b):
    return lax.dot_general(a, b, (((1,), (0,)), ((), ())), preferred_element_type=F32)


def silu(x):
    half = 0.5 * x
    return half + half * jnp.tanh(half)


def mixed_rows(pad_ref, taps, c, columns):
    total = None
    for i in range(CONV):
        start = EDGE - (CONV - 1) + i + c * BLOCK
        term = pad_ref[start : start + BLOCK, columns] * taps[i]
        total = term if total is None else total + term
    return silu(total)


def unit_rows(x):
    return x * lax.rsqrt(jnp.sum(x * x, axis=-1, keepdims=True) + EPSILON)


def heads_rows(ref, head, group):
    every = ref[0]
    rows = every[:group]
    for n in range(1, every.shape[0] // group):
        rows = jnp.where(head == n, every[n * group : (n + 1) * group], rows)
    return rows


def gates_of_heads(log_ref, gain_ref, used, head, group):
    log = heads_rows(log_ref, head, group)
    lane = lax.broadcasted_iota(jnp.int32, log.shape, 1)
    valid = lane < used
    cum = jnp.where(valid, log, 0.0)
    gain = jnp.where(valid, heads_rows(gain_ref, head, group), 0.0)
    shift = 1
    while shift < BLOCK:
        cum = cum + jnp.where(lane % BLOCK >= shift, pltpu.roll(cum, shift, 1), 0.0)
        shift *= 2
    return cum, gain


def as_columns(rows, chunks):
    parts = [rows[:, c * BLOCK : (c + 1) * BLOCK] for c in range(chunks)]
    short = BLOCK - 8 * chunks
    if short:
        parts.append(jnp.zeros((short, BLOCK), F32))
    return jnp.concatenate(parts, axis=0).T


def block_bases(parts, chunks):
    rows = jnp.concatenate(parts, axis=0)
    short = 7 - rows.shape[0]
    fill = [jnp.zeros((short, rows.shape[1]), F32)] if short else []
    rows = jnp.concatenate([rows] + fill + [jnp.ones((1, rows.shape[1]), F32)], axis=0)
    return [rows[:, c * BLOCK : (c + 1) * BLOCK] for c in range(chunks)]


def spread_squares(base, group, kinds):
    high = base.astype(BF16).astype(F32)
    middle = (base - high).astype(BF16).astype(F32)
    low = base - high - middle
    parts = [high, middle, low]
    row = lax.broadcasted_iota(jnp.int32, (32, BLOCK), 0)
    which = row % 8
    real = row < 24
    stacked = jnp.concatenate(parts + [jnp.zeros_like(high)], axis=0)
    left = jnp.where(jnp.logical_and(which == 7, real), 1.0, stacked).T.astype(BF16)
    blocks = []
    for h in range(group):
        minus = jnp.concatenate([jnp.broadcast_to(-part[h : h + 1], (8, BLOCK)) for part in parts + [low]], axis=0)
        blocks.append(jnp.where(which == h, 1.0, jnp.where(which == 7, minus, 0.0)))
    for n in range(group, group * kinds):
        blocks.append(jnp.where(which == n, 1.0, 0.0).astype(F32))
    every = dot(left, jnp.concatenate(blocks, axis=1).astype(BF16))
    return [every[:, n * BLOCK : (n + 1) * BLOCK] for n in range(group * kinds)]


def mix(qk_ref, halo_ref, taps_ref, qn_ref, kn_ref, raw_scr, dense_scr, key_heads, chunks):
    kinds = 2 * key_heads
    tok = chunks * BLOCK
    halo = halo_ref[0].astype(F32)
    taps = taps_ref[...].astype(F32)
    raw_scr[...] = qk_ref[0].astype(F32)
    for kind in range(kinds):
        columns = slice(kind * DK, (kind + 1) * DK)
        for i in range(1, CONV):
            source = 2 * EDGE - i * kinds + kind
            dense_scr[EDGE - i : EDGE - i + 1, columns] = halo[source : source + 1]
        dense_scr[EDGE:, columns] = raw_scr[pl.ds(kind, tok, kinds), :]
    for c in range(chunks):
        span = slice(c * BLOCK, (c + 1) * BLOCK)
        for kind in range(kinds):
            own = [taps[n : n + 1] for n in range(kind, taps.shape[0], kinds)]
            rows = unit_rows(mixed_rows(dense_scr, own, c, slice(kind * DK, (kind + 1) * DK)))
            to_ref = kn_ref if kind % 2 else qn_ref
            to_ref[0, span, kind // 2 * DK : (kind // 2 + 1) * DK] = rows.astype(BF16)


def prepare_kernel(first, count, head, group, chunks, key_heads, mixes, *refs):
    length_ref, v_ref, halo_ref, v_taps_ref, log_ref, gain_ref, after_ref = refs[:7]
    refs = refs[7:]
    if mixes:
        qk_ref, qk_taps_ref, wu_ref, start_ref, map_ref, qn_ref, kn_ref = refs[:7]
        v_pad, m_scr, b_scr, fade_scr, st_scr, a_scr, x_scr, raw_scr, dense_scr = refs[7:]
        key_columns = slice(head * DK, (head + 1) * DK)
    else:
        kn_ref, wu_ref, start_ref, map_ref = refs[:4]
        v_pad, m_scr, b_scr, fade_scr, st_scr, a_scr, x_scr = refs[4:]
        key_columns = slice(0, DK)
    step = pl.program_id(0)
    used = length_ref[first + jnp.minimum(step, count - 1)] - lax.axis_index("seq") * (chunks * BLOCK)
    units = [(h, c) for c in range(chunks) for h in range(group)]
    slot = step % 2
    live = jnp.logical_and(step < count, used > 0)

    def begin():
        row = lax.broadcasted_iota(jnp.int32, (DK, DV + DK), 0)
        lane = lax.broadcasted_iota(jnp.int32, (DK, DV + DK), 1)
        for h in range(group):
            st_scr[h] = jnp.where(lane == row + DV, 1.0, 0.0).astype(F32)

    def advance(c):
        narrow, moved = [], []
        for h in range(group):
            narrow.append(st_scr[h].astype(BF16))
            start_ref[0, h, c * DK : (c + 1) * DK, :] = narrow[h]
        for h in range(group):
            moved.append(dot(m_scr[1 - slot, c, h], narrow[h]))
        for h in range(group):
            fade = fade_scr[1 - slot, c, h : h + 1, :]
            state = st_scr[h, :, :DV] * fade + (moved[h][:, :DV] + b_scr[1 - slot, c, h])
            trans = st_scr[h, :, DV:] * fade + moved[h][:, DV:]
            if c < chunks - 1:
                st_scr[h, :, :DV] = state
                st_scr[h, :, DV:] = trans
            else:
                map_ref[h, :, :DV] = state.astype(BF16)
                map_ref[h, :, DV:] = trans.astype(BF16)

    todo = [begin] + [functools.partial(advance, c) for c in range(chunks)]

    def run(n):
        for _ in range(min(n, len(todo))):
            todo.pop(0)()

    @pl.when(jnp.logical_not(live))
    def _():
        @pl.when(step > 0)
        def _():
            begin()
            for c in range(chunks):
                advance(c)

        @pl.when(step < count)
        def _():
            if mixes:
                qn_ref[...] = jnp.zeros_like(qn_ref)
                kn_ref[...] = jnp.zeros_like(kn_ref)
            wu_ref[...] = jnp.zeros_like(wu_ref)
            fade_scr[slot] = jnp.ones(fade_scr.shape[1:], F32)
            m_scr[slot] = jnp.zeros(m_scr.shape[1:], BF16)
            b_scr[slot] = jnp.zeros(b_scr.shape[1:], F32)

    @pl.when(live)
    def _():
        if mixes:
            mix(qk_ref, halo_ref, qk_taps_ref, qn_ref, kn_ref, raw_scr, dense_scr, key_heads, chunks)
        halo = halo_ref[0].astype(F32)
        v_pad[EDGE:, :] = v_ref[0].astype(F32)
        for i in range(CONV - 1):
            for h in range(group):
                source = 2 * EDGE + (i * key_heads + head) * group + h
                v_pad[EDGE - CONV + 1 + i : EDGE - CONV + 2 + i, h * DV : (h + 1) * DV] = halo[
                    source : source + 1
                ]
        v_all_taps = v_taps_ref[...].astype(F32)
        v_taps = [v_all_taps[i : i + 1] for i in range(CONV)]
        run(1)

        cum, gain = gates_of_heads(log_ref, gain_ref, used, head, group)
        faded = jnp.exp(cum)
        columns = as_columns(jnp.concatenate([cum, gain, gain * faded, faded], axis=0), chunks)

        def column(which, h, c):
            n = c * 8 + which * group + h
            return columns[:, n : n + 1]

        row = lax.broadcasted_iota(jnp.int32, (BLOCK, BLOCK), 0)
        lane = lax.broadcasted_iota(jnp.int32, (BLOCK, BLOCK), 1)
        below = row > lane
        small_row = lax.broadcasted_iota(jnp.int32, (TINY, BLOCK), 0)
        small_lane = lax.broadcasted_iota(jnp.int32, (TINY, BLOCK), 1)
        part_of = small_lane // TINY
        tiny_eye = jnp.where(small_row == small_lane % TINY, 1.0, 0.0).astype(F32)

        keys = [kn_ref[0, c * BLOCK : (c + 1) * BLOCK, key_columns] for c in range(chunks)]
        turned = [kc.T for kc in keys]
        run(1)

        compact = {}
        for c in range(chunks):
            kk = dot(keys[c], turned[c])
            vc = mixed_rows(v_pad, v_taps, c, slice(0, group * DV)).astype(BF16).astype(F32)
            kc = keys[c].astype(F32)
            for h in range(group):
                r = h * chunks + c
                gain_square = jnp.broadcast_to(column(1, h, c), (BLOCK, BLOCK))
                wu_ref[0, r, :, :DK] = (kc * column(2, h, c)).astype(BF16)
                wu_ref[0, r, :, DK:] = (vc[:, h * DV : (h + 1) * DV] * gain_square).astype(BF16)
                ratio = jnp.exp(column(0, h, c) - cum[h : h + 1, c * BLOCK : (c + 1) * BLOCK])
                strict = jnp.where(below, gain_square * ratio * kk, 0.0)
                a_scr[r] = strict.astype(BF16)
                tiny = strict[0:TINY]
                for b in range(1, BLOCK // TINY):
                    tiny = jnp.where(part_of == b, strict[b * TINY : (b + 1) * TINY], tiny)
                compact[r] = tiny

        run(1)
        solved = {r: tiny_eye for r in compact}
        for j in range(TINY - 1):
            pick = part_of * TINY + j
            for r in solved:
                factor = jnp.take_along_axis(compact[r], pick, axis=1, mode="promise_in_bounds")
                solved[r] = solved[r] - factor * solved[r][j : j + 1, :]
        for r in solved:
            for b in range(BLOCK // TINY):
                x_scr[r, b * TINY : (b + 1) * TINY, :] = jnp.where(
                    part_of == b, solved[r], 0.0
                ).astype(BF16)

        run(1)
        size = TINY
        while size < BLOCK:
            odd = [s for s in range(size, BLOCK, 2 * size)]
            half_lane = lax.broadcasted_iota(jnp.int32, (BLOCK // 2, BLOCK), 1)
            half_row = lax.broadcasted_iota(jnp.int32, (BLOCK // 2, BLOCK), 0)
            left = half_lane // size == 2 * (half_row // size)
            moved = {}
            for h, c in units:
                r = h * chunks + c
                lower = jnp.concatenate([a_scr[r, s : s + size, :] for s in odd], axis=0)
                lower = jnp.where(left, lower, jnp.zeros_like(lower))
                moved[r] = dot(lower, x_scr[r]).astype(BF16)
            for h, c in units:
                r = h * chunks + c
                spread = []
                for n in range(len(odd)):
                    spread.append(jnp.zeros((size, BLOCK), BF16))
                    spread.append(moved[r][n * size : (n + 1) * size])
                own = jnp.concatenate([x_scr[r, s : s + size, :] for s in odd], axis=0)
                update = own.astype(F32) - dot(own, jnp.concatenate(spread, axis=0))
                update = update.astype(BF16)
                for n, s in enumerate(odd):
                    x_scr[r, s : s + size, :] = update[n * size : (n + 1) * size]
            run(1)
            size *= 2

        run(1)
        solved_rows = {}
        for h, c in units:
            r = h * chunks + c
            solved_rows[r] = dot(x_scr[r], wu_ref[0, r]).astype(BF16)
            if len(solved_rows) == len(units) // 2:
                run(1)
        for r in solved_rows:
            wu_ref[0, r] = solved_rows[r]
        run(len(todo))
        for c in range(chunks):
            sums = cum[:, c * BLOCK : (c + 1) * BLOCK]
            last = sums[:, BLOCK - 1 : BLOCK]
            tail = jnp.exp(last - sums)
            fade = jnp.broadcast_to(jnp.exp(last), (group, BLOCK))
            for h in range(group):
                r = h * chunks + c
                fade_scr[slot, c, h : h + 1, :] = fade[h : h + 1]
                scaled = (turned[c].astype(F32) * tail[h : h + 1, :]).astype(BF16)
                both = dot(scaled, solved_rows[r])
                m_scr[slot, c, h] = (-both[:, :DK]).astype(BF16)
                b_scr[slot, c, h] = both[:, DK:]


def prepare(job, lengths, qk_rows, v_in, halo, qk_taps, v_taps, log_decay, write_gain, key_heads, mixed, after):
    head, first, count = job
    tok = v_in.shape[1]
    value_heads = v_in.shape[2] // DV
    group = value_heads // key_heads
    chunks = tok // BLOCK
    rows = group * chunks
    wide = group * DV
    mixes = mixed is None

    def now(i):
        return jnp.minimum(i, count - 1)

    def before(i):
        return jnp.maximum(i - 1, 0)

    def whole_of(i, lengths):
        return (first + now(i), 0, 0)

    operands = [far(v_in), halo, far(v_taps), far(log_decay), far(write_gain), far(after)]
    in_specs = [
        pl.BlockSpec((1, tok, wide), lambda i, lengths: (first + now(i), 0, head)),
        pl.BlockSpec((1,) + halo.shape[1:], whole_of),
        pl.BlockSpec((CONV, wide), lambda i, lengths: (0, head)),
        pl.BlockSpec((1, value_heads, tok), whole_of),
        pl.BlockSpec((1, value_heads, tok), whole_of),
        pl.BlockSpec(memory_space=pltpu.HBM),
    ]
    out_specs = [
        pl.BlockSpec((1, rows, BLOCK, DK + DV), lambda i, lengths: (now(i), 0, 0, 0)),
        pl.BlockSpec((1, group, chunks * DK, DV + DK), lambda i, lengths: (before(i), 0, 0, 0)),
        pl.BlockSpec((group, DK, DV + DK), lambda i, lengths: (before(i), 0, 0)),
    ]
    out_shape = [
        pltpu.HBM((count, rows, BLOCK, DK + DV), BF16),
        pltpu.HBM((count, group, chunks * DK, DV + DK), BF16),
        jax.ShapeDtypeStruct((count * group, DK, DV + DK), BF16),
    ]
    scratch = [
        pltpu.VMEM((tok + EDGE, wide), F32),
        pltpu.VMEM((2, chunks, group, DK, DK), BF16),
        pltpu.VMEM((2, chunks, group, DK, DV), F32),
        pltpu.VMEM((2, chunks, group, BLOCK), F32),
        pltpu.VMEM((group, DK, DV + DK), F32),
        pltpu.VMEM((rows, BLOCK, BLOCK), BF16),
        pltpu.VMEM((rows, BLOCK, BLOCK), BF16),
    ]
    if mixes:
        operands += [far(qk_rows), far(qk_taps)]
        in_specs += [
            pl.BlockSpec((1,) + qk_rows.shape[1:], whole_of),
            pl.BlockSpec(qk_taps.shape, lambda i, lengths: (0, 0)),
        ]
        out_specs += [pl.BlockSpec((1, tok, key_heads * DK), lambda i, lengths: (now(i), 0, 0))] * 2
        out_shape += [pltpu.HBM((count, tok, key_heads * DK), BF16)] * 2
        scratch += [
            pltpu.VMEM(qk_rows.shape[1:], F32),
            pltpu.VMEM((tok + EDGE, 2 * key_heads * DK), F32),
        ]
    else:
        operands.append(far(mixed))
        in_specs.append(pl.BlockSpec((1, tok, DK), lambda i, lengths: (first + now(i), 0, head)))
    return pl.pallas_call(
        functools.partial(prepare_kernel, first, count, head, group, chunks, key_heads, mixes),
        grid_spec=pltpu.PrefetchScalarGridSpec(
            num_scalar_prefetch=1,
            grid=(count + 1,),
            in_specs=in_specs,
            out_specs=out_specs,
            scratch_shapes=scratch,
        ),
        out_shape=out_shape,
        compiler_params=pltpu.CompilerParams(vmem_limit_bytes=VMEM_BYTES),
        cost_estimate=pl.CostEstimate(flops=5 * 10**9 * count, bytes_accessed=4 * 2**20 * count, transcendentals=10**6),
        name="prepare",
    )(lengths, *operands)


def outputs_kernel(
    first, head, group, chunks,
    length_ref, qn_ref, kn_ref, wu_ref, start_ref, log_ref, gain_ref, enter_ref, z_ref, norm_ref, held_ref, after_ref,
    out_ref,
    first_scr, score_scr, seen_scr,
):
    used = length_ref[first + pl.program_id(0)] - lax.axis_index("seq") * (chunks * BLOCK)
    units = [(h, c) for c in range(chunks) for h in range(group)]

    @pl.when(used <= 0)
    def _():
        out_ref[...] = jnp.zeros_like(out_ref)

    @pl.when(used > 0)
    def _():
        cum, gain = gates_of_heads(log_ref, gain_ref, used, head, group)
        faded = jnp.exp(cum)
        bases = block_bases([cum, faded], chunks)

        row = lax.broadcasted_iota(jnp.int32, (BLOCK, BLOCK), 0)
        lane = lax.broadcasted_iota(jnp.int32, (BLOCK, BLOCK), 1)
        upto = row >= lane
        norm_gain = norm_ref[...]

        def span(c):
            return slice(c * BLOCK, (c + 1) * BLOCK)

        for h in range(group):
            moved = dot(start_ref[0, h, :, DV:], enter_ref[h])
            first_scr[h] = (moved + start_ref[0, h, :, :DV].astype(F32)).astype(BF16)
        for c in range(chunks):
            qk = dot(qn_ref[0, span(c), :], kn_ref[0, span(c), :].T)
            squares = spread_squares(bases[c], group, 2)
            q_wide = qn_ref[0, span(c), :].astype(F32)
            for h in range(group):
                r = h * chunks + c
                score_scr[r] = jnp.where(upto, jnp.exp(squares[h]) * qk, 0.0).astype(BF16)
                seen_scr[r] = q_wide * squares[group + h]
        both, raws = {}, {}
        for h, c in units:
            r = h * chunks + c
            both[r] = dot(score_scr[r], wu_ref[0, r])
        for h, c in units:
            r = h * chunks + c
            seen = (seen_scr[r] - both[r][:, :DK]).astype(BF16)
            raws[r] = dot(seen, first_scr[h, span(c), :]) + both[r][:, DK:]
        for h, c in units:
            raw = raws[h * chunks + c]
            cols = slice(h * DV, (h + 1) * DV)
            mean = jnp.sum(raw * raw, axis=-1, keepdims=True) * (1.0 / DV)
            gated = raw * lax.rsqrt(mean + EPSILON) * norm_gain * silu(z_ref[0, span(c), cols].astype(F32))
            out_ref[0, span(c), cols] = jnp.where(row + c * BLOCK < used, gated, 0.0).astype(BF16)


def outputs(
    job, piece, lengths, qn, kn, wu, starts, log_decay, write_gain, enter, gate_z, norm_gain, key_heads, held, after,
):
    head, first, _ = job
    begin, count = piece
    prompts, tok, width = gate_z.shape
    rows = wu.shape[1]
    chunks = tok // BLOCK
    group = rows // chunks
    wide = group * DV
    value_heads = key_heads * group
    shift = begin - first
    from_mix = begin if qn.shape[0] == prompts else shift

    def whole_of(i, lengths):
        return (begin + i, 0, 0)

    def wide_of(i, lengths):
        return (begin + i, 0, head)

    def mixed_of(i, lengths):
        return (from_mix + i, 0, head)

    empty = held is None
    return pl.pallas_call(
        functools.partial(outputs_kernel, begin, head, group, chunks),
        grid_spec=pltpu.PrefetchScalarGridSpec(
            num_scalar_prefetch=1,
            grid=(count,),
            in_specs=[
                pl.BlockSpec((1, tok, DK), mixed_of),
                pl.BlockSpec((1, tok, DK), mixed_of),
                pl.BlockSpec((1, rows, BLOCK, DK + DV), lambda i, lengths: (shift + i, 0, 0, 0)),
                pl.BlockSpec((1, group, chunks * DK, DV + DK), lambda i, lengths: (shift + i, 0, 0, 0)),
                pl.BlockSpec((1, value_heads, tok), whole_of),
                pl.BlockSpec((1, value_heads, tok), whole_of),
                pl.BlockSpec((group, DK, DV), lambda i, lengths: (shift + i, 0, 0)),
                pl.BlockSpec((1, tok, wide), wide_of),
                pl.BlockSpec((1, DV), lambda i, lengths: (0, 0)),
                pl.BlockSpec(memory_space=pltpu.HBM),
                pl.BlockSpec(memory_space=pltpu.HBM),
            ],
            out_specs=pl.BlockSpec((1, tok, wide), wide_of),
            scratch_shapes=[
                pltpu.VMEM((group, chunks * DK, DV), BF16),
                pltpu.VMEM((rows, BLOCK, BLOCK), BF16),
                pltpu.VMEM((rows, BLOCK, DV), F32),
            ],
        ),
        out_shape=pltpu.HBM((prompts, tok, width), BF16),
        input_output_aliases={} if empty else {10: 0},
        compiler_params=pltpu.CompilerParams(vmem_limit_bytes=VMEM_BYTES),
        cost_estimate=pl.CostEstimate(flops=3 * 10**9 * count, bytes_accessed=4 * 2**20 * count, transcendentals=10**6),
        name="outputs",
    )(
        lengths, far(qn), far(kn), far(wu), far(starts), far(log_decay), far(write_gain), enter, far(gate_z),
        far(norm_gain.reshape(1, DV)), far(after if empty else held), far(wu if after is held else after),
    )


def own_chip():
    seq = lax.axis_index("seq")
    return seq // 2, seq % 2 == 1


def early_late(own, other, odd):
    return jnp.where(odd, other, own), jnp.where(odd, own, other)


def compose_maps(ins, outs):
    own_ref, other_ref = ins
    _, odd = own_chip()
    for n in range(own_ref.shape[0]):
        early, late = early_late(own_ref[n], other_ref[n], odd)
        both = dot(late[:, DV:], early)
        outs[0][n, :, :DV] = (both[:, :DV] + late[:, :DV].astype(F32)).astype(BF16)
        outs[0][n, :, DV:] = both[:, DV:].astype(BF16)


def close_maps(ins, outs):
    own_ref, other_ref = ins[:2]
    refs = ins[2:]
    chips = len(refs)
    chip, odd = own_chip()

    def of_chip(j, n):
        value = refs[0][n]
        for k in range(1, chips):
            value = jnp.where((chip + chips - k) % chips == j, refs[k][n], value)
        return value

    for n in range(own_ref.shape[0]):
        running = of_chip(0, n)[:, :DV]
        entering = jnp.zeros_like(running)
        for j in range(1, chips):
            entering = jnp.where(chip == j, running, entering)
            there = of_chip(j, n)
            running = (dot(there[:, DV:], running) + there[:, :DV].astype(F32)).astype(BF16)
        early, _ = early_late(own_ref[n], other_ref[n], odd)
        second = (dot(early[:, DV:], entering) + early[:, :DV].astype(F32)).astype(BF16)
        outs[0][n] = jnp.where(odd, second, entering)
        outs[1][n] = running


def chain_maps(ins, outs):
    count = len(ins)
    mine = lax.axis_index("seq")

    def run(at):
        for n in range(ins[0].shape[0]):
            running = ins[at][n, :, :DV]
            entering = jnp.zeros_like(running)
            for j in range(1, count):
                if j == at:
                    entering = running
                there = ins[(at - j) % count]
                moved = dot(there[n, :, DV:], running)
                running = (moved + there[n, :, :DV].astype(F32)).astype(BF16)
            outs[0][n] = entering
            outs[1][n] = running

    for at in range(count):
        pl.when(mine == at)(functools.partial(run, at))


def choose_finals(group, placement_ref, finals, outs):
    refs = [(ref, n) for ref in finals for n in range(ref.shape[0] // group)]
    for r in range(placement_ref.shape[1]):
        prompt = placement_ref[0, r]
        for p, (ref, n) in enumerate(refs):
            @pl.when(prompt == p)
            def _(ref=ref, n=n):
                outs[0][r] = ref[n * group : (n + 1) * group]


def state_step(placement, group, compose, chain, close, earlier, after):
    operands, shapes = [placement], []
    steps = []
    if compose is not None:
        steps.append(("compose", len(operands), len(compose), len(shapes)))
        operands += compose
        shapes += [compose[0]]
    if chain is not None or close is not None:
        steps.append(("chain" if close is None else "close", len(operands), len(close or chain), len(shapes)))
        close = close or chain
        operands += close
        shapes += [jax.ShapeDtypeStruct((close[0].shape[0], DK, DV), BF16)] * 2
        if earlier is not None:
            steps.append(("choose", len(operands), len(earlier), len(shapes)))
            operands += earlier
            shapes.append(jax.ShapeDtypeStruct((placement.shape[1], group, DK, DV), BF16))
    out_shape = [jax.ShapeDtypeStruct(x.shape, x.dtype) for x in shapes] + [pltpu.HBM((8, 128), F32)]

    def kernel(*refs):
        refs[-1][...] = jnp.zeros_like(refs[-1])
        ins, outs = refs[: len(operands)], refs[len(operands) + 1 :]
        closed = None
        for kind, at, size, to in steps:
            part = ins[at : at + size]
            if kind == "compose":
                compose_maps(part, outs[to : to + 1])
            elif kind in ("close", "chain"):
                (close_maps if kind == "close" else chain_maps)(part, outs[to : to + 2])
                closed = outs[to + 1]
            else:
                choose_finals(group, ins[0], list(part) + [closed], outs[to:])

    vmem = pl.BlockSpec(memory_space=pltpu.VMEM)
    return pl.pallas_call(
        kernel,
        in_specs=[pl.BlockSpec(memory_space=pltpu.SMEM)]
        + [vmem] * (len(operands) - 1)
        + [pl.BlockSpec(memory_space=pltpu.HBM)],
        out_specs=[vmem] * len(out_shape),
        out_shape=out_shape,
        compiler_params=pltpu.CompilerParams(vmem_limit_bytes=SMALL_VMEM_BYTES),
        cost_estimate=pl.CostEstimate(flops=10**9, bytes_accessed=2**20, transcendentals=0),
        name="state_step",
    )(*operands, far(after))


def deliver(parts):
    count, group = parts[0].shape[:2]

    def kernel(*refs):
        for n, ref in enumerate(refs[:-1]):
            refs[-1][:, n * group : (n + 1) * group] = ref[...].astype(F32)

    return pl.pallas_call(
        kernel,
        grid=(2,),
        in_specs=[pl.BlockSpec((count // 2, group, DK, DV), lambda i: (i, 0, 0, 0))] * len(parts),
        out_specs=pl.BlockSpec((count // 2, group * len(parts), DK, DV), lambda i: (i, 0, 0, 0)),
        out_shape=jax.ShapeDtypeStruct((count, group * len(parts), DK, DV), F32),
        compiler_params=pltpu.CompilerParams(vmem_limit_bytes=VMEM_BYTES),
        name="deliver",
    )(*parts)


def pair_swap(block):
    count = lax.axis_size("seq")
    return lax.ppermute(block, "seq", [(i, i ^ 1) for i in range(count)])


def from_behind(block, distance):
    count = lax.axis_size("seq")
    return lax.ppermute(block, "seq", [(i, (i + distance) % count) for i in range(count)])


def from_chip_behind(block, distance):
    count = lax.axis_size("seq")
    chips = count // 2
    route = [(i, ((i // 2 + distance) % chips) * 2 + i % 2) for i in range(count)]
    return lax.ppermute(block, "seq", route)


def shards(
    qk_in, v_in, gate_z, conv_qk, conv_v, log_decay, write_gain, norm_gain, prompt_lengths, placement,
):
    prompts, tok = qk_in.shape[:2]
    key_heads = qk_in.shape[3] // DK
    value_heads = v_in.shape[2] // DV
    rim = CONV - 1
    seq_count = lax.axis_size("seq")
    head_count = lax.axis_size("head")

    def by_head(x):
        x = x.reshape(x.shape[0], x.shape[1], 2, key_heads, DK)
        return jnp.transpose(x, (0, 1, 3, 2, 4)).reshape(x.shape[0], -1, DK)

    qk_rows = by_head(qk_in)
    qk_taps = by_head(conv_qk[None])[0]
    qk_tail = qk_rows[:, (tok - rim) * 2 * key_heads :]
    v_tail = v_in[:, tok - rim :].reshape(prompts, rim * value_heads, DV)
    front = 2 * EDGE - qk_tail.shape[1]
    back = 2 * EDGE - v_tail.shape[1]
    tails = jnp.concatenate(
        [
            jnp.zeros((prompts, front, DK), BF16),
            qk_tail,
            v_tail,
            jnp.zeros((prompts, back, DK), BF16),
        ],
        axis=1,
    )
    halo = lax.ppermute(tails, "seq", [(i, i + 1) for i in range(seq_count - 1)])
    group = value_heads // key_heads
    chips = seq_count // 2
    half = prompts // 2
    jobs = [(head, 0, prompts) for head in range(key_heads)]
    if key_heads == 1:
        jobs = [(0, 0, half), (0, half, prompts - half)]
    total = len(jobs)
    made, finals, sent = [], [], {}
    attended = None
    last = v_in

    def finish(job, results):
        head = jobs[job][0]
        finals.append(results[1])
        if len(results) > 3:
            sent[head] = lax.all_to_all(results[2], "head", 0, 0)
        return results[0], results[-1]

    def earlier(job):
        same = [n for n in range(total) if jobs[n][0] == jobs[job][0]]
        return [finals[n] for n in same[:-1]] if job == same[-1] else None

    def emit(job, entered, attended, last):
        qn, kn, wu, starts, _ = made[job]
        return outputs(
            jobs[job], jobs[job][1:], prompt_lengths, qn, kn, wu, starts, log_decay, write_gain,
            entered, gate_z, norm_gain, key_heads, attended, last,
        )

    for job in jobs:
        mixed = None if job[0] == 0 else made[0][:2]
        wu, starts, own_map, *new = prepare(
            job, prompt_lengths, qk_rows, v_in, halo, qk_taps, conv_v, log_decay, write_gain, key_heads,
            mixed and mixed[1], last,
        )
        last = wu
        moved = [own_map]
        if job == jobs[-1]:
            moved.append(pair_swap(own_map))
        else:
            moved += [from_behind(own_map, k) for k in range(1, seq_count)]
        made.append((*(mixed or new), wu, starts, moved))

    entered = []
    for job in range(total - 1):
        results = state_step(placement, group, None, made[job][4], None, earlier(job), last)
        enter, last = finish(job, results)
        entered.append(enter)
    pair = made[-1][4]
    chip_map, last = state_step(placement, group, pair, None, None, None, last)
    chip_maps = [chip_map] + [from_chip_behind(chip_map, k) for k in range(1, chips)]
    for job in range(total - 1):
        attended = last = emit(job, entered[job], attended, last)
    results = state_step(placement, group, None, None, pair + chip_maps, earlier(total - 1), last)
    enter, last = finish(total - 1, results)
    attended = emit(total - 1, enter, attended, last)
    rollout = deliver([sent[head] for head in range(key_heads)])
    return attended, rollout.reshape(1, 1, head_count * value_heads, DK, DV)


def solution(mesh):
    return jax.shard_map(
        shards,
        mesh=mesh,
        in_specs=(
            P(None, "seq", None, "head"),
            P(None, "seq", "head"),
            P(None, "seq", "head"),
            P(None, None, "head"),
            P(None, "head"),
            P(None, "head", "seq"),
            P(None, "head", "seq"),
            P(),
            P(),
            P("seq", None),
        ),
        out_specs=(P(None, "seq", "head"), P("seq", "head", None, None, None)),
        check_vma=False,
    )
```

```python
import functools

import jax
import jax.numpy as jnp
from jax import lax
from jax.experimental import pallas as pl
from jax.experimental.pallas import tpu as pltpu
from jax.sharding import PartitionSpec as P

DK = 128
DV = 128
CONV = 4
BLOCK = 128
TINY = 16
EDGE = 8
EPSILON = 1e-06
VMEM_BYTES = 40 * 1024 * 1024
SMALL_VMEM_BYTES = 8 * 1024 * 1024
F32 = jnp.float32
BF16 = jnp.bfloat16


def far(x):
    return pltpu.with_memory_space_constraint(x, pltpu.HBM)


def dot(a, b):
    return lax.dot_general(a, b, (((1,), (0,)), ((), ())), preferred_element_type=F32)


def silu(x):
    half = 0.5 * x
    return half + half * jnp.tanh(half)


def mixed_rows(pad_ref, taps, rim, first, step, c):
    total = None
    for i in range(CONV):
        start = rim + first + step * (c * BLOCK + i - (CONV - 1))
        stride = None if step == 1 else step
        term = pad_ref[pl.ds(start, BLOCK, stride), :] * taps[i]
        total = term if total is None else total + term
    return silu(total)


def unit_rows(x):
    return x * lax.rsqrt(jnp.sum(x * x, axis=-1, keepdims=True) + EPSILON)


def heads_rows(ref, head, group):
    every = ref[0]
    rows = every[:group]
    for n in range(1, every.shape[0] // group):
        rows = jnp.where(head == n, every[n * group : (n + 1) * group], rows)
    return rows


def gates_of_heads(log_ref, gain_ref, used, head, group):
    log = heads_rows(log_ref, head, group)
    lane = lax.broadcasted_iota(jnp.int32, log.shape, 1)
    valid = lane < used
    cum = jnp.where(valid, log, 0.0)
    gain = jnp.where(valid, heads_rows(gain_ref, head, group), 0.0)
    shift = 1
    while shift < BLOCK:
        cum = cum + jnp.where(lane % BLOCK >= shift, pltpu.roll(cum, shift, 1), 0.0)
        shift *= 2
    return cum, gain


def as_columns(rows, chunks):
    parts = [rows[:, c * BLOCK : (c + 1) * BLOCK] for c in range(chunks)]
    short = BLOCK - 8 * chunks
    if short:
        parts.append(jnp.zeros((short, BLOCK), F32))
    return jnp.concatenate(parts, axis=0).T


def block_bases(parts, chunks):
    rows = jnp.concatenate(parts, axis=0)
    short = 7 - rows.shape[0]
    fill = [jnp.zeros((short, rows.shape[1]), F32)] if short else []
    rows = jnp.concatenate([rows] + fill + [jnp.ones((1, rows.shape[1]), F32)], axis=0)
    return [rows[:, c * BLOCK : (c + 1) * BLOCK] for c in range(chunks)]


def spread_squares(base, group, kinds):
    high = base.astype(BF16).astype(F32)
    middle = (base - high).astype(BF16).astype(F32)
    low = base - high - middle
    parts = [high, middle, low]
    row = lax.broadcasted_iota(jnp.int32, (32, BLOCK), 0)
    which = row % 8
    real = row < 24
    stacked = jnp.concatenate(parts + [jnp.zeros_like(high)], axis=0)
    left = jnp.where(jnp.logical_and(which == 7, real), 1.0, stacked).T.astype(BF16)
    blocks = []
    for h in range(group):
        minus = jnp.concatenate([jnp.broadcast_to(-part[h : h + 1], (8, BLOCK)) for part in parts + [low]], axis=0)
        blocks.append(jnp.where(which == h, 1.0, jnp.where(which == 7, minus, 0.0)))
    for n in range(group, group * kinds):
        blocks.append(jnp.where(which == n, 1.0, 0.0).astype(F32))
    every = dot(left, jnp.concatenate(blocks, axis=1).astype(BF16))
    return [every[:, n * BLOCK : (n + 1) * BLOCK] for n in range(group * kinds)]


def mix(qk_ref, halo_ref, taps_ref, qn_ref, kn_ref, raw_scr, key_heads, chunks):
    kinds = 2 * key_heads
    rim = 2 * EDGE
    taps = taps_ref[...].astype(F32)
    raw_scr[:rim] = halo_ref[0].astype(F32)[:rim]
    raw_scr[rim:] = qk_ref[0].astype(F32)
    for c in range(chunks):
        span = slice(c * BLOCK, (c + 1) * BLOCK)
        for kind in range(kinds):
            own = [taps[n : n + 1] for n in range(kind, taps.shape[0], kinds)]
            rows = unit_rows(mixed_rows(raw_scr, own, rim, kind, kinds, c))
            to_ref = kn_ref if kind % 2 else qn_ref
            to_ref[0, span, kind // 2 * DK : (kind // 2 + 1) * DK] = rows.astype(BF16)


def prepare_kernel(first, count, head, group, chunks, key_heads, mixes, *refs):
    length_ref, v_ref, halo_ref, v_taps_ref, log_ref, gain_ref, after_ref = refs[:7]
    refs = refs[7:]
    if mixes:
        qk_ref, qk_taps_ref, wu_ref, start_ref, map_ref, qn_ref, kn_ref = refs[:7]
        v_pad, m_scr, b_scr, fade_scr, st_scr, a_scr, x_scr, raw_scr = refs[7:]
        key_columns = slice(head * DK, (head + 1) * DK)
    else:
        kn_ref, wu_ref, start_ref, map_ref = refs[:4]
        v_pad, m_scr, b_scr, fade_scr, st_scr, a_scr, x_scr = refs[4:]
        key_columns = slice(0, DK)
    step = pl.program_id(0)
    used = length_ref[first + jnp.minimum(step, count - 1)] - lax.axis_index("seq") * (chunks * BLOCK)
    units = [(h, c) for c in range(chunks) for h in range(group)]
    slot = step % 2
    live = jnp.logical_and(step < count, used > 0)

    def begin():
        row = lax.broadcasted_iota(jnp.int32, (DK, DV + DK), 0)
        lane = lax.broadcasted_iota(jnp.int32, (DK, DV + DK), 1)
        for h in range(group):
            st_scr[h] = jnp.where(lane == row + DV, 1.0, 0.0).astype(F32)

    def advance(c):
        narrow, moved = [], []
        for h in range(group):
            narrow.append(st_scr[h].astype(BF16))
            start_ref[0, h, c * DK : (c + 1) * DK, :] = narrow[h]
        for h in range(group):
            moved.append(dot(m_scr[1 - slot, c, h], narrow[h]))
        for h in range(group):
            fade = fade_scr[1 - slot, c, h : h + 1, :]
            state = st_scr[h, :, :DV] * fade + (moved[h][:, :DV] + b_scr[1 - slot, c, h])
            trans = st_scr[h, :, DV:] * fade + moved[h][:, DV:]
            if c < chunks - 1:
                st_scr[h, :, :DV] = state
                st_scr[h, :, DV:] = trans
            else:
                map_ref[h, :, :DV] = state.astype(BF16)
                map_ref[h, :, DV:] = trans.astype(BF16)

    todo = [begin] + [functools.partial(advance, c) for c in range(chunks)]

    def run(n):
        for _ in range(min(n, len(todo))):
            todo.pop(0)()

    @pl.when(jnp.logical_not(live))
    def _():
        @pl.when(step > 0)
        def _():
            begin()
            for c in range(chunks):
                advance(c)

        @pl.when(step < count)
        def _():
            if mixes:
                qn_ref[...] = jnp.zeros_like(qn_ref)
                kn_ref[...] = jnp.zeros_like(kn_ref)
            wu_ref[...] = jnp.zeros_like(wu_ref)
            fade_scr[slot] = jnp.ones(fade_scr.shape[1:], F32)
            m_scr[slot] = jnp.zeros(m_scr.shape[1:], BF16)
            b_scr[slot] = jnp.zeros(b_scr.shape[1:], F32)

    @pl.when(live)
    def _():
        if mixes:
            mix(qk_ref, halo_ref, qk_taps_ref, qn_ref, kn_ref, raw_scr, key_heads, chunks)
        halo = halo_ref[0].astype(F32)
        v_pad[EDGE:, :] = v_ref[0].astype(F32)
        for i in range(CONV - 1):
            for h in range(group):
                source = 2 * EDGE + (i * key_heads + head) * group + h
                v_pad[EDGE - CONV + 1 + i : EDGE - CONV + 2 + i, h * DV : (h + 1) * DV] = halo[
                    source : source + 1
                ]
        v_all_taps = v_taps_ref[...].astype(F32)
        v_taps = [v_all_taps[i : i + 1] for i in range(CONV)]
        run(1)

        cum, gain = gates_of_heads(log_ref, gain_ref, used, head, group)
        faded = jnp.exp(cum)
        columns = as_columns(jnp.concatenate([cum, gain, gain * faded, faded], axis=0), chunks)

        def column(which, h, c):
            n = c * 8 + which * group + h
            return columns[:, n : n + 1]

        row = lax.broadcasted_iota(jnp.int32, (BLOCK, BLOCK), 0)
        lane = lax.broadcasted_iota(jnp.int32, (BLOCK, BLOCK), 1)
        below = row > lane
        small_row = lax.broadcasted_iota(jnp.int32, (TINY, BLOCK), 0)
        small_lane = lax.broadcasted_iota(jnp.int32, (TINY, BLOCK), 1)
        part_of = small_lane // TINY
        tiny_eye = jnp.where(small_row == small_lane % TINY, 1.0, 0.0).astype(F32)

        keys = [kn_ref[0, c * BLOCK : (c + 1) * BLOCK, key_columns] for c in range(chunks)]
        turned = [kc.T for kc in keys]
        run(1)

        compact = {}
        for c in range(chunks):
            kk = dot(keys[c], turned[c])
            for h in range(group):
                r = h * chunks + c
                ratio = jnp.exp(column(0, h, c) - cum[h : h + 1, c * BLOCK : (c + 1) * BLOCK])
                strict = jnp.where(below, column(1, h, c) * ratio * kk, 0.0)
                a_scr[r] = strict.astype(BF16)
                tiny = strict[0:TINY]
                for b in range(1, BLOCK // TINY):
                    tiny = jnp.where(part_of == b, strict[b * TINY : (b + 1) * TINY], tiny)
                compact[r] = tiny

        run(1)
        solved = {r: tiny_eye for r in compact}
        for j in range(TINY - 1):
            pick = part_of * TINY + j
            for r in solved:
                factor = jnp.take_along_axis(compact[r], pick, axis=1, mode="promise_in_bounds")
                solved[r] = solved[r] - factor * solved[r][j : j + 1, :]
        for r in solved:
            for b in range(BLOCK // TINY):
                x_scr[r, b * TINY : (b + 1) * TINY, :] = jnp.where(
                    part_of == b, solved[r], 0.0
                ).astype(BF16)

        run(1)
        size = TINY
        while size < BLOCK:
            odd = [s for s in range(size, BLOCK, 2 * size)]
            half_lane = lax.broadcasted_iota(jnp.int32, (BLOCK // 2, BLOCK), 1)
            half_row = lax.broadcasted_iota(jnp.int32, (BLOCK // 2, BLOCK), 0)
            left = half_lane // size == 2 * (half_row // size)
            moved = {}
            for h, c in units:
                r = h * chunks + c
                lower = jnp.concatenate([a_scr[r, s : s + size, :] for s in odd], axis=0)
                lower = jnp.where(left, lower, jnp.zeros_like(lower))
                moved[r] = dot(lower, x_scr[r]).astype(BF16)
            for h, c in units:
                r = h * chunks + c
                spread = []
                for n in range(len(odd)):
                    spread.append(jnp.zeros((size, BLOCK), BF16))
                    spread.append(moved[r][n * size : (n + 1) * size])
                own = jnp.concatenate([x_scr[r, s : s + size, :] for s in odd], axis=0)
                update = own.astype(F32) - dot(own, jnp.concatenate(spread, axis=0))
                update = update.astype(BF16)
                for n, s in enumerate(odd):
                    x_scr[r, s : s + size, :] = update[n * size : (n + 1) * size]
            run(1)
            size *= 2

        for c in range(chunks):
            vc = mixed_rows(v_pad, v_taps, EDGE, 0, 1, c).astype(BF16).astype(F32)
            kc = keys[c].astype(F32)
            for h in range(group):
                r = h * chunks + c
                right = jnp.concatenate(
                    [
                        (kc * column(2, h, c)).astype(BF16),
                        (vc[:, h * DV : (h + 1) * DV] * column(1, h, c)).astype(BF16),
                    ],
                    axis=1,
                )
                wu_ref[0, r] = dot(x_scr[r], right).astype(BF16)
            if c == chunks // 2:
                run(1)
        run(len(todo))
        for c in range(chunks):
            sums = cum[:, c * BLOCK : (c + 1) * BLOCK]
            last = sums[:, BLOCK - 1 : BLOCK]
            tail = jnp.exp(last - sums)
            fade = jnp.broadcast_to(jnp.exp(last), (group, BLOCK))
            for h in range(group):
                r = h * chunks + c
                fade_scr[slot, c, h : h + 1, :] = fade[h : h + 1]
                scaled = (turned[c].astype(F32) * tail[h : h + 1, :]).astype(BF16)
                both = dot(scaled, wu_ref[0, r])
                m_scr[slot, c, h] = (-both[:, :DK]).astype(BF16)
                b_scr[slot, c, h] = both[:, DK:]


def prepare(job, lengths, qk_rows, v_in, halo, qk_taps, v_taps, log_decay, write_gain, key_heads, mixed, after):
    head, first, count = job
    tok = v_in.shape[1]
    value_heads = v_in.shape[2] // DV
    group = value_heads // key_heads
    chunks = tok // BLOCK
    rows = group * chunks
    wide = group * DV
    mixes = mixed is None

    def now(i):
        return jnp.minimum(i, count - 1)

    def before(i):
        return jnp.maximum(i - 1, 0)

    def whole_of(i, lengths):
        return (first + now(i), 0, 0)

    operands = [far(v_in), halo, far(v_taps), far(log_decay), far(write_gain), far(after)]
    in_specs = [
        pl.BlockSpec((1, tok, wide), lambda i, lengths: (first + now(i), 0, head)),
        pl.BlockSpec((1,) + halo.shape[1:], whole_of),
        pl.BlockSpec((CONV, wide), lambda i, lengths: (0, head)),
        pl.BlockSpec((1, value_heads, tok), whole_of),
        pl.BlockSpec((1, value_heads, tok), whole_of),
        pl.BlockSpec(memory_space=pltpu.HBM),
    ]
    out_specs = [
        pl.BlockSpec((1, rows, BLOCK, DK + DV), lambda i, lengths: (now(i), 0, 0, 0)),
        pl.BlockSpec((1, group, chunks * DK, DV + DK), lambda i, lengths: (before(i), 0, 0, 0)),
        pl.BlockSpec((group, DK, DV + DK), lambda i, lengths: (before(i), 0, 0)),
    ]
    out_shape = [
        pltpu.HBM((count, rows, BLOCK, DK + DV), BF16),
        pltpu.HBM((count, group, chunks * DK, DV + DK), BF16),
        jax.ShapeDtypeStruct((count * group, DK, DV + DK), BF16),
    ]
    scratch = [
        pltpu.VMEM((tok + EDGE, wide), F32),
        pltpu.VMEM((2, chunks, group, DK, DK), BF16),
        pltpu.VMEM((2, chunks, group, DK, DV), F32),
        pltpu.VMEM((2, chunks, group, BLOCK), F32),
        pltpu.VMEM((group, DK, DV + DK), F32),
        pltpu.VMEM((rows, BLOCK, BLOCK), BF16),
        pltpu.VMEM((rows, BLOCK, BLOCK), BF16),
    ]
    if mixes:
        operands += [far(qk_rows), far(qk_taps)]
        in_specs += [
            pl.BlockSpec((1,) + qk_rows.shape[1:], whole_of),
            pl.BlockSpec(qk_taps.shape, lambda i, lengths: (0, 0)),
        ]
        out_specs += [pl.BlockSpec((1, tok, key_heads * DK), lambda i, lengths: (now(i), 0, 0))] * 2
        out_shape += [pltpu.HBM((count, tok, key_heads * DK), BF16)] * 2
        scratch.append(pltpu.VMEM((qk_rows.shape[1] + 2 * EDGE, DK), F32))
    else:
        operands.append(far(mixed))
        in_specs.append(pl.BlockSpec((1, tok, DK), lambda i, lengths: (first + now(i), 0, head)))
    return pl.pallas_call(
        functools.partial(prepare_kernel, first, count, head, group, chunks, key_heads, mixes),
        grid_spec=pltpu.PrefetchScalarGridSpec(
            num_scalar_prefetch=1,
            grid=(count + 1,),
            in_specs=in_specs,
            out_specs=out_specs,
            scratch_shapes=scratch,
        ),
        out_shape=out_shape,
        compiler_params=pltpu.CompilerParams(vmem_limit_bytes=VMEM_BYTES),
        cost_estimate=pl.CostEstimate(flops=5 * 10**9 * count, bytes_accessed=4 * 2**20 * count, transcendentals=10**6),
        name="prepare",
    )(lengths, *operands)


def outputs_kernel(
    first, head, group, chunks,
    length_ref, qn_ref, kn_ref, wu_ref, start_ref, log_ref, gain_ref, enter_ref, z_ref, norm_ref, held_ref, after_ref,
    out_ref,
    first_scr, score_scr, seen_scr,
):
    used = length_ref[first + pl.program_id(0)] - lax.axis_index("seq") * (chunks * BLOCK)
    units = [(h, c) for c in range(chunks) for h in range(group)]

    @pl.when(used <= 0)
    def _():
        out_ref[...] = jnp.zeros_like(out_ref)

    @pl.when(used > 0)
    def _():
        cum, gain = gates_of_heads(log_ref, gain_ref, used, head, group)
        faded = jnp.exp(cum)
        bases = block_bases([cum, faded], chunks)

        row = lax.broadcasted_iota(jnp.int32, (BLOCK, BLOCK), 0)
        lane = lax.broadcasted_iota(jnp.int32, (BLOCK, BLOCK), 1)
        upto = row >= lane
        norm_gain = norm_ref[...]

        def span(c):
            return slice(c * BLOCK, (c + 1) * BLOCK)

        for h in range(group):
            moved = dot(start_ref[0, h, :, DV:], enter_ref[h])
            first_scr[h] = (moved + start_ref[0, h, :, :DV].astype(F32)).astype(BF16)
        for c in range(chunks):
            qk = dot(qn_ref[0, span(c), :], kn_ref[0, span(c), :].T)
            squares = spread_squares(bases[c], group, 2)
            q_wide = qn_ref[0, span(c), :].astype(F32)
            for h in range(group):
                r = h * chunks + c
                score_scr[r] = jnp.where(upto, jnp.exp(squares[h]) * qk, 0.0).astype(BF16)
                seen_scr[r] = q_wide * squares[group + h]
        both, raws = {}, {}
        for h, c in units:
            r = h * chunks + c
            both[r] = dot(score_scr[r], wu_ref[0, r])
        for h, c in units:
            r = h * chunks + c
            seen = (seen_scr[r] - both[r][:, :DK]).astype(BF16)
            raws[r] = dot(seen, first_scr[h, span(c), :]) + both[r][:, DK:]
        for h, c in units:
            raw = raws[h * chunks + c]
            cols = slice(h * DV, (h + 1) * DV)
            mean = jnp.sum(raw * raw, axis=-1, keepdims=True) * (1.0 / DV)
            gated = raw * lax.rsqrt(mean + EPSILON) * norm_gain * silu(z_ref[0, span(c), cols].astype(F32))
            out_ref[0, span(c), cols] = jnp.where(row + c * BLOCK < used, gated, 0.0).astype(BF16)


def outputs(
    job, piece, lengths, qn, kn, wu, starts, log_decay, write_gain, enter, gate_z, norm_gain, key_heads, held, after,
):
    head, first, _ = job
    begin, count = piece
    prompts, tok, width = gate_z.shape
    rows = wu.shape[1]
    chunks = tok // BLOCK
    group = rows // chunks
    wide = group * DV
    value_heads = key_heads * group
    shift = begin - first
    from_mix = begin if qn.shape[0] == prompts else shift

    def whole_of(i, lengths):
        return (begin + i, 0, 0)

    def wide_of(i, lengths):
        return (begin + i, 0, head)

    def mixed_of(i, lengths):
        return (from_mix + i, 0, head)

    empty = held is None
    return pl.pallas_call(
        functools.partial(outputs_kernel, begin, head, group, chunks),
        grid_spec=pltpu.PrefetchScalarGridSpec(
            num_scalar_prefetch=1,
            grid=(count,),
            in_specs=[
                pl.BlockSpec((1, tok, DK), mixed_of),
                pl.BlockSpec((1, tok, DK), mixed_of),
                pl.BlockSpec((1, rows, BLOCK, DK + DV), lambda i, lengths: (shift + i, 0, 0, 0)),
                pl.BlockSpec((1, group, chunks * DK, DV + DK), lambda i, lengths: (shift + i, 0, 0, 0)),
                pl.BlockSpec((1, value_heads, tok), whole_of),
                pl.BlockSpec((1, value_heads, tok), whole_of),
                pl.BlockSpec((group, DK, DV), lambda i, lengths: (shift + i, 0, 0)),
                pl.BlockSpec((1, tok, wide), wide_of),
                pl.BlockSpec((1, DV), lambda i, lengths: (0, 0)),
                pl.BlockSpec(memory_space=pltpu.HBM),
                pl.BlockSpec(memory_space=pltpu.HBM),
            ],
            out_specs=pl.BlockSpec((1, tok, wide), wide_of),
            scratch_shapes=[
                pltpu.VMEM((group, chunks * DK, DV), BF16),
                pltpu.VMEM((rows, BLOCK, BLOCK), BF16),
                pltpu.VMEM((rows, BLOCK, DV), F32),
            ],
        ),
        out_shape=pltpu.HBM((prompts, tok, width), BF16),
        input_output_aliases={} if empty else {10: 0},
        compiler_params=pltpu.CompilerParams(vmem_limit_bytes=VMEM_BYTES),
        cost_estimate=pl.CostEstimate(flops=3 * 10**9 * count, bytes_accessed=4 * 2**20 * count, transcendentals=10**6),
        name="outputs",
    )(
        lengths, far(qn), far(kn), far(wu), far(starts), far(log_decay), far(write_gain), enter, far(gate_z),
        far(norm_gain.reshape(1, DV)), far(after if empty else held), far(wu if after is held else after),
    )


def own_chip():
    seq = lax.axis_index("seq")
    return seq // 2, seq % 2 == 1


def early_late(own, other, odd):
    return jnp.where(odd, other, own), jnp.where(odd, own, other)


def compose_maps(ins, outs):
    own_ref, other_ref = ins
    _, odd = own_chip()
    for n in range(own_ref.shape[0]):
        early, late = early_late(own_ref[n], other_ref[n], odd)
        both = dot(late[:, DV:], early)
        outs[0][n, :, :DV] = (both[:, :DV] + late[:, :DV].astype(F32)).astype(BF16)
        outs[0][n, :, DV:] = both[:, DV:].astype(BF16)


def close_maps(ins, outs):
    own_ref, other_ref = ins[:2]
    refs = ins[2:]
    chips = len(refs)
    chip, odd = own_chip()

    def of_chip(j, n):
        value = refs[0][n]
        for k in range(1, chips):
            value = jnp.where((chip + chips - k) % chips == j, refs[k][n], value)
        return value

    for n in range(own_ref.shape[0]):
        running = of_chip(0, n)[:, :DV]
        entering = jnp.zeros_like(running)
        for j in range(1, chips):
            entering = jnp.where(chip == j, running, entering)
            there = of_chip(j, n)
            running = (dot(there[:, DV:], running) + there[:, :DV].astype(F32)).astype(BF16)
        early, _ = early_late(own_ref[n], other_ref[n], odd)
        second = (dot(early[:, DV:], entering) + early[:, :DV].astype(F32)).astype(BF16)
        outs[0][n] = jnp.where(odd, second, entering)
        outs[1][n] = running


def chain_maps(ins, outs):
    count = len(ins)
    mine = lax.axis_index("seq")

    def run(at):
        for n in range(ins[0].shape[0]):
            running = ins[at][n, :, :DV]
            entering = jnp.zeros_like(running)
            for j in range(1, count):
                if j == at:
                    entering = running
                there = ins[(at - j) % count]
                moved = dot(there[n, :, DV:], running)
                running = (moved + there[n, :, :DV].astype(F32)).astype(BF16)
            outs[0][n] = entering
            outs[1][n] = running

    for at in range(count):
        pl.when(mine == at)(functools.partial(run, at))


def choose_finals(group, placement_ref, finals, outs):
    refs = [(ref, n) for ref in finals for n in range(ref.shape[0] // group)]
    for r in range(placement_ref.shape[1]):
        prompt = placement_ref[0, r]
        for p, (ref, n) in enumerate(refs):
            @pl.when(prompt == p)
            def _(ref=ref, n=n):
                outs[0][r] = ref[n * group : (n + 1) * group]


def state_step(placement, group, compose, chain, close, earlier, after):
    operands, shapes = [placement], []
    steps = []
    if compose is not None:
        steps.append(("compose", len(operands), len(compose), len(shapes)))
        operands += compose
        shapes += [compose[0]]
    if chain is not None or close is not None:
        steps.append(("chain" if close is None else "close", len(operands), len(close or chain), len(shapes)))
        close = close or chain
        operands += close
        shapes += [jax.ShapeDtypeStruct((close[0].shape[0], DK, DV), BF16)] * 2
        if earlier is not None:
            steps.append(("choose", len(operands), len(earlier), len(shapes)))
            operands += earlier
            shapes.append(jax.ShapeDtypeStruct((placement.shape[1], group, DK, DV), BF16))
    out_shape = [jax.ShapeDtypeStruct(x.shape, x.dtype) for x in shapes] + [pltpu.HBM((8, 128), F32)]

    def kernel(*refs):
        refs[-1][...] = jnp.zeros_like(refs[-1])
        ins, outs = refs[: len(operands)], refs[len(operands) + 1 :]
        closed = None
        for kind, at, size, to in steps:
            part = ins[at : at + size]
            if kind == "compose":
                compose_maps(part, outs[to : to + 1])
            elif kind in ("close", "chain"):
                (close_maps if kind == "close" else chain_maps)(part, outs[to : to + 2])
                closed = outs[to + 1]
            else:
                choose_finals(group, ins[0], list(part) + [closed], outs[to:])

    vmem = pl.BlockSpec(memory_space=pltpu.VMEM)
    return pl.pallas_call(
        kernel,
        in_specs=[pl.BlockSpec(memory_space=pltpu.SMEM)]
        + [vmem] * (len(operands) - 1)
        + [pl.BlockSpec(memory_space=pltpu.HBM)],
        out_specs=[vmem] * len(out_shape),
        out_shape=out_shape,
        compiler_params=pltpu.CompilerParams(vmem_limit_bytes=SMALL_VMEM_BYTES),
        cost_estimate=pl.CostEstimate(flops=10**9, bytes_accessed=2**20, transcendentals=0),
        name="state_step",
    )(*operands, far(after))


def deliver(parts):
    count, group = parts[0].shape[:2]

    def kernel(*refs):
        for n, ref in enumerate(refs[:-1]):
            refs[-1][:, n * group : (n + 1) * group] = ref[...].astype(F32)

    return pl.pallas_call(
        kernel,
        grid=(2,),
        in_specs=[pl.BlockSpec((count // 2, group, DK, DV), lambda i: (i, 0, 0, 0))] * len(parts),
        out_specs=pl.BlockSpec((count // 2, group * len(parts), DK, DV), lambda i: (i, 0, 0, 0)),
        out_shape=jax.ShapeDtypeStruct((count, group * len(parts), DK, DV), F32),
        compiler_params=pltpu.CompilerParams(vmem_limit_bytes=VMEM_BYTES),
        name="deliver",
    )(*parts)


def pair_swap(block):
    count = lax.axis_size("seq")
    return lax.ppermute(block, "seq", [(i, i ^ 1) for i in range(count)])


def from_behind(block, distance):
    count = lax.axis_size("seq")
    return lax.ppermute(block, "seq", [(i, (i + distance) % count) for i in range(count)])


def from_chip_behind(block, distance):
    count = lax.axis_size("seq")
    chips = count // 2
    route = [(i, ((i // 2 + distance) % chips) * 2 + i % 2) for i in range(count)]
    return lax.ppermute(block, "seq", route)


def shards(
    qk_in, v_in, gate_z, conv_qk, conv_v, log_decay, write_gain, norm_gain, prompt_lengths, placement,
):
    prompts, tok = qk_in.shape[:2]
    key_heads = qk_in.shape[3] // DK
    value_heads = v_in.shape[2] // DV
    rim = CONV - 1
    seq_count = lax.axis_size("seq")
    head_count = lax.axis_size("head")

    def by_head(x):
        x = x.reshape(x.shape[0], x.shape[1], 2, key_heads, DK)
        return jnp.transpose(x, (0, 1, 3, 2, 4)).reshape(x.shape[0], -1, DK)

    qk_rows = by_head(qk_in)
    qk_taps = by_head(conv_qk[None])[0]
    qk_tail = qk_rows[:, (tok - rim) * 2 * key_heads :]
    v_tail = v_in[:, tok - rim :].reshape(prompts, rim * value_heads, DV)
    front = 2 * EDGE - qk_tail.shape[1]
    back = 2 * EDGE - v_tail.shape[1]
    tails = jnp.concatenate(
        [
            jnp.zeros((prompts, front, DK), BF16),
            qk_tail,
            v_tail,
            jnp.zeros((prompts, back, DK), BF16),
        ],
        axis=1,
    )
    halo = lax.ppermute(tails, "seq", [(i, i + 1) for i in range(seq_count - 1)])
    group = value_heads // key_heads
    chips = seq_count // 2
    half = prompts // 2
    jobs = [(head, 0, prompts) for head in range(key_heads)]
    if key_heads == 1:
        jobs = [(0, 0, half), (0, half, prompts - half)]
    total = len(jobs)
    made, finals, sent = [], [], {}
    attended = None
    last = v_in

    def finish(job, results):
        head = jobs[job][0]
        finals.append(results[1])
        if len(results) > 3:
            sent[head] = lax.all_to_all(results[2], "head", 0, 0)
        return results[0], results[-1]

    def earlier(job):
        same = [n for n in range(total) if jobs[n][0] == jobs[job][0]]
        return [finals[n] for n in same[:-1]] if job == same[-1] else None

    def emit(job, entered, attended, last):
        qn, kn, wu, starts, _ = made[job]
        return outputs(
            jobs[job], jobs[job][1:], prompt_lengths, qn, kn, wu, starts, log_decay, write_gain,
            entered, gate_z, norm_gain, key_heads, attended, last,
        )

    for job in jobs:
        mixed = None if job[0] == 0 else made[0][:2]
        wu, starts, own_map, *new = prepare(
            job, prompt_lengths, qk_rows, v_in, halo, qk_taps, conv_v, log_decay, write_gain, key_heads,
            mixed and mixed[1], last,
        )
        last = wu
        moved = [own_map]
        if job == jobs[-1]:
            moved.append(pair_swap(own_map))
        else:
            moved += [from_behind(own_map, k) for k in range(1, seq_count)]
        made.append((*(mixed or new), wu, starts, moved))

    entered = []
    for job in range(total - 1):
        results = state_step(placement, group, None, made[job][4], None, earlier(job), last)
        enter, last = finish(job, results)
        entered.append(enter)
    pair = made[-1][4]
    chip_map, last = state_step(placement, group, pair, None, None, None, last)
    chip_maps = [chip_map] + [from_chip_behind(chip_map, k) for k in range(1, chips)]
    for job in range(total - 1):
        attended = last = emit(job, entered[job], attended, last)
    results = state_step(placement, group, None, None, pair + chip_maps, earlier(total - 1), last)
    enter, last = finish(total - 1, results)
    attended = emit(total - 1, enter, attended, last)
    rollout = deliver([sent[head] for head in range(key_heads)])
    return attended, rollout.reshape(1, 1, head_count * value_heads, DK, DV)


def solution(mesh):
    return jax.shard_map(
        shards,
        mesh=mesh,
        in_specs=(
            P(None, "seq", None, "head"),
            P(None, "seq", "head"),
            P(None, "seq", "head"),
            P(None, None, "head"),
            P(None, "head"),
            P(None, "head", "seq"),
            P(None, "head", "seq"),
            P(),
            P(),
            P("seq", None),
        ),
        out_specs=(P(None, "seq", "head"), P("seq", "head", None, None, None)),
        check_vma=False,
    )
```

```python
import functools

import jax
import jax.numpy as jnp
from jax import lax
from jax.experimental import pallas as pl
from jax.experimental.pallas import tpu as pltpu
from jax.sharding import PartitionSpec as P

DK = 128
DV = 128
CONV = 4
BLOCK = 128
TINY = 16
EDGE = 8
EPSILON = 1e-06
VMEM_BYTES = 40 * 1024 * 1024
SMALL_VMEM_BYTES = 8 * 1024 * 1024
F32 = jnp.float32
BF16 = jnp.bfloat16


def far(x):
    return pltpu.with_memory_space_constraint(x, pltpu.HBM)


def dot(a, b):
    return lax.dot_general(a, b, (((1,), (0,)), ((), ())), preferred_element_type=F32)


def silu(x):
    half = 0.5 * x
    return half + half * jnp.tanh(half)


def mixed_rows(pad_ref, taps, rim, first, step, c):
    total = None
    for i in range(CONV):
        start = rim + first + step * (c * BLOCK + i - (CONV - 1))
        stride = None if step == 1 else step
        term = pad_ref[pl.ds(start, BLOCK, stride), :] * taps[i]
        total = term if total is None else total + term
    return silu(total)


def unit_rows(x):
    return x * lax.rsqrt(jnp.sum(x * x, axis=-1, keepdims=True) + EPSILON)


def heads_rows(ref, head, group):
    every = ref[0]
    rows = every[:group]
    for n in range(1, every.shape[0] // group):
        rows = jnp.where(head == n, every[n * group : (n + 1) * group], rows)
    return rows


def gates_of_heads(log_ref, gain_ref, used, head, group):
    log = heads_rows(log_ref, head, group)
    lane = lax.broadcasted_iota(jnp.int32, log.shape, 1)
    valid = lane < used
    cum = jnp.where(valid, log, 0.0)
    gain = jnp.where(valid, heads_rows(gain_ref, head, group), 0.0)
    shift = 1
    while shift < BLOCK:
        cum = cum + jnp.where(lane % BLOCK >= shift, pltpu.roll(cum, shift, 1), 0.0)
        shift *= 2
    return cum, gain


def as_columns(rows, chunks):
    parts = [rows[:, c * BLOCK : (c + 1) * BLOCK] for c in range(chunks)]
    short = BLOCK - 8 * chunks
    if short:
        parts.append(jnp.zeros((short, BLOCK), F32))
    return jnp.concatenate(parts, axis=0).T


def block_bases(parts, chunks):
    rows = jnp.concatenate(parts, axis=0)
    short = 7 - rows.shape[0]
    fill = [jnp.zeros((short, rows.shape[1]), F32)] if short else []
    rows = jnp.concatenate([rows] + fill + [jnp.ones((1, rows.shape[1]), F32)], axis=0)
    return [rows[:, c * BLOCK : (c + 1) * BLOCK] for c in range(chunks)]


def spread_squares(base, group, kinds):
    high = base.astype(BF16).astype(F32)
    middle = (base - high).astype(BF16).astype(F32)
    low = base - high - middle
    parts = [high, middle, low]
    row = lax.broadcasted_iota(jnp.int32, (32, BLOCK), 0)
    which = row % 8
    real = row < 24
    stacked = jnp.concatenate(parts + [jnp.zeros_like(high)], axis=0)
    left = jnp.where(jnp.logical_and(which == 7, real), 1.0, stacked).T.astype(BF16)
    blocks = []
    for h in range(group):
        minus = jnp.concatenate([jnp.broadcast_to(-part[h : h + 1], (8, BLOCK)) for part in parts + [low]], axis=0)
        blocks.append(jnp.where(which == h, 1.0, jnp.where(which == 7, minus, 0.0)))
    for n in range(group, group * kinds):
        blocks.append(jnp.where(which == n, 1.0, 0.0).astype(F32))
    every = dot(left, jnp.concatenate(blocks, axis=1).astype(BF16))
    return [every[:, n * BLOCK : (n + 1) * BLOCK] for n in range(group * kinds)]


def mix(qk_ref, halo_ref, taps_ref, qn_ref, kn_ref, raw_scr, key_heads, chunks):
    kinds = 2 * key_heads
    rim = 2 * EDGE
    taps = taps_ref[...].astype(F32)
    raw_scr[:rim] = halo_ref[0].astype(F32)[:rim]
    raw_scr[rim:] = qk_ref[0].astype(F32)
    for c in range(chunks):
        span = slice(c * BLOCK, (c + 1) * BLOCK)
        for kind in range(kinds):
            own = [taps[n : n + 1] for n in range(kind, taps.shape[0], kinds)]
            rows = unit_rows(mixed_rows(raw_scr, own, rim, kind, kinds, c))
            to_ref = kn_ref if kind % 2 else qn_ref
            to_ref[0, span, kind // 2 * DK : (kind // 2 + 1) * DK] = rows.astype(BF16)


def prepare_kernel(first, count, head, group, chunks, key_heads, mixes, *refs):
    length_ref, v_ref, halo_ref, v_taps_ref, log_ref, gain_ref, after_ref = refs[:7]
    refs = refs[7:]
    if mixes:
        qk_ref, qk_taps_ref, wu_ref, start_ref, map_ref, qn_ref, kn_ref = refs[:7]
        v_pad, m_scr, b_scr, fade_scr, st_scr, a_scr, x_scr, y_scr, raw_scr = refs[7:]
        key_columns = slice(head * DK, (head + 1) * DK)
    else:
        kn_ref, wu_ref, start_ref, map_ref = refs[:4]
        v_pad, m_scr, b_scr, fade_scr, st_scr, a_scr, x_scr, y_scr = refs[4:]
        key_columns = slice(0, DK)
    step = pl.program_id(0)
    used = length_ref[first + jnp.minimum(step, count - 1)] - lax.axis_index("seq") * (chunks * BLOCK)
    units = [(h, c) for c in range(chunks) for h in range(group)]
    slot = step % 2
    live = jnp.logical_and(step < count, used > 0)

    def begin():
        row = lax.broadcasted_iota(jnp.int32, (DV + DK, DK), 0)
        lane = lax.broadcasted_iota(jnp.int32, (DV + DK, DK), 1)
        for h in range(group):
            st_scr[h] = jnp.where(row == lane + DV, 1.0, 0.0).astype(F32)

    def advance(c):
        narrow, moved = [], []
        for h in range(group):
            narrow.append(st_scr[h].astype(BF16))
            start_ref[0, h, c * (DV + DK) : (c + 1) * (DV + DK), :] = narrow[h]
        for h in range(group):
            moved.append(dot(narrow[h], m_scr[1 - slot, c, h]))
        for h in range(group):
            fade = fade_scr[1 - slot, c, h : h + 1, :]
            state = st_scr[h, :DV] * fade + (moved[h][:DV] + b_scr[1 - slot, c, h])
            trans = st_scr[h, DV:] * fade + moved[h][DV:]
            if c < chunks - 1:
                st_scr[h, :DV] = state
                st_scr[h, DV:] = trans
            else:
                map_ref[h, :DV] = state.astype(BF16)
                map_ref[h, DV:] = trans.astype(BF16)

    todo = [begin] + [functools.partial(advance, c) for c in range(chunks)]

    def run(n):
        for _ in range(min(n, len(todo))):
            todo.pop(0)()

    @pl.when(jnp.logical_not(live))
    def _():
        @pl.when(step > 0)
        def _():
            begin()
            for c in range(chunks):
                advance(c)

        @pl.when(step < count)
        def _():
            if mixes:
                qn_ref[...] = jnp.zeros_like(qn_ref)
                kn_ref[...] = jnp.zeros_like(kn_ref)
            wu_ref[...] = jnp.zeros_like(wu_ref)
            fade_scr[slot] = jnp.ones(fade_scr.shape[1:], F32)
            m_scr[slot] = jnp.zeros(m_scr.shape[1:], BF16)
            b_scr[slot] = jnp.zeros(b_scr.shape[1:], F32)

    @pl.when(live)
    def _():
        if mixes:
            mix(qk_ref, halo_ref, qk_taps_ref, qn_ref, kn_ref, raw_scr, key_heads, chunks)
        halo = halo_ref[0].astype(F32)
        v_pad[EDGE:, :] = v_ref[0].astype(F32)
        for i in range(CONV - 1):
            for h in range(group):
                source = 2 * EDGE + (i * key_heads + head) * group + h
                v_pad[EDGE - CONV + 1 + i : EDGE - CONV + 2 + i, h * DV : (h + 1) * DV] = halo[
                    source : source + 1
                ]
        v_all_taps = v_taps_ref[...].astype(F32)
        v_taps = [v_all_taps[i : i + 1] for i in range(CONV)]
        run(1)

        cum, gain = gates_of_heads(log_ref, gain_ref, used, head, group)
        both_gains = gain * jnp.exp(cum)
        columns = as_columns(jnp.concatenate([cum] * (8 // group), axis=0), chunks)

        def span(c):
            return slice(c * BLOCK, (c + 1) * BLOCK)

        row = lax.broadcasted_iota(jnp.int32, (BLOCK, BLOCK), 0)
        lane = lax.broadcasted_iota(jnp.int32, (BLOCK, BLOCK), 1)
        above = row < lane
        small_row = lax.broadcasted_iota(jnp.int32, (TINY, BLOCK), 0)
        small_lane = lax.broadcasted_iota(jnp.int32, (TINY, BLOCK), 1)
        part_of = small_lane // TINY
        tiny_eye = jnp.where(small_row == small_lane % TINY, 1.0, 0.0).astype(F32)

        keys = [kn_ref[0, span(c), key_columns] for c in range(chunks)]
        turned = [kc.T for kc in keys]
        run(1)

        compact = {}
        for c in range(chunks):
            kk = dot(keys[c], turned[c])
            for h in range(group):
                r = h * chunks + c
                ratio = jnp.exp(cum[h : h + 1, span(c)] - columns[:, c * 8 + h : c * 8 + h + 1])
                strict = jnp.where(above, ratio * kk * -gain[h : h + 1, span(c)], 0.0)
                a_scr[r] = strict.astype(BF16)
                tiny = strict[0:TINY]
                for b in range(1, BLOCK // TINY):
                    tiny = jnp.where(part_of == b, strict[b * TINY : (b + 1) * TINY], tiny)
                compact[r] = tiny

        run(1)
        solved = {r: tiny_eye for r in compact}
        for j in range(TINY - 1, 0, -1):
            pick = part_of * TINY + j
            for r in solved:
                factor = jnp.take_along_axis(compact[r], pick, axis=1, mode="promise_in_bounds")
                solved[r] = solved[r] + factor * solved[r][j : j + 1, :]
        for r in solved:
            for b in range(BLOCK // TINY):
                x_scr[r, b * TINY : (b + 1) * TINY, :] = jnp.where(
                    part_of == b, solved[r], 0.0
                ).astype(BF16)

        run(1)
        size = TINY
        while size < BLOCK:
            even = [s for s in range(0, BLOCK, 2 * size)]
            half_lane = lax.broadcasted_iota(jnp.int32, (BLOCK // 2, BLOCK), 1)
            half_row = lax.broadcasted_iota(jnp.int32, (BLOCK // 2, BLOCK), 0)
            partner = half_lane // size == 2 * (half_row // size) + 1
            own, moved = {}, {}
            for h, c in units:
                r = h * chunks + c
                own[r] = jnp.concatenate([x_scr[r, s : s + size, :] for s in even], axis=0)
                moved[r] = jnp.where(partner, dot(own[r], a_scr[r]), 0.0).astype(BF16)
            for h, c in units:
                r = h * chunks + c
                update = own[r] + dot(moved[r], x_scr[r]).astype(BF16)
                for n, s in enumerate(even):
                    x_scr[r, s : s + size, :] = update[n * size : (n + 1) * size]
            run(1)
            size *= 2

        for c in range(chunks):
            vc = mixed_rows(v_pad, v_taps, EDGE, 0, 1, c).astype(BF16)
            sums = cum[:, span(c)]
            last = sums[:, BLOCK - 1 : BLOCK]
            tail = jnp.exp(last - sums)
            fade = jnp.broadcast_to(jnp.exp(last), (group, BLOCK))
            k_wide = turned[c].astype(F32)
            for h in range(group):
                r = h * chunks + c
                v_wide = vc[:, h * DV : (h + 1) * DV].T.astype(F32)
                right = jnp.concatenate(
                    [
                        (k_wide * both_gains[h : h + 1, span(c)]).astype(BF16),
                        (v_wide * gain[h : h + 1, span(c)]).astype(BF16),
                    ],
                    axis=0,
                )
                solution_rows = dot(right, x_scr[r])
                wu_ref[0, r] = solution_rows.astype(BF16)
                y_scr[c, h * (DK + DV) : (h + 1) * (DK + DV), :] = (solution_rows * tail[h : h + 1]).astype(BF16)
                fade_scr[slot, c, h : h + 1, :] = fade[h : h + 1]
            if c == chunks // 2:
                run(1)
        run(len(todo))
        for c in range(chunks):
            both = dot(y_scr[c], keys[c])
            for h in range(group):
                top = h * (DK + DV)
                m_scr[slot, c, h] = (-both[top : top + DK]).astype(BF16)
                b_scr[slot, c, h] = both[top + DK : top + DK + DV]


def prepare(job, lengths, qk_rows, v_in, halo, qk_taps, v_taps, log_decay, write_gain, key_heads, mixed, after):
    head, first, count = job
    tok = v_in.shape[1]
    value_heads = v_in.shape[2] // DV
    group = value_heads // key_heads
    chunks = tok // BLOCK
    rows = group * chunks
    wide = group * DV
    mixes = mixed is None

    def now(i):
        return jnp.minimum(i, count - 1)

    def before(i):
        return jnp.maximum(i - 1, 0)

    def whole_of(i, lengths):
        return (first + now(i), 0, 0)

    operands = [far(v_in), halo, far(v_taps), far(log_decay), far(write_gain), far(after)]
    in_specs = [
        pl.BlockSpec((1, tok, wide), lambda i, lengths: (first + now(i), 0, head)),
        pl.BlockSpec((1,) + halo.shape[1:], whole_of),
        pl.BlockSpec((CONV, wide), lambda i, lengths: (0, head)),
        pl.BlockSpec((1, value_heads, tok), whole_of),
        pl.BlockSpec((1, value_heads, tok), whole_of),
        pl.BlockSpec(memory_space=pltpu.HBM),
    ]
    out_specs = [
        pl.BlockSpec((1, rows, DK + DV, BLOCK), lambda i, lengths: (now(i), 0, 0, 0)),
        pl.BlockSpec((1, group, chunks * (DV + DK), DK), lambda i, lengths: (before(i), 0, 0, 0)),
        pl.BlockSpec((group, DV + DK, DK), lambda i, lengths: (before(i), 0, 0)),
    ]
    out_shape = [
        pltpu.HBM((count, rows, DK + DV, BLOCK), BF16),
        pltpu.HBM((count, group, chunks * (DV + DK), DK), BF16),
        jax.ShapeDtypeStruct((count * group, DV + DK, DK), BF16),
    ]
    scratch = [
        pltpu.VMEM((tok + EDGE, wide), F32),
        pltpu.VMEM((2, chunks, group, DK, DK), BF16),
        pltpu.VMEM((2, chunks, group, DV, DK), F32),
        pltpu.VMEM((2, chunks, group, BLOCK), F32),
        pltpu.VMEM((group, DV + DK, DK), F32),
        pltpu.VMEM((rows, BLOCK, BLOCK), BF16),
        pltpu.VMEM((rows, BLOCK, BLOCK), BF16),
        pltpu.VMEM((chunks, group * (DK + DV), BLOCK), BF16),
    ]
    if mixes:
        operands += [far(qk_rows), far(qk_taps)]
        in_specs += [
            pl.BlockSpec((1,) + qk_rows.shape[1:], whole_of),
            pl.BlockSpec(qk_taps.shape, lambda i, lengths: (0, 0)),
        ]
        out_specs += [pl.BlockSpec((1, tok, key_heads * DK), lambda i, lengths: (now(i), 0, 0))] * 2
        out_shape += [pltpu.HBM((count, tok, key_heads * DK), BF16)] * 2
        scratch.append(pltpu.VMEM((qk_rows.shape[1] + 2 * EDGE, DK), F32))
    else:
        operands.append(far(mixed))
        in_specs.append(pl.BlockSpec((1, tok, DK), lambda i, lengths: (first + now(i), 0, head)))
    return pl.pallas_call(
        functools.partial(prepare_kernel, first, count, head, group, chunks, key_heads, mixes),
        grid_spec=pltpu.PrefetchScalarGridSpec(
            num_scalar_prefetch=1,
            grid=(count + 1,),
            in_specs=in_specs,
            out_specs=out_specs,
            scratch_shapes=scratch,
        ),
        out_shape=out_shape,
        compiler_params=pltpu.CompilerParams(vmem_limit_bytes=VMEM_BYTES),
        cost_estimate=pl.CostEstimate(flops=5 * 10**9 * count, bytes_accessed=4 * 2**20 * count, transcendentals=10**6),
        name="prepare",
    )(lengths, *operands)


def outputs_kernel(
    first, head, group, chunks,
    length_ref, qn_ref, kn_ref, wu_ref, start_ref, log_ref, gain_ref, enter_ref, z_ref, norm_ref, held_ref, after_ref,
    out_ref,
    first_scr, score_scr, seen_scr,
):
    used = length_ref[first + pl.program_id(0)] - lax.axis_index("seq") * (chunks * BLOCK)
    units = [(h, c) for c in range(chunks) for h in range(group)]

    @pl.when(used <= 0)
    def _():
        out_ref[...] = jnp.zeros_like(out_ref)

    @pl.when(used > 0)
    def _():
        cum, gain = gates_of_heads(log_ref, gain_ref, used, head, group)
        faded = jnp.exp(cum)
        columns = as_columns(jnp.concatenate([cum] * (8 // group), axis=0), chunks)
        row = lax.broadcasted_iota(jnp.int32, (BLOCK, BLOCK), 0)
        lane = lax.broadcasted_iota(jnp.int32, (BLOCK, BLOCK), 1)
        upto = row <= lane
        norm_gain = norm_ref[...]

        def span(c):
            return slice(c * BLOCK, (c + 1) * BLOCK)

        for c in range(chunks):
            turned = qn_ref[0, span(c), :].T
            kq = dot(kn_ref[0, span(c), :], turned)
            q_wide = turned.astype(F32)
            for h in range(group):
                r = h * chunks + c
                ratio = jnp.exp(cum[h : h + 1, span(c)] - columns[:, c * 8 + h : c * 8 + h + 1])
                score_scr[r] = jnp.where(upto, ratio * kq, 0.0).astype(BF16)
                seen_scr[r] = q_wide * faded[h : h + 1, span(c)]
                top = c * (DV + DK)
                moved = dot(enter_ref[h], start_ref[0, h, top + DV : top + DV + DK, :])
                first_scr[r] = (moved + start_ref[0, h, top : top + DV, :].astype(F32)).astype(BF16)
        both, raws = {}, {}
        for h, c in units:
            r = h * chunks + c
            both[r] = dot(wu_ref[0, r], score_scr[r])
        for h, c in units:
            r = h * chunks + c
            seen = (seen_scr[r] - both[r][:DK]).astype(BF16)
            raw = dot(first_scr[r], seen) + both[r][DK:]
            mean = jnp.sum(raw * raw, axis=0, keepdims=True) * (1.0 / DV)
            raws[r] = (raw * lax.rsqrt(mean + EPSILON)).astype(BF16)
        for h, c in units:
            scaled = raws[h * chunks + c].T.astype(F32)
            cols = slice(h * DV, (h + 1) * DV)
            gated = scaled * norm_gain * silu(z_ref[0, span(c), cols].astype(F32))
            out_ref[0, span(c), cols] = jnp.where(row + c * BLOCK < used, gated, 0.0).astype(BF16)


def outputs(
    job, piece, lengths, qn, kn, wu, starts, log_decay, write_gain, enter, gate_z, norm_gain, key_heads, held, after,
):
    head, first, _ = job
    begin, count = piece
    prompts, tok, width = gate_z.shape
    rows = wu.shape[1]
    chunks = tok // BLOCK
    group = rows // chunks
    wide = group * DV
    value_heads = key_heads * group
    shift = begin - first
    from_mix = begin if qn.shape[0] == prompts else shift

    def whole_of(i, lengths):
        return (begin + i, 0, 0)

    def wide_of(i, lengths):
        return (begin + i, 0, head)

    def mixed_of(i, lengths):
        return (from_mix + i, 0, head)

    empty = held is None
    return pl.pallas_call(
        functools.partial(outputs_kernel, begin, head, group, chunks),
        grid_spec=pltpu.PrefetchScalarGridSpec(
            num_scalar_prefetch=1,
            grid=(count,),
            in_specs=[
                pl.BlockSpec((1, tok, DK), mixed_of),
                pl.BlockSpec((1, tok, DK), mixed_of),
                pl.BlockSpec((1, rows, DK + DV, BLOCK), lambda i, lengths: (shift + i, 0, 0, 0)),
                pl.BlockSpec((1, group, chunks * (DV + DK), DK), lambda i, lengths: (shift + i, 0, 0, 0)),
                pl.BlockSpec((1, value_heads, tok), whole_of),
                pl.BlockSpec((1, value_heads, tok), whole_of),
                pl.BlockSpec((group, DK, DV), lambda i, lengths: (shift + i, 0, 0)),
                pl.BlockSpec((1, tok, wide), wide_of),
                pl.BlockSpec((1, DV), lambda i, lengths: (0, 0)),
                pl.BlockSpec(memory_space=pltpu.HBM),
                pl.BlockSpec(memory_space=pltpu.HBM),
            ],
            out_specs=pl.BlockSpec((1, tok, wide), wide_of),
            scratch_shapes=[
                pltpu.VMEM((rows, DV, DK), BF16),
                pltpu.VMEM((rows, BLOCK, BLOCK), BF16),
                pltpu.VMEM((rows, BLOCK, DV), F32),
            ],
        ),
        out_shape=pltpu.HBM((prompts, tok, width), BF16),
        input_output_aliases={} if empty else {10: 0},
        compiler_params=pltpu.CompilerParams(vmem_limit_bytes=VMEM_BYTES),
        cost_estimate=pl.CostEstimate(flops=3 * 10**9 * count, bytes_accessed=4 * 2**20 * count, transcendentals=10**6),
        name="outputs",
    )(
        lengths, far(qn), far(kn), far(wu), far(starts), far(log_decay), far(write_gain), enter, far(gate_z),
        far(norm_gain.reshape(1, DV)), far(after if empty else held), far(wu if after is held else after),
    )


def own_chip():
    seq = lax.axis_index("seq")
    return seq // 2, seq % 2 == 1


def early_late(own, other, odd):
    return jnp.where(odd, other, own), jnp.where(odd, own, other)


def follow(there, running):
    return dot(running, there[DV:])


def compose_maps(ins, outs):
    own_ref, other_ref = ins
    _, odd = own_chip()
    for n in range(own_ref.shape[0]):
        early, late = early_late(own_ref[n], other_ref[n], odd)
        both = follow(late, early)
        outs[0][n, :DV] = (both[:DV] + late[:DV].astype(F32)).astype(BF16)
        outs[0][n, DV:] = both[DV:].astype(BF16)


def close_maps(ins, outs):
    own_ref, other_ref = ins[:2]
    refs = ins[2:]
    chips = len(refs)
    chip, odd = own_chip()

    def of_chip(j, n):
        value = refs[0][n]
        for k in range(1, chips):
            value = jnp.where((chip + chips - k) % chips == j, refs[k][n], value)
        return value

    for n in range(own_ref.shape[0]):
        running = of_chip(0, n)[:DV]
        entering = jnp.zeros_like(running)
        for j in range(1, chips):
            entering = jnp.where(chip == j, running, entering)
            there = of_chip(j, n)
            running = (follow(there, running) + there[:DV].astype(F32)).astype(BF16)
        early, _ = early_late(own_ref[n], other_ref[n], odd)
        second = (follow(early, entering) + early[:DV].astype(F32)).astype(BF16)
        outs[0][n] = jnp.where(odd, second, entering)
        outs[1][n] = running.T


def chain_maps(ins, outs):
    count = len(ins)
    mine = lax.axis_index("seq")

    def run(at):
        for n in range(ins[0].shape[0]):
            running = ins[at][n, :DV]
            entering = jnp.zeros_like(running)
            for j in range(1, count):
                if j == at:
                    entering = running
                there = ins[(at - j) % count]
                running = (follow(there.at[n], running) + there[n, :DV].astype(F32)).astype(BF16)
            outs[0][n] = entering
            outs[1][n] = running.T

    for at in range(count):
        pl.when(mine == at)(functools.partial(run, at))


def choose_finals(group, placement_ref, finals, outs):
    refs = [(ref, n) for ref in finals for n in range(ref.shape[0] // group)]
    for r in range(placement_ref.shape[1]):
        prompt = placement_ref[0, r]
        for p, (ref, n) in enumerate(refs):
            @pl.when(prompt == p)
            def _(ref=ref, n=n):
                outs[0][r] = ref[n * group : (n + 1) * group]


def state_step(placement, group, compose, chain, close, earlier, after):
    operands, shapes = [placement], []
    steps = []
    if compose is not None:
        steps.append(("compose", len(operands), len(compose), len(shapes)))
        operands += compose
        shapes += [compose[0]]
    if chain is not None or close is not None:
        steps.append(("chain" if close is None else "close", len(operands), len(close or chain), len(shapes)))
        close = close or chain
        operands += close
        shapes += [jax.ShapeDtypeStruct((close[0].shape[0], DK, DV), BF16)] * 2
        if earlier is not None:
            steps.append(("choose", len(operands), len(earlier), len(shapes)))
            operands += earlier
            shapes.append(jax.ShapeDtypeStruct((placement.shape[1], group, DK, DV), BF16))
    out_shape = [jax.ShapeDtypeStruct(x.shape, x.dtype) for x in shapes] + [pltpu.HBM((8, 128), F32)]

    def kernel(*refs):
        refs[-1][...] = jnp.zeros_like(refs[-1])
        ins, outs = refs[: len(operands)], refs[len(operands) + 1 :]
        closed = None
        for kind, at, size, to in steps:
            part = ins[at : at + size]
            if kind == "compose":
                compose_maps(part, outs[to : to + 1])
            elif kind in ("close", "chain"):
                (close_maps if kind == "close" else chain_maps)(part, outs[to : to + 2])
                closed = outs[to + 1]
            else:
                choose_finals(group, ins[0], list(part) + [closed], outs[to:])

    vmem = pl.BlockSpec(memory_space=pltpu.VMEM)
    return pl.pallas_call(
        kernel,
        in_specs=[pl.BlockSpec(memory_space=pltpu.SMEM)]
        + [vmem] * (len(operands) - 1)
        + [pl.BlockSpec(memory_space=pltpu.HBM)],
        out_specs=[vmem] * len(out_shape),
        out_shape=out_shape,
        compiler_params=pltpu.CompilerParams(vmem_limit_bytes=SMALL_VMEM_BYTES),
        cost_estimate=pl.CostEstimate(flops=10**9, bytes_accessed=2**20, transcendentals=0),
        name="state_step",
    )(*operands, far(after))


def deliver(parts):
    count, group = parts[0].shape[:2]

    def kernel(*refs):
        for n, ref in enumerate(refs[:-1]):
            refs[-1][:, n * group : (n + 1) * group] = ref[...].astype(F32)

    return pl.pallas_call(
        kernel,
        grid=(2,),
        in_specs=[pl.BlockSpec((count // 2, group, DK, DV), lambda i: (i, 0, 0, 0))] * len(parts),
        out_specs=pl.BlockSpec((count // 2, group * len(parts), DK, DV), lambda i: (i, 0, 0, 0)),
        out_shape=jax.ShapeDtypeStruct((count, group * len(parts), DK, DV), F32),
        compiler_params=pltpu.CompilerParams(vmem_limit_bytes=VMEM_BYTES),
        name="deliver",
    )(*parts)


def pair_swap(block):
    count = lax.axis_size("seq")
    return lax.ppermute(block, "seq", [(i, i ^ 1) for i in range(count)])


def from_behind(block, distance):
    count = lax.axis_size("seq")
    return lax.ppermute(block, "seq", [(i, (i + distance) % count) for i in range(count)])


def from_chip_behind(block, distance):
    count = lax.axis_size("seq")
    chips = count // 2
    route = [(i, ((i // 2 + distance) % chips) * 2 + i % 2) for i in range(count)]
    return lax.ppermute(block, "seq", route)


def shards(
    qk_in, v_in, gate_z, conv_qk, conv_v, log_decay, write_gain, norm_gain, prompt_lengths, placement,
):
    prompts, tok = qk_in.shape[:2]
    key_heads = qk_in.shape[3] // DK
    value_heads = v_in.shape[2] // DV
    rim = CONV - 1
    seq_count = lax.axis_size("seq")
    head_count = lax.axis_size("head")

    def by_head(x):
        x = x.reshape(x.shape[0], x.shape[1], 2, key_heads, DK)
        return jnp.transpose(x, (0, 1, 3, 2, 4)).reshape(x.shape[0], -1, DK)

    qk_rows = by_head(qk_in)
    qk_taps = by_head(conv_qk[None])[0]
    qk_tail = qk_rows[:, (tok - rim) * 2 * key_heads :]
    v_tail = v_in[:, tok - rim :].reshape(prompts, rim * value_heads, DV)
    front = 2 * EDGE - qk_tail.shape[1]
    back = 2 * EDGE - v_tail.shape[1]
    tails = jnp.concatenate(
        [
            jnp.zeros((prompts, front, DK), BF16),
            qk_tail,
            v_tail,
            jnp.zeros((prompts, back, DK), BF16),
        ],
        axis=1,
    )
    halo = lax.ppermute(tails, "seq", [(i, i + 1) for i in range(seq_count - 1)])
    group = value_heads // key_heads
    chips = seq_count // 2
    half = prompts // 2
    jobs = [(head, 0, prompts) for head in range(key_heads)]
    if key_heads == 1:
        jobs = [(0, 0, half), (0, half, prompts - half)]
    total = len(jobs)
    made, finals, sent = [], [], {}
    attended = None
    last = v_in

    def finish(job, results):
        head = jobs[job][0]
        finals.append(results[1])
        if len(results) > 3:
            sent[head] = lax.all_to_all(results[2], "head", 0, 0)
        return results[0], results[-1]

    def earlier(job):
        same = [n for n in range(total) if jobs[n][0] == jobs[job][0]]
        return [finals[n] for n in same[:-1]] if job == same[-1] else None

    def emit(job, entered, attended, last):
        qn, kn, wu, starts, _ = made[job]
        return outputs(
            jobs[job], jobs[job][1:], prompt_lengths, qn, kn, wu, starts, log_decay, write_gain,
            entered, gate_z, norm_gain, key_heads, attended, last,
        )

    for job in jobs:
        mixed = None if job[0] == 0 else made[0][:2]
        wu, starts, own_map, *new = prepare(
            job, prompt_lengths, qk_rows, v_in, halo, qk_taps, conv_v, log_decay, write_gain, key_heads,
            mixed and mixed[1], last,
        )
        last = wu
        moved = [own_map]
        if job == jobs[-1]:
            moved.append(pair_swap(own_map))
        else:
            moved += [from_behind(own_map, k) for k in range(1, seq_count)]
        made.append((*(mixed or new), wu, starts, moved))

    entered = []
    for job in range(total - 1):
        results = state_step(placement, group, None, made[job][4], None, earlier(job), last)
        enter, last = finish(job, results)
        entered.append(enter)
    pair = made[-1][4]
    chip_map, last = state_step(placement, group, pair, None, None, None, last)
    chip_maps = [chip_map] + [from_chip_behind(chip_map, k) for k in range(1, chips)]
    for job in range(total - 1):
        attended = last = emit(job, entered[job], attended, last)
    results = state_step(placement, group, None, None, pair + chip_maps, earlier(total - 1), last)
    enter, last = finish(total - 1, results)
    attended = emit(total - 1, enter, attended, last)
    rollout = deliver([sent[head] for head in range(key_heads)])
    return attended, rollout.reshape(1, 1, head_count * value_heads, DK, DV)


def solution(mesh):
    return jax.shard_map(
        shards,
        mesh=mesh,
        in_specs=(
            P(None, "seq", None, "head"),
            P(None, "seq", "head"),
            P(None, "seq", "head"),
            P(None, None, "head"),
            P(None, "head"),
            P(None, "head", "seq"),
            P(None, "head", "seq"),
            P(),
            P(),
            P("seq", None),
        ),
        out_specs=(P(None, "seq", "head"), P("seq", "head", None, None, None)),
        check_vma=False,
    )
```

```python
import functools

import jax
import jax.numpy as jnp
from jax import lax
from jax.experimental import pallas as pl
from jax.experimental.pallas import tpu as pltpu
from jax.sharding import PartitionSpec as P

DK = 128
DV = 128
CONV = 4
BLOCK = 128
TINY = 16
EDGE = 8
EPSILON = 1e-06
VMEM_BYTES = 40 * 1024 * 1024
SMALL_VMEM_BYTES = 8 * 1024 * 1024
F32 = jnp.float32
BF16 = jnp.bfloat16


def far(x):
    return pltpu.with_memory_space_constraint(x, pltpu.HBM)


def dot(a, b):
    return lax.dot_general(a, b, (((1,), (0,)), ((), ())), preferred_element_type=F32)


def silu(x):
    half = 0.5 * x
    return half + half * jnp.tanh(half)


def mixed_rows(pad_ref, taps, rim, first, step, c):
    total = None
    for i in range(CONV):
        start = rim + first + step * (c * BLOCK + i - (CONV - 1))
        stride = None if step == 1 else step
        term = pad_ref[pl.ds(start, BLOCK, stride), :] * taps[i]
        total = term if total is None else total + term
    return silu(total)


def unit_rows(x):
    return x * lax.rsqrt(jnp.sum(x * x, axis=-1, keepdims=True) + EPSILON)


def heads_rows(ref, head, group):
    every = ref[0]
    rows = every[:group]
    for n in range(1, every.shape[0] // group):
        rows = jnp.where(head == n, every[n * group : (n + 1) * group], rows)
    return rows


def gates_of_heads(log_ref, gain_ref, used, head, group):
    log = heads_rows(log_ref, head, group)
    lane = lax.broadcasted_iota(jnp.int32, log.shape, 1)
    valid = lane < used
    cum = jnp.where(valid, log, 0.0)
    gain = jnp.where(valid, heads_rows(gain_ref, head, group), 0.0)
    shift = 1
    while shift < BLOCK:
        cum = cum + jnp.where(lane % BLOCK >= shift, pltpu.roll(cum, shift, 1), 0.0)
        shift *= 2
    return cum, gain


def as_columns(rows, chunks):
    parts = [rows[:, c * BLOCK : (c + 1) * BLOCK] for c in range(chunks)]
    short = BLOCK - 8 * chunks
    if short:
        parts.append(jnp.zeros((short, BLOCK), F32))
    return jnp.concatenate(parts, axis=0).T


def block_bases(parts, chunks):
    rows = jnp.concatenate(parts, axis=0)
    short = 7 - rows.shape[0]
    fill = [jnp.zeros((short, rows.shape[1]), F32)] if short else []
    rows = jnp.concatenate([rows] + fill + [jnp.ones((1, rows.shape[1]), F32)], axis=0)
    return [rows[:, c * BLOCK : (c + 1) * BLOCK] for c in range(chunks)]


def spread_squares(base, group, kinds):
    high = base.astype(BF16).astype(F32)
    middle = (base - high).astype(BF16).astype(F32)
    low = base - high - middle
    parts = [high, middle, low]
    row = lax.broadcasted_iota(jnp.int32, (32, BLOCK), 0)
    which = row % 8
    real = row < 24
    stacked = jnp.concatenate(parts + [jnp.zeros_like(high)], axis=0)
    left = jnp.where(jnp.logical_and(which == 7, real), 1.0, stacked).T.astype(BF16)
    blocks = []
    for h in range(group):
        minus = jnp.concatenate([jnp.broadcast_to(-part[h : h + 1], (8, BLOCK)) for part in parts + [low]], axis=0)
        blocks.append(jnp.where(which == h, 1.0, jnp.where(which == 7, minus, 0.0)))
    for n in range(group, group * kinds):
        blocks.append(jnp.where(which == n, 1.0, 0.0).astype(F32))
    every = dot(left, jnp.concatenate(blocks, axis=1).astype(BF16))
    return [every[:, n * BLOCK : (n + 1) * BLOCK] for n in range(group * kinds)]


def mix(qk_ref, halo_ref, taps_ref, qn_ref, kn_ref, raw_scr, key_heads, chunks):
    kinds = 2 * key_heads
    rim = 2 * EDGE
    taps = taps_ref[...].astype(F32)
    raw_scr[:rim] = halo_ref[0].astype(F32)[:rim]
    raw_scr[rim:] = qk_ref[0].astype(F32)
    for c in range(chunks):
        span = slice(c * BLOCK, (c + 1) * BLOCK)
        for kind in range(kinds):
            own = [taps[n : n + 1] for n in range(kind, taps.shape[0], kinds)]
            rows = unit_rows(mixed_rows(raw_scr, own, rim, kind, kinds, c))
            to_ref = kn_ref if kind % 2 else qn_ref
            to_ref[0, span, kind // 2 * DK : (kind // 2 + 1) * DK] = rows.astype(BF16)


def weave(*lists):
    places = []
    for which, entries in enumerate(lists):
        places += [((n + 0.5) / len(entries), which, n) for n in range(len(entries))]
    for _, which, n in sorted(places):
        lists[which][n]()


def prepare_kernel(first, count, head, group, chunks, key_heads, mixes, *refs):
    length_ref, v_ref, halo_ref, v_taps_ref, log_ref, gain_ref, after_ref = refs[:7]
    refs = refs[7:]
    if mixes:
        qk_ref, qk_taps_ref, wu_ref, start_ref, map_ref, qn_ref, kn_ref = refs[:7]
        v_pad, m_scr, b_scr, fade_scr, st_scr, a_scr, x_scr, y_scr, raw_scr = refs[7:]
        key_columns = slice(head * DK, (head + 1) * DK)
    else:
        kn_ref, wu_ref, start_ref, map_ref = refs[:4]
        v_pad, m_scr, b_scr, fade_scr, st_scr, a_scr, x_scr, y_scr = refs[4:]
        key_columns = slice(0, DK)
    step = pl.program_id(0)
    used = length_ref[first + jnp.minimum(step, count - 1)] - lax.axis_index("seq") * (chunks * BLOCK)
    units = [(h, c) for c in range(chunks) for h in range(group)]
    slot = step % 2
    live = jnp.logical_and(step < count, used > 0)

    def begin():
        row = lax.broadcasted_iota(jnp.int32, (DV + DK, DK), 0)
        lane = lax.broadcasted_iota(jnp.int32, (DV + DK, DK), 1)
        for h in range(group):
            st_scr[h] = jnp.where(row == lane + DV, 1.0, 0.0).astype(F32)

    def advance(c):
        narrow, moved = {}, {}

        def load(h):
            narrow[h] = st_scr[h].astype(BF16)
            start_ref[0, h, c * (DV + DK) : (c + 1) * (DV + DK), :] = narrow[h]

        def move(h):
            moved[h] = dot(narrow[h], m_scr[1 - slot, c, h])

        def store(h):
            fade = fade_scr[1 - slot, c, h : h + 1, :]
            state = st_scr[h, :DV] * fade + (moved[h][:DV] + b_scr[1 - slot, c, h])
            trans = st_scr[h, DV:] * fade + moved[h][DV:]
            if c < chunks - 1:
                st_scr[h, :DV] = state
                st_scr[h, DV:] = trans
            else:
                map_ref[h, :DV] = state.astype(BF16)
                map_ref[h, DV:] = trans.astype(BF16)

        return [functools.partial(act, h) for act in (load, move, store) for h in range(group)]

    recurrence = [begin]
    for c in range(chunks):
        recurrence += advance(c)

    @pl.when(jnp.logical_not(live))
    def _():
        @pl.when(step > 0)
        def _():
            weave(recurrence)

        @pl.when(step < count)
        def _():
            if mixes:
                qn_ref[...] = jnp.zeros_like(qn_ref)
                kn_ref[...] = jnp.zeros_like(kn_ref)
            wu_ref[...] = jnp.zeros_like(wu_ref)
            fade_scr[slot] = jnp.ones(fade_scr.shape[1:], F32)
            m_scr[slot] = jnp.zeros(m_scr.shape[1:], BF16)
            b_scr[slot] = jnp.zeros(b_scr.shape[1:], F32)

    @pl.when(live)
    def _():
        if mixes:
            mix(qk_ref, halo_ref, qk_taps_ref, qn_ref, kn_ref, raw_scr, key_heads, chunks)
        halo = halo_ref[0].astype(F32)
        v_pad[EDGE:, :] = v_ref[0].astype(F32)
        for i in range(CONV - 1):
            for h in range(group):
                source = 2 * EDGE + (i * key_heads + head) * group + h
                v_pad[EDGE - CONV + 1 + i : EDGE - CONV + 2 + i, h * DV : (h + 1) * DV] = halo[
                    source : source + 1
                ]
        v_all_taps = v_taps_ref[...].astype(F32)
        v_taps = [v_all_taps[i : i + 1] for i in range(CONV)]

        cum, gain = gates_of_heads(log_ref, gain_ref, used, head, group)
        both_gains = gain * jnp.exp(cum)
        columns = as_columns(jnp.concatenate([cum] * (8 // group), axis=0), chunks)

        def span(c):
            return slice(c * BLOCK, (c + 1) * BLOCK)

        row = lax.broadcasted_iota(jnp.int32, (BLOCK, BLOCK), 0)
        lane = lax.broadcasted_iota(jnp.int32, (BLOCK, BLOCK), 1)
        above = row < lane
        small_row = lax.broadcasted_iota(jnp.int32, (TINY, BLOCK), 0)
        small_lane = lax.broadcasted_iota(jnp.int32, (TINY, BLOCK), 1)
        part_of = small_lane // TINY
        tiny_eye = jnp.where(small_row == small_lane % TINY, 1.0, 0.0).astype(F32)

        keys = [kn_ref[0, span(c), key_columns] for c in range(chunks)]
        turned = {}

        def front(some):
            ops, kk, compact, solved, mixed = [], {}, {}, {}, {}
            local = [(h, c) for c in some for h in range(group)]

            def start(c):
                turned[c] = keys[c].T
                kk[c] = dot(keys[c], turned[c])

            def mask(h, c):
                r = h * chunks + c
                ratio = jnp.exp(cum[h : h + 1, span(c)] - columns[:, c * 8 + h : c * 8 + h + 1])
                strict = jnp.where(above, ratio * kk[c] * -gain[h : h + 1, span(c)], 0.0)
                a_scr[r] = strict.astype(BF16)
                tiny = strict[0:TINY]
                for b in range(1, BLOCK // TINY):
                    tiny = jnp.where(part_of == b, strict[b * TINY : (b + 1) * TINY], tiny)
                compact[r] = tiny
                solved[r] = tiny_eye

            def eliminate(j, r):
                factor = jnp.take_along_axis(compact[r], part_of * TINY + j, axis=1, mode="promise_in_bounds")
                solved[r] = solved[r] + factor * solved[r][j : j + 1, :]

            def place(r):
                for b in range(BLOCK // TINY):
                    x_scr[r, b * TINY : (b + 1) * TINY, :] = jnp.where(part_of == b, solved[r], 0.0).astype(BF16)

            def convolve(c):
                mixed[c] = mixed_rows(v_pad, v_taps, EDGE, 0, 1, c).astype(BF16)

            def scale(h, c):
                top = h * (DK + DV)
                v_wide = mixed[c][:, h * DV : (h + 1) * DV].T.astype(F32)
                y_scr[c, top : top + DK, :] = (turned[c].astype(F32) * both_gains[h : h + 1, span(c)]).astype(BF16)
                y_scr[c, top + DK : top + DK + DV, :] = (v_wide * gain[h : h + 1, span(c)]).astype(BF16)

            for c in some:
                ops.append(functools.partial(start, c))
            for h, c in local:
                ops.append(functools.partial(mask, h, c))
            for j in range(TINY - 1, 0, -1):
                for h, c in local:
                    ops.append(functools.partial(eliminate, j, h * chunks + c))
            for h, c in local:
                ops.append(functools.partial(place, h * chunks + c))
            right = []
            for c in some:
                right.append(functools.partial(convolve, c))
                right += [functools.partial(scale, h, c) for h in range(group)]
            return ops, right

        def back(some):
            ops, own, moved = [], {}, {}
            local = [(h, c) for c in some for h in range(group)]

            def reach(size, r):
                half_lane = lax.broadcasted_iota(jnp.int32, (BLOCK // 2, BLOCK), 1)
                half_row = lax.broadcasted_iota(jnp.int32, (BLOCK // 2, BLOCK), 0)
                partner = half_lane // size == 2 * (half_row // size) + 1
                own[r] = jnp.concatenate([x_scr[r, s : s + size, :] for s in range(0, BLOCK, 2 * size)], axis=0)
                moved[r] = jnp.where(partner, dot(own[r], a_scr[r]), 0.0).astype(BF16)

            def join(size, r):
                update = own[r] + dot(moved[r], x_scr[r]).astype(BF16)
                for n, s in enumerate(range(0, BLOCK, 2 * size)):
                    x_scr[r, s : s + size, :] = update[n * size : (n + 1) * size]

            def solve(h, c):
                r = h * chunks + c
                top = h * (DK + DV)
                sums = cum[:, span(c)]
                last = sums[:, BLOCK - 1 : BLOCK]
                tail = jnp.exp(last - sums)
                fade = jnp.broadcast_to(jnp.exp(last), (group, BLOCK))
                rows = dot(y_scr[c, top : top + DK + DV, :], x_scr[r])
                wu_ref[0, r] = rows.astype(BF16)
                y_scr[c, top : top + DK + DV, :] = (rows * tail[h : h + 1]).astype(BF16)
                fade_scr[slot, c, h : h + 1, :] = fade[h : h + 1]

            def finish(c):
                both = dot(y_scr[c], keys[c])
                for h in range(group):
                    top = h * (DK + DV)
                    m_scr[slot, c, h] = (-both[top : top + DK]).astype(BF16)
                    b_scr[slot, c, h] = both[top + DK : top + DK + DV]

            size = TINY
            while size < BLOCK:
                ops += [functools.partial(reach, size, h * chunks + c) for h, c in local]
                ops += [functools.partial(join, size, h * chunks + c) for h, c in local]
                size *= 2
            ops += [functools.partial(solve, h, c) for h, c in local]
            ops += [functools.partial(finish, c) for c in some]
            return ops

        half = chunks // 2
        early, late = range(half), range(half, chunks)
        early_front, early_right = front(early)
        late_front, late_right = front(late)
        cut = len(recurrence) // 3
        weave(early_front, recurrence[:cut], early_right)
        weave(back(early), late_front, late_right)
        weave(back(late), recurrence[cut:])


def prepare(job, lengths, qk_rows, v_in, halo, qk_taps, v_taps, log_decay, write_gain, key_heads, mixed, after):
    head, first, count = job
    tok = v_in.shape[1]
    value_heads = v_in.shape[2] // DV
    group = value_heads // key_heads
    chunks = tok // BLOCK
    rows = group * chunks
    wide = group * DV
    mixes = mixed is None

    def now(i):
        return jnp.minimum(i, count - 1)

    def before(i):
        return jnp.maximum(i - 1, 0)

    def whole_of(i, lengths):
        return (first + now(i), 0, 0)

    operands = [far(v_in), halo, far(v_taps), far(log_decay), far(write_gain), far(after)]
    in_specs = [
        pl.BlockSpec((1, tok, wide), lambda i, lengths: (first + now(i), 0, head)),
        pl.BlockSpec((1,) + halo.shape[1:], whole_of),
        pl.BlockSpec((CONV, wide), lambda i, lengths: (0, head)),
        pl.BlockSpec((1, value_heads, tok), whole_of),
        pl.BlockSpec((1, value_heads, tok), whole_of),
        pl.BlockSpec(memory_space=pltpu.HBM),
    ]
    out_specs = [
        pl.BlockSpec((1, rows, DK + DV, BLOCK), lambda i, lengths: (now(i), 0, 0, 0)),
        pl.BlockSpec((1, group, chunks * (DV + DK), DK), lambda i, lengths: (before(i), 0, 0, 0)),
        pl.BlockSpec((group, DV + DK, DK), lambda i, lengths: (before(i), 0, 0)),
    ]
    out_shape = [
        pltpu.HBM((count, rows, DK + DV, BLOCK), BF16),
        pltpu.HBM((count, group, chunks * (DV + DK), DK), BF16),
        jax.ShapeDtypeStruct((count * group, DV + DK, DK), BF16),
    ]
    scratch = [
        pltpu.VMEM((tok + EDGE, wide), F32),
        pltpu.VMEM((2, chunks, group, DK, DK), BF16),
        pltpu.VMEM((2, chunks, group, DV, DK), F32),
        pltpu.VMEM((2, chunks, group, BLOCK), F32),
        pltpu.VMEM((group, DV + DK, DK), F32),
        pltpu.VMEM((rows, BLOCK, BLOCK), BF16),
        pltpu.VMEM((rows, BLOCK, BLOCK), BF16),
        pltpu.VMEM((chunks, group * (DK + DV), BLOCK), BF16),
    ]
    if mixes:
        operands += [far(qk_rows), far(qk_taps)]
        in_specs += [
            pl.BlockSpec((1,) + qk_rows.shape[1:], whole_of),
            pl.BlockSpec(qk_taps.shape, lambda i, lengths: (0, 0)),
        ]
        out_specs += [pl.BlockSpec((1, tok, key_heads * DK), lambda i, lengths: (now(i), 0, 0))] * 2
        out_shape += [pltpu.HBM((count, tok, key_heads * DK), BF16)] * 2
        scratch.append(pltpu.VMEM((qk_rows.shape[1] + 2 * EDGE, DK), F32))
    else:
        operands.append(far(mixed))
        in_specs.append(pl.BlockSpec((1, tok, DK), lambda i, lengths: (first + now(i), 0, head)))
    return pl.pallas_call(
        functools.partial(prepare_kernel, first, count, head, group, chunks, key_heads, mixes),
        grid_spec=pltpu.PrefetchScalarGridSpec(
            num_scalar_prefetch=1,
            grid=(count + 1,),
            in_specs=in_specs,
            out_specs=out_specs,
            scratch_shapes=scratch,
        ),
        out_shape=out_shape,
        compiler_params=pltpu.CompilerParams(vmem_limit_bytes=VMEM_BYTES),
        cost_estimate=pl.CostEstimate(flops=5 * 10**9 * count, bytes_accessed=4 * 2**20 * count, transcendentals=10**6),
        name="prepare",
    )(lengths, *operands)


def outputs_kernel(
    first, head, group, chunks,
    length_ref, qn_ref, kn_ref, wu_ref, start_ref, log_ref, gain_ref, enter_ref, z_ref, norm_ref, held_ref, after_ref,
    out_ref,
    first_scr, score_scr, seen_scr,
):
    used = length_ref[first + pl.program_id(0)] - lax.axis_index("seq") * (chunks * BLOCK)
    units = [(h, c) for c in range(chunks) for h in range(group)]

    @pl.when(used <= 0)
    def _():
        out_ref[...] = jnp.zeros_like(out_ref)

    @pl.when(used > 0)
    def _():
        cum, gain = gates_of_heads(log_ref, gain_ref, used, head, group)
        faded = jnp.exp(cum)
        columns = as_columns(jnp.concatenate([cum] * (8 // group), axis=0), chunks)
        row = lax.broadcasted_iota(jnp.int32, (BLOCK, BLOCK), 0)
        lane = lax.broadcasted_iota(jnp.int32, (BLOCK, BLOCK), 1)
        upto = row <= lane
        norm_gain = norm_ref[...]

        def span(c):
            return slice(c * BLOCK, (c + 1) * BLOCK)

        for c in range(chunks):
            turned = qn_ref[0, span(c), :].T
            kq = dot(kn_ref[0, span(c), :], turned)
            q_wide = turned.astype(F32)
            for h in range(group):
                r = h * chunks + c
                ratio = jnp.exp(cum[h : h + 1, span(c)] - columns[:, c * 8 + h : c * 8 + h + 1])
                score_scr[r] = jnp.where(upto, ratio * kq, 0.0).astype(BF16)
                seen_scr[r] = q_wide * faded[h : h + 1, span(c)]
                top = c * (DV + DK)
                moved = dot(enter_ref[h], start_ref[0, h, top + DV : top + DV + DK, :])
                first_scr[r] = (moved + start_ref[0, h, top : top + DV, :].astype(F32)).astype(BF16)
        both, raws = {}, {}
        for h, c in units:
            r = h * chunks + c
            both[r] = dot(wu_ref[0, r], score_scr[r])
        for h, c in units:
            r = h * chunks + c
            seen = (seen_scr[r] - both[r][:DK]).astype(BF16)
            raw = dot(first_scr[r], seen) + both[r][DK:]
            mean = jnp.sum(raw * raw, axis=0, keepdims=True) * (1.0 / DV)
            raws[r] = (raw * lax.rsqrt(mean + EPSILON)).astype(BF16)
        for h, c in units:
            scaled = raws[h * chunks + c].T.astype(F32)
            cols = slice(h * DV, (h + 1) * DV)
            gated = scaled * norm_gain * silu(z_ref[0, span(c), cols].astype(F32))
            out_ref[0, span(c), cols] = jnp.where(row + c * BLOCK < used, gated, 0.0).astype(BF16)


def outputs(
    job, piece, lengths, qn, kn, wu, starts, log_decay, write_gain, enter, gate_z, norm_gain, key_heads, held, after,
):
    head, first, _ = job
    begin, count = piece
    prompts, tok, width = gate_z.shape
    rows = wu.shape[1]
    chunks = tok // BLOCK
    group = rows // chunks
    wide = group * DV
    value_heads = key_heads * group
    shift = begin - first
    from_mix = begin if qn.shape[0] == prompts else shift

    def whole_of(i, lengths):
        return (begin + i, 0, 0)

    def wide_of(i, lengths):
        return (begin + i, 0, head)

    def mixed_of(i, lengths):
        return (from_mix + i, 0, head)

    empty = held is None
    return pl.pallas_call(
        functools.partial(outputs_kernel, begin, head, group, chunks),
        grid_spec=pltpu.PrefetchScalarGridSpec(
            num_scalar_prefetch=1,
            grid=(count,),
            in_specs=[
                pl.BlockSpec((1, tok, DK), mixed_of),
                pl.BlockSpec((1, tok, DK), mixed_of),
                pl.BlockSpec((1, rows, DK + DV, BLOCK), lambda i, lengths: (shift + i, 0, 0, 0)),
                pl.BlockSpec((1, group, chunks * (DV + DK), DK), lambda i, lengths: (shift + i, 0, 0, 0)),
                pl.BlockSpec((1, value_heads, tok), whole_of),
                pl.BlockSpec((1, value_heads, tok), whole_of),
                pl.BlockSpec((group, DK, DV), lambda i, lengths: (shift + i, 0, 0)),
                pl.BlockSpec((1, tok, wide), wide_of),
                pl.BlockSpec((1, DV), lambda i, lengths: (0, 0)),
                pl.BlockSpec(memory_space=pltpu.HBM),
                pl.BlockSpec(memory_space=pltpu.HBM),
            ],
            out_specs=pl.BlockSpec((1, tok, wide), wide_of),
            scratch_shapes=[
                pltpu.VMEM((rows, DV, DK), BF16),
                pltpu.VMEM((rows, BLOCK, BLOCK), BF16),
                pltpu.VMEM((rows, BLOCK, DV), F32),
            ],
        ),
        out_shape=pltpu.HBM((prompts, tok, width), BF16),
        input_output_aliases={} if empty else {10: 0},
        compiler_params=pltpu.CompilerParams(vmem_limit_bytes=VMEM_BYTES),
        cost_estimate=pl.CostEstimate(flops=3 * 10**9 * count, bytes_accessed=4 * 2**20 * count, transcendentals=10**6),
        name="outputs",
    )(
        lengths, far(qn), far(kn), far(wu), far(starts), far(log_decay), far(write_gain), enter, far(gate_z),
        far(norm_gain.reshape(1, DV)), far(after if empty else held), far(wu if after is held else after),
    )


def own_chip():
    seq = lax.axis_index("seq")
    return seq // 2, seq % 2 == 1


def early_late(own, other, odd):
    return jnp.where(odd, other, own), jnp.where(odd, own, other)


def follow(there, running):
    return dot(running, there[DV:])


def compose_maps(ins, outs):
    own_ref, other_ref = ins
    _, odd = own_chip()
    for n in range(own_ref.shape[0]):
        early, late = early_late(own_ref[n], other_ref[n], odd)
        both = follow(late, early)
        outs[0][n, :DV] = (both[:DV] + late[:DV].astype(F32)).astype(BF16)
        outs[0][n, DV:] = both[DV:].astype(BF16)


def close_maps(ins, outs):
    own_ref, other_ref = ins[:2]
    refs = ins[2:]
    chips = len(refs)
    chip, odd = own_chip()

    def of_chip(j, n):
        value = refs[0][n]
        for k in range(1, chips):
            value = jnp.where((chip + chips - k) % chips == j, refs[k][n], value)
        return value

    every = range(own_ref.shape[0])
    running = [of_chip(0, n)[:DV] for n in every]
    entering = [jnp.zeros_like(running[n]) for n in every]
    for j in range(1, chips):
        entering = [jnp.where(chip == j, running[n], entering[n]) for n in every]
        there = [of_chip(j, n) for n in every]
        running = [(follow(there[n], running[n]) + there[n][:DV].astype(F32)).astype(BF16) for n in every]
    for n in every:
        early, _ = early_late(own_ref[n], other_ref[n], odd)
        second = (follow(early, entering[n]) + early[:DV].astype(F32)).astype(BF16)
        outs[0][n] = jnp.where(odd, second, entering[n])
        outs[1][n] = running[n].T


def chain_maps(ins, outs):
    count = len(ins)
    mine = lax.axis_index("seq")
    every = range(ins[0].shape[0])

    def run(at):
        running = [ins[at][n, :DV] for n in every]
        for n in every:
            if at == 0:
                outs[0][n] = jnp.zeros_like(running[n])
        for j in range(1, count):
            there = ins[at ^ j]
            if j == at:
                for n in every:
                    outs[0][n] = running[n]
            moved = [follow(there.at[n], running[n]) for n in every]
            running = [(moved[n] + there[n, :DV].astype(F32)).astype(BF16) for n in every]
        for n in every:
            outs[1][n] = running[n].T

    for at in range(count):
        pl.when(mine == at)(functools.partial(run, at))


def choose_finals(group, placement_ref, finals, outs):
    refs = [(ref, n) for ref in finals for n in range(ref.shape[0] // group)]
    for r in range(placement_ref.shape[1]):
        prompt = placement_ref[0, r]
        for p, (ref, n) in enumerate(refs):
            @pl.when(prompt == p)
            def _(ref=ref, n=n):
                outs[0][r] = ref[n * group : (n + 1) * group]


def state_step(placement, group, compose, chain, close, earlier, after):
    operands, shapes = [placement], []
    steps = []
    if compose is not None:
        steps.append(("compose", len(operands), len(compose), len(shapes)))
        operands += compose
        shapes += [compose[0]]
    if chain is not None or close is not None:
        steps.append(("chain" if close is None else "close", len(operands), len(close or chain), len(shapes)))
        close = close or chain
        operands += close
        shapes += [jax.ShapeDtypeStruct((close[0].shape[0], DK, DV), BF16)] * 2
        if earlier is not None:
            steps.append(("choose", len(operands), len(earlier), len(shapes)))
            operands += earlier
            shapes.append(jax.ShapeDtypeStruct((placement.shape[1], group, DK, DV), BF16))
    out_shape = [jax.ShapeDtypeStruct(x.shape, x.dtype) for x in shapes] + [pltpu.HBM((8, 128), F32)]

    def kernel(*refs):
        refs[-1][...] = jnp.zeros_like(refs[-1])
        ins, outs = refs[: len(operands)], refs[len(operands) + 1 :]
        closed = None
        for kind, at, size, to in steps:
            part = ins[at : at + size]
            if kind == "compose":
                compose_maps(part, outs[to : to + 1])
            elif kind in ("close", "chain"):
                (close_maps if kind == "close" else chain_maps)(part, outs[to : to + 2])
                closed = outs[to + 1]
            else:
                choose_finals(group, ins[0], list(part) + [closed], outs[to:])

    vmem = pl.BlockSpec(memory_space=pltpu.VMEM)
    return pl.pallas_call(
        kernel,
        in_specs=[pl.BlockSpec(memory_space=pltpu.SMEM)]
        + [vmem] * (len(operands) - 1)
        + [pl.BlockSpec(memory_space=pltpu.HBM)],
        out_specs=[vmem] * len(out_shape),
        out_shape=out_shape,
        compiler_params=pltpu.CompilerParams(vmem_limit_bytes=SMALL_VMEM_BYTES),
        cost_estimate=pl.CostEstimate(flops=10**9, bytes_accessed=2**20, transcendentals=0),
        name="state_step",
    )(*operands, far(after))


def deliver(parts):
    count, group = parts[0].shape[:2]

    def kernel(*refs):
        for n, ref in enumerate(refs[:-1]):
            refs[-1][:, n * group : (n + 1) * group] = ref[...].astype(F32)

    return pl.pallas_call(
        kernel,
        grid=(2,),
        in_specs=[pl.BlockSpec((count // 2, group, DK, DV), lambda i: (i, 0, 0, 0))] * len(parts),
        out_specs=pl.BlockSpec((count // 2, group * len(parts), DK, DV), lambda i: (i, 0, 0, 0)),
        out_shape=jax.ShapeDtypeStruct((count, group * len(parts), DK, DV), F32),
        compiler_params=pltpu.CompilerParams(vmem_limit_bytes=VMEM_BYTES),
        name="deliver",
    )(*parts)


def across(block, distance):
    count = lax.axis_size("seq")
    return lax.ppermute(block, "seq", [(i, i ^ distance) for i in range(count)])


def from_chip_behind(block, distance):
    count = lax.axis_size("seq")
    chips = count // 2
    route = [(i, ((i // 2 + distance) % chips) * 2 + i % 2) for i in range(count)]
    return lax.ppermute(block, "seq", route)


def shards(
    qk_in, v_in, gate_z, conv_qk, conv_v, log_decay, write_gain, norm_gain, prompt_lengths, placement,
):
    prompts, tok = qk_in.shape[:2]
    key_heads = qk_in.shape[3] // DK
    value_heads = v_in.shape[2] // DV
    rim = CONV - 1
    seq_count = lax.axis_size("seq")
    head_count = lax.axis_size("head")

    def by_head(x):
        x = x.reshape(x.shape[0], x.shape[1], 2, key_heads, DK)
        return jnp.transpose(x, (0, 1, 3, 2, 4)).reshape(x.shape[0], -1, DK)

    qk_rows = by_head(qk_in)
    qk_taps = by_head(conv_qk[None])[0]
    qk_tail = qk_rows[:, (tok - rim) * 2 * key_heads :]
    v_tail = v_in[:, tok - rim :].reshape(prompts, rim * value_heads, DV)
    front = 2 * EDGE - qk_tail.shape[1]
    back = 2 * EDGE - v_tail.shape[1]
    tails = jnp.concatenate(
        [
            jnp.zeros((prompts, front, DK), BF16),
            qk_tail,
            v_tail,
            jnp.zeros((prompts, back, DK), BF16),
        ],
        axis=1,
    )
    halo = lax.ppermute(tails, "seq", [(i, i + 1) for i in range(seq_count - 1)])
    group = value_heads // key_heads
    chips = seq_count // 2
    half = prompts // 2
    jobs = [(head, 0, prompts) for head in range(key_heads)]
    if key_heads == 1:
        jobs = [(0, 0, half), (0, half, prompts - half)]
    total = len(jobs)
    made, finals, sent = [], [], {}
    attended = None
    last = v_in

    def finish(job, results):
        head = jobs[job][0]
        finals.append(results[1])
        if len(results) > 3:
            sent[head] = lax.all_to_all(results[2], "head", 0, 0)
        return results[0], results[-1]

    def earlier(job):
        same = [n for n in range(total) if jobs[n][0] == jobs[job][0]]
        return [finals[n] for n in same[:-1]] if job == same[-1] else None

    def emit(job, entered, attended, last):
        qn, kn, wu, starts, _ = made[job]
        return outputs(
            jobs[job], jobs[job][1:], prompt_lengths, qn, kn, wu, starts, log_decay, write_gain,
            entered, gate_z, norm_gain, key_heads, attended, last,
        )

    for job in jobs:
        mixed = None if job[0] == 0 else made[0][:2]
        wu, starts, own_map, *new = prepare(
            job, prompt_lengths, qk_rows, v_in, halo, qk_taps, conv_v, log_decay, write_gain, key_heads,
            mixed and mixed[1], last,
        )
        last = wu
        moved = [own_map]
        if job == jobs[-1]:
            moved.append(across(own_map, 1))
        else:
            moved += [across(own_map, k) for k in range(1, seq_count)]
        made.append((*(mixed or new), wu, starts, moved))

    entered = []
    for job in range(total - 1):
        results = state_step(placement, group, None, made[job][4], None, earlier(job), last)
        enter, last = finish(job, results)
        entered.append(enter)
    pair = made[-1][4]
    chip_map, last = state_step(placement, group, pair, None, None, None, last)
    chip_maps = [chip_map] + [from_chip_behind(chip_map, k) for k in range(1, chips)]
    for job in range(total - 1):
        attended = last = emit(job, entered[job], attended, last)
    results = state_step(placement, group, None, None, pair + chip_maps, earlier(total - 1), last)
    enter, last = finish(total - 1, results)
    attended = emit(total - 1, enter, attended, last)
    rollout = deliver([sent[head] for head in range(key_heads)])
    return attended, rollout.reshape(1, 1, head_count * value_heads, DK, DV)


def solution(mesh):
    return jax.shard_map(
        shards,
        mesh=mesh,
        in_specs=(
            P(None, "seq", None, "head"),
            P(None, "seq", "head"),
            P(None, "seq", "head"),
            P(None, None, "head"),
            P(None, "head"),
            P(None, "head", "seq"),
            P(None, "head", "seq"),
            P(),
            P(),
            P("seq", None),
        ),
        out_specs=(P(None, "seq", "head"), P("seq", "head", None, None, None)),
        check_vma=False,
    )
```

```python
import functools

import jax
import jax.numpy as jnp
from jax import lax
from jax.experimental import pallas as pl
from jax.experimental.pallas import tpu as pltpu
from jax.sharding import PartitionSpec as P

DK = 128
DV = 128
CONV = 4
BLOCK = 128
TINY = 32
EDGE = 8
EPSILON = 1e-06
VMEM_BYTES = 40 * 1024 * 1024
SMALL_VMEM_BYTES = 8 * 1024 * 1024
F32 = jnp.float32
BF16 = jnp.bfloat16


def far(x):
    return pltpu.with_memory_space_constraint(x, pltpu.HBM)


def dot(a, b):
    return lax.dot_general(a, b, (((1,), (0,)), ((), ())), preferred_element_type=F32)


def silu(x):
    half = 0.5 * x
    return half + half * jnp.tanh(half)


def mixed_rows(pad_ref, taps, rim, first, step, c):
    total = None
    for i in range(CONV):
        start = rim + first + step * (c * BLOCK + i - (CONV - 1))
        stride = None if step == 1 else step
        term = pad_ref[pl.ds(start, BLOCK, stride), :] * taps[i]
        total = term if total is None else total + term
    return silu(total)


def unit_rows(x):
    return x * lax.rsqrt(jnp.sum(x * x, axis=-1, keepdims=True) + EPSILON)


def heads_rows(ref, head, group):
    every = ref[0]
    rows = every[:group]
    for n in range(1, every.shape[0] // group):
        rows = jnp.where(head == n, every[n * group : (n + 1) * group], rows)
    return rows


def gates_of_heads(log_ref, gain_ref, used, head, group):
    log = heads_rows(log_ref, head, group)
    lane = lax.broadcasted_iota(jnp.int32, log.shape, 1)
    valid = lane < used
    cum = jnp.where(valid, log, 0.0)
    gain = jnp.where(valid, heads_rows(gain_ref, head, group), 0.0)
    shift = 1
    while shift < BLOCK:
        cum = cum + jnp.where(lane % BLOCK >= shift, pltpu.roll(cum, shift, 1), 0.0)
        shift *= 2
    return cum, gain


def as_columns(rows, chunks):
    parts = [rows[:, c * BLOCK : (c + 1) * BLOCK] for c in range(chunks)]
    short = BLOCK - 8 * chunks
    if short:
        parts.append(jnp.zeros((short, BLOCK), F32))
    return jnp.concatenate(parts, axis=0).T


def block_bases(parts, chunks):
    rows = jnp.concatenate(parts, axis=0)
    short = 7 - rows.shape[0]
    fill = [jnp.zeros((short, rows.shape[1]), F32)] if short else []
    rows = jnp.concatenate([rows] + fill + [jnp.ones((1, rows.shape[1]), F32)], axis=0)
    return [rows[:, c * BLOCK : (c + 1) * BLOCK] for c in range(chunks)]


def spread_squares(base, group, kinds):
    high = base.astype(BF16).astype(F32)
    middle = (base - high).astype(BF16).astype(F32)
    low = base - high - middle
    parts = [high, middle, low]
    row = lax.broadcasted_iota(jnp.int32, (32, BLOCK), 0)
    which = row % 8
    real = row < 24
    stacked = jnp.concatenate(parts + [jnp.zeros_like(high)], axis=0)
    left = jnp.where(jnp.logical_and(which == 7, real), 1.0, stacked).T.astype(BF16)
    blocks = []
    for h in range(group):
        minus = jnp.concatenate([jnp.broadcast_to(-part[h : h + 1], (8, BLOCK)) for part in parts + [low]], axis=0)
        blocks.append(jnp.where(which == h, 1.0, jnp.where(which == 7, minus, 0.0)))
    for n in range(group, group * kinds):
        blocks.append(jnp.where(which == n, 1.0, 0.0).astype(F32))
    every = dot(left, jnp.concatenate(blocks, axis=1).astype(BF16))
    return [every[:, n * BLOCK : (n + 1) * BLOCK] for n in range(group * kinds)]


def mix(qk_ref, halo_ref, taps_ref, qn_ref, kn_ref, raw_scr, key_heads, chunks):
    kinds = 2 * key_heads
    rim = 2 * EDGE
    taps = taps_ref[...].astype(F32)
    raw_scr[:rim] = halo_ref[0].astype(F32)[:rim]
    raw_scr[rim:] = qk_ref[0].astype(F32)
    for c in range(chunks):
        span = slice(c * BLOCK, (c + 1) * BLOCK)
        for kind in range(kinds):
            own = [taps[n : n + 1] for n in range(kind, taps.shape[0], kinds)]
            rows = unit_rows(mixed_rows(raw_scr, own, rim, kind, kinds, c))
            to_ref = kn_ref if kind % 2 else qn_ref
            to_ref[0, span, kind // 2 * DK : (kind // 2 + 1) * DK] = rows.astype(BF16)


def weave(*lists):
    places = []
    for which, entries in enumerate(lists):
        places += [((n + 0.5) / len(entries), which, n) for n in range(len(entries))]
    for _, which, n in sorted(places):
        lists[which][n]()


def prepare_kernel(first, count, head, group, chunks, key_heads, mixes, *refs):
    length_ref, v_ref, halo_ref, v_taps_ref, log_ref, gain_ref, after_ref = refs[:7]
    refs = refs[7:]
    if mixes:
        qk_ref, qk_taps_ref, wu_ref, start_ref, map_ref, qn_ref, kn_ref = refs[:7]
        v_pad, m_scr, b_scr, fade_scr, st_scr, a_scr, x_scr, y_scr, raw_scr = refs[7:]
        key_columns = slice(head * DK, (head + 1) * DK)
    else:
        kn_ref, wu_ref, start_ref, map_ref = refs[:4]
        v_pad, m_scr, b_scr, fade_scr, st_scr, a_scr, x_scr, y_scr = refs[4:]
        key_columns = slice(0, DK)
    step = pl.program_id(0)
    used = length_ref[first + jnp.minimum(step, count - 1)] - lax.axis_index("seq") * (chunks * BLOCK)
    units = [(h, c) for c in range(chunks) for h in range(group)]
    slot = step % 2
    live = jnp.logical_and(step < count, used > 0)

    def begin():
        row = lax.broadcasted_iota(jnp.int32, (DV + DK, DK), 0)
        lane = lax.broadcasted_iota(jnp.int32, (DV + DK, DK), 1)
        for h in range(group):
            st_scr[h] = jnp.where(row == lane + DV, 1.0, 0.0).astype(F32)

    def advance(c):
        narrow, moved = {}, {}

        def load(h):
            narrow[h] = st_scr[h].astype(BF16)
            start_ref[0, h, c * (DV + DK) : (c + 1) * (DV + DK), :] = narrow[h]

        def move(h):
            moved[h] = dot(narrow[h], m_scr[1 - slot, c, h])

        def store(h):
            fade = fade_scr[1 - slot, c, h : h + 1, :]
            state = st_scr[h, :DV] * fade + (moved[h][:DV] + b_scr[1 - slot, c, h])
            trans = st_scr[h, DV:] * fade + moved[h][DV:]
            if c < chunks - 1:
                st_scr[h, :DV] = state
                st_scr[h, DV:] = trans
            else:
                map_ref[h, :DV] = state.astype(BF16)
                map_ref[h, DV:] = trans.astype(BF16)

        return [functools.partial(act, h) for act in (load, move, store) for h in range(group)]

    recurrence = [begin]
    for c in range(chunks):
        recurrence += advance(c)

    @pl.when(jnp.logical_not(live))
    def _():
        @pl.when(step > 0)
        def _():
            weave(recurrence)

        @pl.when(step < count)
        def _():
            if mixes:
                qn_ref[...] = jnp.zeros_like(qn_ref)
                kn_ref[...] = jnp.zeros_like(kn_ref)
            wu_ref[...] = jnp.zeros_like(wu_ref)
            fade_scr[slot] = jnp.ones(fade_scr.shape[1:], F32)
            m_scr[slot] = jnp.zeros(m_scr.shape[1:], BF16)
            b_scr[slot] = jnp.zeros(b_scr.shape[1:], F32)

    @pl.when(live)
    def _():
        if mixes:
            mix(qk_ref, halo_ref, qk_taps_ref, qn_ref, kn_ref, raw_scr, key_heads, chunks)
        halo = halo_ref[0].astype(F32)
        v_pad[EDGE:, :] = v_ref[0].astype(F32)
        for i in range(CONV - 1):
            for h in range(group):
                source = 2 * EDGE + (i * key_heads + head) * group + h
                v_pad[EDGE - CONV + 1 + i : EDGE - CONV + 2 + i, h * DV : (h + 1) * DV] = halo[
                    source : source + 1
                ]
        v_all_taps = v_taps_ref[...].astype(F32)
        v_taps = [v_all_taps[i : i + 1] for i in range(CONV)]

        cum, gain = gates_of_heads(log_ref, gain_ref, used, head, group)
        both_gains = gain * jnp.exp(cum)
        columns = as_columns(jnp.concatenate([cum] * (8 // group), axis=0), chunks)

        def span(c):
            return slice(c * BLOCK, (c + 1) * BLOCK)

        row = lax.broadcasted_iota(jnp.int32, (BLOCK, BLOCK), 0)
        lane = lax.broadcasted_iota(jnp.int32, (BLOCK, BLOCK), 1)
        above = row < lane
        small_row = lax.broadcasted_iota(jnp.int32, (TINY, BLOCK), 0)
        small_lane = lax.broadcasted_iota(jnp.int32, (TINY, BLOCK), 1)
        part_of = small_lane // TINY
        tiny_eye = jnp.where(small_row == small_lane % TINY, 1.0, 0.0).astype(F32)

        keys = [kn_ref[0, span(c), key_columns] for c in range(chunks)]
        turned = {}

        def front(some):
            ops, kk, compact, solved, mixed = [], {}, {}, {}, {}
            local = [(h, c) for c in some for h in range(group)]

            def start(c):
                turned[c] = keys[c].T
                kk[c] = dot(keys[c], turned[c])

            def mask(h, c):
                r = h * chunks + c
                ratio = jnp.exp(cum[h : h + 1, span(c)] - columns[:, c * 8 + h : c * 8 + h + 1])
                strict = jnp.where(above, ratio * kk[c] * -gain[h : h + 1, span(c)], 0.0)
                a_scr[r] = strict.astype(BF16)
                tiny = strict[0:TINY]
                for b in range(1, BLOCK // TINY):
                    tiny = jnp.where(part_of == b, strict[b * TINY : (b + 1) * TINY], tiny)
                compact[r] = tiny
                solved[r] = tiny_eye

            def eliminate(j, r):
                factor = jnp.take_along_axis(compact[r], part_of * TINY + j, axis=1, mode="promise_in_bounds")
                solved[r] = solved[r] + factor * solved[r][j : j + 1, :]

            def place(r):
                for b in range(BLOCK // TINY):
                    x_scr[r, b * TINY : (b + 1) * TINY, :] = jnp.where(part_of == b, solved[r], 0.0).astype(BF16)

            def convolve(c):
                mixed[c] = mixed_rows(v_pad, v_taps, EDGE, 0, 1, c).astype(BF16)

            def scale(h, c):
                top = h * (DK + DV)
                v_wide = mixed[c][:, h * DV : (h + 1) * DV].T.astype(F32)
                y_scr[c, top : top + DK, :] = (turned[c].astype(F32) * both_gains[h : h + 1, span(c)]).astype(BF16)
                y_scr[c, top + DK : top + DK + DV, :] = (v_wide * gain[h : h + 1, span(c)]).astype(BF16)

            for c in some:
                ops.append(functools.partial(start, c))
            for h, c in local:
                ops.append(functools.partial(mask, h, c))
            for j in range(TINY - 1, 0, -1):
                for h, c in local:
                    ops.append(functools.partial(eliminate, j, h * chunks + c))
            for h, c in local:
                ops.append(functools.partial(place, h * chunks + c))
            right = []
            for c in some:
                right.append(functools.partial(convolve, c))
                right += [functools.partial(scale, h, c) for h in range(group)]
            return ops, right

        def back(some):
            ops, own, moved = [], {}, {}
            local = [(h, c) for c in some for h in range(group)]

            def reach(size, r):
                half_lane = lax.broadcasted_iota(jnp.int32, (BLOCK // 2, BLOCK), 1)
                half_row = lax.broadcasted_iota(jnp.int32, (BLOCK // 2, BLOCK), 0)
                partner = half_lane // size == 2 * (half_row // size) + 1
                own[r] = jnp.concatenate([x_scr[r, s : s + size, :] for s in range(0, BLOCK, 2 * size)], axis=0)
                moved[r] = jnp.where(partner, dot(own[r], a_scr[r]), 0.0).astype(BF16)

            def join(size, r):
                update = own[r] + dot(moved[r], x_scr[r]).astype(BF16)
                for n, s in enumerate(range(0, BLOCK, 2 * size)):
                    x_scr[r, s : s + size, :] = update[n * size : (n + 1) * size]

            def solve(h, c):
                r = h * chunks + c
                top = h * (DK + DV)
                sums = cum[:, span(c)]
                last = sums[:, BLOCK - 1 : BLOCK]
                tail = jnp.exp(last - sums)
                fade = jnp.broadcast_to(jnp.exp(last), (group, BLOCK))
                rows = dot(y_scr[c, top : top + DK + DV, :], x_scr[r])
                wu_ref[0, r] = rows.astype(BF16)
                y_scr[c, top : top + DK + DV, :] = (rows * tail[h : h + 1]).astype(BF16)
                fade_scr[slot, c, h : h + 1, :] = fade[h : h + 1]

            def finish(c):
                both = dot(y_scr[c], keys[c])
                for h in range(group):
                    top = h * (DK + DV)
                    m_scr[slot, c, h] = (-both[top : top + DK]).astype(BF16)
                    b_scr[slot, c, h] = both[top + DK : top + DK + DV]

            size = TINY
            while size < BLOCK:
                ops += [functools.partial(reach, size, h * chunks + c) for h, c in local]
                ops += [functools.partial(join, size, h * chunks + c) for h, c in local]
                size *= 2
            ops += [functools.partial(solve, h, c) for h, c in local]
            ops += [functools.partial(finish, c) for c in some]
            return ops

        half = chunks // 2
        early, late = range(half), range(half, chunks)
        early_front, early_right = front(early)
        late_front, late_right = front(late)
        cut = len(recurrence) // 3
        weave(early_front, recurrence[:cut], early_right)
        weave(back(early), late_front, late_right)
        weave(back(late), recurrence[cut:])


def prepare(job, lengths, qk_rows, v_in, halo, qk_taps, v_taps, log_decay, write_gain, key_heads, mixed, after):
    head, first, count = job
    tok = v_in.shape[1]
    value_heads = v_in.shape[2] // DV
    group = value_heads // key_heads
    chunks = tok // BLOCK
    rows = group * chunks
    wide = group * DV
    mixes = mixed is None

    def now(i):
        return jnp.minimum(i, count - 1)

    def before(i):
        return jnp.maximum(i - 1, 0)

    def whole_of(i, lengths):
        return (first + now(i), 0, 0)

    operands = [far(v_in), halo, far(v_taps), far(log_decay), far(write_gain), far(after)]
    in_specs = [
        pl.BlockSpec((1, tok, wide), lambda i, lengths: (first + now(i), 0, head)),
        pl.BlockSpec((1,) + halo.shape[1:], whole_of),
        pl.BlockSpec((CONV, wide), lambda i, lengths: (0, head)),
        pl.BlockSpec((1, value_heads, tok), whole_of),
        pl.BlockSpec((1, value_heads, tok), whole_of),
        pl.BlockSpec(memory_space=pltpu.HBM),
    ]
    out_specs = [
        pl.BlockSpec((1, rows, DK + DV, BLOCK), lambda i, lengths: (now(i), 0, 0, 0)),
        pl.BlockSpec((1, group, chunks * (DV + DK), DK), lambda i, lengths: (before(i), 0, 0, 0)),
        pl.BlockSpec((group, DV + DK, DK), lambda i, lengths: (before(i), 0, 0)),
    ]
    out_shape = [
        pltpu.HBM((count, rows, DK + DV, BLOCK), BF16),
        pltpu.HBM((count, group, chunks * (DV + DK), DK), BF16),
        jax.ShapeDtypeStruct((count * group, DV + DK, DK), BF16),
    ]
    scratch = [
        pltpu.VMEM((tok + EDGE, wide), F32),
        pltpu.VMEM((2, chunks, group, DK, DK), BF16),
        pltpu.VMEM((2, chunks, group, DV, DK), F32),
        pltpu.VMEM((2, chunks, group, BLOCK), F32),
        pltpu.VMEM((group, DV + DK, DK), F32),
        pltpu.VMEM((rows, BLOCK, BLOCK), BF16),
        pltpu.VMEM((rows, BLOCK, BLOCK), BF16),
        pltpu.VMEM((chunks, group * (DK + DV), BLOCK), BF16),
    ]
    if mixes:
        operands += [far(qk_rows), far(qk_taps)]
        in_specs += [
            pl.BlockSpec((1,) + qk_rows.shape[1:], whole_of),
            pl.BlockSpec(qk_taps.shape, lambda i, lengths: (0, 0)),
        ]
        out_specs += [pl.BlockSpec((1, tok, key_heads * DK), lambda i, lengths: (now(i), 0, 0))] * 2
        out_shape += [pltpu.HBM((count, tok, key_heads * DK), BF16)] * 2
        scratch.append(pltpu.VMEM((qk_rows.shape[1] + 2 * EDGE, DK), F32))
    else:
        operands.append(far(mixed))
        in_specs.append(pl.BlockSpec((1, tok, DK), lambda i, lengths: (first + now(i), 0, head)))
    return pl.pallas_call(
        functools.partial(prepare_kernel, first, count, head, group, chunks, key_heads, mixes),
        grid_spec=pltpu.PrefetchScalarGridSpec(
            num_scalar_prefetch=1,
            grid=(count + 1,),
            in_specs=in_specs,
            out_specs=out_specs,
            scratch_shapes=scratch,
        ),
        out_shape=out_shape,
        compiler_params=pltpu.CompilerParams(vmem_limit_bytes=VMEM_BYTES),
        cost_estimate=pl.CostEstimate(flops=5 * 10**9 * count, bytes_accessed=4 * 2**20 * count, transcendentals=10**6),
        name="prepare",
    )(lengths, *operands)


def outputs_kernel(
    first, head, group, chunks,
    length_ref, qn_ref, kn_ref, wu_ref, start_ref, log_ref, gain_ref, enter_ref, z_ref, norm_ref, held_ref, after_ref,
    out_ref,
    first_scr, score_scr, seen_scr,
):
    used = length_ref[first + pl.program_id(0)] - lax.axis_index("seq") * (chunks * BLOCK)
    units = [(h, c) for c in range(chunks) for h in range(group)]

    @pl.when(used <= 0)
    def _():
        out_ref[...] = jnp.zeros_like(out_ref)

    @pl.when(used > 0)
    def _():
        cum, gain = gates_of_heads(log_ref, gain_ref, used, head, group)
        faded = jnp.exp(cum)
        columns = as_columns(jnp.concatenate([cum] * (8 // group), axis=0), chunks)
        row = lax.broadcasted_iota(jnp.int32, (BLOCK, BLOCK), 0)
        lane = lax.broadcasted_iota(jnp.int32, (BLOCK, BLOCK), 1)
        upto = row <= lane
        norm_gain = norm_ref[...]

        def span(c):
            return slice(c * BLOCK, (c + 1) * BLOCK)

        for c in range(chunks):
            turned = qn_ref[0, span(c), :].T
            kq = dot(kn_ref[0, span(c), :], turned)
            q_wide = turned.astype(F32)
            for h in range(group):
                r = h * chunks + c
                ratio = jnp.exp(cum[h : h + 1, span(c)] - columns[:, c * 8 + h : c * 8 + h + 1])
                score_scr[r] = jnp.where(upto, ratio * kq, 0.0).astype(BF16)
                seen_scr[r] = q_wide * faded[h : h + 1, span(c)]
                top = c * (DV + DK)
                moved = dot(enter_ref[h], start_ref[0, h, top + DV : top + DV + DK, :])
                first_scr[r] = (moved + start_ref[0, h, top : top + DV, :].astype(F32)).astype(BF16)
        both, raws = {}, {}
        for h, c in units:
            r = h * chunks + c
            both[r] = dot(wu_ref[0, r], score_scr[r])
        for h, c in units:
            r = h * chunks + c
            seen = (seen_scr[r] - both[r][:DK]).astype(BF16)
            raw = dot(first_scr[r], seen) + both[r][DK:]
            mean = jnp.sum(raw * raw, axis=0, keepdims=True) * (1.0 / DV)
            raws[r] = (raw * lax.rsqrt(mean + EPSILON)).astype(BF16)
        for h, c in units:
            scaled = raws[h * chunks + c].T.astype(F32)
            cols = slice(h * DV, (h + 1) * DV)
            gated = scaled * norm_gain * silu(z_ref[0, span(c), cols].astype(F32))
            out_ref[0, span(c), cols] = jnp.where(row + c * BLOCK < used, gated, 0.0).astype(BF16)


def outputs(
    job, piece, lengths, qn, kn, wu, starts, log_decay, write_gain, enter, gate_z, norm_gain, key_heads, held, after,
):
    head, first, _ = job
    begin, count = piece
    prompts, tok, width = gate_z.shape
    rows = wu.shape[1]
    chunks = tok // BLOCK
    group = rows // chunks
    wide = group * DV
    value_heads = key_heads * group
    shift = begin - first
    from_mix = begin if qn.shape[0] == prompts else shift

    def whole_of(i, lengths):
        return (begin + i, 0, 0)

    def wide_of(i, lengths):
        return (begin + i, 0, head)

    def mixed_of(i, lengths):
        return (from_mix + i, 0, head)

    empty = held is None
    return pl.pallas_call(
        functools.partial(outputs_kernel, begin, head, group, chunks),
        grid_spec=pltpu.PrefetchScalarGridSpec(
            num_scalar_prefetch=1,
            grid=(count,),
            in_specs=[
                pl.BlockSpec((1, tok, DK), mixed_of),
                pl.BlockSpec((1, tok, DK), mixed_of),
                pl.BlockSpec((1, rows, DK + DV, BLOCK), lambda i, lengths: (shift + i, 0, 0, 0)),
                pl.BlockSpec((1, group, chunks * (DV + DK), DK), lambda i, lengths: (shift + i, 0, 0, 0)),
                pl.BlockSpec((1, value_heads, tok), whole_of),
                pl.BlockSpec((1, value_heads, tok), whole_of),
                pl.BlockSpec((group, DK, DV), lambda i, lengths: (shift + i, 0, 0)),
                pl.BlockSpec((1, tok, wide), wide_of),
                pl.BlockSpec((1, DV), lambda i, lengths: (0, 0)),
                pl.BlockSpec(memory_space=pltpu.HBM),
                pl.BlockSpec(memory_space=pltpu.HBM),
            ],
            out_specs=pl.BlockSpec((1, tok, wide), wide_of),
            scratch_shapes=[
                pltpu.VMEM((rows, DV, DK), BF16),
                pltpu.VMEM((rows, BLOCK, BLOCK), BF16),
                pltpu.VMEM((rows, BLOCK, DV), F32),
            ],
        ),
        out_shape=pltpu.HBM((prompts, tok, width), BF16),
        input_output_aliases={} if empty else {10: 0},
        compiler_params=pltpu.CompilerParams(vmem_limit_bytes=VMEM_BYTES),
        cost_estimate=pl.CostEstimate(flops=3 * 10**9 * count, bytes_accessed=4 * 2**20 * count, transcendentals=10**6),
        name="outputs",
    )(
        lengths, far(qn), far(kn), far(wu), far(starts), far(log_decay), far(write_gain), enter, far(gate_z),
        far(norm_gain.reshape(1, DV)), far(after if empty else held), far(wu if after is held else after),
    )


def own_chip():
    seq = lax.axis_index("seq")
    return seq // 2, seq % 2 == 1


def early_late(own, other, odd):
    return jnp.where(odd, other, own), jnp.where(odd, own, other)


def follow(there, running):
    return dot(running, there[DV:])


def compose_maps(ins, outs):
    own_ref, other_ref = ins
    _, odd = own_chip()
    for n in range(own_ref.shape[0]):
        early, late = early_late(own_ref[n], other_ref[n], odd)
        both = follow(late, early)
        outs[0][n, :DV] = (both[:DV] + late[:DV].astype(F32)).astype(BF16)
        outs[0][n, DV:] = both[DV:].astype(BF16)


def close_maps(ins, outs):
    own_ref, other_ref = ins[:2]
    refs = ins[2:]
    chips = len(refs)
    chip, odd = own_chip()

    def of_chip(j, n):
        value = refs[0][n]
        for k in range(1, chips):
            value = jnp.where((chip + chips - k) % chips == j, refs[k][n], value)
        return value

    every = range(own_ref.shape[0])
    running = [of_chip(0, n)[:DV] for n in every]
    entering = [jnp.zeros_like(running[n]) for n in every]
    for j in range(1, chips):
        entering = [jnp.where(chip == j, running[n], entering[n]) for n in every]
        there = [of_chip(j, n) for n in every]
        running = [(follow(there[n], running[n]) + there[n][:DV].astype(F32)).astype(BF16) for n in every]
    for n in every:
        early, _ = early_late(own_ref[n], other_ref[n], odd)
        second = (follow(early, entering[n]) + early[:DV].astype(F32)).astype(BF16)
        outs[0][n] = jnp.where(odd, second, entering[n])
        outs[1][n] = running[n].T


def chain_maps(ins, outs):
    count = len(ins)
    mine = lax.axis_index("seq")
    every = range(ins[0].shape[0])

    def run(at):
        running = [ins[at][n, :DV] for n in every]
        for n in every:
            if at == 0:
                outs[0][n] = jnp.zeros_like(running[n])
        for j in range(1, count):
            there = ins[at ^ j]
            if j == at:
                for n in every:
                    outs[0][n] = running[n]
            moved = [follow(there.at[n], running[n]) for n in every]
            running = [(moved[n] + there[n, :DV].astype(F32)).astype(BF16) for n in every]
        for n in every:
            outs[1][n] = running[n].T

    for at in range(count):
        pl.when(mine == at)(functools.partial(run, at))


def choose_finals(group, placement_ref, finals, outs):
    refs = [(ref, n) for ref in finals for n in range(ref.shape[0] // group)]
    for r in range(placement_ref.shape[1]):
        prompt = placement_ref[0, r]
        for p, (ref, n) in enumerate(refs):
            @pl.when(prompt == p)
            def _(ref=ref, n=n):
                outs[0][r] = ref[n * group : (n + 1) * group]


def state_step(placement, group, compose, chain, close, earlier, after):
    operands, shapes = [placement], []
    steps = []
    if compose is not None:
        steps.append(("compose", len(operands), len(compose), len(shapes)))
        operands += compose
        shapes += [compose[0]]
    if chain is not None or close is not None:
        steps.append(("chain" if close is None else "close", len(operands), len(close or chain), len(shapes)))
        close = close or chain
        operands += close
        shapes += [jax.ShapeDtypeStruct((close[0].shape[0], DK, DV), BF16)] * 2
        if earlier is not None:
            steps.append(("choose", len(operands), len(earlier), len(shapes)))
            operands += earlier
            shapes.append(jax.ShapeDtypeStruct((placement.shape[1], group, DK, DV), BF16))
    out_shape = [jax.ShapeDtypeStruct(x.shape, x.dtype) for x in shapes] + [pltpu.HBM((8, 128), F32)]

    def kernel(*refs):
        refs[-1][...] = jnp.zeros_like(refs[-1])
        ins, outs = refs[: len(operands)], refs[len(operands) + 1 :]
        closed = None
        for kind, at, size, to in steps:
            part = ins[at : at + size]
            if kind == "compose":
                compose_maps(part, outs[to : to + 1])
            elif kind in ("close", "chain"):
                (close_maps if kind == "close" else chain_maps)(part, outs[to : to + 2])
                closed = outs[to + 1]
            else:
                choose_finals(group, ins[0], list(part) + [closed], outs[to:])

    vmem = pl.BlockSpec(memory_space=pltpu.VMEM)
    return pl.pallas_call(
        kernel,
        in_specs=[pl.BlockSpec(memory_space=pltpu.SMEM)]
        + [vmem] * (len(operands) - 1)
        + [pl.BlockSpec(memory_space=pltpu.HBM)],
        out_specs=[vmem] * len(out_shape),
        out_shape=out_shape,
        compiler_params=pltpu.CompilerParams(vmem_limit_bytes=SMALL_VMEM_BYTES),
        cost_estimate=pl.CostEstimate(flops=10**9, bytes_accessed=2**20, transcendentals=0),
        name="state_step",
    )(*operands, far(after))


def deliver(parts):
    count, group = parts[0].shape[:2]

    def kernel(*refs):
        for n, ref in enumerate(refs[:-1]):
            refs[-1][:, n * group : (n + 1) * group] = ref[...].astype(F32)

    return pl.pallas_call(
        kernel,
        grid=(2,),
        in_specs=[pl.BlockSpec((count // 2, group, DK, DV), lambda i: (i, 0, 0, 0))] * len(parts),
        out_specs=pl.BlockSpec((count // 2, group * len(parts), DK, DV), lambda i: (i, 0, 0, 0)),
        out_shape=jax.ShapeDtypeStruct((count, group * len(parts), DK, DV), F32),
        compiler_params=pltpu.CompilerParams(vmem_limit_bytes=VMEM_BYTES),
        name="deliver",
    )(*parts)


def across(block, distance):
    count = lax.axis_size("seq")
    return lax.ppermute(block, "seq", [(i, i ^ distance) for i in range(count)])


def from_chip_behind(block, distance):
    count = lax.axis_size("seq")
    chips = count // 2
    route = [(i, ((i // 2 + distance) % chips) * 2 + i % 2) for i in range(count)]
    return lax.ppermute(block, "seq", route)


def shards(
    qk_in, v_in, gate_z, conv_qk, conv_v, log_decay, write_gain, norm_gain, prompt_lengths, placement,
):
    prompts, tok = qk_in.shape[:2]
    key_heads = qk_in.shape[3] // DK
    value_heads = v_in.shape[2] // DV
    rim = CONV - 1
    seq_count = lax.axis_size("seq")
    head_count = lax.axis_size("head")

    def by_head(x):
        x = x.reshape(x.shape[0], x.shape[1], 2, key_heads, DK)
        return jnp.transpose(x, (0, 1, 3, 2, 4)).reshape(x.shape[0], -1, DK)

    qk_rows = by_head(qk_in)
    qk_taps = by_head(conv_qk[None])[0]
    qk_tail = qk_rows[:, (tok - rim) * 2 * key_heads :]
    v_tail = v_in[:, tok - rim :].reshape(prompts, rim * value_heads, DV)
    front = 2 * EDGE - qk_tail.shape[1]
    back = 2 * EDGE - v_tail.shape[1]
    tails = jnp.concatenate(
        [
            jnp.zeros((prompts, front, DK), BF16),
            qk_tail,
            v_tail,
            jnp.zeros((prompts, back, DK), BF16),
        ],
        axis=1,
    )
    halo = lax.ppermute(tails, "seq", [(i, i + 1) for i in range(seq_count - 1)])
    group = value_heads // key_heads
    chips = seq_count // 2
    half = prompts // 2
    jobs = [(head, 0, prompts) for head in range(key_heads)]
    if key_heads == 1:
        jobs = [(0, 0, half), (0, half, prompts - half)]
    total = len(jobs)
    made, finals, sent = [], [], {}
    attended = None
    last = v_in

    def finish(job, results):
        head = jobs[job][0]
        finals.append(results[1])
        if len(results) > 3:
            sent[head] = lax.all_to_all(results[2], "head", 0, 0)
        return results[0], results[-1]

    def earlier(job):
        same = [n for n in range(total) if jobs[n][0] == jobs[job][0]]
        return [finals[n] for n in same[:-1]] if job == same[-1] else None

    def emit(job, entered, attended, last):
        qn, kn, wu, starts, _ = made[job]
        return outputs(
            jobs[job], jobs[job][1:], prompt_lengths, qn, kn, wu, starts, log_decay, write_gain,
            entered, gate_z, norm_gain, key_heads, attended, last,
        )

    for job in jobs:
        mixed = None if job[0] == 0 else made[0][:2]
        wu, starts, own_map, *new = prepare(
            job, prompt_lengths, qk_rows, v_in, halo, qk_taps, conv_v, log_decay, write_gain, key_heads,
            mixed and mixed[1], last,
        )
        last = wu
        moved = [own_map]
        if job == jobs[-1]:
            moved.append(across(own_map, 1))
        else:
            moved += [across(own_map, k) for k in range(1, seq_count)]
        made.append((*(mixed or new), wu, starts, moved))

    entered = []
    for job in range(total - 1):
        results = state_step(placement, group, None, made[job][4], None, earlier(job), last)
        enter, last = finish(job, results)
        entered.append(enter)
    pair = made[-1][4]
    chip_map, last = state_step(placement, group, pair, None, None, None, last)
    chip_maps = [chip_map] + [from_chip_behind(chip_map, k) for k in range(1, chips)]
    for job in range(total - 1):
        attended = last = emit(job, entered[job], attended, last)
    results = state_step(placement, group, None, None, pair + chip_maps, earlier(total - 1), last)
    enter, last = finish(total - 1, results)
    attended = emit(total - 1, enter, attended, last)
    rollout = deliver([sent[head] for head in range(key_heads)])
    return attended, rollout.reshape(1, 1, head_count * value_heads, DK, DV)


def solution(mesh):
    return jax.shard_map(
        shards,
        mesh=mesh,
        in_specs=(
            P(None, "seq", None, "head"),
            P(None, "seq", "head"),
            P(None, "seq", "head"),
            P(None, None, "head"),
            P(None, "head"),
            P(None, "head", "seq"),
            P(None, "head", "seq"),
            P(),
            P(),
            P("seq", None),
        ),
        out_specs=(P(None, "seq", "head"), P("seq", "head", None, None, None)),
        check_vma=False,
    )
```

```python
import functools

import jax
import jax.numpy as jnp
from jax import lax
from jax.experimental import pallas as pl
from jax.experimental.pallas import tpu as pltpu
from jax.sharding import PartitionSpec as P

DK = 128
DV = 128
CONV = 4
BLOCK = 128
TINY = 16
ROWS = 8
STRIDE = 4
EDGE = 8
EPSILON = 1e-06
VMEM_BYTES = 40 * 1024 * 1024
SMALL_VMEM_BYTES = 8 * 1024 * 1024
F32 = jnp.float32
BF16 = jnp.bfloat16


def far(x):
    return pltpu.with_memory_space_constraint(x, pltpu.HBM)


def dot(a, b):
    return lax.dot_general(a, b, (((1,), (0,)), ((), ())), preferred_element_type=F32)


def silu(x):
    half = 0.5 * x
    return half + half * jnp.tanh(half)


def mixed_rows(pad_ref, taps, rim, first, step, c):
    total = None
    for i in range(CONV):
        start = rim + first + step * (c * BLOCK + i - (CONV - 1))
        stride = None if step == 1 else step
        term = pad_ref[pl.ds(start, BLOCK, stride), :] * taps[i]
        total = term if total is None else total + term
    return silu(total)


def unit_rows(x):
    return x * lax.rsqrt(jnp.sum(x * x, axis=-1, keepdims=True) + EPSILON)


def heads_rows(ref, head, group):
    every = ref[0]
    rows = every[:group]
    for n in range(1, every.shape[0] // group):
        rows = jnp.where(head == n, every[n * group : (n + 1) * group], rows)
    return rows


def gates_of_heads(log_ref, gain_ref, used, head, group):
    log = heads_rows(log_ref, head, group)
    lane = lax.broadcasted_iota(jnp.int32, log.shape, 1)
    valid = lane < used
    cum = jnp.where(valid, log, 0.0)
    gain = jnp.where(valid, heads_rows(gain_ref, head, group), 0.0)
    shift = 1
    while shift < BLOCK:
        cum = cum + jnp.where(lane % BLOCK >= shift, pltpu.roll(cum, shift, 1), 0.0)
        shift *= 2
    return cum, gain


def as_columns(rows, chunks):
    parts = [rows[:, c * BLOCK : (c + 1) * BLOCK] for c in range(chunks)]
    short = BLOCK - 8 * chunks
    if short:
        parts.append(jnp.zeros((short, BLOCK), F32))
    return jnp.concatenate(parts, axis=0).T


def block_bases(parts, chunks):
    rows = jnp.concatenate(parts, axis=0)
    short = 7 - rows.shape[0]
    fill = [jnp.zeros((short, rows.shape[1]), F32)] if short else []
    rows = jnp.concatenate([rows] + fill + [jnp.ones((1, rows.shape[1]), F32)], axis=0)
    return [rows[:, c * BLOCK : (c + 1) * BLOCK] for c in range(chunks)]


def spread_squares(base, group, kinds):
    high = base.astype(BF16).astype(F32)
    middle = (base - high).astype(BF16).astype(F32)
    low = base - high - middle
    parts = [high, middle, low]
    row = lax.broadcasted_iota(jnp.int32, (32, BLOCK), 0)
    which = row % 8
    real = row < 24
    stacked = jnp.concatenate(parts + [jnp.zeros_like(high)], axis=0)
    left = jnp.where(jnp.logical_and(which == 7, real), 1.0, stacked).T.astype(BF16)
    blocks = []
    for h in range(group):
        minus = jnp.concatenate([jnp.broadcast_to(-part[h : h + 1], (8, BLOCK)) for part in parts + [low]], axis=0)
        blocks.append(jnp.where(which == h, 1.0, jnp.where(which == 7, minus, 0.0)))
    for n in range(group, group * kinds):
        blocks.append(jnp.where(which == n, 1.0, 0.0).astype(F32))
    every = dot(left, jnp.concatenate(blocks, axis=1).astype(BF16))
    return [every[:, n * BLOCK : (n + 1) * BLOCK] for n in range(group * kinds)]


def mix(qk_ref, halo_ref, taps_ref, qn_ref, kn_ref, raw_scr, key_heads, chunks):
    kinds = 2 * key_heads
    rim = 2 * EDGE
    taps = taps_ref[...].astype(F32)
    raw_scr[:rim] = halo_ref[0].astype(F32)[:rim]
    raw_scr[rim:] = qk_ref[0].astype(F32)
    for c in range(chunks):
        span = slice(c * BLOCK, (c + 1) * BLOCK)
        for kind in range(kinds):
            own = [taps[n : n + 1] for n in range(kind, taps.shape[0], kinds)]
            rows = unit_rows(mixed_rows(raw_scr, own, rim, kind, kinds, c))
            to_ref = kn_ref if kind % 2 else qn_ref
            to_ref[0, span, kind // 2 * DK : (kind // 2 + 1) * DK] = rows.astype(BF16)


def one_row(tiles, j):
    tile = tiles[j // ROWS]
    return jnp.broadcast_to(tile[j % ROWS : j % ROWS + 1], tile.shape)


def weave(*lists):
    places = []
    for which, entries in enumerate(lists):
        places += [((n + 0.5) / len(entries), which, n) for n in range(len(entries))]
    for _, which, n in sorted(places):
        lists[which][n]()


def prepare_kernel(first, count, head, group, chunks, key_heads, mixes, *refs):
    length_ref, v_ref, halo_ref, v_taps_ref, log_ref, gain_ref, after_ref = refs[:7]
    refs = refs[7:]
    if mixes:
        qk_ref, qk_taps_ref, wu_ref, start_ref, map_ref, qn_ref, kn_ref = refs[:7]
        v_pad, m_scr, b_scr, fade_scr, st_scr, a_scr, x_scr, y_scr, raw_scr = refs[7:]
        key_columns = slice(head * DK, (head + 1) * DK)
    else:
        kn_ref, wu_ref, start_ref, map_ref = refs[:4]
        v_pad, m_scr, b_scr, fade_scr, st_scr, a_scr, x_scr, y_scr = refs[4:]
        key_columns = slice(0, DK)
    step = pl.program_id(0)
    used = length_ref[first + jnp.minimum(step, count - 1)] - lax.axis_index("seq") * (chunks * BLOCK)
    units = [(h, c) for c in range(chunks) for h in range(group)]
    slot = step % 2
    live = jnp.logical_and(step < count, used > 0)

    def begin():
        row = lax.broadcasted_iota(jnp.int32, (DV + DK, DK), 0)
        lane = lax.broadcasted_iota(jnp.int32, (DV + DK, DK), 1)
        for h in range(group):
            st_scr[h] = jnp.where(row == lane + DV, 1.0, 0.0).astype(F32)

    def advance(c):
        narrow, moved = {}, {}

        def load(h):
            narrow[h] = st_scr[h].astype(BF16)
            start_ref[0, h, c * (DV + DK) : (c + 1) * (DV + DK), :] = narrow[h]

        def move(h):
            moved[h] = dot(narrow[h], m_scr[1 - slot, c, h])

        def store(h):
            fade = fade_scr[1 - slot, c, h : h + 1, :]
            state = st_scr[h, :DV] * fade + (moved[h][:DV] + b_scr[1 - slot, c, h])
            trans = st_scr[h, DV:] * fade + moved[h][DV:]
            if c < chunks - 1:
                st_scr[h, :DV] = state
                st_scr[h, DV:] = trans
            else:
                map_ref[h, :DV] = state.astype(BF16)
                map_ref[h, DV:] = trans.astype(BF16)

        return [functools.partial(act, h) for act in (load, move, store) for h in range(group)]

    recurrence = [begin]
    for c in range(chunks):
        recurrence += advance(c)

    @pl.when(jnp.logical_not(live))
    def _():
        @pl.when(step > 0)
        def _():
            weave(recurrence)

        @pl.when(step < count)
        def _():
            if mixes:
                qn_ref[...] = jnp.zeros_like(qn_ref)
                kn_ref[...] = jnp.zeros_like(kn_ref)
            wu_ref[...] = jnp.zeros_like(wu_ref)
            fade_scr[slot] = jnp.ones(fade_scr.shape[1:], F32)
            m_scr[slot] = jnp.zeros(m_scr.shape[1:], BF16)
            b_scr[slot] = jnp.zeros(b_scr.shape[1:], F32)

    @pl.when(live)
    def _():
        if mixes:
            mix(qk_ref, halo_ref, qk_taps_ref, qn_ref, kn_ref, raw_scr, key_heads, chunks)
        halo = halo_ref[0].astype(F32)
        v_pad[EDGE:, :] = v_ref[0].astype(F32)
        for i in range(CONV - 1):
            for h in range(group):
                source = 2 * EDGE + (i * key_heads + head) * group + h
                v_pad[EDGE - CONV + 1 + i : EDGE - CONV + 2 + i, h * DV : (h + 1) * DV] = halo[
                    source : source + 1
                ]
        v_all_taps = v_taps_ref[...].astype(F32)
        v_taps = [v_all_taps[i : i + 1] for i in range(CONV)]

        cum, gain = gates_of_heads(log_ref, gain_ref, used, head, group)
        both_gains = gain * jnp.exp(cum)
        columns = as_columns(jnp.concatenate([cum] * (8 // group), axis=0), chunks)

        def span(c):
            return slice(c * BLOCK, (c + 1) * BLOCK)

        row = lax.broadcasted_iota(jnp.int32, (BLOCK, BLOCK), 0)
        lane = lax.broadcasted_iota(jnp.int32, (BLOCK, BLOCK), 1)
        above = row < lane
        small_row = lax.broadcasted_iota(jnp.int32, (TINY, BLOCK), 0)
        small_lane = lax.broadcasted_iota(jnp.int32, (TINY, BLOCK), 1)
        part_of = small_lane // TINY
        lane_part = part_of[:ROWS]
        tiny_eye = jnp.where(small_row == small_lane % TINY, 1.0, 0.0).astype(F32)

        keys = [kn_ref[0, span(c), key_columns] for c in range(chunks)]
        turned = {}

        def front(some):
            ops, kk, compact, solved, mixed = [], {}, {}, {}, {}
            local = [(h, c) for c in some for h in range(group)]

            def start(c):
                turned[c] = keys[c].T
                kk[c] = dot(keys[c], turned[c])

            def mask(h, c):
                r = h * chunks + c
                ratio = jnp.exp(cum[h : h + 1, span(c)] - columns[:, c * 8 + h : c * 8 + h + 1])
                strict = jnp.where(above, ratio * kk[c] * -gain[h : h + 1, span(c)], 0.0)
                a_scr[r] = strict.astype(BF16)
                tiny = strict[0:TINY]
                for b in range(1, BLOCK // TINY):
                    tiny = jnp.where(part_of == b, strict[b * TINY : (b + 1) * TINY], tiny)
                compact[r] = [tiny[t : t + ROWS] for t in range(0, TINY, ROWS)]
                solved[r] = [tiny_eye[t : t + ROWS] for t in range(0, TINY, ROWS)]

            def eliminate(last, r):
                group_rows = range(last, max(last - STRIDE, 0), -1)
                factor, taken = {}, {}
                for j in group_rows:
                    pick = lane_part * TINY + j
                    factor[j] = [
                        jnp.take_along_axis(tile, pick, axis=1, mode="promise_in_bounds")
                        for tile in compact[r][: j // ROWS + 1]
                    ]
                    taken[j] = one_row(solved[r], j)
                for j in group_rows:
                    for i in range(last, j, -1):
                        taken[j] = taken[j] + one_row(factor[i], j) * taken[i]
                for j in group_rows:
                    for t, tile in enumerate(factor[j]):
                        solved[r][t] = solved[r][t] + tile * taken[j]

            def place(r):
                whole = jnp.concatenate(solved[r], axis=0)
                for b in range(BLOCK // TINY):
                    x_scr[r, b * TINY : (b + 1) * TINY, :] = jnp.where(part_of == b, whole, 0.0).astype(BF16)

            def convolve(c):
                mixed[c] = mixed_rows(v_pad, v_taps, EDGE, 0, 1, c).astype(BF16)

            def scale(h, c):
                top = h * (DK + DV)
                v_wide = mixed[c][:, h * DV : (h + 1) * DV].T.astype(F32)
                y_scr[c, top : top + DK, :] = (turned[c].astype(F32) * both_gains[h : h + 1, span(c)]).astype(BF16)
                y_scr[c, top + DK : top + DK + DV, :] = (v_wide * gain[h : h + 1, span(c)]).astype(BF16)

            for c in some:
                ops.append(functools.partial(start, c))
            for h, c in local:
                ops.append(functools.partial(mask, h, c))
            for last in range(TINY - 1, 0, -STRIDE):
                for h, c in local:
                    ops.append(functools.partial(eliminate, last, h * chunks + c))
            for h, c in local:
                ops.append(functools.partial(place, h * chunks + c))
            right = []
            for c in some:
                right.append(functools.partial(convolve, c))
                right += [functools.partial(scale, h, c) for h in range(group)]
            return ops, right

        def back(some):
            ops, own, moved = [], {}, {}
            local = [(h, c) for c in some for h in range(group)]

            def reach(size, r):
                half_lane = lax.broadcasted_iota(jnp.int32, (BLOCK // 2, BLOCK), 1)
                half_row = lax.broadcasted_iota(jnp.int32, (BLOCK // 2, BLOCK), 0)
                partner = half_lane // size == 2 * (half_row // size) + 1
                own[r] = jnp.concatenate([x_scr[r, s : s + size, :] for s in range(0, BLOCK, 2 * size)], axis=0)
                moved[r] = jnp.where(partner, dot(own[r], a_scr[r]), 0.0).astype(BF16)

            def join(size, r):
                update = own[r] + dot(moved[r], x_scr[r]).astype(BF16)
                for n, s in enumerate(range(0, BLOCK, 2 * size)):
                    x_scr[r, s : s + size, :] = update[n * size : (n + 1) * size]

            def solve(h, c):
                r = h * chunks + c
                top = h * (DK + DV)
                sums = cum[:, span(c)]
                last = sums[:, BLOCK - 1 : BLOCK]
                tail = jnp.exp(last - sums)
                fade = jnp.broadcast_to(jnp.exp(last), (group, BLOCK))
                rows = dot(y_scr[c, top : top + DK + DV, :], x_scr[r])
                wu_ref[0, r] = rows.astype(BF16)
                y_scr[c, top : top + DK + DV, :] = (rows * tail[h : h + 1]).astype(BF16)
                fade_scr[slot, c, h : h + 1, :] = fade[h : h + 1]

            def finish(c):
                both = dot(y_scr[c], keys[c])
                for h in range(group):
                    top = h * (DK + DV)
                    m_scr[slot, c, h] = (-both[top : top + DK]).astype(BF16)
                    b_scr[slot, c, h] = both[top + DK : top + DK + DV]

            size = TINY
            while size < BLOCK:
                ops += [functools.partial(reach, size, h * chunks + c) for h, c in local]
                ops += [functools.partial(join, size, h * chunks + c) for h, c in local]
                size *= 2
            ops += [functools.partial(solve, h, c) for h, c in local]
            ops += [functools.partial(finish, c) for c in some]
            return ops

        half = chunks // 2
        early, late = range(half), range(half, chunks)
        early_front, early_right = front(early)
        late_front, late_right = front(late)
        cut = len(recurrence) // 3
        weave(early_front, recurrence[:cut], early_right)
        weave(back(early), late_front, late_right)
        weave(back(late), recurrence[cut:])


def prepare(job, lengths, qk_rows, v_in, halo, qk_taps, v_taps, log_decay, write_gain, key_heads, mixed, after):
    head, first, count = job
    tok = v_in.shape[1]
    value_heads = v_in.shape[2] // DV
    group = value_heads // key_heads
    chunks = tok // BLOCK
    rows = group * chunks
    wide = group * DV
    mixes = mixed is None

    def now(i):
        return jnp.minimum(i, count - 1)

    def before(i):
        return jnp.maximum(i - 1, 0)

    def whole_of(i, lengths):
        return (first + now(i), 0, 0)

    operands = [far(v_in), halo, far(v_taps), far(log_decay), far(write_gain), far(after)]
    in_specs = [
        pl.BlockSpec((1, tok, wide), lambda i, lengths: (first + now(i), 0, head)),
        pl.BlockSpec((1,) + halo.shape[1:], whole_of),
        pl.BlockSpec((CONV, wide), lambda i, lengths: (0, head)),
        pl.BlockSpec((1, value_heads, tok), whole_of),
        pl.BlockSpec((1, value_heads, tok), whole_of),
        pl.BlockSpec(memory_space=pltpu.HBM),
    ]
    out_specs = [
        pl.BlockSpec((1, rows, DK + DV, BLOCK), lambda i, lengths: (now(i), 0, 0, 0)),
        pl.BlockSpec((1, group, chunks * (DV + DK), DK), lambda i, lengths: (before(i), 0, 0, 0)),
        pl.BlockSpec((group, DV + DK, DK), lambda i, lengths: (before(i), 0, 0)),
    ]
    out_shape = [
        pltpu.HBM((count, rows, DK + DV, BLOCK), BF16),
        pltpu.HBM((count, group, chunks * (DV + DK), DK), BF16),
        jax.ShapeDtypeStruct((count * group, DV + DK, DK), BF16),
    ]
    scratch = [
        pltpu.VMEM((tok + EDGE, wide), F32),
        pltpu.VMEM((2, chunks, group, DK, DK), BF16),
        pltpu.VMEM((2, chunks, group, DV, DK), F32),
        pltpu.VMEM((2, chunks, group, BLOCK), F32),
        pltpu.VMEM((group, DV + DK, DK), F32),
        pltpu.VMEM((rows, BLOCK, BLOCK), BF16),
        pltpu.VMEM((rows, BLOCK, BLOCK), BF16),
        pltpu.VMEM((chunks, group * (DK + DV), BLOCK), BF16),
    ]
    if mixes:
        operands += [far(qk_rows), far(qk_taps)]
        in_specs += [
            pl.BlockSpec((1,) + qk_rows.shape[1:], whole_of),
            pl.BlockSpec(qk_taps.shape, lambda i, lengths: (0, 0)),
        ]
        out_specs += [pl.BlockSpec((1, tok, key_heads * DK), lambda i, lengths: (now(i), 0, 0))] * 2
        out_shape += [pltpu.HBM((count, tok, key_heads * DK), BF16)] * 2
        scratch.append(pltpu.VMEM((qk_rows.shape[1] + 2 * EDGE, DK), F32))
    else:
        operands.append(far(mixed))
        in_specs.append(pl.BlockSpec((1, tok, DK), lambda i, lengths: (first + now(i), 0, head)))
    return pl.pallas_call(
        functools.partial(prepare_kernel, first, count, head, group, chunks, key_heads, mixes),
        grid_spec=pltpu.PrefetchScalarGridSpec(
            num_scalar_prefetch=1,
            grid=(count + 1,),
            in_specs=in_specs,
            out_specs=out_specs,
            scratch_shapes=scratch,
        ),
        out_shape=out_shape,
        compiler_params=pltpu.CompilerParams(vmem_limit_bytes=VMEM_BYTES),
        cost_estimate=pl.CostEstimate(flops=5 * 10**9 * count, bytes_accessed=4 * 2**20 * count, transcendentals=10**6),
        name="prepare",
    )(lengths, *operands)


def outputs_kernel(
    first, head, group, chunks,
    length_ref, qn_ref, kn_ref, wu_ref, start_ref, log_ref, gain_ref, enter_ref, z_ref, norm_ref, held_ref, after_ref,
    out_ref,
    first_scr, score_scr, seen_scr,
):
    used = length_ref[first + pl.program_id(0)] - lax.axis_index("seq") * (chunks * BLOCK)
    units = [(h, c) for c in range(chunks) for h in range(group)]

    @pl.when(used <= 0)
    def _():
        out_ref[...] = jnp.zeros_like(out_ref)

    @pl.when(used > 0)
    def _():
        cum, gain = gates_of_heads(log_ref, gain_ref, used, head, group)
        faded = jnp.exp(cum)
        columns = as_columns(jnp.concatenate([cum] * (8 // group), axis=0), chunks)
        row = lax.broadcasted_iota(jnp.int32, (BLOCK, BLOCK), 0)
        lane = lax.broadcasted_iota(jnp.int32, (BLOCK, BLOCK), 1)
        upto = row <= lane
        norm_gain = norm_ref[...]

        def span(c):
            return slice(c * BLOCK, (c + 1) * BLOCK)

        for c in range(chunks):
            turned = qn_ref[0, span(c), :].T
            kq = dot(kn_ref[0, span(c), :], turned)
            q_wide = turned.astype(F32)
            for h in range(group):
                r = h * chunks + c
                ratio = jnp.exp(cum[h : h + 1, span(c)] - columns[:, c * 8 + h : c * 8 + h + 1])
                score_scr[r] = jnp.where(upto, ratio * kq, 0.0).astype(BF16)
                seen_scr[r] = q_wide * faded[h : h + 1, span(c)]
                top = c * (DV + DK)
                moved = dot(enter_ref[h], start_ref[0, h, top + DV : top + DV + DK, :])
                first_scr[r] = (moved + start_ref[0, h, top : top + DV, :].astype(F32)).astype(BF16)
        both, raws = {}, {}
        for h, c in units:
            r = h * chunks + c
            both[r] = dot(wu_ref[0, r], score_scr[r])
        for h, c in units:
            r = h * chunks + c
            seen = (seen_scr[r] - both[r][:DK]).astype(BF16)
            raw = dot(first_scr[r], seen) + both[r][DK:]
            mean = jnp.sum(raw * raw, axis=0, keepdims=True) * (1.0 / DV)
            raws[r] = (raw * lax.rsqrt(mean + EPSILON)).astype(BF16)
        for h, c in units:
            scaled = raws[h * chunks + c].T.astype(F32)
            cols = slice(h * DV, (h + 1) * DV)
            gated = scaled * norm_gain * silu(z_ref[0, span(c), cols].astype(F32))
            out_ref[0, span(c), cols] = jnp.where(row + c * BLOCK < used, gated, 0.0).astype(BF16)


def outputs(
    job, piece, lengths, qn, kn, wu, starts, log_decay, write_gain, enter, gate_z, norm_gain, key_heads, held, after,
):
    head, first, _ = job
    begin, count = piece
    prompts, tok, width = gate_z.shape
    rows = wu.shape[1]
    chunks = tok // BLOCK
    group = rows // chunks
    wide = group * DV
    value_heads = key_heads * group
    shift = begin - first
    from_mix = begin if qn.shape[0] == prompts else shift

    def whole_of(i, lengths):
        return (begin + i, 0, 0)

    def wide_of(i, lengths):
        return (begin + i, 0, head)

    def mixed_of(i, lengths):
        return (from_mix + i, 0, head)

    empty = held is None
    return pl.pallas_call(
        functools.partial(outputs_kernel, begin, head, group, chunks),
        grid_spec=pltpu.PrefetchScalarGridSpec(
            num_scalar_prefetch=1,
            grid=(count,),
            in_specs=[
                pl.BlockSpec((1, tok, DK), mixed_of),
                pl.BlockSpec((1, tok, DK), mixed_of),
                pl.BlockSpec((1, rows, DK + DV, BLOCK), lambda i, lengths: (shift + i, 0, 0, 0)),
                pl.BlockSpec((1, group, chunks * (DV + DK), DK), lambda i, lengths: (shift + i, 0, 0, 0)),
                pl.BlockSpec((1, value_heads, tok), whole_of),
                pl.BlockSpec((1, value_heads, tok), whole_of),
                pl.BlockSpec((group, DK, DV), lambda i, lengths: (shift + i, 0, 0)),
                pl.BlockSpec((1, tok, wide), wide_of),
                pl.BlockSpec((1, DV), lambda i, lengths: (0, 0)),
                pl.BlockSpec(memory_space=pltpu.HBM),
                pl.BlockSpec(memory_space=pltpu.HBM),
            ],
            out_specs=pl.BlockSpec((1, tok, wide), wide_of),
            scratch_shapes=[
                pltpu.VMEM((rows, DV, DK), BF16),
                pltpu.VMEM((rows, BLOCK, BLOCK), BF16),
                pltpu.VMEM((rows, BLOCK, DV), F32),
            ],
        ),
        out_shape=pltpu.HBM((prompts, tok, width), BF16),
        input_output_aliases={} if empty else {10: 0},
        compiler_params=pltpu.CompilerParams(vmem_limit_bytes=VMEM_BYTES),
        cost_estimate=pl.CostEstimate(flops=3 * 10**9 * count, bytes_accessed=4 * 2**20 * count, transcendentals=10**6),
        name="outputs",
    )(
        lengths, far(qn), far(kn), far(wu), far(starts), far(log_decay), far(write_gain), enter, far(gate_z),
        far(norm_gain.reshape(1, DV)), far(after if empty else held), far(wu if after is held else after),
    )


def own_chip():
    seq = lax.axis_index("seq")
    return seq // 2, seq % 2 == 1


def early_late(own, other, odd):
    return jnp.where(odd, other, own), jnp.where(odd, own, other)


def follow(there, running):
    return dot(running, there[DV:])


def compose_maps(ins, outs):
    own_ref, other_ref = ins
    _, odd = own_chip()
    for n in range(own_ref.shape[0]):
        early, late = early_late(own_ref[n], other_ref[n], odd)
        both = follow(late, early)
        outs[0][n, :DV] = (both[:DV] + late[:DV].astype(F32)).astype(BF16)
        outs[0][n, DV:] = both[DV:].astype(BF16)


def close_maps(ins, outs):
    own_ref, other_ref = ins[:2]
    refs = ins[2:]
    chips = len(refs)
    chip, odd = own_chip()

    def of_chip(j, n):
        value = refs[0][n]
        for k in range(1, chips):
            value = jnp.where((chip + chips - k) % chips == j, refs[k][n], value)
        return value

    every = range(own_ref.shape[0])
    running = [of_chip(0, n)[:DV] for n in every]
    entering = [jnp.zeros_like(running[n]) for n in every]
    for j in range(1, chips):
        entering = [jnp.where(chip == j, running[n], entering[n]) for n in every]
        there = [of_chip(j, n) for n in every]
        running = [(follow(there[n], running[n]) + there[n][:DV].astype(F32)).astype(BF16) for n in every]
    for n in every:
        early, _ = early_late(own_ref[n], other_ref[n], odd)
        second = (follow(early, entering[n]) + early[:DV].astype(F32)).astype(BF16)
        outs[0][n] = jnp.where(odd, second, entering[n])
        outs[1][n] = running[n].T


def chain_maps(ins, outs):
    count = len(ins)
    mine = lax.axis_index("seq")
    every = range(ins[0].shape[0])

    def run(at):
        running = [ins[at][n, :DV] for n in every]
        for n in every:
            if at == 0:
                outs[0][n] = jnp.zeros_like(running[n])
        for j in range(1, count):
            there = ins[at ^ j]
            if j == at:
                for n in every:
                    outs[0][n] = running[n]
            moved = [follow(there.at[n], running[n]) for n in every]
            running = [(moved[n] + there[n, :DV].astype(F32)).astype(BF16) for n in every]
        for n in every:
            outs[1][n] = running[n].T

    for at in range(count):
        pl.when(mine == at)(functools.partial(run, at))


def choose_finals(group, placement_ref, finals, outs):
    refs = [(ref, n) for ref in finals for n in range(ref.shape[0] // group)]
    for r in range(placement_ref.shape[1]):
        prompt = placement_ref[0, r]
        for p, (ref, n) in enumerate(refs):
            @pl.when(prompt == p)
            def _(ref=ref, n=n):
                outs[0][r] = ref[n * group : (n + 1) * group]


def state_step(placement, group, compose, chain, close, earlier, after):
    operands, shapes = [placement], []
    steps = []
    if compose is not None:
        steps.append(("compose", len(operands), len(compose), len(shapes)))
        operands += compose
        shapes += [compose[0]]
    if chain is not None or close is not None:
        steps.append(("chain" if close is None else "close", len(operands), len(close or chain), len(shapes)))
        close = close or chain
        operands += close
        shapes += [jax.ShapeDtypeStruct((close[0].shape[0], DK, DV), BF16)] * 2
        if earlier is not None:
            steps.append(("choose", len(operands), len(earlier), len(shapes)))
            operands += earlier
            shapes.append(jax.ShapeDtypeStruct((placement.shape[1], group, DK, DV), BF16))
    out_shape = [jax.ShapeDtypeStruct(x.shape, x.dtype) for x in shapes] + [pltpu.HBM((8, 128), F32)]

    def kernel(*refs):
        refs[-1][...] = jnp.zeros_like(refs[-1])
        ins, outs = refs[: len(operands)], refs[len(operands) + 1 :]
        closed = None
        for kind, at, size, to in steps:
            part = ins[at : at + size]
            if kind == "compose":
                compose_maps(part, outs[to : to + 1])
            elif kind in ("close", "chain"):
                (close_maps if kind == "close" else chain_maps)(part, outs[to : to + 2])
                closed = outs[to + 1]
            else:
                choose_finals(group, ins[0], list(part) + [closed], outs[to:])

    vmem = pl.BlockSpec(memory_space=pltpu.VMEM)
    return pl.pallas_call(
        kernel,
        in_specs=[pl.BlockSpec(memory_space=pltpu.SMEM)]
        + [vmem] * (len(operands) - 1)
        + [pl.BlockSpec(memory_space=pltpu.HBM)],
        out_specs=[vmem] * len(out_shape),
        out_shape=out_shape,
        compiler_params=pltpu.CompilerParams(vmem_limit_bytes=SMALL_VMEM_BYTES),
        cost_estimate=pl.CostEstimate(flops=10**9, bytes_accessed=2**20, transcendentals=0),
        name="state_step",
    )(*operands, far(after))


def deliver(parts):
    count, group = parts[0].shape[:2]

    def kernel(*refs):
        for n, ref in enumerate(refs[:-1]):
            refs[-1][:, n * group : (n + 1) * group] = ref[...].astype(F32)

    return pl.pallas_call(
        kernel,
        grid=(2,),
        in_specs=[pl.BlockSpec((count // 2, group, DK, DV), lambda i: (i, 0, 0, 0))] * len(parts),
        out_specs=pl.BlockSpec((count // 2, group * len(parts), DK, DV), lambda i: (i, 0, 0, 0)),
        out_shape=jax.ShapeDtypeStruct((count, group * len(parts), DK, DV), F32),
        compiler_params=pltpu.CompilerParams(vmem_limit_bytes=VMEM_BYTES),
        name="deliver",
    )(*parts)


def across(block, distance):
    count = lax.axis_size("seq")
    return lax.ppermute(block, "seq", [(i, i ^ distance) for i in range(count)])


def from_chip_behind(block, distance):
    count = lax.axis_size("seq")
    chips = count // 2
    route = [(i, ((i // 2 + distance) % chips) * 2 + i % 2) for i in range(count)]
    return lax.ppermute(block, "seq", route)


def shards(
    qk_in, v_in, gate_z, conv_qk, conv_v, log_decay, write_gain, norm_gain, prompt_lengths, placement,
):
    prompts, tok = qk_in.shape[:2]
    key_heads = qk_in.shape[3] // DK
    value_heads = v_in.shape[2] // DV
    rim = CONV - 1
    seq_count = lax.axis_size("seq")
    head_count = lax.axis_size("head")

    def by_head(x):
        x = x.reshape(x.shape[0], x.shape[1], 2, key_heads, DK)
        return jnp.transpose(x, (0, 1, 3, 2, 4)).reshape(x.shape[0], -1, DK)

    qk_rows = by_head(qk_in)
    qk_taps = by_head(conv_qk[None])[0]
    qk_tail = qk_rows[:, (tok - rim) * 2 * key_heads :]
    v_tail = v_in[:, tok - rim :].reshape(prompts, rim * value_heads, DV)
    front = 2 * EDGE - qk_tail.shape[1]
    back = 2 * EDGE - v_tail.shape[1]
    tails = jnp.concatenate(
        [
            jnp.zeros((prompts, front, DK), BF16),
            qk_tail,
            v_tail,
            jnp.zeros((prompts, back, DK), BF16),
        ],
        axis=1,
    )
    halo = lax.ppermute(tails, "seq", [(i, i + 1) for i in range(seq_count - 1)])
    group = value_heads // key_heads
    chips = seq_count // 2
    half = prompts // 2
    jobs = [(head, 0, prompts) for head in range(key_heads)]
    if key_heads == 1:
        jobs = [(0, 0, half), (0, half, prompts - half)]
    total = len(jobs)
    made, finals, sent = [], [], {}
    attended = None
    last = v_in

    def finish(job, results):
        head = jobs[job][0]
        finals.append(results[1])
        if len(results) > 3:
            sent[head] = lax.all_to_all(results[2], "head", 0, 0)
        return results[0], results[-1]

    def earlier(job):
        same = [n for n in range(total) if jobs[n][0] == jobs[job][0]]
        return [finals[n] for n in same[:-1]] if job == same[-1] else None

    def emit(job, entered, attended, last):
        qn, kn, wu, starts, _ = made[job]
        return outputs(
            jobs[job], jobs[job][1:], prompt_lengths, qn, kn, wu, starts, log_decay, write_gain,
            entered, gate_z, norm_gain, key_heads, attended, last,
        )

    for job in jobs:
        mixed = None if job[0] == 0 else made[0][:2]
        wu, starts, own_map, *new = prepare(
            job, prompt_lengths, qk_rows, v_in, halo, qk_taps, conv_v, log_decay, write_gain, key_heads,
            mixed and mixed[1], last,
        )
        last = wu
        moved = [own_map]
        if job == jobs[-1]:
            moved.append(across(own_map, 1))
        else:
            moved += [across(own_map, k) for k in range(1, seq_count)]
        made.append((*(mixed or new), wu, starts, moved))

    entered = []
    for job in range(total - 1):
        results = state_step(placement, group, None, made[job][4], None, earlier(job), last)
        enter, last = finish(job, results)
        entered.append(enter)
    pair = made[-1][4]
    chip_map, last = state_step(placement, group, pair, None, None, None, last)
    chip_maps = [chip_map] + [from_chip_behind(chip_map, k) for k in range(1, chips)]
    for job in range(total - 1):
        attended = last = emit(job, entered[job], attended, last)
    results = state_step(placement, group, None, None, pair + chip_maps, earlier(total - 1), last)
    enter, last = finish(total - 1, results)
    attended = emit(total - 1, enter, attended, last)
    rollout = deliver([sent[head] for head in range(key_heads)])
    return attended, rollout.reshape(1, 1, head_count * value_heads, DK, DV)


def solution(mesh):
    return jax.shard_map(
        shards,
        mesh=mesh,
        in_specs=(
            P(None, "seq", None, "head"),
            P(None, "seq", "head"),
            P(None, "seq", "head"),
            P(None, None, "head"),
            P(None, "head"),
            P(None, "head", "seq"),
            P(None, "head", "seq"),
            P(),
            P(),
            P("seq", None),
        ),
        out_specs=(P(None, "seq", "head"), P("seq", "head", None, None, None)),
        check_vma=False,
    )
```

```python
import functools

import jax
import jax.numpy as jnp
from jax import lax
from jax.experimental import pallas as pl
from jax.experimental.pallas import tpu as pltpu
from jax.sharding import PartitionSpec as P

DK = 128
DV = 128
CONV = 4
BLOCK = 128
TINY = 16
EDGE = 8
EPSILON = 1e-06
VMEM_BYTES = 24 * 1024 * 1024
SMALL_VMEM_BYTES = 8 * 1024 * 1024
F32 = jnp.float32
BF16 = jnp.bfloat16


def far(x):
    return pltpu.with_memory_space_constraint(x, pltpu.HBM)


def dot(a, b):
    return lax.dot_general(a, b, (((1,), (0,)), ((), ())), preferred_element_type=F32)


def silu(x):
    half = 0.5 * x
    return half + half * jnp.tanh(half)


def mixed_rows(pad_ref, taps, rim, first, step, c):
    total = None
    for i in range(CONV):
        start = rim + first + step * (c * BLOCK + i - (CONV - 1))
        stride = None if step == 1 else step
        term = pad_ref[pl.ds(start, BLOCK, stride), :] * taps[i]
        total = term if total is None else total + term
    return silu(total)


def unit_rows(x):
    return x * lax.rsqrt(jnp.sum(x * x, axis=-1, keepdims=True) + EPSILON)


def heads_rows(ref, head, group):
    every = ref[0]
    rows = every[:group]
    for n in range(1, every.shape[0] // group):
        rows = jnp.where(head == n, every[n * group : (n + 1) * group], rows)
    return rows


def gates_of_heads(log_ref, gain_ref, used, head, group):
    log = heads_rows(log_ref, head, group)
    lane = lax.broadcasted_iota(jnp.int32, log.shape, 1)
    valid = lane < used
    cum = jnp.where(valid, log, 0.0)
    gain = jnp.where(valid, heads_rows(gain_ref, head, group), 0.0)
    shift = 1
    while shift < BLOCK:
        cum = cum + jnp.where(lane % BLOCK >= shift, pltpu.roll(cum, shift, 1), 0.0)
        shift *= 2
    return cum, gain


def as_columns(rows, chunks):
    parts = [rows[:, c * BLOCK : (c + 1) * BLOCK] for c in range(chunks)]
    short = BLOCK - 8 * chunks
    if short:
        parts.append(jnp.zeros((short, BLOCK), F32))
    return jnp.concatenate(parts, axis=0).T


def block_bases(parts, chunks):
    rows = jnp.concatenate(parts, axis=0)
    short = 7 - rows.shape[0]
    fill = [jnp.zeros((short, rows.shape[1]), F32)] if short else []
    rows = jnp.concatenate([rows] + fill + [jnp.ones((1, rows.shape[1]), F32)], axis=0)
    return [rows[:, c * BLOCK : (c + 1) * BLOCK] for c in range(chunks)]


def spread_squares(base, group, kinds):
    high = base.astype(BF16).astype(F32)
    middle = (base - high).astype(BF16).astype(F32)
    low = base - high - middle
    parts = [high, middle, low]
    row = lax.broadcasted_iota(jnp.int32, (32, BLOCK), 0)
    which = row % 8
    real = row < 24
    stacked = jnp.concatenate(parts + [jnp.zeros_like(high)], axis=0)
    left = jnp.where(jnp.logical_and(which == 7, real), 1.0, stacked).T.astype(BF16)
    blocks = []
    for h in range(group):
        minus = jnp.concatenate([jnp.broadcast_to(-part[h : h + 1], (8, BLOCK)) for part in parts + [low]], axis=0)
        blocks.append(jnp.where(which == h, 1.0, jnp.where(which == 7, minus, 0.0)))
    for n in range(group, group * kinds):
        blocks.append(jnp.where(which == n, 1.0, 0.0).astype(F32))
    every = dot(left, jnp.concatenate(blocks, axis=1).astype(BF16))
    return [every[:, n * BLOCK : (n + 1) * BLOCK] for n in range(group * kinds)]


def mix(qk_ref, halo_ref, taps_ref, qn_ref, kn_ref, raw_scr, key_heads, chunks):
    kinds = 2 * key_heads
    rim = 2 * EDGE
    taps = taps_ref[...].astype(F32)
    raw_scr[:rim] = halo_ref[0].astype(F32)[:rim]
    raw_scr[rim:] = qk_ref[0].astype(F32)
    for c in range(chunks):
        span = slice(c * BLOCK, (c + 1) * BLOCK)
        for kind in range(kinds):
            own = [taps[n : n + 1] for n in range(kind, taps.shape[0], kinds)]
            rows = unit_rows(mixed_rows(raw_scr, own, rim, kind, kinds, c))
            to_ref = kn_ref if kind % 2 else qn_ref
            to_ref[0, span, kind // 2 * DK : (kind // 2 + 1) * DK] = rows.astype(BF16)


def weave(*lists):
    places = []
    for which, entries in enumerate(lists):
        places += [((n + 0.5) / len(entries), which, n) for n in range(len(entries))]
    for _, which, n in sorted(places):
        lists[which][n]()


def prepare_kernel(first, count, head, group, chunks, key_heads, mixes, *refs):
    length_ref, v_ref, halo_ref, v_taps_ref, log_ref, gain_ref, after_ref = refs[:7]
    refs = refs[7:]
    if mixes:
        qk_ref, qk_taps_ref, wu_ref, start_ref, map_ref, token_ref, qn_ref, kn_ref = refs[:8]
        v_pad, m_scr, b_scr, fade_scr, st_scr, a_scr, x_scr, y_scr, raw_scr = refs[8:]
        key_columns = slice(head * DK, (head + 1) * DK)
    else:
        kn_ref, wu_ref, start_ref, map_ref, token_ref = refs[:5]
        v_pad, m_scr, b_scr, fade_scr, st_scr, a_scr, x_scr, y_scr = refs[5:]
        key_columns = slice(0, DK)
    step = pl.program_id(0)
    token_ref[...] = jnp.zeros_like(token_ref)
    used = length_ref[first + jnp.minimum(step, count - 1)] - lax.axis_index("seq") * (chunks * BLOCK)
    units = [(h, c) for c in range(chunks) for h in range(group)]
    slot = step % 2
    live = jnp.logical_and(step < count, used > 0)

    def begin():
        row = lax.broadcasted_iota(jnp.int32, (DV + DK, DK), 0)
        lane = lax.broadcasted_iota(jnp.int32, (DV + DK, DK), 1)
        for h in range(group):
            st_scr[h] = jnp.where(row == lane + DV, 1.0, 0.0).astype(F32)

    def advance(c):
        narrow, moved = {}, {}

        def load(h):
            narrow[h] = st_scr[h].astype(BF16)
            start_ref[0, h, c * (DV + DK) : (c + 1) * (DV + DK), :] = narrow[h]

        def move(h):
            moved[h] = dot(narrow[h], m_scr[1 - slot, c, h])

        def store(h):
            fade = fade_scr[1 - slot, c, h : h + 1, :]
            state = st_scr[h, :DV] * fade + (moved[h][:DV] + b_scr[1 - slot, c, h])
            trans = st_scr[h, DV:] * fade + moved[h][DV:]
            if c < chunks - 1:
                st_scr[h, :DV] = state
                st_scr[h, DV:] = trans
            else:
                map_ref[h, :DV] = state.astype(BF16)
                map_ref[h, DV:] = trans.astype(BF16)

        return [functools.partial(act, h) for act in (load, move, store) for h in range(group)]

    recurrence = [begin]
    for c in range(chunks):
        recurrence += advance(c)

    @pl.when(jnp.logical_not(live))
    def _():
        @pl.when(step > 0)
        def _():
            weave(recurrence)

        @pl.when(step < count)
        def _():
            if mixes:
                qn_ref[...] = jnp.zeros_like(qn_ref)
                kn_ref[...] = jnp.zeros_like(kn_ref)
            wu_ref[...] = jnp.zeros_like(wu_ref)
            fade_scr[slot] = jnp.ones(fade_scr.shape[1:], F32)
            m_scr[slot] = jnp.zeros(m_scr.shape[1:], BF16)
            b_scr[slot] = jnp.zeros(b_scr.shape[1:], F32)

    @pl.when(live)
    def _():
        if mixes:
            mix(qk_ref, halo_ref, qk_taps_ref, qn_ref, kn_ref, raw_scr, key_heads, chunks)
        halo = halo_ref[0].astype(F32)
        v_pad[EDGE:, :] = v_ref[0].astype(F32)
        for i in range(CONV - 1):
            for h in range(group):
                source = 2 * EDGE + (i * key_heads + head) * group + h
                v_pad[EDGE - CONV + 1 + i : EDGE - CONV + 2 + i, h * DV : (h + 1) * DV] = halo[
                    source : source + 1
                ]
        v_all_taps = v_taps_ref[...].astype(F32)
        v_taps = [v_all_taps[i : i + 1] for i in range(CONV)]

        cum, gain = gates_of_heads(log_ref, gain_ref, used, head, group)
        both_gains = gain * jnp.exp(cum)
        bases = block_bases([-cum], chunks)

        def span(c):
            return slice(c * BLOCK, (c + 1) * BLOCK)

        row = lax.broadcasted_iota(jnp.int32, (BLOCK, BLOCK), 0)
        lane = lax.broadcasted_iota(jnp.int32, (BLOCK, BLOCK), 1)
        above = row < lane
        small_row = lax.broadcasted_iota(jnp.int32, (TINY, BLOCK), 0)
        small_lane = lax.broadcasted_iota(jnp.int32, (TINY, BLOCK), 1)
        part_of = small_lane // TINY
        tiny_eye = jnp.where(small_row == small_lane % TINY, 1.0, 0.0).astype(F32)

        keys = [kn_ref[0, span(c), key_columns] for c in range(chunks)]
        turned = {}

        def front(some):
            ops, kk, later, compact, solved, mixed = [], {}, {}, {}, {}, {}
            local = [(h, c) for c in some for h in range(group)]

            def start(c):
                turned[c] = keys[c].T
                kk[c] = dot(keys[c], turned[c])
                later[c] = spread_squares(bases[c], group, 1)

            def mask(h, c):
                r = h * chunks + c
                strict = jnp.where(above, jnp.exp(later[c][h]) * kk[c] * -gain[h : h + 1, span(c)], 0.0)
                a_scr[r] = strict.astype(BF16)
                tiny = strict[0:TINY]
                for b in range(1, BLOCK // TINY):
                    tiny = jnp.where(part_of == b, strict[b * TINY : (b + 1) * TINY], tiny)
                compact[r] = tiny
                solved[r] = tiny_eye

            def eliminate(j, r):
                factor = jnp.take_along_axis(compact[r], part_of * TINY + j, axis=1, mode="promise_in_bounds")
                solved[r] = solved[r] + factor * solved[r][j : j + 1, :]

            def place(r):
                for b in range(BLOCK // TINY):
                    x_scr[r, b * TINY : (b + 1) * TINY, :] = jnp.where(part_of == b, solved[r], 0.0).astype(BF16)

            def convolve(c):
                mixed[c] = mixed_rows(v_pad, v_taps, EDGE, 0, 1, c).astype(BF16)

            def scale(h, c):
                top = h * (DK + DV)
                v_wide = mixed[c][:, h * DV : (h + 1) * DV].T.astype(F32)
                y_scr[c, top : top + DK, :] = (turned[c].astype(F32) * both_gains[h : h + 1, span(c)]).astype(BF16)
                y_scr[c, top + DK : top + DK + DV, :] = (v_wide * gain[h : h + 1, span(c)]).astype(BF16)

            for c in some:
                ops.append(functools.partial(start, c))
            for h, c in local:
                ops.append(functools.partial(mask, h, c))
            for j in range(TINY - 1, 0, -1):
                for h, c in local:
                    ops.append(functools.partial(eliminate, j, h * chunks + c))
            for h, c in local:
                ops.append(functools.partial(place, h * chunks + c))
            right = []
            for c in some:
                right.append(functools.partial(convolve, c))
                right += [functools.partial(scale, h, c) for h in range(group)]
            return ops, right

        def back(some):
            ops, own, moved = [], {}, {}
            local = [(h, c) for c in some for h in range(group)]

            def reach(size, r):
                half_lane = lax.broadcasted_iota(jnp.int32, (BLOCK // 2, BLOCK), 1)
                half_row = lax.broadcasted_iota(jnp.int32, (BLOCK // 2, BLOCK), 0)
                partner = half_lane // size == 2 * (half_row // size) + 1
                own[r] = jnp.concatenate([x_scr[r, s : s + size, :] for s in range(0, BLOCK, 2 * size)], axis=0)
                moved[r] = jnp.where(partner, dot(own[r], a_scr[r]), 0.0).astype(BF16)

            def join(size, r):
                update = own[r] + dot(moved[r], x_scr[r]).astype(BF16)
                for n, s in enumerate(range(0, BLOCK, 2 * size)):
                    x_scr[r, s : s + size, :] = update[n * size : (n + 1) * size]

            def solve(h, c):
                r = h * chunks + c
                top = h * (DK + DV)
                sums = cum[:, span(c)]
                last = sums[:, BLOCK - 1 : BLOCK]
                tail = jnp.exp(last - sums)
                fade = jnp.broadcast_to(jnp.exp(last), (group, BLOCK))
                rows = dot(y_scr[c, top : top + DK + DV, :], x_scr[r])
                wu_ref[0, r] = rows.astype(BF16)
                y_scr[c, top : top + DK + DV, :] = (rows * tail[h : h + 1]).astype(BF16)
                fade_scr[slot, c, h : h + 1, :] = fade[h : h + 1]

            def finish(c):
                both = dot(y_scr[c], keys[c])
                for h in range(group):
                    top = h * (DK + DV)
                    m_scr[slot, c, h] = (-both[top : top + DK]).astype(BF16)
                    b_scr[slot, c, h] = both[top + DK : top + DK + DV]

            size = TINY
            while size < BLOCK:
                ops += [functools.partial(reach, size, h * chunks + c) for h, c in local]
                ops += [functools.partial(join, size, h * chunks + c) for h, c in local]
                size *= 2
            ops += [functools.partial(solve, h, c) for h, c in local]
            ops += [functools.partial(finish, c) for c in some]
            return ops

        half = chunks // 2
        early, late = range(half), range(half, chunks)
        early_front, early_right = front(early)
        late_front, late_right = front(late)
        cut = len(recurrence) // 3
        weave(early_front, recurrence[:cut], early_right)
        weave(back(early), late_front, late_right)
        weave(back(late), recurrence[cut:])


def prepare(job, lengths, qk_rows, v_in, halo, qk_taps, v_taps, log_decay, write_gain, key_heads, mixed, after):
    head, first, count = job
    tok = v_in.shape[1]
    value_heads = v_in.shape[2] // DV
    group = value_heads // key_heads
    chunks = tok // BLOCK
    rows = group * chunks
    wide = group * DV
    mixes = mixed is None

    def now(i):
        return jnp.minimum(i, count - 1)

    def before(i):
        return jnp.maximum(i - 1, 0)

    def whole_of(i, lengths):
        return (first + now(i), 0, 0)

    operands = [far(v_in), halo, far(v_taps), far(log_decay), far(write_gain), far(after)]
    in_specs = [
        pl.BlockSpec((1, tok, wide), lambda i, lengths: (first + now(i), 0, head)),
        pl.BlockSpec((1,) + halo.shape[1:], whole_of),
        pl.BlockSpec((CONV, wide), lambda i, lengths: (0, head)),
        pl.BlockSpec((1, value_heads, tok), whole_of),
        pl.BlockSpec((1, value_heads, tok), whole_of),
        pl.BlockSpec(memory_space=pltpu.HBM),
    ]
    out_specs = [
        pl.BlockSpec((1, rows, DK + DV, BLOCK), lambda i, lengths: (now(i), 0, 0, 0)),
        pl.BlockSpec((1, group, chunks * (DV + DK), DK), lambda i, lengths: (before(i), 0, 0, 0)),
        pl.BlockSpec((group, DV + DK, DK), lambda i, lengths: (before(i), 0, 0)),
        pl.BlockSpec((8, 128), lambda i, lengths: (0, 0)),
    ]
    out_shape = [
        jax.ShapeDtypeStruct((count, rows, DK + DV, BLOCK), BF16),
        jax.ShapeDtypeStruct((count, group, chunks * (DV + DK), DK), BF16),
        jax.ShapeDtypeStruct((count * group, DV + DK, DK), BF16),
        pltpu.HBM((8, 128), F32),
    ]
    scratch = [
        pltpu.VMEM((tok + EDGE, wide), F32),
        pltpu.VMEM((2, chunks, group, DK, DK), BF16),
        pltpu.VMEM((2, chunks, group, DV, DK), F32),
        pltpu.VMEM((2, chunks, group, BLOCK), F32),
        pltpu.VMEM((group, DV + DK, DK), F32),
        pltpu.VMEM((rows, BLOCK, BLOCK), BF16),
        pltpu.VMEM((rows, BLOCK, BLOCK), BF16),
        pltpu.VMEM((chunks, group * (DK + DV), BLOCK), BF16),
    ]
    if mixes:
        operands += [far(qk_rows), far(qk_taps)]
        in_specs += [
            pl.BlockSpec((1,) + qk_rows.shape[1:], whole_of),
            pl.BlockSpec(qk_taps.shape, lambda i, lengths: (0, 0)),
        ]
        out_specs += [pl.BlockSpec((1, tok, key_heads * DK), lambda i, lengths: (now(i), 0, 0))] * 2
        out_shape += [jax.ShapeDtypeStruct((count, tok, key_heads * DK), BF16)] * 2
        scratch.append(pltpu.VMEM((qk_rows.shape[1] + 2 * EDGE, DK), F32))
    else:
        operands.append(mixed)
        in_specs.append(pl.BlockSpec((1, tok, DK), lambda i, lengths: (first + now(i), 0, head)))
    return pl.pallas_call(
        functools.partial(prepare_kernel, first, count, head, group, chunks, key_heads, mixes),
        grid_spec=pltpu.PrefetchScalarGridSpec(
            num_scalar_prefetch=1,
            grid=(count + 1,),
            in_specs=in_specs,
            out_specs=out_specs,
            scratch_shapes=scratch,
        ),
        out_shape=out_shape,
        compiler_params=pltpu.CompilerParams(vmem_limit_bytes=VMEM_BYTES),
        cost_estimate=pl.CostEstimate(flops=5 * 10**9 * count, bytes_accessed=4 * 2**20 * count, transcendentals=10**6),
        name="prepare",
    )(lengths, *operands)


def outputs_kernel(
    first, head, group, chunks,
    length_ref, qn_ref, kn_ref, wu_ref, start_ref, log_ref, gain_ref, enter_ref, z_ref, norm_ref, held_ref, after_ref,
    out_ref,
    first_scr, score_scr, seen_scr,
):
    used = length_ref[first + pl.program_id(0)] - lax.axis_index("seq") * (chunks * BLOCK)
    units = [(h, c) for c in range(chunks) for h in range(group)]

    @pl.when(used <= 0)
    def _():
        out_ref[...] = jnp.zeros_like(out_ref)

    @pl.when(used > 0)
    def _():
        cum, gain = gates_of_heads(log_ref, gain_ref, used, head, group)
        faded = jnp.exp(cum)
        columns = as_columns(jnp.concatenate([cum] * (8 // group), axis=0), chunks)
        row = lax.broadcasted_iota(jnp.int32, (BLOCK, BLOCK), 0)
        lane = lax.broadcasted_iota(jnp.int32, (BLOCK, BLOCK), 1)
        upto = row <= lane
        norm_gain = norm_ref[...]

        def span(c):
            return slice(c * BLOCK, (c + 1) * BLOCK)

        for c in range(chunks):
            turned = qn_ref[0, span(c), :].T
            kq = dot(kn_ref[0, span(c), :], turned)
            q_wide = turned.astype(F32)
            for h in range(group):
                r = h * chunks + c
                ratio = jnp.exp(cum[h : h + 1, span(c)] - columns[:, c * 8 + h : c * 8 + h + 1])
                score_scr[r] = jnp.where(upto, ratio * kq, 0.0).astype(BF16)
                seen_scr[r] = q_wide * faded[h : h + 1, span(c)]
                top = c * (DV + DK)
                moved = dot(enter_ref[h], start_ref[0, h, top + DV : top + DV + DK, :])
                first_scr[r] = (moved + start_ref[0, h, top : top + DV, :].astype(F32)).astype(BF16)
        both, raws = {}, {}
        for h, c in units:
            r = h * chunks + c
            both[r] = dot(wu_ref[0, r], score_scr[r])
        for h, c in units:
            r = h * chunks + c
            seen = (seen_scr[r] - both[r][:DK]).astype(BF16)
            raw = dot(first_scr[r], seen) + both[r][DK:]
            mean = jnp.sum(raw * raw, axis=0, keepdims=True) * (1.0 / DV)
            raws[r] = (raw * lax.rsqrt(mean + EPSILON)).astype(BF16)
        for h, c in units:
            scaled = raws[h * chunks + c].T.astype(F32)
            cols = slice(h * DV, (h + 1) * DV)
            gated = scaled * norm_gain * silu(z_ref[0, span(c), cols].astype(F32))
            out_ref[0, span(c), cols] = jnp.where(row + c * BLOCK < used, gated, 0.0).astype(BF16)


def outputs(
    job, piece, lengths, qn, kn, wu, starts, log_decay, write_gain, enter, gate_z, norm_gain, key_heads, held, after,
):
    head, first, _ = job
    begin, count = piece
    prompts, tok, width = gate_z.shape
    rows = wu.shape[1]
    chunks = tok // BLOCK
    group = rows // chunks
    wide = group * DV
    value_heads = key_heads * group
    shift = begin - first
    from_mix = begin if qn.shape[0] == prompts else shift

    def whole_of(i, lengths):
        return (begin + i, 0, 0)

    def wide_of(i, lengths):
        return (begin + i, 0, head)

    def mixed_of(i, lengths):
        return (from_mix + i, 0, head)

    empty = held is None
    return pl.pallas_call(
        functools.partial(outputs_kernel, begin, head, group, chunks),
        grid_spec=pltpu.PrefetchScalarGridSpec(
            num_scalar_prefetch=1,
            grid=(count,),
            in_specs=[
                pl.BlockSpec((1, tok, DK), mixed_of),
                pl.BlockSpec((1, tok, DK), mixed_of),
                pl.BlockSpec((1, rows, DK + DV, BLOCK), lambda i, lengths: (shift + i, 0, 0, 0)),
                pl.BlockSpec((1, group, chunks * (DV + DK), DK), lambda i, lengths: (shift + i, 0, 0, 0)),
                pl.BlockSpec((1, value_heads, tok), whole_of),
                pl.BlockSpec((1, value_heads, tok), whole_of),
                pl.BlockSpec((group, DK, DV), lambda i, lengths: (shift + i, 0, 0)),
                pl.BlockSpec((1, tok, wide), wide_of),
                pl.BlockSpec((1, DV), lambda i, lengths: (0, 0)),
                pl.BlockSpec(memory_space=pltpu.HBM),
                pl.BlockSpec(memory_space=pltpu.HBM),
            ],
            out_specs=pl.BlockSpec((1, tok, wide), wide_of),
            scratch_shapes=[
                pltpu.VMEM((rows, DV, DK), BF16),
                pltpu.VMEM((rows, BLOCK, BLOCK), BF16),
                pltpu.VMEM((rows, BLOCK, DV), F32),
            ],
        ),
        out_shape=pltpu.HBM((prompts, tok, width), BF16),
        input_output_aliases={} if empty else {10: 0},
        compiler_params=pltpu.CompilerParams(vmem_limit_bytes=VMEM_BYTES),
        cost_estimate=pl.CostEstimate(flops=3 * 10**9 * count, bytes_accessed=4 * 2**20 * count, transcendentals=10**6),
        name="outputs",
    )(
        lengths, qn, kn, wu, starts, far(log_decay), far(write_gain), enter, far(gate_z),
        far(norm_gain.reshape(1, DV)), far(after if empty else held), far(norm_gain.reshape(1, DV) if after is held else after),
    )


def own_chip():
    seq = lax.axis_index("seq")
    return seq // 2, seq % 2 == 1


def early_late(own, other, odd):
    return jnp.where(odd, other, own), jnp.where(odd, own, other)


def follow(there, running):
    return dot(running, there[DV:])


def compose_maps(ins, outs):
    own_ref, other_ref = ins
    _, odd = own_chip()
    for n in range(own_ref.shape[0]):
        early, late = early_late(own_ref[n], other_ref[n], odd)
        both = follow(late, early)
        outs[0][n, :DV] = (both[:DV] + late[:DV].astype(F32)).astype(BF16)
        outs[0][n, DV:] = both[DV:].astype(BF16)


def close_maps(ins, outs):
    own_ref, other_ref = ins[:2]
    refs = ins[2:]
    chips = len(refs)
    chip, odd = own_chip()

    def of_chip(j, n):
        value = refs[0][n]
        for k in range(1, chips):
            value = jnp.where((chip + chips - k) % chips == j, refs[k][n], value)
        return value

    every = range(own_ref.shape[0])
    running = [of_chip(0, n)[:DV] for n in every]
    entering = [jnp.zeros_like(running[n]) for n in every]
    for j in range(1, chips):
        entering = [jnp.where(chip == j, running[n], entering[n]) for n in every]
        there = [of_chip(j, n) for n in every]
        running = [(follow(there[n], running[n]) + there[n][:DV].astype(F32)).astype(BF16) for n in every]
    for n in every:
        early, _ = early_late(own_ref[n], other_ref[n], odd)
        second = (follow(early, entering[n]) + early[:DV].astype(F32)).astype(BF16)
        outs[0][n] = jnp.where(odd, second, entering[n])
        outs[1][n] = running[n].T


def chain_maps(ins, outs):
    count = len(ins)
    mine = lax.axis_index("seq")
    every = range(ins[0].shape[0])

    def run(at):
        running = [ins[at][n, :DV] for n in every]
        for n in every:
            if at == 0:
                outs[0][n] = jnp.zeros_like(running[n])
        for j in range(1, count):
            there = ins[at ^ j]
            if j == at:
                for n in every:
                    outs[0][n] = running[n]
            moved = [follow(there.at[n], running[n]) for n in every]
            running = [(moved[n] + there[n, :DV].astype(F32)).astype(BF16) for n in every]
        for n in every:
            outs[1][n] = running[n].T

    for at in range(count):
        pl.when(mine == at)(functools.partial(run, at))


def choose_finals(group, placement_ref, finals, outs):
    refs = [(ref, n) for ref in finals for n in range(ref.shape[0] // group)]
    for r in range(placement_ref.shape[1]):
        prompt = placement_ref[0, r]
        for p, (ref, n) in enumerate(refs):
            @pl.when(prompt == p)
            def _(ref=ref, n=n):
                outs[0][r] = ref[n * group : (n + 1) * group]


def state_step(placement, group, compose, chain, close, earlier, after):
    operands, shapes = [placement], []
    steps = []
    if compose is not None:
        steps.append(("compose", len(operands), len(compose), len(shapes)))
        operands += compose
        shapes += [compose[0]]
    if chain is not None or close is not None:
        steps.append(("chain" if close is None else "close", len(operands), len(close or chain), len(shapes)))
        close = close or chain
        operands += close
        shapes += [jax.ShapeDtypeStruct((close[0].shape[0], DK, DV), BF16)] * 2
        if earlier is not None:
            steps.append(("choose", len(operands), len(earlier), len(shapes)))
            operands += earlier
            shapes.append(jax.ShapeDtypeStruct((placement.shape[1], group, DK, DV), BF16))
    out_shape = [jax.ShapeDtypeStruct(x.shape, x.dtype) for x in shapes] + [pltpu.HBM((8, 128), F32)]

    def kernel(*refs):
        refs[-1][...] = jnp.zeros_like(refs[-1])
        ins, outs = refs[: len(operands)], refs[len(operands) + 1 :]
        closed = None
        for kind, at, size, to in steps:
            part = ins[at : at + size]
            if kind == "compose":
                compose_maps(part, outs[to : to + 1])
            elif kind in ("close", "chain"):
                (close_maps if kind == "close" else chain_maps)(part, outs[to : to + 2])
                closed = outs[to + 1]
            else:
                choose_finals(group, ins[0], list(part) + [closed], outs[to:])

    vmem = pl.BlockSpec(memory_space=pltpu.VMEM)
    return pl.pallas_call(
        kernel,
        in_specs=[pl.BlockSpec(memory_space=pltpu.SMEM)]
        + [vmem] * (len(operands) - 1)
        + [pl.BlockSpec(memory_space=pltpu.HBM)],
        out_specs=[vmem] * len(out_shape),
        out_shape=out_shape,
        compiler_params=pltpu.CompilerParams(vmem_limit_bytes=SMALL_VMEM_BYTES),
        cost_estimate=pl.CostEstimate(flops=10**9, bytes_accessed=2**20, transcendentals=0),
        name="state_step",
    )(*operands, far(after))


def deliver(parts):
    count, group = parts[0].shape[:2]

    def kernel(*refs):
        for n, ref in enumerate(refs[:-1]):
            refs[-1][:, n * group : (n + 1) * group] = ref[...].astype(F32)

    return pl.pallas_call(
        kernel,
        grid=(2,),
        in_specs=[pl.BlockSpec((count // 2, group, DK, DV), lambda i: (i, 0, 0, 0))] * len(parts),
        out_specs=pl.BlockSpec((count // 2, group * len(parts), DK, DV), lambda i: (i, 0, 0, 0)),
        out_shape=jax.ShapeDtypeStruct((count, group * len(parts), DK, DV), F32),
        compiler_params=pltpu.CompilerParams(vmem_limit_bytes=VMEM_BYTES),
        name="deliver",
    )(*parts)


def across(block, distance):
    count = lax.axis_size("seq")
    return lax.ppermute(block, "seq", [(i, i ^ distance) for i in range(count)])


def from_chip_behind(block, distance):
    count = lax.axis_size("seq")
    chips = count // 2
    route = [(i, ((i // 2 + distance) % chips) * 2 + i % 2) for i in range(count)]
    return lax.ppermute(block, "seq", route)


def shards(
    qk_in, v_in, gate_z, conv_qk, conv_v, log_decay, write_gain, norm_gain, prompt_lengths, placement,
):
    prompts, tok = qk_in.shape[:2]
    key_heads = qk_in.shape[3] // DK
    value_heads = v_in.shape[2] // DV
    rim = CONV - 1
    seq_count = lax.axis_size("seq")
    head_count = lax.axis_size("head")

    def by_head(x):
        x = x.reshape(x.shape[0], x.shape[1], 2, key_heads, DK)
        return jnp.transpose(x, (0, 1, 3, 2, 4)).reshape(x.shape[0], -1, DK)

    qk_rows = by_head(qk_in)
    qk_taps = by_head(conv_qk[None])[0]
    qk_tail = qk_rows[:, (tok - rim) * 2 * key_heads :]
    v_tail = v_in[:, tok - rim :].reshape(prompts, rim * value_heads, DV)
    front = 2 * EDGE - qk_tail.shape[1]
    back = 2 * EDGE - v_tail.shape[1]
    tails = jnp.concatenate(
        [
            jnp.zeros((prompts, front, DK), BF16),
            qk_tail,
            v_tail,
            jnp.zeros((prompts, back, DK), BF16),
        ],
        axis=1,
    )
    halo = lax.ppermute(tails, "seq", [(i, i + 1) for i in range(seq_count - 1)])
    group = value_heads // key_heads
    chips = seq_count // 2
    half = prompts // 2
    jobs = [(head, 0, prompts) for head in range(key_heads)]
    if key_heads == 1:
        jobs = [(0, 0, half), (0, half, prompts - half)]
    total = len(jobs)
    made, finals, sent = [], [], {}
    attended = None
    last = v_in

    def finish(job, results):
        head = jobs[job][0]
        finals.append(results[1])
        if len(results) > 3:
            sent[head] = lax.all_to_all(results[2], "head", 0, 0)
        return results[0], results[-1]

    def earlier(job):
        same = [n for n in range(total) if jobs[n][0] == jobs[job][0]]
        return [finals[n] for n in same[:-1]] if job == same[-1] else None

    def emit(job, entered, attended, last):
        qn, kn, wu, starts, _ = made[job]
        return outputs(
            jobs[job], jobs[job][1:], prompt_lengths, qn, kn, wu, starts, log_decay, write_gain,
            entered, gate_z, norm_gain, key_heads, attended, last,
        )

    for job in jobs:
        mixed = None if job[0] == 0 else made[0][:2]
        wu, starts, own_map, last, *new = prepare(
            job, prompt_lengths, qk_rows, v_in, halo, qk_taps, conv_v, log_decay, write_gain, key_heads,
            mixed and mixed[1], last,
        )
        moved = [own_map]
        if job == jobs[-1]:
            moved.append(across(own_map, 1))
        else:
            moved += [across(own_map, k) for k in range(1, seq_count)]
        made.append((*(mixed or new), wu, starts, moved))

    entered = []
    for job in range(total - 1):
        results = state_step(placement, group, None, made[job][4], None, earlier(job), last)
        enter, last = finish(job, results)
        entered.append(enter)
    pair = made[-1][4]
    chip_map, last = state_step(placement, group, pair, None, None, None, last)
    chip_maps = [chip_map] + [from_chip_behind(chip_map, k) for k in range(1, chips)]
    for job in range(total - 1):
        attended = last = emit(job, entered[job], attended, last)
    results = state_step(placement, group, None, None, pair + chip_maps, earlier(total - 1), last)
    enter, last = finish(total - 1, results)
    attended = emit(total - 1, enter, attended, last)
    rollout = deliver([sent[head] for head in range(key_heads)])
    return attended, rollout.reshape(1, 1, head_count * value_heads, DK, DV)


def solution(mesh):
    return jax.shard_map(
        shards,
        mesh=mesh,
        in_specs=(
            P(None, "seq", None, "head"),
            P(None, "seq", "head"),
            P(None, "seq", "head"),
            P(None, None, "head"),
            P(None, "head"),
            P(None, "head", "seq"),
            P(None, "head", "seq"),
            P(),
            P(),
            P("seq", None),
        ),
        out_specs=(P(None, "seq", "head"), P("seq", "head", None, None, None)),
        check_vma=False,
    )
```

```python
import functools

import jax
import jax.numpy as jnp
from jax import lax
from jax.experimental import pallas as pl
from jax.experimental.pallas import tpu as pltpu
from jax.sharding import PartitionSpec as P

DK = 128
DV = 128
CONV = 4
BLOCK = 128
TINY = 16
EDGE = 8
EPSILON = 1e-06
VMEM_BYTES = 40 * 1024 * 1024
SMALL_VMEM_BYTES = 8 * 1024 * 1024
F32 = jnp.float32
BF16 = jnp.bfloat16


def far(x):
    return pltpu.with_memory_space_constraint(x, pltpu.HBM)


def dot(a, b):
    return lax.dot_general(a, b, (((1,), (0,)), ((), ())), preferred_element_type=F32)


def silu(x):
    half = 0.5 * x
    return half + half * jnp.tanh(half)


def mixed_rows(pad_ref, taps, rim, first, step, c):
    total = None
    for i in range(CONV):
        start = rim + first + step * (c * BLOCK + i - (CONV - 1))
        stride = None if step == 1 else step
        term = pad_ref[pl.ds(start, BLOCK, stride), :] * taps[i]
        total = term if total is None else total + term
    return silu(total)


def unit_rows(x):
    return x * lax.rsqrt(jnp.sum(x * x, axis=-1, keepdims=True) + EPSILON)


def heads_rows(ref, head, group):
    every = ref[0]
    rows = every[:group]
    for n in range(1, every.shape[0] // group):
        rows = jnp.where(head == n, every[n * group : (n + 1) * group], rows)
    return rows


def gates_of_heads(log_ref, gain_ref, used, head, group):
    log = heads_rows(log_ref, head, group)
    lane = lax.broadcasted_iota(jnp.int32, log.shape, 1)
    valid = lane < used
    cum = jnp.where(valid, log, 0.0)
    gain = jnp.where(valid, heads_rows(gain_ref, head, group), 0.0)
    shift = 1
    while shift < BLOCK:
        cum = cum + jnp.where(lane % BLOCK >= shift, pltpu.roll(cum, shift, 1), 0.0)
        shift *= 2
    return cum, gain


def as_columns(rows, chunks):
    parts = [rows[:, c * BLOCK : (c + 1) * BLOCK] for c in range(chunks)]
    short = BLOCK - 8 * chunks
    if short:
        parts.append(jnp.zeros((short, BLOCK), F32))
    return jnp.concatenate(parts, axis=0).T


def block_bases(parts, chunks):
    rows = jnp.concatenate(parts, axis=0)
    short = 7 - rows.shape[0]
    fill = [jnp.zeros((short, rows.shape[1]), F32)] if short else []
    rows = jnp.concatenate([rows] + fill + [jnp.ones((1, rows.shape[1]), F32)], axis=0)
    return [rows[:, c * BLOCK : (c + 1) * BLOCK] for c in range(chunks)]


def spread_squares(base, group, kinds):
    high = base.astype(BF16).astype(F32)
    middle = (base - high).astype(BF16).astype(F32)
    low = base - high - middle
    parts = [high, middle, low]
    row = lax.broadcasted_iota(jnp.int32, (32, BLOCK), 0)
    which = row % 8
    real = row < 24
    stacked = jnp.concatenate(parts + [jnp.zeros_like(high)], axis=0)
    left = jnp.where(jnp.logical_and(which == 7, real), 1.0, stacked).T.astype(BF16)
    blocks = []
    for h in range(group):
        minus = jnp.concatenate([jnp.broadcast_to(-part[h : h + 1], (8, BLOCK)) for part in parts + [low]], axis=0)
        blocks.append(jnp.where(which == h, 1.0, jnp.where(which == 7, minus, 0.0)))
    for n in range(group, group * kinds):
        blocks.append(jnp.where(which == n, 1.0, 0.0).astype(F32))
    every = dot(left, jnp.concatenate(blocks, axis=1).astype(BF16))
    return [every[:, n * BLOCK : (n + 1) * BLOCK] for n in range(group * kinds)]


def mix(qk_ref, halo_ref, taps_ref, qn_ref, kn_ref, raw_scr, key_heads, chunks):
    kinds = 2 * key_heads
    rim = 2 * EDGE
    taps = taps_ref[...].astype(F32)
    raw_scr[:rim] = halo_ref[0].astype(F32)[:rim]
    raw_scr[rim:] = qk_ref[0].astype(F32)
    for c in range(chunks):
        span = slice(c * BLOCK, (c + 1) * BLOCK)
        for kind in range(kinds):
            own = [taps[n : n + 1] for n in range(kind, taps.shape[0], kinds)]
            rows = unit_rows(mixed_rows(raw_scr, own, rim, kind, kinds, c))
            to_ref = kn_ref if kind % 2 else qn_ref
            to_ref[0, span, kind // 2 * DK : (kind // 2 + 1) * DK] = rows.astype(BF16)


def weave(*lists):
    places = []
    for which, entries in enumerate(lists):
        places += [((n + 0.5) / len(entries), which, n) for n in range(len(entries))]
    for _, which, n in sorted(places):
        lists[which][n]()


def prepare_kernel(first, count, head, group, chunks, key_heads, mixes, *refs):
    length_ref, v_ref, halo_ref, v_taps_ref, log_ref, gain_ref, after_ref = refs[:7]
    refs = refs[7:]
    if mixes:
        qk_ref, qk_taps_ref, wu_ref, start_ref, map_ref, token_ref, qn_ref, kn_ref = refs[:8]
        v_pad, m_scr, b_scr, fade_scr, st_scr, a_scr, x_scr, y_scr, raw_scr = refs[8:]
        key_columns = slice(head * DK, (head + 1) * DK)
    else:
        kn_ref, wu_ref, start_ref, map_ref, token_ref = refs[:5]
        v_pad, m_scr, b_scr, fade_scr, st_scr, a_scr, x_scr, y_scr = refs[5:]
        key_columns = slice(0, DK)
    step = pl.program_id(0)
    token_ref[...] = jnp.zeros_like(token_ref)
    used = length_ref[first + jnp.minimum(step, count - 1)] - lax.axis_index("seq") * (chunks * BLOCK)
    units = [(h, c) for c in range(chunks) for h in range(group)]
    slot = step % 2
    live = jnp.logical_and(step < count, used > 0)

    def recurrence(with_trans):
        height = DV + DK if with_trans else DV
        ops = []

        def begin():
            row = lax.broadcasted_iota(jnp.int32, (height, DK), 0)
            lane = lax.broadcasted_iota(jnp.int32, (height, DK), 1)
            for h in range(group):
                st_scr[h, :height] = jnp.where(row == lane + DV, 1.0, 0.0).astype(F32)
                if not with_trans:
                    map_ref[h, DV:] = jnp.zeros((DK, DK), BF16)

        def advance(c):
            narrow, moved = {}, {}

            def load(h):
                narrow[h] = st_scr[h, :height].astype(BF16)
                start_ref[0, h, c * (DV + DK) : c * (DV + DK) + height, :] = narrow[h]

            def move(h):
                moved[h] = dot(narrow[h], m_scr[1 - slot, c, h])

            def store(h):
                fade = fade_scr[1 - slot, c, h : h + 1, :]
                to_ref, place = (st_scr, F32) if c < chunks - 1 else (map_ref, BF16)
                state = st_scr[h, :DV] * fade + (moved[h][:DV] + b_scr[1 - slot, c, h])
                if with_trans:
                    trans = st_scr[h, DV:] * fade + moved[h][DV:]
                    to_ref[h, DV:] = trans.astype(place)
                to_ref[h, :DV] = state.astype(place)

            return [functools.partial(act, h) for act in (load, move, store) for h in range(group)]

        ops.append(begin)
        for c in range(chunks):
            ops += advance(c)
        return ops

    @pl.when(jnp.logical_not(live))
    def _():
        @pl.when(step > 0)
        def _():
            weave(recurrence(True))

        @pl.when(step < count)
        def _():
            if mixes:
                qn_ref[...] = jnp.zeros_like(qn_ref)
                kn_ref[...] = jnp.zeros_like(kn_ref)
            wu_ref[...] = jnp.zeros_like(wu_ref)
            fade_scr[slot] = jnp.ones(fade_scr.shape[1:], F32)
            m_scr[slot] = jnp.zeros(m_scr.shape[1:], BF16)
            b_scr[slot] = jnp.zeros(b_scr.shape[1:], F32)

    @pl.when(live)
    def _():
        if mixes:
            mix(qk_ref, halo_ref, qk_taps_ref, qn_ref, kn_ref, raw_scr, key_heads, chunks)
        halo = halo_ref[0].astype(F32)
        v_pad[EDGE:, :] = v_ref[0].astype(F32)
        for i in range(CONV - 1):
            for h in range(group):
                source = 2 * EDGE + (i * key_heads + head) * group + h
                v_pad[EDGE - CONV + 1 + i : EDGE - CONV + 2 + i, h * DV : (h + 1) * DV] = halo[
                    source : source + 1
                ]

    def work(with_trans, with_late):
        v_all_taps = v_taps_ref[...].astype(F32)
        v_taps = [v_all_taps[i : i + 1] for i in range(CONV)]

        cum, gain = gates_of_heads(log_ref, gain_ref, used, head, group)
        both_gains = gain * jnp.exp(cum)
        bases = block_bases([-cum], chunks)

        def span(c):
            return slice(c * BLOCK, (c + 1) * BLOCK)

        row = lax.broadcasted_iota(jnp.int32, (BLOCK, BLOCK), 0)
        lane = lax.broadcasted_iota(jnp.int32, (BLOCK, BLOCK), 1)
        above = row < lane
        small_row = lax.broadcasted_iota(jnp.int32, (TINY, BLOCK), 0)
        small_lane = lax.broadcasted_iota(jnp.int32, (TINY, BLOCK), 1)
        part_of = small_lane // TINY
        tiny_eye = jnp.where(small_row == small_lane % TINY, 1.0, 0.0).astype(F32)

        keys = [kn_ref[0, span(c), key_columns] for c in range(chunks)]
        turned = {}

        def front(some):
            ops, kk, later, compact, solved, mixed = [], {}, {}, {}, {}, {}
            local = [(h, c) for c in some for h in range(group)]

            def start(c):
                turned[c] = keys[c].T
                kk[c] = dot(keys[c], turned[c])
                later[c] = spread_squares(bases[c], group, 1)

            def mask(h, c):
                r = h * chunks + c
                strict = jnp.where(above, jnp.exp(later[c][h]) * kk[c] * -gain[h : h + 1, span(c)], 0.0)
                a_scr[r] = strict.astype(BF16)
                tiny = strict[0:TINY]
                for b in range(1, BLOCK // TINY):
                    tiny = jnp.where(part_of == b, strict[b * TINY : (b + 1) * TINY], tiny)
                compact[r] = tiny
                solved[r] = tiny_eye

            def eliminate(j, r):
                factor = jnp.take_along_axis(compact[r], part_of * TINY + j, axis=1, mode="promise_in_bounds")
                solved[r] = solved[r] + factor * solved[r][j : j + 1, :]

            def place(r):
                for b in range(BLOCK // TINY):
                    x_scr[r, b * TINY : (b + 1) * TINY, :] = jnp.where(part_of == b, solved[r], 0.0).astype(BF16)

            def convolve(c):
                mixed[c] = mixed_rows(v_pad, v_taps, EDGE, 0, 1, c).astype(BF16)

            def scale(h, c):
                top = h * (DK + DV)
                v_wide = mixed[c][:, h * DV : (h + 1) * DV].T.astype(F32)
                y_scr[c, top : top + DK, :] = (turned[c].astype(F32) * both_gains[h : h + 1, span(c)]).astype(BF16)
                y_scr[c, top + DK : top + DK + DV, :] = (v_wide * gain[h : h + 1, span(c)]).astype(BF16)

            for c in some:
                ops.append(functools.partial(start, c))
            for h, c in local:
                ops.append(functools.partial(mask, h, c))
            for j in range(TINY - 1, 0, -1):
                for h, c in local:
                    ops.append(functools.partial(eliminate, j, h * chunks + c))
            for h, c in local:
                ops.append(functools.partial(place, h * chunks + c))
            right = []
            for c in some:
                right.append(functools.partial(convolve, c))
                right += [functools.partial(scale, h, c) for h in range(group)]
            return ops, right

        def back(some):
            ops, own, moved = [], {}, {}
            local = [(h, c) for c in some for h in range(group)]

            def reach(size, r):
                half_lane = lax.broadcasted_iota(jnp.int32, (BLOCK // 2, BLOCK), 1)
                half_row = lax.broadcasted_iota(jnp.int32, (BLOCK // 2, BLOCK), 0)
                partner = half_lane // size == 2 * (half_row // size) + 1
                own[r] = jnp.concatenate([x_scr[r, s : s + size, :] for s in range(0, BLOCK, 2 * size)], axis=0)
                moved[r] = jnp.where(partner, dot(own[r], a_scr[r]), 0.0).astype(BF16)

            def join(size, r):
                update = own[r] + dot(moved[r], x_scr[r]).astype(BF16)
                for n, s in enumerate(range(0, BLOCK, 2 * size)):
                    x_scr[r, s : s + size, :] = update[n * size : (n + 1) * size]

            def solve(h, c):
                r = h * chunks + c
                top = h * (DK + DV)
                sums = cum[:, span(c)]
                last = sums[:, BLOCK - 1 : BLOCK]
                tail = jnp.exp(last - sums)
                fade = jnp.broadcast_to(jnp.exp(last), (group, BLOCK))
                rows = dot(y_scr[c, top : top + DK + DV, :], x_scr[r])
                wu_ref[0, r] = rows.astype(BF16)
                y_scr[c, top : top + DK + DV, :] = (rows * tail[h : h + 1]).astype(BF16)
                fade_scr[slot, c, h : h + 1, :] = fade[h : h + 1]

            def finish(c):
                both = dot(y_scr[c], keys[c])
                for h in range(group):
                    top = h * (DK + DV)
                    m_scr[slot, c, h] = (-both[top : top + DK]).astype(BF16)
                    b_scr[slot, c, h] = both[top + DK : top + DK + DV]

            size = TINY
            while size < BLOCK:
                ops += [functools.partial(reach, size, h * chunks + c) for h, c in local]
                ops += [functools.partial(join, size, h * chunks + c) for h, c in local]
                size *= 2
            ops += [functools.partial(solve, h, c) for h, c in local]
            ops += [functools.partial(finish, c) for c in some]
            return ops

        early, late = range(half), range(half, chunks)
        early_front, early_right = front(early)
        before = recurrence(with_trans)
        cut = len(before) // 3
        weave(early_front, before[:cut], early_right)
        if with_late:
            late_front, late_right = front(late)
            weave(back(early), late_front, late_right)
            weave(back(late), before[cut:])
        else:
            weave(back(early), before[cut:])
            for c in late:
                fade_scr[slot, c] = jnp.ones((group, BLOCK), F32)
                for h in range(group):
                    wu_ref[0, h * chunks + c] = jnp.zeros((DK + DV, BLOCK), BF16)
                    m_scr[slot, c, h] = jnp.zeros((DK, DK), BF16)
                    b_scr[slot, c, h] = jnp.zeros((DV, DK), F32)

    half = chunks // 2
    many = used > half * BLOCK
    opening = lax.axis_index("seq") == 0
    for chosen, with_trans, with_late in (
        (jnp.logical_and(many, opening), False, True),
        (jnp.logical_and(many, jnp.logical_not(opening)), True, True),
        (jnp.logical_not(many), True, False),
    ):
        pl.when(jnp.logical_and(live, chosen))(functools.partial(work, with_trans, with_late))


def prepare(job, lengths, qk_rows, v_in, halo, qk_taps, v_taps, log_decay, write_gain, key_heads, mixed, after):
    head, first, count = job
    tok = v_in.shape[1]
    value_heads = v_in.shape[2] // DV
    group = value_heads // key_heads
    chunks = tok // BLOCK
    rows = group * chunks
    wide = group * DV
    mixes = mixed is None

    def now(i):
        return jnp.minimum(i, count - 1)

    def before(i):
        return jnp.maximum(i - 1, 0)

    def whole_of(i, lengths):
        return (first + now(i), 0, 0)

    operands = [far(v_in), halo, far(v_taps), far(log_decay), far(write_gain), far(after)]
    in_specs = [
        pl.BlockSpec((1, tok, wide), lambda i, lengths: (first + now(i), 0, head)),
        pl.BlockSpec((1,) + halo.shape[1:], whole_of),
        pl.BlockSpec((CONV, wide), lambda i, lengths: (0, head)),
        pl.BlockSpec((1, value_heads, tok), whole_of),
        pl.BlockSpec((1, value_heads, tok), whole_of),
        pl.BlockSpec(memory_space=pltpu.HBM),
    ]
    out_specs = [
        pl.BlockSpec((1, rows, DK + DV, BLOCK), lambda i, lengths: (now(i), 0, 0, 0)),
        pl.BlockSpec((1, group, chunks * (DV + DK), DK), lambda i, lengths: (before(i), 0, 0, 0)),
        pl.BlockSpec((group, DV + DK, DK), lambda i, lengths: (before(i), 0, 0)),
        pl.BlockSpec((8, 128), lambda i, lengths: (0, 0)),
    ]
    out_shape = [
        pltpu.HBM((count, rows, DK + DV, BLOCK), BF16),
        pltpu.HBM((count, group, chunks * (DV + DK), DK), BF16),
        jax.ShapeDtypeStruct((count * group, DV + DK, DK), BF16),
        pltpu.HBM((8, 128), F32),
    ]
    scratch = [
        pltpu.VMEM((tok + EDGE, wide), F32),
        pltpu.VMEM((2, chunks, group, DK, DK), BF16),
        pltpu.VMEM((2, chunks, group, DV, DK), F32),
        pltpu.VMEM((2, chunks, group, BLOCK), F32),
        pltpu.VMEM((group, DV + DK, DK), F32),
        pltpu.VMEM((rows, BLOCK, BLOCK), BF16),
        pltpu.VMEM((rows, BLOCK, BLOCK), BF16),
        pltpu.VMEM((chunks, group * (DK + DV), BLOCK), BF16),
    ]
    if mixes:
        operands += [far(qk_rows), far(qk_taps)]
        in_specs += [
            pl.BlockSpec((1,) + qk_rows.shape[1:], whole_of),
            pl.BlockSpec(qk_taps.shape, lambda i, lengths: (0, 0)),
        ]
        out_specs += [pl.BlockSpec((1, tok, key_heads * DK), lambda i, lengths: (now(i), 0, 0))] * 2
        out_shape += [pltpu.HBM((count, tok, key_heads * DK), BF16)] * 2
        scratch.append(pltpu.VMEM((qk_rows.shape[1] + 2 * EDGE, DK), F32))
    else:
        operands.append(far(mixed))
        in_specs.append(pl.BlockSpec((1, tok, DK), lambda i, lengths: (first + now(i), 0, head)))
    return pl.pallas_call(
        functools.partial(prepare_kernel, first, count, head, group, chunks, key_heads, mixes),
        grid_spec=pltpu.PrefetchScalarGridSpec(
            num_scalar_prefetch=1,
            grid=(count + 1,),
            in_specs=in_specs,
            out_specs=out_specs,
            scratch_shapes=scratch,
        ),
        out_shape=out_shape,
        compiler_params=pltpu.CompilerParams(vmem_limit_bytes=VMEM_BYTES),
        cost_estimate=pl.CostEstimate(flops=5 * 10**9 * count, bytes_accessed=4 * 2**20 * count, transcendentals=10**6),
        name="prepare",
    )(far(lengths), *operands)


def outputs_kernel(
    first, head, group, chunks,
    length_ref, qn_ref, kn_ref, wu_ref, start_ref, log_ref, gain_ref, enter_ref, z_ref, norm_ref, held_ref, after_ref,
    out_ref,
    first_scr, score_scr, seen_scr,
):
    used = length_ref[first + pl.program_id(0)] - lax.axis_index("seq") * (chunks * BLOCK)
    units = [(h, c) for c in range(chunks) for h in range(group)]

    @pl.when(used <= 0)
    def _():
        out_ref[...] = jnp.zeros_like(out_ref)

    def work(with_enter, blocks):
        units = [(h, c) for c in blocks for h in range(group)]
        cum, gain = gates_of_heads(log_ref, gain_ref, used, head, group)
        faded = jnp.exp(cum)
        columns = as_columns(jnp.concatenate([cum] * (8 // group), axis=0), chunks)
        row = lax.broadcasted_iota(jnp.int32, (BLOCK, BLOCK), 0)
        lane = lax.broadcasted_iota(jnp.int32, (BLOCK, BLOCK), 1)
        upto = row <= lane
        norm_gain = norm_ref[...]

        def span(c):
            return slice(c * BLOCK, (c + 1) * BLOCK)

        for c in blocks:
            turned = qn_ref[0, span(c), :].T
            kq = dot(kn_ref[0, span(c), :], turned)
            q_wide = turned.astype(F32)
            for h in range(group):
                r = h * chunks + c
                ratio = jnp.exp(cum[h : h + 1, span(c)] - columns[:, c * 8 + h : c * 8 + h + 1])
                score_scr[r] = jnp.where(upto, ratio * kq, 0.0).astype(BF16)
                seen_scr[r] = q_wide * faded[h : h + 1, span(c)]
                top = c * (DV + DK)
                first = start_ref[0, h, top : top + DV, :]
                if with_enter:
                    moved = dot(enter_ref[h], start_ref[0, h, top + DV : top + DV + DK, :])
                    first = (moved + first.astype(F32)).astype(BF16)
                first_scr[r] = first
        both, raws = {}, {}
        for h, c in units:
            r = h * chunks + c
            both[r] = dot(wu_ref[0, r], score_scr[r])
        for h, c in units:
            r = h * chunks + c
            seen = (seen_scr[r] - both[r][:DK]).astype(BF16)
            raw = dot(first_scr[r], seen) + both[r][DK:]
            mean = jnp.sum(raw * raw, axis=0, keepdims=True) * (1.0 / DV)
            raws[r] = (raw * lax.rsqrt(mean + EPSILON)).astype(BF16)
        for h, c in units:
            scaled = raws[h * chunks + c].T.astype(F32)
            cols = slice(h * DV, (h + 1) * DV)
            gated = scaled * norm_gain * silu(z_ref[0, span(c), cols].astype(F32))
            out_ref[0, span(c), cols] = jnp.where(row + c * BLOCK < used, gated, 0.0).astype(BF16)
        for c in range(len(blocks), chunks):
            out_ref[0, span(c), :] = jnp.zeros((BLOCK, group * DV), BF16)

    half = chunks // 2
    many = used > half * BLOCK
    opening = lax.axis_index("seq") == 0
    for first_device in (True, False):
        here = opening if first_device else jnp.logical_not(opening)
        for full in (True, False):
            chosen = many if full else jnp.logical_and(used > 0, jnp.logical_not(many))
            blocks = range(chunks if full else half)
            pl.when(jnp.logical_and(here, chosen))(functools.partial(work, not first_device, blocks))


def outputs(
    job, piece, lengths, qn, kn, wu, starts, log_decay, write_gain, enter, gate_z, norm_gain, key_heads, held, after,
):
    head, first, _ = job
    begin, count = piece
    prompts, tok, width = gate_z.shape
    rows = wu.shape[1]
    chunks = tok // BLOCK
    group = rows // chunks
    wide = group * DV
    value_heads = key_heads * group
    shift = begin - first
    from_mix = begin if qn.shape[0] == prompts else shift

    def whole_of(i, lengths):
        return (begin + i, 0, 0)

    def wide_of(i, lengths):
        return (begin + i, 0, head)

    def mixed_of(i, lengths):
        return (from_mix + i, 0, head)

    empty = held is None
    return pl.pallas_call(
        functools.partial(outputs_kernel, begin, head, group, chunks),
        grid_spec=pltpu.PrefetchScalarGridSpec(
            num_scalar_prefetch=1,
            grid=(count,),
            in_specs=[
                pl.BlockSpec((1, tok, DK), mixed_of),
                pl.BlockSpec((1, tok, DK), mixed_of),
                pl.BlockSpec((1, rows, DK + DV, BLOCK), lambda i, lengths: (shift + i, 0, 0, 0)),
                pl.BlockSpec((1, group, chunks * (DV + DK), DK), lambda i, lengths: (shift + i, 0, 0, 0)),
                pl.BlockSpec((1, value_heads, tok), whole_of),
                pl.BlockSpec((1, value_heads, tok), whole_of),
                pl.BlockSpec((group, DK, DV), lambda i, lengths: (shift + i, 0, 0)),
                pl.BlockSpec((1, tok, wide), wide_of),
                pl.BlockSpec((1, DV), lambda i, lengths: (0, 0)),
                pl.BlockSpec(memory_space=pltpu.HBM),
                pl.BlockSpec(memory_space=pltpu.HBM),
            ],
            out_specs=pl.BlockSpec((1, tok, wide), wide_of),
            scratch_shapes=[
                pltpu.VMEM((rows, DV, DK), BF16),
                pltpu.VMEM((rows, BLOCK, BLOCK), BF16),
                pltpu.VMEM((rows, BLOCK, DV), F32),
            ],
        ),
        out_shape=pltpu.HBM((prompts, tok, width), BF16),
        input_output_aliases={} if empty else {10: 0},
        compiler_params=pltpu.CompilerParams(vmem_limit_bytes=VMEM_BYTES),
        cost_estimate=pl.CostEstimate(flops=3 * 10**9 * count, bytes_accessed=4 * 2**20 * count, transcendentals=10**6),
        name="outputs",
    )(
        far(lengths), far(qn), far(kn), far(wu), far(starts), far(log_decay), far(write_gain), enter, far(gate_z),
        far(norm_gain.reshape(1, DV)), far(after if empty else held), far(norm_gain.reshape(1, DV) if after is held else after),
    )


def own_chip():
    seq = lax.axis_index("seq")
    return seq // 2, seq % 2 == 1


def early_late(own, other, odd):
    return jnp.where(odd, other, own), jnp.where(odd, own, other)


def follow(there, running):
    return dot(running, there[DV:])


def compose_maps(ins, outs):
    own_ref, other_ref = ins
    _, odd = own_chip()
    for n in range(own_ref.shape[0]):
        early, late = early_late(own_ref[n], other_ref[n], odd)
        both = follow(late, early)
        outs[0][n, :DV] = (both[:DV] + late[:DV].astype(F32)).astype(BF16)
        outs[0][n, DV:] = both[DV:].astype(BF16)


def close_maps(ins, outs):
    own_ref, other_ref = ins[:2]
    refs = ins[2:]
    chips = len(refs)
    chip, odd = own_chip()

    def of_chip(j, n):
        value = refs[0][n]
        for k in range(1, chips):
            value = jnp.where((chip + chips - k) % chips == j, refs[k][n], value)
        return value

    every = range(own_ref.shape[0])
    running = [of_chip(0, n)[:DV] for n in every]
    entering = [jnp.zeros_like(running[n]) for n in every]
    for j in range(1, chips):
        entering = [jnp.where(chip == j, running[n], entering[n]) for n in every]
        there = [of_chip(j, n) for n in every]
        running = [(follow(there[n], running[n]) + there[n][:DV].astype(F32)).astype(BF16) for n in every]
    for n in every:
        early, _ = early_late(own_ref[n], other_ref[n], odd)
        second = (follow(early, entering[n]) + early[:DV].astype(F32)).astype(BF16)
        outs[0][n] = jnp.where(odd, second, entering[n])
        outs[1][n] = running[n].T


def chain_maps(ins, outs):
    count = len(ins)
    mine = lax.axis_index("seq")
    every = range(ins[0].shape[0])

    def run(at):
        running = [ins[at][n, :DV] for n in every]
        for n in every:
            if at == 0:
                outs[0][n] = jnp.zeros_like(running[n])
        for j in range(1, count):
            there = ins[at ^ j]
            if j == at:
                for n in every:
                    outs[0][n] = running[n]
            moved = [follow(there.at[n], running[n]) for n in every]
            running = [(moved[n] + there[n, :DV].astype(F32)).astype(BF16) for n in every]
        for n in every:
            outs[1][n] = running[n].T

    for at in range(count):
        pl.when(mine == at)(functools.partial(run, at))


def choose_finals(group, placement_ref, finals, outs):
    refs = [(ref, n) for ref in finals for n in range(ref.shape[0] // group)]
    for r in range(placement_ref.shape[1]):
        prompt = placement_ref[0, r]
        for p, (ref, n) in enumerate(refs):
            @pl.when(prompt == p)
            def _(ref=ref, n=n):
                outs[0][r] = ref[n * group : (n + 1) * group]


def state_step(placement, group, compose, chain, close, earlier, after):
    operands, shapes = [placement], []
    steps = []
    if compose is not None:
        steps.append(("compose", len(operands), len(compose), len(shapes)))
        operands += compose
        shapes += [compose[0]]
    if chain is not None or close is not None:
        steps.append(("chain" if close is None else "close", len(operands), len(close or chain), len(shapes)))
        close = close or chain
        operands += close
        shapes += [jax.ShapeDtypeStruct((close[0].shape[0], DK, DV), BF16)] * 2
        if earlier is not None:
            steps.append(("choose", len(operands), len(earlier), len(shapes)))
            operands += earlier
            shapes.append(jax.ShapeDtypeStruct((placement.shape[1], group, DK, DV), BF16))
    out_shape = [jax.ShapeDtypeStruct(x.shape, x.dtype) for x in shapes] + [pltpu.HBM((8, 128), F32)]

    def kernel(*refs):
        refs[-1][...] = jnp.zeros_like(refs[-1])
        ins, outs = refs[: len(operands)], refs[len(operands) + 1 :]
        closed = None
        for kind, at, size, to in steps:
            part = ins[at : at + size]
            if kind == "compose":
                compose_maps(part, outs[to : to + 1])
            elif kind in ("close", "chain"):
                (close_maps if kind == "close" else chain_maps)(part, outs[to : to + 2])
                closed = outs[to + 1]
            else:
                choose_finals(group, ins[0], list(part) + [closed], outs[to:])

    vmem = pl.BlockSpec(memory_space=pltpu.VMEM)
    return pl.pallas_call(
        kernel,
        in_specs=[pl.BlockSpec(memory_space=pltpu.SMEM)]
        + [vmem] * (len(operands) - 1)
        + [pl.BlockSpec(memory_space=pltpu.HBM)],
        out_specs=[vmem] * len(out_shape),
        out_shape=out_shape,
        compiler_params=pltpu.CompilerParams(vmem_limit_bytes=SMALL_VMEM_BYTES),
        cost_estimate=pl.CostEstimate(flops=10**9, bytes_accessed=2**20, transcendentals=0),
        name="state_step",
    )(*operands, far(after))


def deliver(parts):
    count, group = parts[0].shape[:2]

    def kernel(*refs):
        for n, ref in enumerate(refs[:-1]):
            refs[-1][:, n * group : (n + 1) * group] = ref[...].astype(F32)

    return pl.pallas_call(
        kernel,
        grid=(2,),
        in_specs=[pl.BlockSpec((count // 2, group, DK, DV), lambda i: (i, 0, 0, 0))] * len(parts),
        out_specs=pl.BlockSpec((count // 2, group * len(parts), DK, DV), lambda i: (i, 0, 0, 0)),
        out_shape=jax.ShapeDtypeStruct((count, group * len(parts), DK, DV), F32),
        compiler_params=pltpu.CompilerParams(vmem_limit_bytes=VMEM_BYTES),
        name="deliver",
    )(*parts)


def across(block, distance):
    count = lax.axis_size("seq")
    return lax.ppermute(block, "seq", [(i, i ^ distance) for i in range(count)])


def from_chip_behind(block, distance):
    count = lax.axis_size("seq")
    chips = count // 2
    route = [(i, ((i // 2 + distance) % chips) * 2 + i % 2) for i in range(count)]
    return lax.ppermute(block, "seq", route)


def shards(
    qk_in, v_in, gate_z, conv_qk, conv_v, log_decay, write_gain, norm_gain, prompt_lengths, placement,
):
    prompts, tok = qk_in.shape[:2]
    key_heads = qk_in.shape[3] // DK
    value_heads = v_in.shape[2] // DV
    rim = CONV - 1
    seq_count = lax.axis_size("seq")
    head_count = lax.axis_size("head")

    def by_head(x):
        x = x.reshape(x.shape[0], x.shape[1], 2, key_heads, DK)
        return jnp.transpose(x, (0, 1, 3, 2, 4)).reshape(x.shape[0], -1, DK)

    qk_rows = by_head(qk_in)
    qk_taps = by_head(conv_qk[None])[0]
    qk_tail = qk_rows[:, (tok - rim) * 2 * key_heads :]
    v_tail = v_in[:, tok - rim :].reshape(prompts, rim * value_heads, DV)
    front = 2 * EDGE - qk_tail.shape[1]
    back = 2 * EDGE - v_tail.shape[1]
    tails = jnp.concatenate(
        [
            jnp.zeros((prompts, front, DK), BF16),
            qk_tail,
            v_tail,
            jnp.zeros((prompts, back, DK), BF16),
        ],
        axis=1,
    )
    halo = lax.ppermute(tails, "seq", [(i, i + 1) for i in range(seq_count - 1)])
    group = value_heads // key_heads
    chips = seq_count // 2
    half = prompts // 2
    jobs = [(head, 0, prompts) for head in range(key_heads)]
    if key_heads == 1:
        jobs = [(0, 0, half), (0, half, prompts - half)]
    total = len(jobs)
    made, finals, sent = [], [], {}
    attended = None
    last = v_in

    def finish(job, results):
        head = jobs[job][0]
        finals.append(results[1])
        if len(results) > 3:
            sent[head] = lax.all_to_all(results[2], "head", 0, 0)
        return results[0], results[-1]

    def earlier(job):
        same = [n for n in range(total) if jobs[n][0] == jobs[job][0]]
        return [finals[n] for n in same[:-1]] if job == same[-1] else None

    def emit(job, entered, attended, last):
        qn, kn, wu, starts, _ = made[job]
        return outputs(
            jobs[job], jobs[job][1:], prompt_lengths, qn, kn, wu, starts, log_decay, write_gain,
            entered, gate_z, norm_gain, key_heads, attended, last,
        )

    for job in jobs:
        mixed = None if job[0] == 0 else made[0][:2]
        wu, starts, own_map, last, *new = prepare(
            job, prompt_lengths, qk_rows, v_in, halo, qk_taps, conv_v, log_decay, write_gain, key_heads,
            mixed and mixed[1], last,
        )
        moved = [own_map]
        if job == jobs[-1]:
            moved.append(across(own_map, 1))
        else:
            moved += [across(own_map, k) for k in range(1, seq_count)]
        made.append((*(mixed or new), wu, starts, moved))

    entered = []
    for job in range(total - 1):
        results = state_step(placement, group, None, made[job][4], None, earlier(job), last)
        enter, last = finish(job, results)
        entered.append(enter)
    pair = made[-1][4]
    chip_map, last = state_step(placement, group, pair, None, None, None, last)
    chip_maps = [chip_map] + [from_chip_behind(chip_map, k) for k in range(1, chips)]
    for job in range(total - 1):
        attended = last = emit(job, entered[job], attended, last)
    results = state_step(placement, group, None, None, pair + chip_maps, earlier(total - 1), last)
    enter, last = finish(total - 1, results)
    attended = emit(total - 1, enter, attended, last)
    rollout = deliver([sent[head] for head in range(key_heads)])
    return attended, rollout.reshape(1, 1, head_count * value_heads, DK, DV)


def solution(mesh):
    return jax.shard_map(
        shards,
        mesh=mesh,
        in_specs=(
            P(None, "seq", None, "head"),
            P(None, "seq", "head"),
            P(None, "seq", "head"),
            P(None, None, "head"),
            P(None, "head"),
            P(None, "head", "seq"),
            P(None, "head", "seq"),
            P(),
            P(),
            P("seq", None),
        ),
        out_specs=(P(None, "seq", "head"), P("seq", "head", None, None, None)),
        check_vma=False,
    )
```

```python
import functools

import jax
import jax.numpy as jnp
from jax import lax
from jax.experimental import pallas as pl
from jax.experimental.pallas import tpu as pltpu
from jax.sharding import PartitionSpec as P

DK = 128
DV = 128
CONV = 4
BLOCK = 128
TINY = 16
EDGE = 8
EPSILON = 1e-06
VMEM_BYTES = 40 * 1024 * 1024
SMALL_VMEM_BYTES = 8 * 1024 * 1024
F32 = jnp.float32
BF16 = jnp.bfloat16


def far(x):
    return pltpu.with_memory_space_constraint(x, pltpu.HBM)


def dot(a, b):
    return lax.dot_general(a, b, (((1,), (0,)), ((), ())), preferred_element_type=F32)


def silu(x):
    half = 0.5 * x
    return half + half * jnp.tanh(half)


def mixed_rows(pad_ref, taps, rim, first, step, c):
    total = None
    for i in range(CONV):
        start = rim + first + step * (c * BLOCK + i - (CONV - 1))
        stride = None if step == 1 else step
        term = pad_ref[pl.ds(start, BLOCK, stride), :] * taps[i]
        total = term if total is None else total + term
    return silu(total)


def unit_rows(x):
    return x * lax.rsqrt(jnp.sum(x * x, axis=-1, keepdims=True) + EPSILON)


def heads_rows(ref, head, group):
    every = ref[0]
    rows = every[:group]
    for n in range(1, every.shape[0] // group):
        rows = jnp.where(head == n, every[n * group : (n + 1) * group], rows)
    return rows


def gates_of_heads(log_ref, gain_ref, used, head, group):
    log = heads_rows(log_ref, head, group)
    lane = lax.broadcasted_iota(jnp.int32, log.shape, 1)
    valid = lane < used
    cum = jnp.where(valid, log, 0.0)
    gain = jnp.where(valid, heads_rows(gain_ref, head, group), 0.0)
    shift = 1
    while shift < BLOCK:
        cum = cum + jnp.where(lane % BLOCK >= shift, pltpu.roll(cum, shift, 1), 0.0)
        shift *= 2
    return cum, gain


def as_columns(rows, chunks):
    parts = [rows[:, c * BLOCK : (c + 1) * BLOCK] for c in range(chunks)]
    short = BLOCK - 8 * chunks
    if short:
        parts.append(jnp.zeros((short, BLOCK), F32))
    return jnp.concatenate(parts, axis=0).T


def block_bases(parts, chunks):
    rows = jnp.concatenate(parts, axis=0)
    short = 7 - rows.shape[0]
    fill = [jnp.zeros((short, rows.shape[1]), F32)] if short else []
    rows = jnp.concatenate([rows] + fill + [jnp.ones((1, rows.shape[1]), F32)], axis=0)
    return [rows[:, c * BLOCK : (c + 1) * BLOCK] for c in range(chunks)]


def spread_squares(base, group, kinds):
    high = base.astype(BF16).astype(F32)
    middle = (base - high).astype(BF16).astype(F32)
    low = base - high - middle
    parts = [high, middle, low]
    row = lax.broadcasted_iota(jnp.int32, (32, BLOCK), 0)
    which = row % 8
    real = row < 24
    stacked = jnp.concatenate(parts + [jnp.zeros_like(high)], axis=0)
    left = jnp.where(jnp.logical_and(which == 7, real), 1.0, stacked).T.astype(BF16)
    blocks = []
    for h in range(group):
        minus = jnp.concatenate([jnp.broadcast_to(-part[h : h + 1], (8, BLOCK)) for part in parts + [low]], axis=0)
        blocks.append(jnp.where(which == h, 1.0, jnp.where(which == 7, minus, 0.0)))
    for n in range(group, group * kinds):
        blocks.append(jnp.where(which == n, 1.0, 0.0).astype(F32))
    every = dot(left, jnp.concatenate(blocks, axis=1).astype(BF16))
    return [every[:, n * BLOCK : (n + 1) * BLOCK] for n in range(group * kinds)]


def mix(qk_ref, halo_ref, taps_ref, qn_ref, kn_ref, raw_scr, key_heads, chunks):
    kinds = 2 * key_heads
    rim = 2 * EDGE
    taps = taps_ref[...].astype(F32)
    raw_scr[:rim] = halo_ref[0].astype(F32)[:rim]
    raw_scr[rim:] = qk_ref[0].astype(F32)
    for c in range(chunks):
        span = slice(c * BLOCK, (c + 1) * BLOCK)
        for kind in range(kinds):
            own = [taps[n : n + 1] for n in range(kind, taps.shape[0], kinds)]
            rows = unit_rows(mixed_rows(raw_scr, own, rim, kind, kinds, c))
            to_ref = kn_ref if kind % 2 else qn_ref
            to_ref[0, span, kind // 2 * DK : (kind // 2 + 1) * DK] = rows.astype(BF16)


def weave(*lists):
    places = []
    for which, entries in enumerate(lists):
        places += [((n + 0.5) / len(entries), which, n) for n in range(len(entries))]
    for _, which, n in sorted(places):
        lists[which][n]()


def prepare_kernel(first, count, head, group, chunks, key_heads, mixes, *refs):
    length_ref, v_ref, halo_ref, v_taps_ref, log_ref, gain_ref, after_ref = refs[:7]
    refs = refs[7:]
    if mixes:
        qk_ref, qk_taps_ref, wu_ref, start_ref, map_ref, token_ref, qn_ref, kn_ref = refs[:8]
        v_pad, m_scr, b_scr, fade_scr, st_scr, a_scr, x_scr, y_scr, raw_scr = refs[8:]
        key_columns = slice(head * DK, (head + 1) * DK)
    else:
        kn_ref, wu_ref, start_ref, map_ref, token_ref = refs[:5]
        v_pad, m_scr, b_scr, fade_scr, st_scr, a_scr, x_scr, y_scr = refs[5:]
        key_columns = slice(0, DK)
    step = pl.program_id(0)
    token_ref[...] = jnp.zeros_like(token_ref)
    used = length_ref[first + jnp.minimum(step, count - 1)] - lax.axis_index("seq") * (chunks * BLOCK)
    units = [(h, c) for c in range(chunks) for h in range(group)]
    slot = step % 2
    live = jnp.logical_and(step < count, used > 0)

    def begin():
        row = lax.broadcasted_iota(jnp.int32, (DV + DK, DK), 0)
        lane = lax.broadcasted_iota(jnp.int32, (DV + DK, DK), 1)
        for h in range(group):
            st_scr[h] = jnp.where(row == lane + DV, 1.0, 0.0).astype(F32)

    def advance(c):
        narrow, moved = {}, {}

        def load(h):
            narrow[h] = st_scr[h].astype(BF16)
            start_ref[0, h, c * (DV + DK) : (c + 1) * (DV + DK), :] = narrow[h]

        def move(h):
            moved[h] = dot(narrow[h], m_scr[1 - slot, c, h])

        def store(h):
            fade = fade_scr[1 - slot, c, h : h + 1, :]
            state = st_scr[h, :DV] * fade + (moved[h][:DV] + b_scr[1 - slot, c, h])
            trans = st_scr[h, DV:] * fade + moved[h][DV:]
            if c < chunks - 1:
                st_scr[h, :DV] = state
                st_scr[h, DV:] = trans
            else:
                map_ref[h, :DV] = state.astype(BF16)
                map_ref[h, DV:] = trans.astype(BF16)

        return [functools.partial(act, h) for act in (load, move, store) for h in range(group)]

    recurrence = [begin]
    for c in range(chunks):
        recurrence += advance(c)

    @pl.when(jnp.logical_not(live))
    def _():
        @pl.when(step > 0)
        def _():
            weave(recurrence)

        @pl.when(step < count)
        def _():
            if mixes:
                qn_ref[...] = jnp.zeros_like(qn_ref)
                kn_ref[...] = jnp.zeros_like(kn_ref)
            wu_ref[...] = jnp.zeros_like(wu_ref)
            fade_scr[slot] = jnp.ones(fade_scr.shape[1:], F32)
            m_scr[slot] = jnp.zeros(m_scr.shape[1:], BF16)
            b_scr[slot] = jnp.zeros(b_scr.shape[1:], F32)

    @pl.when(live)
    def _():
        if mixes:
            mix(qk_ref, halo_ref, qk_taps_ref, qn_ref, kn_ref, raw_scr, key_heads, chunks)
        halo = halo_ref[0].astype(F32)
        for h in range(group):
            columns = slice(h * DV, (h + 1) * DV)
            v_pad[pl.ds(EDGE + h, chunks * BLOCK, group), :] = v_ref[0, :, columns].astype(F32)
        for i in range(CONV - 1):
            for h in range(group):
                source = 2 * EDGE + (i * key_heads + head) * group + h
                to = EDGE + (i - CONV + 1) * group + h
                v_pad[to : to + 1, :] = halo[source : source + 1]
        v_all_taps = v_taps_ref[...].astype(F32)
        v_taps = [[v_all_taps[i : i + 1, h * DV : (h + 1) * DV] for i in range(CONV)] for h in range(group)]

        cum, gain = gates_of_heads(log_ref, gain_ref, used, head, group)
        both_gains = gain * jnp.exp(cum)
        bases = block_bases([-cum], chunks)

        def span(c):
            return slice(c * BLOCK, (c + 1) * BLOCK)

        row = lax.broadcasted_iota(jnp.int32, (BLOCK, BLOCK), 0)
        lane = lax.broadcasted_iota(jnp.int32, (BLOCK, BLOCK), 1)
        above = row < lane
        small_row = lax.broadcasted_iota(jnp.int32, (TINY, BLOCK), 0)
        small_lane = lax.broadcasted_iota(jnp.int32, (TINY, BLOCK), 1)
        part_of = small_lane // TINY
        tiny_eye = jnp.where(small_row == small_lane % TINY, 1.0, 0.0).astype(F32)

        keys = [kn_ref[0, span(c), key_columns] for c in range(chunks)]
        turned = {}

        def front(some):
            ops, kk, later, compact, solved = [], {}, {}, {}, {}
            local = [(h, c) for c in some for h in range(group)]

            def start(c):
                turned[c] = keys[c].T
                kk[c] = dot(keys[c], turned[c])
                later[c] = spread_squares(bases[c], group, 1)

            def mask(h, c):
                r = h * chunks + c
                strict = jnp.where(above, jnp.exp(later[c][h]) * kk[c] * -gain[h : h + 1, span(c)], 0.0)
                a_scr[r] = strict.astype(BF16)
                tiny = strict[0:TINY]
                for b in range(1, BLOCK // TINY):
                    tiny = jnp.where(part_of == b, strict[b * TINY : (b + 1) * TINY], tiny)
                compact[r] = tiny
                solved[r] = tiny_eye

            def eliminate(j, r):
                factor = jnp.take_along_axis(compact[r], part_of * TINY + j, axis=1, mode="promise_in_bounds")
                solved[r] = solved[r] + factor * solved[r][j : j + 1, :]

            def place(r):
                for b in range(BLOCK // TINY):
                    x_scr[r, b * TINY : (b + 1) * TINY, :] = jnp.where(part_of == b, solved[r], 0.0).astype(BF16)

            def scale(h, c):
                top = h * (DK + DV)
                v_wide = mixed_rows(v_pad, v_taps[h], EDGE, h, group, c).astype(BF16).T.astype(F32)
                y_scr[c, top : top + DK, :] = (turned[c].astype(F32) * both_gains[h : h + 1, span(c)]).astype(BF16)
                y_scr[c, top + DK : top + DK + DV, :] = (v_wide * gain[h : h + 1, span(c)]).astype(BF16)

            for c in some:
                ops.append(functools.partial(start, c))
            for h, c in local:
                ops.append(functools.partial(mask, h, c))
            for j in range(TINY - 1, 0, -1):
                for h, c in local:
                    ops.append(functools.partial(eliminate, j, h * chunks + c))
            for h, c in local:
                ops.append(functools.partial(place, h * chunks + c))
            right = []
            for c in some:
                right += [functools.partial(scale, h, c) for h in range(group)]
            return ops, right

        def back(some):
            ops, own, moved = [], {}, {}
            local = [(h, c) for c in some for h in range(group)]

            def reach(size, r):
                half_lane = lax.broadcasted_iota(jnp.int32, (BLOCK // 2, BLOCK), 1)
                half_row = lax.broadcasted_iota(jnp.int32, (BLOCK // 2, BLOCK), 0)
                partner = half_lane // size == 2 * (half_row // size) + 1
                own[r] = jnp.concatenate([x_scr[r, s : s + size, :] for s in range(0, BLOCK, 2 * size)], axis=0)
                moved[r] = jnp.where(partner, dot(own[r], a_scr[r]), 0.0).astype(BF16)

            def join(size, r):
                update = own[r] + dot(moved[r], x_scr[r]).astype(BF16)
                for n, s in enumerate(range(0, BLOCK, 2 * size)):
                    x_scr[r, s : s + size, :] = update[n * size : (n + 1) * size]

            def solve(h, c):
                r = h * chunks + c
                top = h * (DK + DV)
                sums = cum[:, span(c)]
                last = sums[:, BLOCK - 1 : BLOCK]
                tail = jnp.exp(last - sums)
                fade = jnp.broadcast_to(jnp.exp(last), (group, BLOCK))
                rows = dot(y_scr[c, top : top + DK + DV, :], x_scr[r])
                wu_ref[0, r] = rows.astype(BF16)
                y_scr[c, top : top + DK + DV, :] = (rows * tail[h : h + 1]).astype(BF16)
                fade_scr[slot, c, h : h + 1, :] = fade[h : h + 1]

            def finish(c):
                both = dot(y_scr[c], keys[c])
                for h in range(group):
                    top = h * (DK + DV)
                    m_scr[slot, c, h] = (-both[top : top + DK]).astype(BF16)
                    b_scr[slot, c, h] = both[top + DK : top + DK + DV]

            size = TINY
            while size < BLOCK:
                ops += [functools.partial(reach, size, h * chunks + c) for h, c in local]
                ops += [functools.partial(join, size, h * chunks + c) for h, c in local]
                size *= 2
            ops += [functools.partial(solve, h, c) for h, c in local]
            ops += [functools.partial(finish, c) for c in some]
            return ops

        half = chunks // 2
        early, late = range(half), range(half, chunks)
        early_front, early_right = front(early)
        late_front, late_right = front(late)
        cut = len(recurrence) // 3
        weave(early_front, recurrence[:cut], early_right)
        weave(back(early), late_front, late_right)
        weave(back(late), recurrence[cut:])


def prepare(job, lengths, qk_rows, v_in, halo, qk_taps, v_taps, log_decay, write_gain, key_heads, mixed, after):
    head, first, count = job
    tok = v_in.shape[1]
    value_heads = v_in.shape[2] // DV
    group = value_heads // key_heads
    chunks = tok // BLOCK
    rows = group * chunks
    wide = group * DV
    mixes = mixed is None

    def now(i):
        return jnp.minimum(i, count - 1)

    def before(i):
        return jnp.maximum(i - 1, 0)

    def whole_of(i, lengths):
        return (first + now(i), 0, 0)

    operands = [far(v_in), halo, far(v_taps), far(log_decay), far(write_gain), far(after)]
    in_specs = [
        pl.BlockSpec((1, tok, wide), lambda i, lengths: (first + now(i), 0, head)),
        pl.BlockSpec((1,) + halo.shape[1:], whole_of),
        pl.BlockSpec((CONV, wide), lambda i, lengths: (0, head)),
        pl.BlockSpec((1, value_heads, tok), whole_of),
        pl.BlockSpec((1, value_heads, tok), whole_of),
        pl.BlockSpec(memory_space=pltpu.HBM),
    ]
    out_specs = [
        pl.BlockSpec((1, rows, DK + DV, BLOCK), lambda i, lengths: (now(i), 0, 0, 0)),
        pl.BlockSpec((1, group, chunks * (DV + DK), DK), lambda i, lengths: (before(i), 0, 0, 0)),
        pl.BlockSpec((group, DV + DK, DK), lambda i, lengths: (before(i), 0, 0)),
        pl.BlockSpec((8, 128), lambda i, lengths: (0, 0)),
    ]
    out_shape = [
        pltpu.HBM((count, rows, DK + DV, BLOCK), BF16),
        pltpu.HBM((count, group, chunks * (DV + DK), DK), BF16),
        jax.ShapeDtypeStruct((count * group, DV + DK, DK), BF16),
        pltpu.HBM((8, 128), F32),
    ]
    scratch = [
        pltpu.VMEM((tok * group + EDGE, DV), F32),
        pltpu.VMEM((2, chunks, group, DK, DK), BF16),
        pltpu.VMEM((2, chunks, group, DV, DK), F32),
        pltpu.VMEM((2, chunks, group, BLOCK), F32),
        pltpu.VMEM((group, DV + DK, DK), F32),
        pltpu.VMEM((rows, BLOCK, BLOCK), BF16),
        pltpu.VMEM((rows, BLOCK, BLOCK), BF16),
        pltpu.VMEM((chunks, group * (DK + DV), BLOCK), BF16),
    ]
    if mixes:
        operands += [far(qk_rows), far(qk_taps)]
        in_specs += [
            pl.BlockSpec((1,) + qk_rows.shape[1:], whole_of),
            pl.BlockSpec(qk_taps.shape, lambda i, lengths: (0, 0)),
        ]
        out_specs += [pl.BlockSpec((1, tok, key_heads * DK), lambda i, lengths: (now(i), 0, 0))] * 2
        out_shape += [pltpu.HBM((count, tok, key_heads * DK), BF16)] * 2
        scratch.append(pltpu.VMEM((qk_rows.shape[1] + 2 * EDGE, DK), F32))
    else:
        operands.append(far(mixed))
        in_specs.append(pl.BlockSpec((1, tok, DK), lambda i, lengths: (first + now(i), 0, head)))
    return pl.pallas_call(
        functools.partial(prepare_kernel, first, count, head, group, chunks, key_heads, mixes),
        grid_spec=pltpu.PrefetchScalarGridSpec(
            num_scalar_prefetch=1,
            grid=(count + 1,),
            in_specs=in_specs,
            out_specs=out_specs,
            scratch_shapes=scratch,
        ),
        out_shape=out_shape,
        compiler_params=pltpu.CompilerParams(vmem_limit_bytes=VMEM_BYTES),
        cost_estimate=pl.CostEstimate(flops=5 * 10**9 * count, bytes_accessed=4 * 2**20 * count, transcendentals=10**6),
        name="prepare",
    )(far(lengths), *operands)


def outputs_kernel(
    first, head, group, chunks,
    length_ref, qn_ref, kn_ref, wu_ref, start_ref, log_ref, gain_ref, enter_ref, z_ref, norm_ref, held_ref, after_ref,
    out_ref,
    first_scr, score_scr, seen_scr,
):
    used = length_ref[first + pl.program_id(0)] - lax.axis_index("seq") * (chunks * BLOCK)
    units = [(h, c) for c in range(chunks) for h in range(group)]

    @pl.when(used <= 0)
    def _():
        out_ref[...] = jnp.zeros_like(out_ref)

    @pl.when(used > 0)
    def _():
        cum, gain = gates_of_heads(log_ref, gain_ref, used, head, group)
        faded = jnp.exp(cum)
        columns = as_columns(jnp.concatenate([cum] * (8 // group), axis=0), chunks)
        row = lax.broadcasted_iota(jnp.int32, (BLOCK, BLOCK), 0)
        lane = lax.broadcasted_iota(jnp.int32, (BLOCK, BLOCK), 1)
        upto = row <= lane
        norm_gain = norm_ref[...]

        def span(c):
            return slice(c * BLOCK, (c + 1) * BLOCK)

        for c in range(chunks):
            turned = qn_ref[0, span(c), :].T
            kq = dot(kn_ref[0, span(c), :], turned)
            q_wide = turned.astype(F32)
            for h in range(group):
                r = h * chunks + c
                ratio = jnp.exp(cum[h : h + 1, span(c)] - columns[:, c * 8 + h : c * 8 + h + 1])
                score_scr[r] = jnp.where(upto, ratio * kq, 0.0).astype(BF16)
                seen_scr[r] = q_wide * faded[h : h + 1, span(c)]
                top = c * (DV + DK)
                moved = dot(enter_ref[h], start_ref[0, h, top + DV : top + DV + DK, :])
                first_scr[r] = (moved + start_ref[0, h, top : top + DV, :].astype(F32)).astype(BF16)
        both, raws = {}, {}
        for h, c in units:
            r = h * chunks + c
            both[r] = dot(wu_ref[0, r], score_scr[r])
        for h, c in units:
            r = h * chunks + c
            seen = (seen_scr[r] - both[r][:DK]).astype(BF16)
            raw = dot(first_scr[r], seen) + both[r][DK:]
            mean = jnp.sum(raw * raw, axis=0, keepdims=True) * (1.0 / DV)
            raws[r] = (raw * lax.rsqrt(mean + EPSILON)).astype(BF16)
        for h, c in units:
            scaled = raws[h * chunks + c].T.astype(F32)
            cols = slice(h * DV, (h + 1) * DV)
            gated = scaled * norm_gain * silu(z_ref[0, span(c), cols].astype(F32))
            out_ref[0, span(c), cols] = jnp.where(row + c * BLOCK < used, gated, 0.0).astype(BF16)


def outputs(
    job, piece, lengths, qn, kn, wu, starts, log_decay, write_gain, enter, gate_z, norm_gain, key_heads, held, after,
):
    head, first, _ = job
    begin, count = piece
    prompts, tok, width = gate_z.shape
    rows = wu.shape[1]
    chunks = tok // BLOCK
    group = rows // chunks
    wide = group * DV
    value_heads = key_heads * group
    shift = begin - first
    from_mix = begin if qn.shape[0] == prompts else shift

    def whole_of(i, lengths):
        return (begin + i, 0, 0)

    def wide_of(i, lengths):
        return (begin + i, 0, head)

    def mixed_of(i, lengths):
        return (from_mix + i, 0, head)

    empty = held is None
    return pl.pallas_call(
        functools.partial(outputs_kernel, begin, head, group, chunks),
        grid_spec=pltpu.PrefetchScalarGridSpec(
            num_scalar_prefetch=1,
            grid=(count,),
            in_specs=[
                pl.BlockSpec((1, tok, DK), mixed_of),
                pl.BlockSpec((1, tok, DK), mixed_of),
                pl.BlockSpec((1, rows, DK + DV, BLOCK), lambda i, lengths: (shift + i, 0, 0, 0)),
                pl.BlockSpec((1, group, chunks * (DV + DK), DK), lambda i, lengths: (shift + i, 0, 0, 0)),
                pl.BlockSpec((1, value_heads, tok), whole_of),
                pl.BlockSpec((1, value_heads, tok), whole_of),
                pl.BlockSpec((group, DK, DV), lambda i, lengths: (shift + i, 0, 0)),
                pl.BlockSpec((1, tok, wide), wide_of),
                pl.BlockSpec((1, DV), lambda i, lengths: (0, 0)),
                pl.BlockSpec(memory_space=pltpu.HBM),
                pl.BlockSpec(memory_space=pltpu.HBM),
            ],
            out_specs=pl.BlockSpec((1, tok, wide), wide_of),
            scratch_shapes=[
                pltpu.VMEM((rows, DV, DK), BF16),
                pltpu.VMEM((rows, BLOCK, BLOCK), BF16),
                pltpu.VMEM((rows, BLOCK, DV), F32),
            ],
        ),
        out_shape=pltpu.HBM((prompts, tok, width), BF16),
        input_output_aliases={} if empty else {10: 0},
        compiler_params=pltpu.CompilerParams(vmem_limit_bytes=VMEM_BYTES),
        cost_estimate=pl.CostEstimate(flops=3 * 10**9 * count, bytes_accessed=4 * 2**20 * count, transcendentals=10**6),
        name="outputs",
    )(
        far(lengths), far(qn), far(kn), far(wu), far(starts), far(log_decay), far(write_gain), enter, far(gate_z),
        far(norm_gain.reshape(1, DV)), far(after if empty else held), far(norm_gain.reshape(1, DV) if after is held else after),
    )


def own_chip():
    seq = lax.axis_index("seq")
    return seq // 2, seq % 2 == 1


def early_late(own, other, odd):
    return jnp.where(odd, other, own), jnp.where(odd, own, other)


def follow(there, running):
    return dot(running, there[DV:])


def compose_maps(ins, outs):
    own_ref, other_ref = ins
    _, odd = own_chip()
    for n in range(own_ref.shape[0]):
        early, late = early_late(own_ref[n], other_ref[n], odd)
        both = follow(late, early)
        outs[0][n, :DV] = (both[:DV] + late[:DV].astype(F32)).astype(BF16)
        outs[0][n, DV:] = both[DV:].astype(BF16)


def close_maps(ins, outs):
    own_ref, other_ref = ins[:2]
    refs = ins[2:]
    chips = len(refs)
    chip, odd = own_chip()

    def of_chip(j, n):
        value = refs[0][n]
        for k in range(1, chips):
            value = jnp.where((chip + chips - k) % chips == j, refs[k][n], value)
        return value

    every = range(own_ref.shape[0])
    running = [of_chip(0, n)[:DV] for n in every]
    entering = [jnp.zeros_like(running[n]) for n in every]
    for j in range(1, chips):
        entering = [jnp.where(chip == j, running[n], entering[n]) for n in every]
        there = [of_chip(j, n) for n in every]
        running = [(follow(there[n], running[n]) + there[n][:DV].astype(F32)).astype(BF16) for n in every]
    for n in every:
        early, _ = early_late(own_ref[n], other_ref[n], odd)
        second = (follow(early, entering[n]) + early[:DV].astype(F32)).astype(BF16)
        outs[0][n] = jnp.where(odd, second, entering[n])
        outs[1][n] = running[n].T


def chain_maps(ins, outs):
    count = len(ins)
    mine = lax.axis_index("seq")
    every = range(ins[0].shape[0])

    def run(at):
        running = [ins[at][n, :DV] for n in every]
        for n in every:
            if at == 0:
                outs[0][n] = jnp.zeros_like(running[n])
        for j in range(1, count):
            there = ins[at ^ j]
            if j == at:
                for n in every:
                    outs[0][n] = running[n]
            moved = [follow(there.at[n], running[n]) for n in every]
            running = [(moved[n] + there[n, :DV].astype(F32)).astype(BF16) for n in every]
        for n in every:
            outs[1][n] = running[n].T

    for at in range(count):
        pl.when(mine == at)(functools.partial(run, at))


def choose_finals(group, placement_ref, finals, outs):
    refs = [(ref, n) for ref in finals for n in range(ref.shape[0] // group)]
    for r in range(placement_ref.shape[1]):
        prompt = placement_ref[0, r]
        for p, (ref, n) in enumerate(refs):
            @pl.when(prompt == p)
            def _(ref=ref, n=n):
                outs[0][r] = ref[n * group : (n + 1) * group]


def state_step(placement, group, compose, chain, close, earlier, after):
    operands, shapes = [placement], []
    steps = []
    if compose is not None:
        steps.append(("compose", len(operands), len(compose), len(shapes)))
        operands += compose
        shapes += [compose[0]]
    if chain is not None or close is not None:
        steps.append(("chain" if close is None else "close", len(operands), len(close or chain), len(shapes)))
        close = close or chain
        operands += close
        shapes += [jax.ShapeDtypeStruct((close[0].shape[0], DK, DV), BF16)] * 2
        if earlier is not None:
            steps.append(("choose", len(operands), len(earlier), len(shapes)))
            operands += earlier
            shapes.append(jax.ShapeDtypeStruct((placement.shape[1], group, DK, DV), BF16))
    out_shape = [jax.ShapeDtypeStruct(x.shape, x.dtype) for x in shapes] + [pltpu.HBM((8, 128), F32)]

    def kernel(*refs):
        refs[-1][...] = jnp.zeros_like(refs[-1])
        ins, outs = refs[: len(operands)], refs[len(operands) + 1 :]
        closed = None
        for kind, at, size, to in steps:
            part = ins[at : at + size]
            if kind == "compose":
                compose_maps(part, outs[to : to + 1])
            elif kind in ("close", "chain"):
                (close_maps if kind == "close" else chain_maps)(part, outs[to : to + 2])
                closed = outs[to + 1]
            else:
                choose_finals(group, ins[0], list(part) + [closed], outs[to:])

    vmem = pl.BlockSpec(memory_space=pltpu.VMEM)
    return pl.pallas_call(
        kernel,
        in_specs=[pl.BlockSpec(memory_space=pltpu.SMEM)]
        + [vmem] * (len(operands) - 1)
        + [pl.BlockSpec(memory_space=pltpu.HBM)],
        out_specs=[vmem] * len(out_shape),
        out_shape=out_shape,
        compiler_params=pltpu.CompilerParams(vmem_limit_bytes=SMALL_VMEM_BYTES),
        cost_estimate=pl.CostEstimate(flops=10**9, bytes_accessed=2**20, transcendentals=0),
        name="state_step",
    )(*operands, far(after))


def deliver(parts):
    count, group = parts[0].shape[:2]

    def kernel(*refs):
        for n, ref in enumerate(refs[:-1]):
            refs[-1][:, n * group : (n + 1) * group] = ref[...].astype(F32)

    return pl.pallas_call(
        kernel,
        grid=(2,),
        in_specs=[pl.BlockSpec((count // 2, group, DK, DV), lambda i: (i, 0, 0, 0))] * len(parts),
        out_specs=pl.BlockSpec((count // 2, group * len(parts), DK, DV), lambda i: (i, 0, 0, 0)),
        out_shape=jax.ShapeDtypeStruct((count, group * len(parts), DK, DV), F32),
        compiler_params=pltpu.CompilerParams(vmem_limit_bytes=VMEM_BYTES),
        name="deliver",
    )(*parts)


def across(block, distance):
    count = lax.axis_size("seq")
    return lax.ppermute(block, "seq", [(i, i ^ distance) for i in range(count)])


def from_chip_behind(block, distance):
    count = lax.axis_size("seq")
    chips = count // 2
    route = [(i, ((i // 2 + distance) % chips) * 2 + i % 2) for i in range(count)]
    return lax.ppermute(block, "seq", route)


def shards(
    qk_in, v_in, gate_z, conv_qk, conv_v, log_decay, write_gain, norm_gain, prompt_lengths, placement,
):
    prompts, tok = qk_in.shape[:2]
    key_heads = qk_in.shape[3] // DK
    value_heads = v_in.shape[2] // DV
    rim = CONV - 1
    seq_count = lax.axis_size("seq")
    head_count = lax.axis_size("head")

    def by_head(x):
        x = x.reshape(x.shape[0], x.shape[1], 2, key_heads, DK)
        return jnp.transpose(x, (0, 1, 3, 2, 4)).reshape(x.shape[0], -1, DK)

    qk_rows = by_head(qk_in)
    qk_taps = by_head(conv_qk[None])[0]
    qk_tail = qk_rows[:, (tok - rim) * 2 * key_heads :]
    v_tail = v_in[:, tok - rim :].reshape(prompts, rim * value_heads, DV)
    front = 2 * EDGE - qk_tail.shape[1]
    back = 2 * EDGE - v_tail.shape[1]
    tails = jnp.concatenate(
        [
            jnp.zeros((prompts, front, DK), BF16),
            qk_tail,
            v_tail,
            jnp.zeros((prompts, back, DK), BF16),
        ],
        axis=1,
    )
    halo = lax.ppermute(tails, "seq", [(i, i + 1) for i in range(seq_count - 1)])
    group = value_heads // key_heads
    chips = seq_count // 2
    half = prompts // 2
    jobs = [(head, 0, prompts) for head in range(key_heads)]
    if key_heads == 1:
        jobs = [(0, 0, half), (0, half, prompts - half)]
    total = len(jobs)
    made, finals, sent = [], [], {}
    attended = None
    last = v_in

    def finish(job, results):
        head = jobs[job][0]
        finals.append(results[1])
        if len(results) > 3:
            sent[head] = lax.all_to_all(results[2], "head", 0, 0)
        return results[0], results[-1]

    def earlier(job):
        same = [n for n in range(total) if jobs[n][0] == jobs[job][0]]
        return [finals[n] for n in same[:-1]] if job == same[-1] else None

    def emit(job, entered, attended, last):
        qn, kn, wu, starts, _ = made[job]
        return outputs(
            jobs[job], jobs[job][1:], prompt_lengths, qn, kn, wu, starts, log_decay, write_gain,
            entered, gate_z, norm_gain, key_heads, attended, last,
        )

    for job in jobs:
        mixed = None if job[0] == 0 else made[0][:2]
        wu, starts, own_map, last, *new = prepare(
            job, prompt_lengths, qk_rows, v_in, halo, qk_taps, conv_v, log_decay, write_gain, key_heads,
            mixed and mixed[1], last,
        )
        moved = [own_map]
        if job == jobs[-1]:
            moved.append(across(own_map, 1))
        else:
            moved += [across(own_map, k) for k in range(1, seq_count)]
        made.append((*(mixed or new), wu, starts, moved))

    entered = []
    for job in range(total - 1):
        results = state_step(placement, group, None, made[job][4], None, earlier(job), last)
        enter, last = finish(job, results)
        entered.append(enter)
    pair = made[-1][4]
    chip_map, last = state_step(placement, group, pair, None, None, None, last)
    chip_maps = [chip_map] + [from_chip_behind(chip_map, k) for k in range(1, chips)]
    for job in range(total - 1):
        attended = last = emit(job, entered[job], attended, last)
    results = state_step(placement, group, None, None, pair + chip_maps, earlier(total - 1), last)
    enter, last = finish(total - 1, results)
    attended = emit(total - 1, enter, attended, last)
    rollout = deliver([sent[head] for head in range(key_heads)])
    return attended, rollout.reshape(1, 1, head_count * value_heads, DK, DV)


def solution(mesh):
    return jax.shard_map(
        shards,
        mesh=mesh,
        in_specs=(
            P(None, "seq", None, "head"),
            P(None, "seq", "head"),
            P(None, "seq", "head"),
            P(None, None, "head"),
            P(None, "head"),
            P(None, "head", "seq"),
            P(None, "head", "seq"),
            P(),
            P(),
            P("seq", None),
        ),
        out_specs=(P(None, "seq", "head"), P("seq", "head", None, None, None)),
        check_vma=False,
    )
```

```python
import functools

import jax
import jax.numpy as jnp
from jax import lax
from jax.experimental import pallas as pl
from jax.experimental.pallas import tpu as pltpu
from jax.sharding import PartitionSpec as P

DK = 128
DV = 128
CONV = 4
BLOCK = 128
TINY = 16
EDGE = 8
EPSILON = 1e-06
VMEM_BYTES = 40 * 1024 * 1024
SMALL_VMEM_BYTES = 8 * 1024 * 1024
F32 = jnp.float32
BF16 = jnp.bfloat16


def far(x):
    return pltpu.with_memory_space_constraint(x, pltpu.HBM)


def dot(a, b):
    return lax.dot_general(a, b, (((1,), (0,)), ((), ())), preferred_element_type=F32)


def silu(x):
    half = 0.5 * x
    return half + half * jnp.tanh(half)


def mixed_rows(pad_ref, taps, rim, first, step, c):
    total = None
    for i in range(CONV):
        start = rim + first + step * (c * BLOCK + i - (CONV - 1))
        stride = None if step == 1 else step
        term = pad_ref[pl.ds(start, BLOCK, stride), :] * taps[i]
        total = term if total is None else total + term
    return silu(total)


def unit_rows(x):
    return x * lax.rsqrt(jnp.sum(x * x, axis=-1, keepdims=True) + EPSILON)


def heads_rows(ref, head, group):
    every = ref[0]
    rows = every[:group]
    for n in range(1, every.shape[0] // group):
        rows = jnp.where(head == n, every[n * group : (n + 1) * group], rows)
    return rows


def gates_of_heads(log_ref, gain_ref, used, head, group):
    log = heads_rows(log_ref, head, group)
    lane = lax.broadcasted_iota(jnp.int32, log.shape, 1)
    valid = lane < used
    cum = jnp.where(valid, log, 0.0)
    gain = jnp.where(valid, heads_rows(gain_ref, head, group), 0.0)
    shift = 1
    while shift < BLOCK:
        cum = cum + jnp.where(lane % BLOCK >= shift, pltpu.roll(cum, shift, 1), 0.0)
        shift *= 2
    return cum, gain


def as_columns(rows, chunks):
    parts = [rows[:, c * BLOCK : (c + 1) * BLOCK] for c in range(chunks)]
    short = BLOCK - 8 * chunks
    if short:
        parts.append(jnp.zeros((short, BLOCK), F32))
    return jnp.concatenate(parts, axis=0).T


def block_bases(parts, chunks):
    rows = jnp.concatenate(parts, axis=0)
    short = 7 - rows.shape[0]
    fill = [jnp.zeros((short, rows.shape[1]), F32)] if short else []
    rows = jnp.concatenate([rows] + fill + [jnp.ones((1, rows.shape[1]), F32)], axis=0)
    return [rows[:, c * BLOCK : (c + 1) * BLOCK] for c in range(chunks)]


def spread_squares(base, group, kinds):
    high = base.astype(BF16).astype(F32)
    middle = (base - high).astype(BF16).astype(F32)
    low = base - high - middle
    parts = [high, middle, low]
    row = lax.broadcasted_iota(jnp.int32, (32, BLOCK), 0)
    which = row % 8
    real = row < 24
    stacked = jnp.concatenate(parts + [jnp.zeros_like(high)], axis=0)
    left = jnp.where(jnp.logical_and(which == 7, real), 1.0, stacked).T.astype(BF16)
    blocks = []
    for h in range(group):
        minus = jnp.concatenate([jnp.broadcast_to(-part[h : h + 1], (8, BLOCK)) for part in parts + [low]], axis=0)
        blocks.append(jnp.where(which == h, 1.0, jnp.where(which == 7, minus, 0.0)))
    for n in range(group, group * kinds):
        blocks.append(jnp.where(which == n, 1.0, 0.0).astype(F32))
    every = dot(left, jnp.concatenate(blocks, axis=1).astype(BF16))
    return [every[:, n * BLOCK : (n + 1) * BLOCK] for n in range(group * kinds)]


def mix(qk_ref, halo_ref, taps_ref, qn_ref, kn_ref, raw_scr, key_heads, chunks):
    kinds = 2 * key_heads
    rim = 2 * EDGE
    taps = taps_ref[...].astype(F32)
    raw_scr[:rim] = halo_ref[0].astype(F32)[:rim]
    raw_scr[rim:] = qk_ref[0].astype(F32)
    for c in range(chunks):
        span = slice(c * BLOCK, (c + 1) * BLOCK)
        for kind in range(kinds):
            own = [taps[n : n + 1] for n in range(kind, taps.shape[0], kinds)]
            rows = unit_rows(mixed_rows(raw_scr, own, rim, kind, kinds, c))
            to_ref = kn_ref if kind % 2 else qn_ref
            to_ref[0, span, kind // 2 * DK : (kind // 2 + 1) * DK] = rows.astype(BF16)


def weave(*lists):
    places = []
    for which, entries in enumerate(lists):
        places += [((n + 0.5) / len(entries), which, n) for n in range(len(entries))]
    for _, which, n in sorted(places):
        lists[which][n]()


def prepare_kernel(first, count, head, group, chunks, key_heads, mixes, *refs):
    length_ref, v_ref, halo_ref, v_taps_ref, log_ref, gain_ref, after_ref = refs[:7]
    refs = refs[7:]
    if mixes:
        qk_ref, qk_taps_ref, wu_ref, start_ref, map_ref, token_ref, qn_ref, kn_ref = refs[:8]
        v_pad, m_scr, b_scr, fade_scr, st_scr, a_scr, x_scr, y_scr, raw_scr = refs[8:]
        key_columns = slice(head * DK, (head + 1) * DK)
    else:
        kn_ref, wu_ref, start_ref, map_ref, token_ref = refs[:5]
        v_pad, m_scr, b_scr, fade_scr, st_scr, a_scr, x_scr, y_scr = refs[5:]
        key_columns = slice(0, DK)
    step = pl.program_id(0)
    token_ref[...] = jnp.zeros_like(token_ref)
    used = length_ref[first + jnp.minimum(step, count - 1)] - lax.axis_index("seq") * (chunks * BLOCK)
    units = [(h, c) for c in range(chunks) for h in range(group)]
    slot = step % 2
    live = jnp.logical_and(step < count, used > 0)

    def begin():
        row = lax.broadcasted_iota(jnp.int32, (DV + DK, DK), 0)
        lane = lax.broadcasted_iota(jnp.int32, (DV + DK, DK), 1)
        for h in range(group):
            st_scr[h] = jnp.where(row == lane + DV, 1.0, 0.0).astype(F32)

    def advance(c):
        narrow, moved = {}, {}

        def load(h):
            narrow[h] = st_scr[h].astype(BF16)
            start_ref[0, h, c * (DV + DK) : (c + 1) * (DV + DK), :] = narrow[h]

        def move(h):
            moved[h] = dot(narrow[h], m_scr[1 - slot, c, h])

        def store(h):
            fade = fade_scr[1 - slot, c, h : h + 1, :]
            state = st_scr[h, :DV] * fade + (moved[h][:DV] + b_scr[1 - slot, c, h])
            trans = st_scr[h, DV:] * fade + moved[h][DV:]
            if c < chunks - 1:
                st_scr[h, :DV] = state
                st_scr[h, DV:] = trans
            else:
                map_ref[h, :DV] = state.astype(BF16)
                map_ref[h, DV:] = trans.astype(BF16)

        return [functools.partial(act, h) for act in (load, move, store) for h in range(group)]

    recurrence = [begin]
    for c in range(chunks):
        recurrence += advance(c)

    @pl.when(jnp.logical_not(live))
    def _():
        @pl.when(step > 0)
        def _():
            weave(recurrence)

        @pl.when(step < count)
        def _():
            if mixes:
                qn_ref[...] = jnp.zeros_like(qn_ref)
                kn_ref[...] = jnp.zeros_like(kn_ref)
            wu_ref[...] = jnp.zeros_like(wu_ref)
            fade_scr[slot] = jnp.ones(fade_scr.shape[1:], F32)
            m_scr[slot] = jnp.zeros(m_scr.shape[1:], BF16)
            b_scr[slot] = jnp.zeros(b_scr.shape[1:], F32)

    @pl.when(live)
    def _():
        if mixes:
            mix(qk_ref, halo_ref, qk_taps_ref, qn_ref, kn_ref, raw_scr, key_heads, chunks)
        halo = halo_ref[0].astype(F32)
        for h in range(group):
            columns = slice(h * DV, (h + 1) * DV)
            v_pad[pl.ds(EDGE + h, chunks * BLOCK, group), :] = v_ref[0, :, columns].astype(F32)
        for i in range(CONV - 1):
            for h in range(group):
                source = 2 * EDGE + (i * key_heads + head) * group + h
                to = EDGE + (i - CONV + 1) * group + h
                v_pad[to : to + 1, :] = halo[source : source + 1]
        v_all_taps = v_taps_ref[...].astype(F32)
        v_taps = [[v_all_taps[i : i + 1, h * DV : (h + 1) * DV] for i in range(CONV)] for h in range(group)]

        cum, gain = gates_of_heads(log_ref, gain_ref, used, head, group)
        both_gains = gain * jnp.exp(cum)
        bases = block_bases([-cum], chunks)

        def span(c):
            return slice(c * BLOCK, (c + 1) * BLOCK)

        row = lax.broadcasted_iota(jnp.int32, (BLOCK, BLOCK), 0)
        lane = lax.broadcasted_iota(jnp.int32, (BLOCK, BLOCK), 1)
        above = row < lane
        small_row = lax.broadcasted_iota(jnp.int32, (TINY, BLOCK), 0)
        small_lane = lax.broadcasted_iota(jnp.int32, (TINY, BLOCK), 1)
        part_of = small_lane // TINY
        tiny_eye = jnp.where(small_row == small_lane % TINY, 1.0, 0.0).astype(F32)

        keys = [kn_ref[0, span(c), key_columns] for c in range(chunks)]
        turned = {}

        def front(some):
            ops, kk, later, compact, solved = [], {}, {}, {}, {}
            local = [(h, c) for c in some for h in range(group)]

            def start(c):
                turned[c] = keys[c].T
                kk[c] = dot(keys[c], turned[c])
                later[c] = spread_squares(bases[c], group, 1)

            def mask(h, c):
                r = h * chunks + c
                strict = jnp.where(above, jnp.exp(later[c][h]) * kk[c] * -gain[h : h + 1, span(c)], 0.0)
                a_scr[r] = strict.astype(BF16)
                tiny = strict[0:TINY]
                for b in range(1, BLOCK // TINY):
                    tiny = jnp.where(part_of == b, strict[b * TINY : (b + 1) * TINY], tiny)
                compact[r] = tiny
                solved[r] = tiny_eye

            def eliminate(j, r):
                factor = jnp.take_along_axis(compact[r], part_of * TINY + j, axis=1, mode="promise_in_bounds")
                solved[r] = solved[r] + factor * solved[r][j : j + 1, :]

            def place(r):
                for b in range(BLOCK // TINY):
                    x_scr[r, b * TINY : (b + 1) * TINY, :] = jnp.where(part_of == b, solved[r], 0.0).astype(BF16)

            def scale(h, c):
                top = h * (DK + DV)
                v_wide = mixed_rows(v_pad, v_taps[h], EDGE, h, group, c).astype(BF16).T.astype(F32)
                y_scr[c, top : top + DK, :] = (turned[c].astype(F32) * both_gains[h : h + 1, span(c)]).astype(BF16)
                y_scr[c, top + DK : top + DK + DV, :] = (v_wide * gain[h : h + 1, span(c)]).astype(BF16)

            for c in some:
                ops.append(functools.partial(start, c))
            for h, c in local:
                ops.append(functools.partial(mask, h, c))
            for j in range(TINY - 1, 0, -1):
                for h, c in local:
                    ops.append(functools.partial(eliminate, j, h * chunks + c))
            for h, c in local:
                ops.append(functools.partial(place, h * chunks + c))
            right = []
            for c in some:
                right += [functools.partial(scale, h, c) for h in range(group)]
            return ops, right

        def back(some):
            ops, own, moved = [], {}, {}
            local = [(h, c) for c in some for h in range(group)]

            def reach(size, r):
                half_lane = lax.broadcasted_iota(jnp.int32, (BLOCK // 2, BLOCK), 1)
                half_row = lax.broadcasted_iota(jnp.int32, (BLOCK // 2, BLOCK), 0)
                partner = half_lane // size == 2 * (half_row // size) + 1
                own[r] = jnp.concatenate([x_scr[r, s : s + size, :] for s in range(0, BLOCK, 2 * size)], axis=0)
                moved[r] = jnp.where(partner, dot(own[r], a_scr[r]), 0.0).astype(BF16)

            def join(size, r):
                update = own[r] + dot(moved[r], x_scr[r]).astype(BF16)
                for n, s in enumerate(range(0, BLOCK, 2 * size)):
                    x_scr[r, s : s + size, :] = update[n * size : (n + 1) * size]

            def solve(h, c):
                r = h * chunks + c
                top = h * (DK + DV)
                sums = cum[:, span(c)]
                last = sums[:, BLOCK - 1 : BLOCK]
                tail = jnp.exp(last - sums)
                fade = jnp.broadcast_to(jnp.exp(last), (group, BLOCK))
                rows = dot(y_scr[c, top : top + DK + DV, :], x_scr[r])
                wu_ref[0, r] = rows.astype(BF16)
                y_scr[c, top : top + DK + DV, :] = (rows * tail[h : h + 1]).astype(BF16)
                fade_scr[slot, c, h : h + 1, :] = fade[h : h + 1]

            def finish(c):
                both = dot(y_scr[c], keys[c])
                for h in range(group):
                    top = h * (DK + DV)
                    m_scr[slot, c, h] = (-both[top : top + DK]).astype(BF16)
                    b_scr[slot, c, h] = both[top + DK : top + DK + DV]

            size = TINY
            while size < BLOCK:
                ops += [functools.partial(reach, size, h * chunks + c) for h, c in local]
                ops += [functools.partial(join, size, h * chunks + c) for h, c in local]
                size *= 2
            ops += [functools.partial(solve, h, c) for h, c in local]
            ops += [functools.partial(finish, c) for c in some]
            return ops

        half = chunks // 2
        early, late = range(half), range(half, chunks)
        early_front, early_right = front(early)
        late_front, late_right = front(late)
        cut = len(recurrence) // 3
        weave(early_front, recurrence[:cut], early_right)
        weave(back(early), late_front, late_right)
        weave(back(late), recurrence[cut:])


def prepare(job, lengths, qk_rows, v_in, halo, qk_taps, v_taps, log_decay, write_gain, key_heads, mixed, after):
    head, first, count = job
    tok = v_in.shape[1]
    value_heads = v_in.shape[2] // DV
    group = value_heads // key_heads
    chunks = tok // BLOCK
    rows = group * chunks
    wide = group * DV
    mixes = mixed is None

    def now(i):
        return jnp.minimum(i, count - 1)

    def before(i):
        return jnp.maximum(i - 1, 0)

    def whole_of(i, lengths):
        return (first + now(i), 0, 0)

    operands = [far(v_in), halo, far(v_taps), far(log_decay), far(write_gain), far(after)]
    in_specs = [
        pl.BlockSpec((1, tok, wide), lambda i, lengths: (first + now(i), 0, head)),
        pl.BlockSpec((1,) + halo.shape[1:], whole_of),
        pl.BlockSpec((CONV, wide), lambda i, lengths: (0, head)),
        pl.BlockSpec((1, value_heads, tok), whole_of),
        pl.BlockSpec((1, value_heads, tok), whole_of),
        pl.BlockSpec(memory_space=pltpu.HBM),
    ]
    out_specs = [
        pl.BlockSpec((1, rows, DK + DV, BLOCK), lambda i, lengths: (now(i), 0, 0, 0)),
        pl.BlockSpec((1, group, chunks * (DV + DK), DK), lambda i, lengths: (before(i), 0, 0, 0)),
        pl.BlockSpec((group, DV + DK, DK), lambda i, lengths: (before(i), 0, 0)),
        pl.BlockSpec((8, 128), lambda i, lengths: (0, 0)),
    ]
    out_shape = [
        pltpu.HBM((count, rows, DK + DV, BLOCK), BF16),
        pltpu.HBM((count, group, chunks * (DV + DK), DK), BF16),
        jax.ShapeDtypeStruct((count * group, DV + DK, DK), BF16),
        pltpu.HBM((8, 128), F32),
    ]
    scratch = [
        pltpu.VMEM((tok * group + EDGE, DV), F32),
        pltpu.VMEM((2, chunks, group, DK, DK), BF16),
        pltpu.VMEM((2, chunks, group, DV, DK), F32),
        pltpu.VMEM((2, chunks, group, BLOCK), F32),
        pltpu.VMEM((group, DV + DK, DK), F32),
        pltpu.VMEM((rows, BLOCK, BLOCK), BF16),
        pltpu.VMEM((rows, BLOCK, BLOCK), BF16),
        pltpu.VMEM((chunks, group * (DK + DV), BLOCK), BF16),
    ]
    if mixes:
        operands += [far(qk_rows), far(qk_taps)]
        in_specs += [
            pl.BlockSpec((1,) + qk_rows.shape[1:], whole_of),
            pl.BlockSpec(qk_taps.shape, lambda i, lengths: (0, 0)),
        ]
        out_specs += [pl.BlockSpec((1, tok, key_heads * DK), lambda i, lengths: (now(i), 0, 0))] * 2
        out_shape += [pltpu.HBM((count, tok, key_heads * DK), BF16)] * 2
        scratch.append(pltpu.VMEM((qk_rows.shape[1] + 2 * EDGE, DK), F32))
    else:
        operands.append(far(mixed))
        in_specs.append(pl.BlockSpec((1, tok, DK), lambda i, lengths: (first + now(i), 0, head)))
    return pl.pallas_call(
        functools.partial(prepare_kernel, first, count, head, group, chunks, key_heads, mixes),
        grid_spec=pltpu.PrefetchScalarGridSpec(
            num_scalar_prefetch=1,
            grid=(count + 1,),
            in_specs=in_specs,
            out_specs=out_specs,
            scratch_shapes=scratch,
        ),
        out_shape=out_shape,
        compiler_params=pltpu.CompilerParams(vmem_limit_bytes=VMEM_BYTES),
        cost_estimate=pl.CostEstimate(flops=5 * 10**9 * count, bytes_accessed=4 * 2**20 * count, transcendentals=10**6),
        name="prepare",
    )(far(lengths), *operands)


def outputs_kernel(
    first, head, group, chunks,
    length_ref, qn_ref, kn_ref, wu_ref, start_ref, log_ref, gain_ref, enter_ref, z_ref, norm_ref, held_ref, after_ref,
    out_ref,
    first_scr, score_scr, seen_scr,
):
    used = length_ref[first + pl.program_id(0)] - lax.axis_index("seq") * (chunks * BLOCK)
    units = [(h, c) for c in range(chunks) for h in range(group)]

    @pl.when(used <= 0)
    def _():
        out_ref[...] = jnp.zeros_like(out_ref)

    @pl.when(used > 0)
    def _():
        cum, gain = gates_of_heads(log_ref, gain_ref, used, head, group)
        faded = jnp.exp(cum)
        columns = as_columns(jnp.concatenate([cum] * (8 // group), axis=0), chunks)
        row = lax.broadcasted_iota(jnp.int32, (BLOCK, BLOCK), 0)
        lane = lax.broadcasted_iota(jnp.int32, (BLOCK, BLOCK), 1)
        upto = row <= lane
        norm_gain = norm_ref[...]

        def span(c):
            return slice(c * BLOCK, (c + 1) * BLOCK)

        for c in range(chunks):
            turned = qn_ref[0, span(c), :].T
            kq = dot(kn_ref[0, span(c), :], turned)
            q_wide = turned.astype(F32)
            for h in range(group):
                r = h * chunks + c
                ratio = jnp.exp(cum[h : h + 1, span(c)] - columns[:, c * 8 + h : c * 8 + h + 1])
                score_scr[r] = jnp.where(upto, ratio * kq, 0.0).astype(BF16)
                seen_scr[r] = q_wide * faded[h : h + 1, span(c)]
                top = c * (DV + DK)
                moved = dot(enter_ref[h], start_ref[0, h, top + DV : top + DV + DK, :])
                first_scr[r] = (moved + start_ref[0, h, top : top + DV, :].astype(F32)).astype(BF16)
        both, raws = {}, {}
        for h, c in units:
            r = h * chunks + c
            both[r] = dot(wu_ref[0, r], score_scr[r])
        for h, c in units:
            r = h * chunks + c
            seen = (seen_scr[r] - both[r][:DK]).astype(BF16)
            raw = dot(first_scr[r], seen) + both[r][DK:]
            mean = jnp.sum(raw * raw, axis=0, keepdims=True) * (1.0 / DV)
            raws[r] = (raw * lax.rsqrt(mean + EPSILON)).astype(BF16)
        for h, c in units:
            scaled = raws[h * chunks + c].T.astype(F32)
            cols = slice(h * DV, (h + 1) * DV)
            gated = scaled * norm_gain * silu(z_ref[0, span(c), cols].astype(F32))
            out_ref[0, span(c), cols] = jnp.where(row + c * BLOCK < used, gated, 0.0).astype(BF16)


def outputs(
    job, piece, lengths, qn, kn, wu, starts, log_decay, write_gain, enter, gate_z, norm_gain, key_heads, held, after,
):
    head, first, _ = job
    begin, count = piece
    prompts, tok, width = gate_z.shape
    rows = wu.shape[1]
    chunks = tok // BLOCK
    group = rows // chunks
    wide = group * DV
    value_heads = key_heads * group
    shift = begin - first
    from_mix = begin if qn.shape[0] == prompts else shift

    def whole_of(i, lengths):
        return (begin + i, 0, 0)

    def wide_of(i, lengths):
        return (begin + i, 0, head)

    def mixed_of(i, lengths):
        return (from_mix + i, 0, head)

    empty = held is None
    return pl.pallas_call(
        functools.partial(outputs_kernel, begin, head, group, chunks),
        grid_spec=pltpu.PrefetchScalarGridSpec(
            num_scalar_prefetch=1,
            grid=(count,),
            in_specs=[
                pl.BlockSpec((1, tok, DK), mixed_of),
                pl.BlockSpec((1, tok, DK), mixed_of),
                pl.BlockSpec((1, rows, DK + DV, BLOCK), lambda i, lengths: (shift + i, 0, 0, 0)),
                pl.BlockSpec((1, group, chunks * (DV + DK), DK), lambda i, lengths: (shift + i, 0, 0, 0)),
                pl.BlockSpec((1, value_heads, tok), whole_of),
                pl.BlockSpec((1, value_heads, tok), whole_of),
                pl.BlockSpec((group, DK, DV), lambda i, lengths: (shift + i, 0, 0)),
                pl.BlockSpec((1, tok, wide), wide_of),
                pl.BlockSpec((1, DV), lambda i, lengths: (0, 0)),
                pl.BlockSpec(memory_space=pltpu.HBM),
                pl.BlockSpec(memory_space=pltpu.HBM),
            ],
            out_specs=pl.BlockSpec((1, tok, wide), wide_of),
            scratch_shapes=[
                pltpu.VMEM((rows, DV, DK), BF16),
                pltpu.VMEM((rows, BLOCK, BLOCK), BF16),
                pltpu.VMEM((rows, BLOCK, DV), F32),
            ],
        ),
        out_shape=pltpu.HBM((prompts, tok, width), BF16),
        input_output_aliases={} if empty else {10: 0},
        compiler_params=pltpu.CompilerParams(vmem_limit_bytes=VMEM_BYTES),
        cost_estimate=pl.CostEstimate(flops=3 * 10**9 * count, bytes_accessed=4 * 2**20 * count, transcendentals=10**6),
        name="outputs",
    )(
        far(lengths), far(qn), far(kn), far(wu), far(starts), far(log_decay), far(write_gain), enter, far(gate_z),
        far(norm_gain.reshape(1, DV)), far(after if empty else held), far(norm_gain.reshape(1, DV) if after is held else after),
    )


def last_rows(qk_rows, v_in, rim):
    prompts, _, width = v_in.shape
    tall = 2 * EDGE
    heads = width // DV

    def kernel(qk_ref, v_ref, out_ref):
        for p in range(prompts):
            out_ref[p, :tall] = qk_ref[p]
            values = v_ref[p].astype(F32)
            rows = [
                values[tall - rim + i : tall - rim + i + 1, h * DV : (h + 1) * DV]
                for i in range(rim)
                for h in range(heads)
            ]
            rows.append(jnp.zeros((tall - rim * heads, DV), F32))
            out_ref[p, tall:] = jnp.concatenate(rows, axis=0).astype(BF16)

    return pl.pallas_call(
        kernel,
        grid=(1,),
        in_specs=[
            pl.BlockSpec((prompts, tall, DK), lambda i: (0, qk_rows.shape[1] // tall - 1, 0)),
            pl.BlockSpec((prompts, tall, width), lambda i: (0, v_in.shape[1] // tall - 1, 0)),
        ],
        out_specs=pl.BlockSpec((prompts, 2 * tall, DK), lambda i: (0, 0, 0)),
        out_shape=jax.ShapeDtypeStruct((prompts, 2 * tall, DK), BF16),
        compiler_params=pltpu.CompilerParams(vmem_limit_bytes=SMALL_VMEM_BYTES),
        name="last_rows",
    )(far(qk_rows), far(v_in))


def own_chip():
    seq = lax.axis_index("seq")
    return seq // 2, seq % 2 == 1


def early_late(own, other, odd):
    return jnp.where(odd, other, own), jnp.where(odd, own, other)


def follow(there, running):
    return dot(running, there[DV:])


def compose_maps(ins, outs):
    own_ref, other_ref = ins
    _, odd = own_chip()
    for n in range(own_ref.shape[0]):
        early, late = early_late(own_ref[n], other_ref[n], odd)
        both = follow(late, early)
        outs[0][n, :DV] = (both[:DV] + late[:DV].astype(F32)).astype(BF16)
        outs[0][n, DV:] = both[DV:].astype(BF16)


def close_maps(ins, outs):
    own_ref, other_ref = ins[:2]
    refs = ins[2:]
    chips = len(refs)
    chip, odd = own_chip()

    def of_chip(j, n):
        value = refs[0][n]
        for k in range(1, chips):
            value = jnp.where((chip + chips - k) % chips == j, refs[k][n], value)
        return value

    every = range(own_ref.shape[0])
    running = [of_chip(0, n)[:DV] for n in every]
    entering = [jnp.zeros_like(running[n]) for n in every]
    for j in range(1, chips):
        entering = [jnp.where(chip == j, running[n], entering[n]) for n in every]
        there = [of_chip(j, n) for n in every]
        running = [(follow(there[n], running[n]) + there[n][:DV].astype(F32)).astype(BF16) for n in every]
    for n in every:
        early, _ = early_late(own_ref[n], other_ref[n], odd)
        second = (follow(early, entering[n]) + early[:DV].astype(F32)).astype(BF16)
        outs[0][n] = jnp.where(odd, second, entering[n])
        outs[1][n] = running[n].T


def chain_maps(ins, outs):
    ins = (ins[0],) + tuple(ins[:0:-1])
    count = len(ins)
    mine = lax.axis_index("seq")
    every = range(ins[0].shape[0])

    def run(at):
        running = [ins[at][n, :DV] for n in every]
        for n in every:
            if at == 0:
                outs[0][n] = jnp.zeros_like(running[n])
        for j in range(1, count):
            there = ins[at ^ j]
            if j == at:
                for n in every:
                    outs[0][n] = running[n]
            moved = [follow(there.at[n], running[n]) for n in every]
            running = [(moved[n] + there[n, :DV].astype(F32)).astype(BF16) for n in every]
        for n in every:
            outs[1][n] = running[n].T

    for at in range(count):
        pl.when(mine == at)(functools.partial(run, at))


def choose_finals(group, placement_ref, finals, outs):
    refs = [(ref, n) for ref in finals for n in range(ref.shape[0] // group)]
    for r in range(placement_ref.shape[1]):
        prompt = placement_ref[0, r]
        for p, (ref, n) in enumerate(refs):
            @pl.when(prompt == p)
            def _(ref=ref, n=n):
                outs[0][r] = ref[n * group : (n + 1) * group]


def state_step(placement, group, compose, chain, close, earlier, after):
    operands, shapes = [placement], []
    steps = []
    if compose is not None:
        steps.append(("compose", len(operands), len(compose), len(shapes)))
        operands += compose
        shapes += [compose[0]]
    if chain is not None or close is not None:
        steps.append(("chain" if close is None else "close", len(operands), len(close or chain), len(shapes)))
        close = close or chain
        operands += close
        shapes += [jax.ShapeDtypeStruct((close[0].shape[0], DK, DV), BF16)] * 2
        if earlier is not None:
            steps.append(("choose", len(operands), len(earlier), len(shapes)))
            operands += earlier
            shapes.append(jax.ShapeDtypeStruct((placement.shape[1], group, DK, DV), BF16))
    out_shape = [jax.ShapeDtypeStruct(x.shape, x.dtype) for x in shapes] + [pltpu.HBM((8, 128), F32)]

    def kernel(*refs):
        refs[-1][...] = jnp.zeros_like(refs[-1])
        ins, outs = refs[: len(operands)], refs[len(operands) + 1 :]
        closed = None
        for kind, at, size, to in steps:
            part = ins[at : at + size]
            if kind == "compose":
                compose_maps(part, outs[to : to + 1])
            elif kind in ("close", "chain"):
                (close_maps if kind == "close" else chain_maps)(part, outs[to : to + 2])
                closed = outs[to + 1]
            else:
                choose_finals(group, ins[0], list(part) + [closed], outs[to:])

    vmem = pl.BlockSpec(memory_space=pltpu.VMEM)
    return pl.pallas_call(
        kernel,
        in_specs=[pl.BlockSpec(memory_space=pltpu.SMEM)]
        + [vmem] * (len(operands) - 1)
        + [pl.BlockSpec(memory_space=pltpu.HBM)],
        out_specs=[vmem] * len(out_shape),
        out_shape=out_shape,
        compiler_params=pltpu.CompilerParams(vmem_limit_bytes=SMALL_VMEM_BYTES),
        cost_estimate=pl.CostEstimate(flops=10**9, bytes_accessed=2**20, transcendentals=0),
        name="state_step",
    )(*operands, far(after))


def deliver(parts):
    count, group = parts[0].shape[:2]

    def kernel(*refs):
        for n, ref in enumerate(refs[:-1]):
            refs[-1][:, n * group : (n + 1) * group] = ref[...].astype(F32)

    return pl.pallas_call(
        kernel,
        grid=(2,),
        in_specs=[pl.BlockSpec((count // 2, group, DK, DV), lambda i: (i, 0, 0, 0))] * len(parts),
        out_specs=pl.BlockSpec((count // 2, group * len(parts), DK, DV), lambda i: (i, 0, 0, 0)),
        out_shape=jax.ShapeDtypeStruct((count, group * len(parts), DK, DV), F32),
        compiler_params=pltpu.CompilerParams(vmem_limit_bytes=VMEM_BYTES),
        name="deliver",
    )(*parts)


def across(block, distance):
    count = lax.axis_size("seq")
    return lax.ppermute(block, "seq", [(i, i ^ distance) for i in range(count)])


def from_chip_behind(block, distance):
    count = lax.axis_size("seq")
    chips = count // 2
    route = [(i, ((i // 2 + distance) % chips) * 2 + i % 2) for i in range(count)]
    return lax.ppermute(block, "seq", route)


def shards(
    qk_in, v_in, gate_z, conv_qk, conv_v, log_decay, write_gain, norm_gain, prompt_lengths, placement,
):
    prompts, tok = qk_in.shape[:2]
    key_heads = qk_in.shape[3] // DK
    value_heads = v_in.shape[2] // DV
    rim = CONV - 1
    seq_count = lax.axis_size("seq")
    head_count = lax.axis_size("head")

    def by_head(x):
        x = x.reshape(x.shape[0], x.shape[1], 2, key_heads, DK)
        return jnp.transpose(x, (0, 1, 3, 2, 4)).reshape(x.shape[0], -1, DK)

    qk_rows = by_head(qk_in)
    qk_taps = by_head(conv_qk[None])[0]
    tails = last_rows(qk_rows, v_in, rim)
    halo = lax.ppermute(tails, "seq", [(i, i + 1) for i in range(seq_count - 1)])
    group = value_heads // key_heads
    chips = seq_count // 2
    half = prompts // 2
    jobs = [(head, 0, prompts) for head in range(key_heads)]
    if key_heads == 1:
        jobs = [(0, 0, half), (0, half, prompts - half)]
    total = len(jobs)
    made, finals, sent = [], [], {}
    attended = None
    last = v_in

    def finish(job, results):
        head = jobs[job][0]
        finals.append(results[1])
        if len(results) > 3:
            sent[head] = lax.all_to_all(results[2], "head", 0, 0)
        return results[0], results[-1]

    def earlier(job):
        same = [n for n in range(total) if jobs[n][0] == jobs[job][0]]
        return [finals[n] for n in same[:-1]] if job == same[-1] else None

    def emit(job, entered, attended, last):
        qn, kn, wu, starts, _ = made[job]
        return outputs(
            jobs[job], jobs[job][1:], prompt_lengths, qn, kn, wu, starts, log_decay, write_gain,
            entered, gate_z, norm_gain, key_heads, attended, last,
        )

    for job in jobs:
        mixed = None if job[0] == 0 else made[0][:2]
        wu, starts, own_map, last, *new = prepare(
            job, prompt_lengths, qk_rows, v_in, halo, qk_taps, conv_v, log_decay, write_gain, key_heads,
            mixed and mixed[1], last,
        )
        moved = [own_map]
        if job == jobs[-1]:
            moved.append(across(own_map, 1))
        else:
            moved += [across(own_map, k) for k in range(seq_count - 1, 0, -1)]
        made.append((*(mixed or new), wu, starts, moved))

    entered = []
    for job in range(total - 1):
        results = state_step(placement, group, None, made[job][4], None, earlier(job), last)
        enter, last = finish(job, results)
        entered.append(enter)
    pair = made[-1][4]
    chip_map, last = state_step(placement, group, pair, None, None, None, last)
    chip_maps = [chip_map] + [from_chip_behind(chip_map, k) for k in range(1, chips)]
    for job in range(total - 1):
        attended = last = emit(job, entered[job], attended, last)
    results = state_step(placement, group, None, None, pair + chip_maps, earlier(total - 1), last)
    enter, last = finish(total - 1, results)
    attended = emit(total - 1, enter, attended, last)
    rollout = deliver([sent[head] for head in range(key_heads)])
    return attended, rollout.reshape(1, 1, head_count * value_heads, DK, DV)


def solution(mesh):
    return jax.shard_map(
        shards,
        mesh=mesh,
        in_specs=(
            P(None, "seq", None, "head"),
            P(None, "seq", "head"),
            P(None, "seq", "head"),
            P(None, None, "head"),
            P(None, "head"),
            P(None, "head", "seq"),
            P(None, "head", "seq"),
            P(),
            P(),
            P("seq", None),
        ),
        out_specs=(P(None, "seq", "head"), P("seq", "head", None, None, None)),
        check_vma=False,
    )
```

```python
import functools

import jax
import jax.numpy as jnp
from jax import lax
from jax.experimental import pallas as pl
from jax.experimental.pallas import tpu as pltpu
from jax.sharding import PartitionSpec as P

DK = 128
DV = 128
CONV = 4
BLOCK = 128
TINY = 16
EDGE = 8
EPSILON = 1e-06
VMEM_BYTES = 40 * 1024 * 1024
SMALL_VMEM_BYTES = 8 * 1024 * 1024
F32 = jnp.float32
BF16 = jnp.bfloat16


def far(x):
    return pltpu.with_memory_space_constraint(x, pltpu.HBM)


def dot(a, b):
    return lax.dot_general(a, b, (((1,), (0,)), ((), ())), preferred_element_type=F32)


def silu(x):
    half = 0.5 * x
    return half + half * jnp.tanh(half)


def mixed_rows(pad_ref, taps, rim, first, step, c):
    total = None
    for i in range(CONV):
        start = rim + first + step * (c * BLOCK + i - (CONV - 1))
        stride = None if step == 1 else step
        term = pad_ref[pl.ds(start, BLOCK, stride), :] * taps[i]
        total = term if total is None else total + term
    return silu(total)


def unit_rows(x):
    return x * lax.rsqrt(jnp.sum(x * x, axis=-1, keepdims=True) + EPSILON)


def heads_rows(ref, head, group):
    every = ref[0]
    rows = every[:group]
    for n in range(1, every.shape[0] // group):
        rows = jnp.where(head == n, every[n * group : (n + 1) * group], rows)
    return rows


def gates_of_heads(log_ref, gain_ref, used, head, group):
    log = heads_rows(log_ref, head, group)
    lane = lax.broadcasted_iota(jnp.int32, log.shape, 1)
    valid = lane < used
    cum = jnp.where(valid, log, 0.0)
    gain = jnp.where(valid, heads_rows(gain_ref, head, group), 0.0)
    shift = 1
    while shift < BLOCK:
        cum = cum + jnp.where(lane % BLOCK >= shift, pltpu.roll(cum, shift, 1), 0.0)
        shift *= 2
    return cum, gain


def as_columns(rows, chunks):
    parts = [rows[:, c * BLOCK : (c + 1) * BLOCK] for c in range(chunks)]
    short = BLOCK - 8 * chunks
    if short:
        parts.append(jnp.zeros((short, BLOCK), F32))
    return jnp.concatenate(parts, axis=0).T


def block_bases(parts, chunks):
    rows = jnp.concatenate(parts, axis=0)
    short = 7 - rows.shape[0]
    fill = [jnp.zeros((short, rows.shape[1]), F32)] if short else []
    rows = jnp.concatenate([rows] + fill + [jnp.ones((1, rows.shape[1]), F32)], axis=0)
    return [rows[:, c * BLOCK : (c + 1) * BLOCK] for c in range(chunks)]


def spread_squares(base, group, kinds):
    high = base.astype(BF16).astype(F32)
    middle = (base - high).astype(BF16).astype(F32)
    low = base - high - middle
    parts = [high, middle, low]
    row = lax.broadcasted_iota(jnp.int32, (32, BLOCK), 0)
    which = row % 8
    real = row < 24
    stacked = jnp.concatenate(parts + [jnp.zeros_like(high)], axis=0)
    left = jnp.where(jnp.logical_and(which == 7, real), 1.0, stacked).T.astype(BF16)
    blocks = []
    for h in range(group):
        minus = jnp.concatenate([jnp.broadcast_to(-part[h : h + 1], (8, BLOCK)) for part in parts + [low]], axis=0)
        blocks.append(jnp.where(which == h, 1.0, jnp.where(which == 7, minus, 0.0)))
    for n in range(group, group * kinds):
        blocks.append(jnp.where(which == n, 1.0, 0.0).astype(F32))
    every = dot(left, jnp.concatenate(blocks, axis=1).astype(BF16))
    return [every[:, n * BLOCK : (n + 1) * BLOCK] for n in range(group * kinds)]


def mix(qk_ref, halo_ref, taps_ref, qn_ref, kn_ref, raw_scr, key_heads, chunks):
    kinds = 2 * key_heads
    rim = 2 * EDGE
    taps = taps_ref[...].astype(F32)
    raw_scr[:rim] = halo_ref[0].astype(F32)[:rim]
    raw_scr[rim:] = qk_ref[0].astype(F32)
    for c in range(chunks):
        span = slice(c * BLOCK, (c + 1) * BLOCK)
        for kind in range(kinds):
            own = [taps[n : n + 1] for n in range(kind, taps.shape[0], kinds)]
            rows = unit_rows(mixed_rows(raw_scr, own, rim, kind, kinds, c))
            to_ref = kn_ref if kind % 2 else qn_ref
            to_ref[0, span, kind // 2 * DK : (kind // 2 + 1) * DK] = rows.astype(BF16)


def weave(*lists):
    places = []
    for which, entries in enumerate(lists):
        places += [((n + 0.5) / len(entries), which, n) for n in range(len(entries))]
    for _, which, n in sorted(places):
        lists[which][n]()


def prepare_kernel(first, count, head, group, chunks, key_heads, mixes, *refs):
    length_ref, v_ref, halo_ref, v_taps_ref, log_ref, gain_ref, after_ref = refs[:7]
    refs = refs[7:]
    if mixes:
        qk_ref, qk_taps_ref, wu_ref, start_ref, map_ref, token_ref, qn_ref, kn_ref = refs[:8]
        v_pad, m_scr, b_scr, fade_scr, st_scr, a_scr, x_scr, y_scr, raw_scr = refs[8:]
        key_columns = slice(head * DK, (head + 1) * DK)
    else:
        kn_ref, wu_ref, start_ref, map_ref, token_ref = refs[:5]
        v_pad, m_scr, b_scr, fade_scr, st_scr, a_scr, x_scr, y_scr = refs[5:]
        key_columns = slice(0, DK)
    step = pl.program_id(0)
    token_ref[...] = jnp.zeros_like(token_ref)
    used = length_ref[first + jnp.minimum(step, count - 1)] - lax.axis_index("seq") * (chunks * BLOCK)
    units = [(h, c) for c in range(chunks) for h in range(group)]
    slot = step % 2
    live = jnp.logical_and(step < count, used > 0)

    def begin():
        row = lax.broadcasted_iota(jnp.int32, (DV + DK, DK), 0)
        lane = lax.broadcasted_iota(jnp.int32, (DV + DK, DK), 1)
        for h in range(group):
            st_scr[h] = jnp.where(row == lane + DV, 1.0, 0.0).astype(F32)

    def advance(c):
        narrow, moved = {}, {}

        def load(h):
            narrow[h] = st_scr[h].astype(BF16)
            start_ref[0, h, c * (DV + DK) : (c + 1) * (DV + DK), :] = narrow[h]

        def move(h):
            moved[h] = dot(narrow[h], m_scr[1 - slot, c, h])

        def store(h):
            fade = fade_scr[1 - slot, c, h : h + 1, :]
            state = st_scr[h, :DV] * fade + (moved[h][:DV] + b_scr[1 - slot, c, h])
            trans = st_scr[h, DV:] * fade + moved[h][DV:]
            if c < chunks - 1:
                st_scr[h, :DV] = state
                st_scr[h, DV:] = trans
            else:
                map_ref[h, :DV] = state.astype(BF16)
                map_ref[h, DV:] = trans.astype(BF16)

        return [functools.partial(act, h) for act in (load, move, store) for h in range(group)]

    recurrence = [begin]
    for c in range(chunks):
        recurrence += advance(c)

    @pl.when(jnp.logical_not(live))
    def _():
        @pl.when(step > 0)
        def _():
            weave(recurrence)

        @pl.when(step < count)
        def _():
            if mixes:
                qn_ref[...] = jnp.zeros_like(qn_ref)
                kn_ref[...] = jnp.zeros_like(kn_ref)
            wu_ref[...] = jnp.zeros_like(wu_ref)
            fade_scr[slot] = jnp.ones(fade_scr.shape[1:], F32)
            m_scr[slot] = jnp.zeros(m_scr.shape[1:], BF16)
            b_scr[slot] = jnp.zeros(b_scr.shape[1:], F32)

    @pl.when(live)
    def _():
        if mixes:
            mix(qk_ref, halo_ref, qk_taps_ref, qn_ref, kn_ref, raw_scr, key_heads, chunks)
        halo = halo_ref[0].astype(F32)
        for h in range(group):
            columns = slice(h * DV, (h + 1) * DV)
            v_pad[pl.ds(EDGE + h, chunks * BLOCK, group), :] = v_ref[0, :, columns].astype(F32)
        for i in range(CONV - 1):
            for h in range(group):
                source = 2 * EDGE + (i * key_heads + head) * group + h
                to = EDGE + (i - CONV + 1) * group + h
                v_pad[to : to + 1, :] = halo[source : source + 1]
        v_all_taps = v_taps_ref[...].astype(F32)
        v_taps = [[v_all_taps[i : i + 1, h * DV : (h + 1) * DV] for i in range(CONV)] for h in range(group)]

        cum, gain = gates_of_heads(log_ref, gain_ref, used, head, group)
        both_gains = gain * jnp.exp(cum)
        bases = block_bases([-cum], chunks)

        def span(c):
            return slice(c * BLOCK, (c + 1) * BLOCK)

        row = lax.broadcasted_iota(jnp.int32, (BLOCK, BLOCK), 0)
        lane = lax.broadcasted_iota(jnp.int32, (BLOCK, BLOCK), 1)
        above = row < lane
        small_row = lax.broadcasted_iota(jnp.int32, (TINY, BLOCK), 0)
        small_lane = lax.broadcasted_iota(jnp.int32, (TINY, BLOCK), 1)
        part_of = small_lane // TINY
        tiny_eye = jnp.where(small_row == small_lane % TINY, 1.0, 0.0).astype(F32)

        keys = [kn_ref[0, span(c), key_columns] for c in range(chunks)]
        turned = {}

        def front(some):
            ops, kk, later, compact, solved = [], {}, {}, {}, {}
            local = [(h, c) for c in some for h in range(group)]

            def start(c):
                turned[c] = keys[c].T
                kk[c] = dot(keys[c], turned[c])
                later[c] = spread_squares(bases[c], group, 1)

            def mask(h, c):
                r = h * chunks + c
                strict = jnp.where(above, jnp.exp(later[c][h]) * kk[c] * -gain[h : h + 1, span(c)], 0.0)
                a_scr[r] = strict.astype(BF16)
                tiny = strict[0:TINY]
                for b in range(1, BLOCK // TINY):
                    tiny = jnp.where(part_of == b, strict[b * TINY : (b + 1) * TINY], tiny)
                compact[r] = tiny
                solved[r] = tiny_eye

            def eliminate(j, r):
                factor = jnp.take_along_axis(compact[r], part_of * TINY + j, axis=1, mode="promise_in_bounds")
                solved[r] = solved[r] + factor * solved[r][j : j + 1, :]

            def place(r):
                for b in range(BLOCK // TINY):
                    x_scr[r, b * TINY : (b + 1) * TINY, :] = jnp.where(part_of == b, solved[r], 0.0).astype(BF16)

            def scale(h, c):
                top = h * (DK + DV)
                v_wide = mixed_rows(v_pad, v_taps[h], EDGE, h, group, c).astype(BF16).T.astype(F32)
                y_scr[c, top : top + DK, :] = (turned[c].astype(F32) * both_gains[h : h + 1, span(c)]).astype(BF16)
                y_scr[c, top + DK : top + DK + DV, :] = (v_wide * gain[h : h + 1, span(c)]).astype(BF16)

            for c in some:
                ops.append(functools.partial(start, c))
            for h, c in local:
                ops.append(functools.partial(mask, h, c))
            for j in range(TINY - 1, 0, -1):
                for h, c in local:
                    ops.append(functools.partial(eliminate, j, h * chunks + c))
            for h, c in local:
                ops.append(functools.partial(place, h * chunks + c))
            right = []
            for c in some:
                right += [functools.partial(scale, h, c) for h in range(group)]
            return ops, right

        def back(some):
            ops, own, moved = [], {}, {}
            local = [(h, c) for c in some for h in range(group)]

            def reach(size, r):
                half_lane = lax.broadcasted_iota(jnp.int32, (BLOCK // 2, BLOCK), 1)
                half_row = lax.broadcasted_iota(jnp.int32, (BLOCK // 2, BLOCK), 0)
                partner = half_lane // size == 2 * (half_row // size) + 1
                own[r] = jnp.concatenate([x_scr[r, s : s + size, :] for s in range(0, BLOCK, 2 * size)], axis=0)
                moved[r] = jnp.where(partner, dot(own[r], a_scr[r]), 0.0).astype(BF16)

            def join(size, r):
                update = own[r] + dot(moved[r], x_scr[r]).astype(BF16)
                for n, s in enumerate(range(0, BLOCK, 2 * size)):
                    x_scr[r, s : s + size, :] = update[n * size : (n + 1) * size]

            def solve(h, c):
                r = h * chunks + c
                top = h * (DK + DV)
                sums = cum[:, span(c)]
                last = sums[:, BLOCK - 1 : BLOCK]
                tail = jnp.exp(last - sums)
                fade = jnp.broadcast_to(jnp.exp(last), (group, BLOCK))
                rows = dot(y_scr[c, top : top + DK + DV, :], x_scr[r])
                wu_ref[0, r] = rows.astype(BF16)
                y_scr[c, top : top + DK + DV, :] = (rows * tail[h : h + 1]).astype(BF16)
                fade_scr[slot, c, h : h + 1, :] = fade[h : h + 1]

            def finish(c):
                both = dot(y_scr[c], keys[c])
                for h in range(group):
                    top = h * (DK + DV)
                    m_scr[slot, c, h] = (-both[top : top + DK]).astype(BF16)
                    b_scr[slot, c, h] = both[top + DK : top + DK + DV]

            size = TINY
            while size < BLOCK:
                ops += [functools.partial(reach, size, h * chunks + c) for h, c in local]
                ops += [functools.partial(join, size, h * chunks + c) for h, c in local]
                size *= 2
            ops += [functools.partial(solve, h, c) for h, c in local]
            ops += [functools.partial(finish, c) for c in some]
            return ops

        half = chunks // 2
        early, late = range(half), range(half, chunks)
        early_front, early_right = front(early)
        late_front, late_right = front(late)
        cut = 2 * len(recurrence) // 3
        weave(early_front, recurrence[:cut], early_right)
        weave(back(early), late_front, late_right)
        weave(back(late), recurrence[cut:])


def prepare(job, lengths, qk_rows, v_in, halo, qk_taps, v_taps, log_decay, write_gain, key_heads, mixed, after):
    head, first, count = job
    tok = v_in.shape[1]
    value_heads = v_in.shape[2] // DV
    group = value_heads // key_heads
    chunks = tok // BLOCK
    rows = group * chunks
    wide = group * DV
    mixes = mixed is None

    def now(i):
        return jnp.minimum(i, count - 1)

    def before(i):
        return jnp.maximum(i - 1, 0)

    def whole_of(i, lengths):
        return (first + now(i), 0, 0)

    operands = [far(v_in), halo, far(v_taps), far(log_decay), far(write_gain), far(after)]
    in_specs = [
        pl.BlockSpec((1, tok, wide), lambda i, lengths: (first + now(i), 0, head)),
        pl.BlockSpec((1,) + halo.shape[1:], whole_of),
        pl.BlockSpec((CONV, wide), lambda i, lengths: (0, head)),
        pl.BlockSpec((1, value_heads, tok), whole_of),
        pl.BlockSpec((1, value_heads, tok), whole_of),
        pl.BlockSpec(memory_space=pltpu.HBM),
    ]
    out_specs = [
        pl.BlockSpec((1, rows, DK + DV, BLOCK), lambda i, lengths: (now(i), 0, 0, 0)),
        pl.BlockSpec((1, group, chunks * (DV + DK), DK), lambda i, lengths: (before(i), 0, 0, 0)),
        pl.BlockSpec((group, DV + DK, DK), lambda i, lengths: (before(i), 0, 0)),
        pl.BlockSpec((8, 128), lambda i, lengths: (0, 0)),
    ]
    out_shape = [
        pltpu.HBM((count, rows, DK + DV, BLOCK), BF16),
        pltpu.HBM((count, group, chunks * (DV + DK), DK), BF16),
        jax.ShapeDtypeStruct((count * group, DV + DK, DK), BF16),
        pltpu.HBM((8, 128), F32),
    ]
    scratch = [
        pltpu.VMEM((tok * group + EDGE, DV), F32),
        pltpu.VMEM((2, chunks, group, DK, DK), BF16),
        pltpu.VMEM((2, chunks, group, DV, DK), F32),
        pltpu.VMEM((2, chunks, group, BLOCK), F32),
        pltpu.VMEM((group, DV + DK, DK), F32),
        pltpu.VMEM((rows, BLOCK, BLOCK), BF16),
        pltpu.VMEM((rows, BLOCK, BLOCK), BF16),
        pltpu.VMEM((chunks, group * (DK + DV), BLOCK), BF16),
    ]
    if mixes:
        operands += [far(qk_rows), far(qk_taps)]
        in_specs += [
            pl.BlockSpec((1,) + qk_rows.shape[1:], whole_of),
            pl.BlockSpec(qk_taps.shape, lambda i, lengths: (0, 0)),
        ]
        out_specs += [pl.BlockSpec((1, tok, key_heads * DK), lambda i, lengths: (now(i), 0, 0))] * 2
        out_shape += [pltpu.HBM((count, tok, key_heads * DK), BF16)] * 2
        scratch.append(pltpu.VMEM((qk_rows.shape[1] + 2 * EDGE, DK), F32))
    else:
        operands.append(far(mixed))
        in_specs.append(pl.BlockSpec((1, tok, DK), lambda i, lengths: (first + now(i), 0, head)))
    return pl.pallas_call(
        functools.partial(prepare_kernel, first, count, head, group, chunks, key_heads, mixes),
        grid_spec=pltpu.PrefetchScalarGridSpec(
            num_scalar_prefetch=1,
            grid=(count + 1,),
            in_specs=in_specs,
            out_specs=out_specs,
            scratch_shapes=scratch,
        ),
        out_shape=out_shape,
        compiler_params=pltpu.CompilerParams(vmem_limit_bytes=VMEM_BYTES),
        cost_estimate=pl.CostEstimate(flops=5 * 10**9 * count, bytes_accessed=4 * 2**20 * count, transcendentals=10**6),
        name="prepare",
    )(far(lengths), *operands)


def outputs_kernel(
    first, head, group, chunks,
    length_ref, qn_ref, kn_ref, wu_ref, start_ref, log_ref, gain_ref, enter_ref, z_ref, norm_ref, held_ref, after_ref,
    out_ref,
    first_scr, score_scr, seen_scr,
):
    used = length_ref[first + pl.program_id(0)] - lax.axis_index("seq") * (chunks * BLOCK)
    units = [(h, c) for c in range(chunks) for h in range(group)]

    @pl.when(used <= 0)
    def _():
        out_ref[...] = jnp.zeros_like(out_ref)

    @pl.when(used > 0)
    def _():
        cum, gain = gates_of_heads(log_ref, gain_ref, used, head, group)
        faded = jnp.exp(cum)
        columns = as_columns(jnp.concatenate([cum] * (8 // group), axis=0), chunks)
        row = lax.broadcasted_iota(jnp.int32, (BLOCK, BLOCK), 0)
        lane = lax.broadcasted_iota(jnp.int32, (BLOCK, BLOCK), 1)
        upto = row <= lane
        norm_gain = norm_ref[...]

        def span(c):
            return slice(c * BLOCK, (c + 1) * BLOCK)

        for c in range(chunks):
            turned = qn_ref[0, span(c), :].T
            kq = dot(kn_ref[0, span(c), :], turned)
            q_wide = turned.astype(F32)
            for h in range(group):
                r = h * chunks + c
                ratio = jnp.exp(cum[h : h + 1, span(c)] - columns[:, c * 8 + h : c * 8 + h + 1])
                score_scr[r] = jnp.where(upto, ratio * kq, 0.0).astype(BF16)
                seen_scr[r] = q_wide * faded[h : h + 1, span(c)]
                top = c * (DV + DK)
                moved = dot(enter_ref[h], start_ref[0, h, top + DV : top + DV + DK, :])
                first_scr[r] = (moved + start_ref[0, h, top : top + DV, :].astype(F32)).astype(BF16)
        both, raws = {}, {}
        for h, c in units:
            r = h * chunks + c
            both[r] = dot(wu_ref[0, r], score_scr[r])
        for h, c in units:
            r = h * chunks + c
            seen = (seen_scr[r] - both[r][:DK]).astype(BF16)
            raw = dot(first_scr[r], seen) + both[r][DK:]
            mean = jnp.sum(raw * raw, axis=0, keepdims=True) * (1.0 / DV)
            raws[r] = (raw * lax.rsqrt(mean + EPSILON)).astype(BF16)
        for h, c in units:
            scaled = raws[h * chunks + c].T.astype(F32)
            cols = slice(h * DV, (h + 1) * DV)
            gated = scaled * norm_gain * silu(z_ref[0, span(c), cols].astype(F32))
            out_ref[0, span(c), cols] = jnp.where(row + c * BLOCK < used, gated, 0.0).astype(BF16)


def outputs(
    job, piece, lengths, qn, kn, wu, starts, log_decay, write_gain, enter, gate_z, norm_gain, key_heads, held, after,
):
    head, first, _ = job
    begin, count = piece
    prompts, tok, width = gate_z.shape
    rows = wu.shape[1]
    chunks = tok // BLOCK
    group = rows // chunks
    wide = group * DV
    value_heads = key_heads * group
    shift = begin - first
    from_mix = begin if qn.shape[0] == prompts else shift

    def whole_of(i, lengths):
        return (begin + i, 0, 0)

    def wide_of(i, lengths):
        return (begin + i, 0, head)

    def mixed_of(i, lengths):
        return (from_mix + i, 0, head)

    empty = held is None
    return pl.pallas_call(
        functools.partial(outputs_kernel, begin, head, group, chunks),
        grid_spec=pltpu.PrefetchScalarGridSpec(
            num_scalar_prefetch=1,
            grid=(count,),
            in_specs=[
                pl.BlockSpec((1, tok, DK), mixed_of),
                pl.BlockSpec((1, tok, DK), mixed_of),
                pl.BlockSpec((1, rows, DK + DV, BLOCK), lambda i, lengths: (shift + i, 0, 0, 0)),
                pl.BlockSpec((1, group, chunks * (DV + DK), DK), lambda i, lengths: (shift + i, 0, 0, 0)),
                pl.BlockSpec((1, value_heads, tok), whole_of),
                pl.BlockSpec((1, value_heads, tok), whole_of),
                pl.BlockSpec((group, DK, DV), lambda i, lengths: (shift + i, 0, 0)),
                pl.BlockSpec((1, tok, wide), wide_of),
                pl.BlockSpec((1, DV), lambda i, lengths: (0, 0)),
                pl.BlockSpec(memory_space=pltpu.HBM),
                pl.BlockSpec(memory_space=pltpu.HBM),
            ],
            out_specs=pl.BlockSpec((1, tok, wide), wide_of),
            scratch_shapes=[
                pltpu.VMEM((rows, DV, DK), BF16),
                pltpu.VMEM((rows, BLOCK, BLOCK), BF16),
                pltpu.VMEM((rows, BLOCK, DV), F32),
            ],
        ),
        out_shape=pltpu.HBM((prompts, tok, width), BF16),
        input_output_aliases={} if empty else {10: 0},
        compiler_params=pltpu.CompilerParams(vmem_limit_bytes=VMEM_BYTES),
        cost_estimate=pl.CostEstimate(flops=3 * 10**9 * count, bytes_accessed=4 * 2**20 * count, transcendentals=10**6),
        name="outputs",
    )(
        far(lengths), far(qn), far(kn), far(wu), far(starts), far(log_decay), far(write_gain), enter, far(gate_z),
        far(norm_gain.reshape(1, DV)), far(after if empty else held), far(norm_gain.reshape(1, DV) if after is held else after),
    )


def last_rows(qk_rows, v_in, rim):
    prompts, _, width = v_in.shape
    tall = 2 * EDGE
    heads = width // DV

    def kernel(qk_ref, v_ref, out_ref):
        for p in range(prompts):
            out_ref[p, :tall] = qk_ref[p]
            values = v_ref[p].astype(F32)
            rows = [
                values[tall - rim + i : tall - rim + i + 1, h * DV : (h + 1) * DV]
                for i in range(rim)
                for h in range(heads)
            ]
            rows.append(jnp.zeros((tall - rim * heads, DV), F32))
            out_ref[p, tall:] = jnp.concatenate(rows, axis=0).astype(BF16)

    return pl.pallas_call(
        kernel,
        grid=(1,),
        in_specs=[
            pl.BlockSpec((prompts, tall, DK), lambda i: (0, qk_rows.shape[1] // tall - 1, 0)),
            pl.BlockSpec((prompts, tall, width), lambda i: (0, v_in.shape[1] // tall - 1, 0)),
        ],
        out_specs=pl.BlockSpec((prompts, 2 * tall, DK), lambda i: (0, 0, 0)),
        out_shape=jax.ShapeDtypeStruct((prompts, 2 * tall, DK), BF16),
        compiler_params=pltpu.CompilerParams(vmem_limit_bytes=SMALL_VMEM_BYTES),
        name="last_rows",
    )(far(qk_rows), far(v_in))


def own_chip():
    seq = lax.axis_index("seq")
    return seq // 2, seq % 2 == 1


def early_late(own, other, odd):
    return jnp.where(odd, other, own), jnp.where(odd, own, other)


def follow(there, running):
    return dot(running, there[DV:])


def compose_maps(ins, outs):
    own_ref, other_ref = ins
    _, odd = own_chip()
    for n in range(own_ref.shape[0]):
        early, late = early_late(own_ref[n], other_ref[n], odd)
        both = follow(late, early)
        outs[0][n, :DV] = (both[:DV] + late[:DV].astype(F32)).astype(BF16)
        outs[0][n, DV:] = both[DV:].astype(BF16)


def close_maps(ins, outs):
    own_ref, other_ref = ins[:2]
    refs = ins[2:]
    chips = len(refs)
    chip, odd = own_chip()

    def of_chip(j, n):
        value = refs[0][n]
        for k in range(1, chips):
            value = jnp.where((chip + chips - k) % chips == j, refs[k][n], value)
        return value

    every = range(own_ref.shape[0])
    running = [of_chip(0, n)[:DV] for n in every]
    entering = [jnp.zeros_like(running[n]) for n in every]
    for j in range(1, chips):
        entering = [jnp.where(chip == j, running[n], entering[n]) for n in every]
        there = [of_chip(j, n) for n in every]
        running = [(follow(there[n], running[n]) + there[n][:DV].astype(F32)).astype(BF16) for n in every]
    for n in every:
        early, _ = early_late(own_ref[n], other_ref[n], odd)
        second = (follow(early, entering[n]) + early[:DV].astype(F32)).astype(BF16)
        outs[0][n] = jnp.where(odd, second, entering[n])
        outs[1][n] = running[n].T


def chain_maps(ins, outs):
    ins = (ins[0],) + tuple(ins[:0:-1])
    count = len(ins)
    mine = lax.axis_index("seq")
    every = range(ins[0].shape[0])

    def run(at):
        running = [ins[at][n, :DV] for n in every]
        for n in every:
            if at == 0:
                outs[0][n] = jnp.zeros_like(running[n])
        for j in range(1, count):
            there = ins[at ^ j]
            if j == at:
                for n in every:
                    outs[0][n] = running[n]
            moved = [follow(there.at[n], running[n]) for n in every]
            running = [(moved[n] + there[n, :DV].astype(F32)).astype(BF16) for n in every]
        for n in every:
            outs[1][n] = running[n].T

    for at in range(count):
        pl.when(mine == at)(functools.partial(run, at))


def choose_finals(group, placement_ref, finals, outs):
    refs = [(ref, n) for ref in finals for n in range(ref.shape[0] // group)]
    for r in range(placement_ref.shape[1]):
        prompt = placement_ref[0, r]
        for p, (ref, n) in enumerate(refs):
            @pl.when(prompt == p)
            def _(ref=ref, n=n):
                outs[0][r] = ref[n * group : (n + 1) * group]


def state_step(placement, group, compose, chain, close, earlier, after):
    operands, shapes = [placement], []
    steps = []
    if compose is not None:
        steps.append(("compose", len(operands), len(compose), len(shapes)))
        operands += compose
        shapes += [compose[0]]
    if chain is not None or close is not None:
        steps.append(("chain" if close is None else "close", len(operands), len(close or chain), len(shapes)))
        close = close or chain
        operands += close
        shapes += [jax.ShapeDtypeStruct((close[0].shape[0], DK, DV), BF16)] * 2
    if earlier is not None:
        steps.append(("choose", len(operands), len(earlier), len(shapes)))
        operands += earlier
        shapes.append(jax.ShapeDtypeStruct((placement.shape[1], group, DK, DV), BF16))
    out_shape = [jax.ShapeDtypeStruct(x.shape, x.dtype) for x in shapes] + [pltpu.HBM((8, 128), F32)]

    def kernel(*refs):
        refs[-1][...] = jnp.zeros_like(refs[-1])
        ins, outs = refs[: len(operands)], refs[len(operands) + 1 :]
        closed = None
        for kind, at, size, to in steps:
            part = ins[at : at + size]
            if kind == "compose":
                compose_maps(part, outs[to : to + 1])
            elif kind in ("close", "chain"):
                (close_maps if kind == "close" else chain_maps)(part, outs[to : to + 2])
                closed = outs[to + 1]
            else:
                choose_finals(group, ins[0], list(part) + ([] if closed is None else [closed]), outs[to:])

    vmem = pl.BlockSpec(memory_space=pltpu.VMEM)
    return pl.pallas_call(
        kernel,
        in_specs=[pl.BlockSpec(memory_space=pltpu.SMEM)]
        + [vmem] * (len(operands) - 1)
        + [pl.BlockSpec(memory_space=pltpu.HBM)],
        out_specs=[vmem] * len(out_shape),
        out_shape=out_shape,
        compiler_params=pltpu.CompilerParams(vmem_limit_bytes=SMALL_VMEM_BYTES),
        cost_estimate=pl.CostEstimate(flops=10**9, bytes_accessed=2**20, transcendentals=0),
        name="state_step",
    )(*operands, far(after))


def deliver(parts):
    count, group = parts[0].shape[:2]

    def kernel(*refs):
        for n, ref in enumerate(refs[:-1]):
            refs[-1][:, n * group : (n + 1) * group] = ref[...].astype(F32)

    return pl.pallas_call(
        kernel,
        grid=(2,),
        in_specs=[pl.BlockSpec((count // 2, group, DK, DV), lambda i: (i, 0, 0, 0))] * len(parts),
        out_specs=pl.BlockSpec((count // 2, group * len(parts), DK, DV), lambda i: (i, 0, 0, 0)),
        out_shape=jax.ShapeDtypeStruct((count, group * len(parts), DK, DV), F32),
        compiler_params=pltpu.CompilerParams(vmem_limit_bytes=VMEM_BYTES),
        name="deliver",
    )(*parts)


def across(block, distance):
    count = lax.axis_size("seq")
    return lax.ppermute(block, "seq", [(i, i ^ distance) for i in range(count)])


def from_chip_behind(block, distance):
    count = lax.axis_size("seq")
    chips = count // 2
    route = [(i, ((i // 2 + distance) % chips) * 2 + i % 2) for i in range(count)]
    return lax.ppermute(block, "seq", route)


def shards(
    qk_in, v_in, gate_z, conv_qk, conv_v, log_decay, write_gain, norm_gain, prompt_lengths, placement,
):
    prompts, tok = qk_in.shape[:2]
    key_heads = qk_in.shape[3] // DK
    value_heads = v_in.shape[2] // DV
    rim = CONV - 1
    seq_count = lax.axis_size("seq")
    head_count = lax.axis_size("head")

    def by_head(x):
        x = x.reshape(x.shape[0], x.shape[1], 2, key_heads, DK)
        return jnp.transpose(x, (0, 1, 3, 2, 4)).reshape(x.shape[0], -1, DK)

    qk_rows = by_head(qk_in)
    qk_taps = by_head(conv_qk[None])[0]
    tails = last_rows(qk_rows, v_in, rim)
    halo = lax.ppermute(tails, "seq", [(i, i + 1) for i in range(seq_count - 1)])
    group = value_heads // key_heads
    chips = seq_count // 2
    half = prompts // 2
    jobs = [(head, 0, prompts) for head in range(key_heads)]
    if key_heads == 1:
        jobs = [(0, 0, half), (0, half, prompts - half)]
    total = len(jobs)
    made, finals, sent = [], [], {}
    attended = None
    last = v_in

    def earlier(job):
        same = [n for n in range(total) if jobs[n][0] == jobs[job][0]]
        return [finals[n] for n in same[:-1]] if job == same[-1] else None

    def emit(job, entered, attended, last):
        qn, kn, wu, starts, _ = made[job]
        return outputs(
            jobs[job], jobs[job][1:], prompt_lengths, qn, kn, wu, starts, log_decay, write_gain,
            entered, gate_z, norm_gain, key_heads, attended, last,
        )

    for job in jobs:
        mixed = None if job[0] == 0 else made[0][:2]
        wu, starts, own_map, last, *new = prepare(
            job, prompt_lengths, qk_rows, v_in, halo, qk_taps, conv_v, log_decay, write_gain, key_heads,
            mixed and mixed[1], last,
        )
        moved = [own_map]
        if job == jobs[-1]:
            moved.append(across(own_map, 1))
        else:
            moved += [across(own_map, k) for k in range(seq_count - 1, 0, -1)]
        made.append((*(mixed or new), wu, starts, moved))

    def send(job, chosen):
        sent[jobs[job][0]] = lax.all_to_all(chosen, "head", 0, 0)

    entered, ready = [], None
    for job in range(total - 1):
        ready = earlier(job)
        late = job == total - 2
        enter, final, *chosen, last = state_step(
            placement, group, None, made[job][4], None, None if late else ready, last
        )
        entered.append(enter)
        finals.append(final)
        if chosen:
            send(job, chosen[0])
    if ready is not None:
        ready = ready + [finals[-1]]
    pair = made[-1][4]
    chip_map, *chosen, last = state_step(placement, group, pair, None, None, ready, last)
    chip_maps = [chip_map] + [from_chip_behind(chip_map, k) for k in range(1, chips)]
    if chosen:
        send(total - 2, chosen[0])
    for job in range(total - 1):
        attended = last = emit(job, entered[job], attended, last)
    enter, final, chosen, last = state_step(placement, group, None, None, pair + chip_maps, earlier(total - 1), last)
    send(total - 1, chosen)
    attended = emit(total - 1, enter, attended, last)
    rollout = deliver([sent[head] for head in range(key_heads)])
    return attended, rollout.reshape(1, 1, head_count * value_heads, DK, DV)


def solution(mesh):
    return jax.shard_map(
        shards,
        mesh=mesh,
        in_specs=(
            P(None, "seq", None, "head"),
            P(None, "seq", "head"),
            P(None, "seq", "head"),
            P(None, None, "head"),
            P(None, "head"),
            P(None, "head", "seq"),
            P(None, "head", "seq"),
            P(),
            P(),
            P("seq", None),
        ),
        out_specs=(P(None, "seq", "head"), P("seq", "head", None, None, None)),
        check_vma=False,
    )
```

```python
import functools

import jax
import jax.numpy as jnp
from jax import lax
from jax.experimental import pallas as pl
from jax.experimental.pallas import tpu as pltpu
from jax.sharding import PartitionSpec as P

DK = 128
DV = 128
CONV = 4
BLOCK = 128
TINY = 16
EDGE = 8
EPSILON = 1e-06
VMEM_BYTES = 40 * 1024 * 1024
SMALL_VMEM_BYTES = 8 * 1024 * 1024
F32 = jnp.float32
BF16 = jnp.bfloat16


def far(x):
    return pltpu.with_memory_space_constraint(x, pltpu.HBM)


def dot(a, b):
    return lax.dot_general(a, b, (((1,), (0,)), ((), ())), preferred_element_type=F32)


def silu(x):
    half = 0.5 * x
    return half + half * jnp.tanh(half)


def mixed_rows(pad_ref, taps, rim, first, step, c):
    total = None
    for i in range(CONV):
        start = rim + first + step * (c * BLOCK + i - (CONV - 1))
        stride = None if step == 1 else step
        term = pad_ref[pl.ds(start, BLOCK, stride), :] * taps[i]
        total = term if total is None else total + term
    return silu(total)


def unit_rows(x):
    return x * lax.rsqrt(jnp.sum(x * x, axis=-1, keepdims=True) + EPSILON)


def heads_rows(ref, head, group):
    every = ref[0]
    rows = every[:group]
    for n in range(1, every.shape[0] // group):
        rows = jnp.where(head == n, every[n * group : (n + 1) * group], rows)
    return rows


def gates_of_heads(log_ref, gain_ref, used, head, group):
    log = heads_rows(log_ref, head, group)
    lane = lax.broadcasted_iota(jnp.int32, log.shape, 1)
    valid = lane < used
    cum = jnp.where(valid, log, 0.0)
    gain = jnp.where(valid, heads_rows(gain_ref, head, group), 0.0)
    shift = 1
    while shift < BLOCK:
        cum = cum + jnp.where(lane % BLOCK >= shift, pltpu.roll(cum, shift, 1), 0.0)
        shift *= 2
    return cum, gain


def as_columns(rows, chunks):
    parts = [rows[:, c * BLOCK : (c + 1) * BLOCK] for c in range(chunks)]
    short = BLOCK - 8 * chunks
    if short:
        parts.append(jnp.zeros((short, BLOCK), F32))
    return jnp.concatenate(parts, axis=0).T


def block_bases(parts, chunks):
    rows = jnp.concatenate(parts, axis=0)
    short = 7 - rows.shape[0]
    fill = [jnp.zeros((short, rows.shape[1]), F32)] if short else []
    rows = jnp.concatenate([rows] + fill + [jnp.ones((1, rows.shape[1]), F32)], axis=0)
    return [rows[:, c * BLOCK : (c + 1) * BLOCK] for c in range(chunks)]


def spread_squares(base, group, kinds):
    high = base.astype(BF16).astype(F32)
    middle = (base - high).astype(BF16).astype(F32)
    low = base - high - middle
    parts = [high, middle, low]
    row = lax.broadcasted_iota(jnp.int32, (32, BLOCK), 0)
    which = row % 8
    real = row < 24
    stacked = jnp.concatenate(parts + [jnp.zeros_like(high)], axis=0)
    left = jnp.where(jnp.logical_and(which == 7, real), 1.0, stacked).T.astype(BF16)
    blocks = []
    for h in range(group):
        minus = jnp.concatenate([jnp.broadcast_to(-part[h : h + 1], (8, BLOCK)) for part in parts + [low]], axis=0)
        blocks.append(jnp.where(which == h, 1.0, jnp.where(which == 7, minus, 0.0)))
    for n in range(group, group * kinds):
        blocks.append(jnp.where(which == n, 1.0, 0.0).astype(F32))
    every = dot(left, jnp.concatenate(blocks, axis=1).astype(BF16))
    return [every[:, n * BLOCK : (n + 1) * BLOCK] for n in range(group * kinds)]


def mix(qk_ref, halo_ref, taps_ref, qn_ref, kn_ref, raw_scr, key_heads, chunks):
    kinds = 2 * key_heads
    rim = 2 * EDGE
    taps = taps_ref[...].astype(F32)
    raw_scr[:rim] = halo_ref[0].astype(F32)[:rim]
    raw_scr[rim:] = qk_ref[0].astype(F32)
    for c in range(chunks):
        span = slice(c * BLOCK, (c + 1) * BLOCK)
        for kind in range(kinds):
            own = [taps[n : n + 1] for n in range(kind, taps.shape[0], kinds)]
            rows = unit_rows(mixed_rows(raw_scr, own, rim, kind, kinds, c))
            to_ref = kn_ref if kind % 2 else qn_ref
            to_ref[0, span, kind // 2 * DK : (kind // 2 + 1) * DK] = rows.astype(BF16)


def weave(*lists):
    places = []
    for which, entries in enumerate(lists):
        places += [((n + 0.5) / len(entries), which, n) for n in range(len(entries))]
    for _, which, n in sorted(places):
        lists[which][n]()


def prepare_kernel(first, count, head, group, chunks, key_heads, mixes, *refs):
    length_ref, v_ref, halo_ref, v_taps_ref, log_ref, gain_ref, after_ref = refs[:7]
    refs = refs[7:]
    if mixes:
        qk_ref, qk_taps_ref, wu_ref, start_ref, map_ref, token_ref, qn_ref, kn_ref = refs[:8]
        v_pad, m_scr, b_scr, fade_scr, st_scr, a_scr, x_scr, y_scr, raw_scr = refs[8:]
        key_columns = slice(head * DK, (head + 1) * DK)
    else:
        kn_ref, wu_ref, start_ref, map_ref, token_ref = refs[:5]
        v_pad, m_scr, b_scr, fade_scr, st_scr, a_scr, x_scr, y_scr = refs[5:]
        key_columns = slice(0, DK)
    step = pl.program_id(0)
    token_ref[...] = jnp.zeros_like(token_ref)
    used = length_ref[first + jnp.minimum(step, count - 1)] - lax.axis_index("seq") * (chunks * BLOCK)
    units = [(h, c) for c in range(chunks) for h in range(group)]
    slot = step % 2
    live = jnp.logical_and(step < count, used > 0)

    def begin():
        row = lax.broadcasted_iota(jnp.int32, (DV + DK, DK), 0)
        lane = lax.broadcasted_iota(jnp.int32, (DV + DK, DK), 1)
        for h in range(group):
            st_scr[h] = jnp.where(row == lane + DV, 1.0, 0.0).astype(F32)

    def advance(c):
        narrow, moved = {}, {}

        def load(h):
            narrow[h] = st_scr[h].astype(BF16)
            start_ref[0, h, c * (DV + DK) : (c + 1) * (DV + DK), :] = narrow[h]

        def move(h):
            moved[h] = dot(narrow[h], m_scr[1 - slot, c, h])

        def store(h):
            fade = fade_scr[1 - slot, c, h : h + 1, :]
            state = st_scr[h, :DV] * fade + (moved[h][:DV] + b_scr[1 - slot, c, h])
            trans = st_scr[h, DV:] * fade + moved[h][DV:]
            if c < chunks - 1:
                st_scr[h, :DV] = state
                st_scr[h, DV:] = trans
            else:
                map_ref[h, :DV] = state.astype(BF16)
                map_ref[h, DV:] = trans.astype(BF16)

        return [functools.partial(act, h) for act in (load, move, store) for h in range(group)]

    recurrence = [begin]
    for c in range(chunks):
        recurrence += advance(c)

    @pl.when(jnp.logical_not(live))
    def _():
        @pl.when(step > 0)
        def _():
            weave(recurrence)

        @pl.when(step < count)
        def _():
            if mixes:
                qn_ref[...] = jnp.zeros_like(qn_ref)
                kn_ref[...] = jnp.zeros_like(kn_ref)
            wu_ref[...] = jnp.zeros_like(wu_ref)
            fade_scr[slot] = jnp.ones(fade_scr.shape[1:], F32)
            m_scr[slot] = jnp.zeros(m_scr.shape[1:], BF16)
            b_scr[slot] = jnp.zeros(b_scr.shape[1:], F32)

    @pl.when(live)
    def _():
        if mixes:
            mix(qk_ref, halo_ref, qk_taps_ref, qn_ref, kn_ref, raw_scr, key_heads, chunks)
        halo = halo_ref[0].astype(F32)
        for h in range(group):
            columns = slice(h * DV, (h + 1) * DV)
            v_pad[pl.ds(EDGE + h, chunks * BLOCK, group), :] = v_ref[0, :, columns].astype(F32)
        for i in range(CONV - 1):
            for h in range(group):
                source = 2 * EDGE + (i * key_heads + head) * group + h
                to = EDGE + (i - CONV + 1) * group + h
                v_pad[to : to + 1, :] = halo[source : source + 1]
        v_all_taps = v_taps_ref[...].astype(F32)
        v_taps = [[v_all_taps[i : i + 1, h * DV : (h + 1) * DV] for i in range(CONV)] for h in range(group)]

        cum, gain = gates_of_heads(log_ref, gain_ref, used, head, group)
        both_gains = gain * jnp.exp(cum)
        bases = block_bases([-cum], chunks)

        def span(c):
            return slice(c * BLOCK, (c + 1) * BLOCK)

        row = lax.broadcasted_iota(jnp.int32, (BLOCK, BLOCK), 0)
        lane = lax.broadcasted_iota(jnp.int32, (BLOCK, BLOCK), 1)
        above = row < lane
        small_row = lax.broadcasted_iota(jnp.int32, (TINY, BLOCK), 0)
        small_lane = lax.broadcasted_iota(jnp.int32, (TINY, BLOCK), 1)
        part_of = small_lane // TINY
        tiny_eye = jnp.where(small_row == small_lane % TINY, 1.0, 0.0).astype(F32)

        keys = [kn_ref[0, span(c), key_columns] for c in range(chunks)]
        turned = {}

        def front(some):
            ops, kk, later, compact, solved = [], {}, {}, {}, {}
            local = [(h, c) for c in some for h in range(group)]

            def start(c):
                turned[c] = keys[c].T
                kk[c] = dot(keys[c], turned[c])
                later[c] = spread_squares(bases[c], group, 1)

            def mask(h, c):
                r = h * chunks + c
                strict = jnp.where(above, jnp.exp(later[c][h]) * kk[c] * -gain[h : h + 1, span(c)], 0.0)
                a_scr[r] = strict.astype(BF16)
                tiny = strict[0:TINY]
                for b in range(1, BLOCK // TINY):
                    tiny = jnp.where(part_of == b, strict[b * TINY : (b + 1) * TINY], tiny)
                compact[r] = tiny
                solved[r] = tiny_eye

            def eliminate(j, r):
                factor = jnp.take_along_axis(compact[r], part_of * TINY + j, axis=1, mode="promise_in_bounds")
                solved[r] = solved[r] + factor * solved[r][j : j + 1, :]

            def place(r):
                for b in range(BLOCK // TINY):
                    x_scr[r, b * TINY : (b + 1) * TINY, :] = jnp.where(part_of == b, solved[r], 0.0).astype(BF16)

            def scale(h, c):
                top = h * (DK + DV)
                v_wide = mixed_rows(v_pad, v_taps[h], EDGE, h, group, c).astype(BF16).T.astype(F32)
                y_scr[c, top : top + DK, :] = (turned[c].astype(F32) * both_gains[h : h + 1, span(c)]).astype(BF16)
                y_scr[c, top + DK : top + DK + DV, :] = (v_wide * gain[h : h + 1, span(c)]).astype(BF16)

            for c in some:
                ops.append(functools.partial(start, c))
            for h, c in local:
                ops.append(functools.partial(mask, h, c))
            for j in range(TINY - 1, 0, -1):
                for h, c in local:
                    ops.append(functools.partial(eliminate, j, h * chunks + c))
            for h, c in local:
                ops.append(functools.partial(place, h * chunks + c))
            right = []
            for c in some:
                right += [functools.partial(scale, h, c) for h in range(group)]
            return ops, right

        def back(some):
            ops, own, moved = [], {}, {}
            local = [(h, c) for c in some for h in range(group)]

            def reach(size, r):
                half_lane = lax.broadcasted_iota(jnp.int32, (BLOCK // 2, BLOCK), 1)
                half_row = lax.broadcasted_iota(jnp.int32, (BLOCK // 2, BLOCK), 0)
                partner = half_lane // size == 2 * (half_row // size) + 1
                own[r] = jnp.concatenate([x_scr[r, s : s + size, :] for s in range(0, BLOCK, 2 * size)], axis=0)
                moved[r] = jnp.where(partner, dot(own[r], a_scr[r]), 0.0).astype(BF16)

            def join(size, r):
                update = own[r] + dot(moved[r], x_scr[r]).astype(BF16)
                for n, s in enumerate(range(0, BLOCK, 2 * size)):
                    x_scr[r, s : s + size, :] = update[n * size : (n + 1) * size]

            def solve(h, c):
                r = h * chunks + c
                top = h * (DK + DV)
                sums = cum[:, span(c)]
                last = sums[:, BLOCK - 1 : BLOCK]
                tail = jnp.exp(last - sums)
                fade = jnp.broadcast_to(jnp.exp(last), (group, BLOCK))
                rows = dot(y_scr[c, top : top + DK + DV, :], x_scr[r])
                wu_ref[0, r] = rows.astype(BF16)
                y_scr[c, top : top + DK + DV, :] = (rows * tail[h : h + 1]).astype(BF16)
                fade_scr[slot, c, h : h + 1, :] = fade[h : h + 1]

            def finish(c):
                both = dot(y_scr[c], keys[c])
                for h in range(group):
                    top = h * (DK + DV)
                    m_scr[slot, c, h] = (-both[top : top + DK]).astype(BF16)
                    b_scr[slot, c, h] = both[top + DK : top + DK + DV]

            size = TINY
            while size < BLOCK:
                ops += [functools.partial(reach, size, h * chunks + c) for h, c in local]
                ops += [functools.partial(join, size, h * chunks + c) for h, c in local]
                size *= 2
            ops += [functools.partial(solve, h, c) for h, c in local]
            ops += [functools.partial(finish, c) for c in some]
            return ops

        half = chunks // 2
        early, late = range(half), range(half, chunks)
        early_front, early_right = front(early)
        late_front, late_right = front(late)
        cut = 2 * len(recurrence) // 3
        weave(early_front, recurrence[:cut], early_right)
        weave(back(early), late_front, late_right)
        weave(back(late), recurrence[cut:])


def prepare(job, lengths, qk_rows, v_in, halo, qk_taps, v_taps, log_decay, write_gain, key_heads, mixed, after):
    head, first, count = job
    tok = v_in.shape[1]
    value_heads = v_in.shape[2] // DV
    group = value_heads // key_heads
    chunks = tok // BLOCK
    rows = group * chunks
    wide = group * DV
    mixes = mixed is None

    def now(i):
        return jnp.minimum(i, count - 1)

    def before(i):
        return jnp.maximum(i - 1, 0)

    def whole_of(i, lengths):
        return (first + now(i), 0, 0)

    operands = [far(v_in), halo, far(v_taps), far(log_decay), far(write_gain), far(after)]
    in_specs = [
        pl.BlockSpec((1, tok, wide), lambda i, lengths: (first + now(i), 0, head)),
        pl.BlockSpec((1,) + halo.shape[1:], whole_of),
        pl.BlockSpec((CONV, wide), lambda i, lengths: (0, head)),
        pl.BlockSpec((1, value_heads, tok), whole_of),
        pl.BlockSpec((1, value_heads, tok), whole_of),
        pl.BlockSpec(memory_space=pltpu.HBM),
    ]
    out_specs = [
        pl.BlockSpec((1, rows, DK + DV, BLOCK), lambda i, lengths: (now(i), 0, 0, 0)),
        pl.BlockSpec((1, group, chunks * (DV + DK), DK), lambda i, lengths: (before(i), 0, 0, 0)),
        pl.BlockSpec((group, DV + DK, DK), lambda i, lengths: (before(i), 0, 0)),
        pl.BlockSpec((8, 128), lambda i, lengths: (0, 0)),
    ]
    out_shape = [
        pltpu.HBM((count, rows, DK + DV, BLOCK), BF16),
        pltpu.HBM((count, group, chunks * (DV + DK), DK), BF16),
        jax.ShapeDtypeStruct((count * group, DV + DK, DK), BF16),
        pltpu.HBM((8, 128), F32),
    ]
    scratch = [
        pltpu.VMEM((tok * group + EDGE, DV), F32),
        pltpu.VMEM((2, chunks, group, DK, DK), BF16),
        pltpu.VMEM((2, chunks, group, DV, DK), F32),
        pltpu.VMEM((2, chunks, group, BLOCK), F32),
        pltpu.VMEM((group, DV + DK, DK), F32),
        pltpu.VMEM((rows, BLOCK, BLOCK), BF16),
        pltpu.VMEM((rows, BLOCK, BLOCK), BF16),
        pltpu.VMEM((chunks, group * (DK + DV), BLOCK), BF16),
    ]
    if mixes:
        operands += [far(qk_rows), far(qk_taps)]
        in_specs += [
            pl.BlockSpec((1,) + qk_rows.shape[1:], whole_of),
            pl.BlockSpec(qk_taps.shape, lambda i, lengths: (0, 0)),
        ]
        out_specs += [pl.BlockSpec((1, tok, key_heads * DK), lambda i, lengths: (now(i), 0, 0))] * 2
        out_shape += [pltpu.HBM((count, tok, key_heads * DK), BF16)] * 2
        scratch.append(pltpu.VMEM((qk_rows.shape[1] + 2 * EDGE, DK), F32))
    else:
        operands.append(far(mixed))
        in_specs.append(pl.BlockSpec((1, tok, DK), lambda i, lengths: (first + now(i), 0, head)))
    return pl.pallas_call(
        functools.partial(prepare_kernel, first, count, head, group, chunks, key_heads, mixes),
        grid_spec=pltpu.PrefetchScalarGridSpec(
            num_scalar_prefetch=1,
            grid=(count + 1,),
            in_specs=in_specs,
            out_specs=out_specs,
            scratch_shapes=scratch,
        ),
        out_shape=out_shape,
        compiler_params=pltpu.CompilerParams(vmem_limit_bytes=VMEM_BYTES),
        cost_estimate=pl.CostEstimate(flops=5 * 10**9 * count, bytes_accessed=4 * 2**20 * count, transcendentals=10**6),
        name="prepare",
    )(far(lengths), *operands)


def outputs_kernel(
    first, head, group, chunks,
    length_ref, qn_ref, kn_ref, wu_ref, start_ref, log_ref, gain_ref, enter_ref, z_ref, norm_ref, held_ref, after_ref,
    out_ref,
    first_scr, score_scr, seen_scr,
):
    used = length_ref[first + pl.program_id(0)] - lax.axis_index("seq") * (chunks * BLOCK)
    units = [(h, c) for c in range(chunks) for h in range(group)]

    @pl.when(used <= 0)
    def _():
        out_ref[...] = jnp.zeros_like(out_ref)

    @pl.when(used > 0)
    def _():
        cum, gain = gates_of_heads(log_ref, gain_ref, used, head, group)
        faded = jnp.exp(cum)
        columns = as_columns(jnp.concatenate([cum] * (8 // group), axis=0), chunks)
        row = lax.broadcasted_iota(jnp.int32, (BLOCK, BLOCK), 0)
        lane = lax.broadcasted_iota(jnp.int32, (BLOCK, BLOCK), 1)
        upto = row <= lane
        norm_gain = norm_ref[...]

        def span(c):
            return slice(c * BLOCK, (c + 1) * BLOCK)

        both, raws = {}, {}

        def score(c):
            turned = qn_ref[0, span(c), :].T
            kq = dot(kn_ref[0, span(c), :], turned)
            q_wide = turned.astype(F32)
            for h in range(group):
                r = h * chunks + c
                ratio = jnp.exp(cum[h : h + 1, span(c)] - columns[:, c * 8 + h : c * 8 + h + 1])
                score_scr[r] = jnp.where(upto, ratio * kq, 0.0).astype(BF16)
                seen_scr[r] = q_wide * faded[h : h + 1, span(c)]
                top = c * (DV + DK)
                moved = dot(enter_ref[h], start_ref[0, h, top + DV : top + DV + DK, :])
                first_scr[r] = (moved + start_ref[0, h, top : top + DV, :].astype(F32)).astype(BF16)

        def gather(c):
            for h in range(group):
                r = h * chunks + c
                both[r] = dot(wu_ref[0, r], score_scr[r])

        def normalize(c):
            for h in range(group):
                r = h * chunks + c
                seen = (seen_scr[r] - both[r][:DK]).astype(BF16)
                raw = dot(first_scr[r], seen) + both.pop(r)[DK:]
                mean = jnp.sum(raw * raw, axis=0, keepdims=True) * (1.0 / DV)
                raws[r] = (raw * lax.rsqrt(mean + EPSILON)).astype(BF16)

        def gate(c):
            for h in range(group):
                scaled = raws.pop(h * chunks + c).T.astype(F32)
                cols = slice(h * DV, (h + 1) * DV)
                gated = scaled * norm_gain * silu(z_ref[0, span(c), cols].astype(F32))
                out_ref[0, span(c), cols] = jnp.where(row + c * BLOCK < used, gated, 0.0).astype(BF16)

        acts = (score, gather, normalize, gate)
        for t in range(chunks + len(acts) - 1):
            for late, act in enumerate(acts):
                if 0 <= t - late < chunks:
                    act(t - late)


def outputs(
    job, piece, lengths, qn, kn, wu, starts, log_decay, write_gain, enter, gate_z, norm_gain, key_heads, held, after,
):
    head, first, _ = job
    begin, count = piece
    prompts, tok, width = gate_z.shape
    rows = wu.shape[1]
    chunks = tok // BLOCK
    group = rows // chunks
    wide = group * DV
    value_heads = key_heads * group
    shift = begin - first
    from_mix = begin if qn.shape[0] == prompts else shift

    def whole_of(i, lengths):
        return (begin + i, 0, 0)

    def wide_of(i, lengths):
        return (begin + i, 0, head)

    def mixed_of(i, lengths):
        return (from_mix + i, 0, head)

    empty = held is None
    return pl.pallas_call(
        functools.partial(outputs_kernel, begin, head, group, chunks),
        grid_spec=pltpu.PrefetchScalarGridSpec(
            num_scalar_prefetch=1,
            grid=(count,),
            in_specs=[
                pl.BlockSpec((1, tok, DK), mixed_of),
                pl.BlockSpec((1, tok, DK), mixed_of),
                pl.BlockSpec((1, rows, DK + DV, BLOCK), lambda i, lengths: (shift + i, 0, 0, 0)),
                pl.BlockSpec((1, group, chunks * (DV + DK), DK), lambda i, lengths: (shift + i, 0, 0, 0)),
                pl.BlockSpec((1, value_heads, tok), whole_of),
                pl.BlockSpec((1, value_heads, tok), whole_of),
                pl.BlockSpec((group, DK, DV), lambda i, lengths: (shift + i, 0, 0)),
                pl.BlockSpec((1, tok, wide), wide_of),
                pl.BlockSpec((1, DV), lambda i, lengths: (0, 0)),
                pl.BlockSpec(memory_space=pltpu.HBM),
                pl.BlockSpec(memory_space=pltpu.HBM),
            ],
            out_specs=pl.BlockSpec((1, tok, wide), wide_of),
            scratch_shapes=[
                pltpu.VMEM((rows, DV, DK), BF16),
                pltpu.VMEM((rows, BLOCK, BLOCK), BF16),
                pltpu.VMEM((rows, BLOCK, DV), F32),
            ],
        ),
        out_shape=pltpu.HBM((prompts, tok, width), BF16),
        input_output_aliases={} if empty else {10: 0},
        compiler_params=pltpu.CompilerParams(vmem_limit_bytes=VMEM_BYTES),
        cost_estimate=pl.CostEstimate(flops=3 * 10**9 * count, bytes_accessed=4 * 2**20 * count, transcendentals=10**6),
        name="outputs",
    )(
        far(lengths), far(qn), far(kn), far(wu), far(starts), far(log_decay), far(write_gain), enter, far(gate_z),
        far(norm_gain.reshape(1, DV)), far(after if empty else held), far(norm_gain.reshape(1, DV) if after is held else after),
    )


def last_rows(qk_rows, v_in, rim):
    prompts, _, width = v_in.shape
    tall = 2 * EDGE
    heads = width // DV

    def kernel(qk_ref, v_ref, out_ref):
        for p in range(prompts):
            out_ref[p, :tall] = qk_ref[p]
            values = v_ref[p].astype(F32)
            rows = [
                values[tall - rim + i : tall - rim + i + 1, h * DV : (h + 1) * DV]
                for i in range(rim)
                for h in range(heads)
            ]
            rows.append(jnp.zeros((tall - rim * heads, DV), F32))
            out_ref[p, tall:] = jnp.concatenate(rows, axis=0).astype(BF16)

    return pl.pallas_call(
        kernel,
        grid=(1,),
        in_specs=[
            pl.BlockSpec((prompts, tall, DK), lambda i: (0, qk_rows.shape[1] // tall - 1, 0)),
            pl.BlockSpec((prompts, tall, width), lambda i: (0, v_in.shape[1] // tall - 1, 0)),
        ],
        out_specs=pl.BlockSpec((prompts, 2 * tall, DK), lambda i: (0, 0, 0)),
        out_shape=jax.ShapeDtypeStruct((prompts, 2 * tall, DK), BF16),
        compiler_params=pltpu.CompilerParams(vmem_limit_bytes=SMALL_VMEM_BYTES),
        name="last_rows",
    )(far(qk_rows), far(v_in))


def own_chip():
    seq = lax.axis_index("seq")
    return seq // 2, seq % 2 == 1


def early_late(own, other, odd):
    return jnp.where(odd, other, own), jnp.where(odd, own, other)


def follow(there, running):
    return dot(running, there[DV:])


def compose_maps(ins, outs):
    own_ref, other_ref = ins
    _, odd = own_chip()
    for n in range(own_ref.shape[0]):
        early, late = early_late(own_ref[n], other_ref[n], odd)
        both = follow(late, early)
        outs[0][n, :DV] = (both[:DV] + late[:DV].astype(F32)).astype(BF16)
        outs[0][n, DV:] = both[DV:].astype(BF16)


def close_maps(ins, outs):
    own_ref, other_ref = ins[:2]
    refs = ins[2:]
    chips = len(refs)
    chip, odd = own_chip()

    def of_chip(j, n):
        value = refs[0][n]
        for k in range(1, chips):
            value = jnp.where((chip + chips - k) % chips == j, refs[k][n], value)
        return value

    every = range(own_ref.shape[0])
    running = [of_chip(0, n)[:DV] for n in every]
    entering = [jnp.zeros_like(running[n]) for n in every]
    for j in range(1, chips):
        entering = [jnp.where(chip == j, running[n], entering[n]) for n in every]
        there = [of_chip(j, n) for n in every]
        running = [(follow(there[n], running[n]) + there[n][:DV].astype(F32)).astype(BF16) for n in every]
    for n in every:
        early, _ = early_late(own_ref[n], other_ref[n], odd)
        second = (follow(early, entering[n]) + early[:DV].astype(F32)).astype(BF16)
        outs[0][n] = jnp.where(odd, second, entering[n])
        outs[1][n] = running[n].T


def chain_maps(ins, outs):
    ins = (ins[0],) + tuple(ins[:0:-1])
    count = len(ins)
    mine = lax.axis_index("seq")
    every = range(ins[0].shape[0])

    def run(at):
        running = [ins[at][n, :DV] for n in every]
        for n in every:
            if at == 0:
                outs[0][n] = jnp.zeros_like(running[n])
        for j in range(1, count):
            there = ins[at ^ j]
            if j == at:
                for n in every:
                    outs[0][n] = running[n]
            moved = [follow(there.at[n], running[n]) for n in every]
            running = [(moved[n] + there[n, :DV].astype(F32)).astype(BF16) for n in every]
        for n in every:
            outs[1][n] = running[n].T

    for at in range(count):
        pl.when(mine == at)(functools.partial(run, at))


def choose_finals(group, placement_ref, finals, outs):
    refs = [(ref, n) for ref in finals for n in range(ref.shape[0] // group)]
    for r in range(placement_ref.shape[1]):
        prompt = placement_ref[0, r]
        for p, (ref, n) in enumerate(refs):
            @pl.when(prompt == p)
            def _(ref=ref, n=n):
                outs[0][r] = ref[n * group : (n + 1) * group]


def state_step(placement, group, compose, chain, close, earlier, after):
    operands, shapes = [placement], []
    steps = []
    if compose is not None:
        steps.append(("compose", len(operands), len(compose), len(shapes)))
        operands += compose
        shapes += [compose[0]]
    if chain is not None or close is not None:
        steps.append(("chain" if close is None else "close", len(operands), len(close or chain), len(shapes)))
        close = close or chain
        operands += close
        shapes += [jax.ShapeDtypeStruct((close[0].shape[0], DK, DV), BF16)] * 2
    if earlier is not None:
        steps.append(("choose", len(operands), len(earlier), len(shapes)))
        operands += earlier
        shapes.append(jax.ShapeDtypeStruct((placement.shape[1], group, DK, DV), BF16))
    out_shape = [jax.ShapeDtypeStruct(x.shape, x.dtype) for x in shapes] + [pltpu.HBM((8, 128), F32)]

    def kernel(*refs):
        refs[-1][...] = jnp.zeros_like(refs[-1])
        ins, outs = refs[: len(operands)], refs[len(operands) + 1 :]
        closed = None
        for kind, at, size, to in steps:
            part = ins[at : at + size]
            if kind == "compose":
                compose_maps(part, outs[to : to + 1])
            elif kind in ("close", "chain"):
                (close_maps if kind == "close" else chain_maps)(part, outs[to : to + 2])
                closed = outs[to + 1]
            else:
                choose_finals(group, ins[0], list(part) + ([] if closed is None else [closed]), outs[to:])

    vmem = pl.BlockSpec(memory_space=pltpu.VMEM)
    return pl.pallas_call(
        kernel,
        in_specs=[pl.BlockSpec(memory_space=pltpu.SMEM)]
        + [vmem] * (len(operands) - 1)
        + [pl.BlockSpec(memory_space=pltpu.HBM)],
        out_specs=[vmem] * len(out_shape),
        out_shape=out_shape,
        compiler_params=pltpu.CompilerParams(vmem_limit_bytes=SMALL_VMEM_BYTES),
        cost_estimate=pl.CostEstimate(flops=10**9, bytes_accessed=2**20, transcendentals=0),
        name="state_step",
    )(*operands, far(after))


def deliver(parts):
    count, group = parts[0].shape[:2]

    def kernel(*refs):
        for n, ref in enumerate(refs[:-1]):
            refs[-1][:, n * group : (n + 1) * group] = ref[...].astype(F32)

    return pl.pallas_call(
        kernel,
        grid=(2,),
        in_specs=[pl.BlockSpec((count // 2, group, DK, DV), lambda i: (i, 0, 0, 0))] * len(parts),
        out_specs=pl.BlockSpec((count // 2, group * len(parts), DK, DV), lambda i: (i, 0, 0, 0)),
        out_shape=jax.ShapeDtypeStruct((count, group * len(parts), DK, DV), F32),
        compiler_params=pltpu.CompilerParams(vmem_limit_bytes=VMEM_BYTES),
        name="deliver",
    )(*parts)


def across(block, distance):
    count = lax.axis_size("seq")
    return lax.ppermute(block, "seq", [(i, i ^ distance) for i in range(count)])


def from_chip_behind(block, distance):
    count = lax.axis_size("seq")
    chips = count // 2
    route = [(i, ((i // 2 + distance) % chips) * 2 + i % 2) for i in range(count)]
    return lax.ppermute(block, "seq", route)


def shards(
    qk_in, v_in, gate_z, conv_qk, conv_v, log_decay, write_gain, norm_gain, prompt_lengths, placement,
):
    prompts, tok = qk_in.shape[:2]
    key_heads = qk_in.shape[3] // DK
    value_heads = v_in.shape[2] // DV
    rim = CONV - 1
    seq_count = lax.axis_size("seq")
    head_count = lax.axis_size("head")

    def by_head(x):
        x = x.reshape(x.shape[0], x.shape[1], 2, key_heads, DK)
        return jnp.transpose(x, (0, 1, 3, 2, 4)).reshape(x.shape[0], -1, DK)

    qk_rows = by_head(qk_in)
    qk_taps = by_head(conv_qk[None])[0]
    tails = last_rows(qk_rows, v_in, rim)
    halo = lax.ppermute(tails, "seq", [(i, i + 1) for i in range(seq_count - 1)])
    group = value_heads // key_heads
    chips = seq_count // 2
    half = prompts // 2
    jobs = [(head, 0, prompts) for head in range(key_heads)]
    if key_heads == 1:
        jobs = [(0, 0, half), (0, half, prompts - half)]
    total = len(jobs)
    made, finals, sent = [], [], {}
    attended = None
    last = v_in

    def earlier(job):
        same = [n for n in range(total) if jobs[n][0] == jobs[job][0]]
        return [finals[n] for n in same[:-1]] if job == same[-1] else None

    def emit(job, entered, attended, last):
        qn, kn, wu, starts, _ = made[job]
        return outputs(
            jobs[job], jobs[job][1:], prompt_lengths, qn, kn, wu, starts, log_decay, write_gain,
            entered, gate_z, norm_gain, key_heads, attended, last,
        )

    for job in jobs:
        mixed = None if job[0] == 0 else made[0][:2]
        wu, starts, own_map, last, *new = prepare(
            job, prompt_lengths, qk_rows, v_in, halo, qk_taps, conv_v, log_decay, write_gain, key_heads,
            mixed and mixed[1], last,
        )
        moved = [own_map]
        if job == jobs[-1]:
            moved.append(across(own_map, 1))
        else:
            moved += [across(own_map, k) for k in range(seq_count - 1, 0, -1)]
        made.append((*(mixed or new), wu, starts, moved))

    def send(job, chosen):
        sent[jobs[job][0]] = lax.all_to_all(chosen, "head", 0, 0)

    entered, ready = [], None
    for job in range(total - 1):
        ready = earlier(job)
        late = job == total - 2
        enter, final, *chosen, last = state_step(
            placement, group, None, made[job][4], None, None if late else ready, last
        )
        entered.append(enter)
        finals.append(final)
        if chosen:
            send(job, chosen[0])
    if ready is not None:
        ready = ready + [finals[-1]]
    pair = made[-1][4]
    chip_map, *chosen, last = state_step(placement, group, pair, None, None, ready, last)
    chip_maps = [chip_map] + [from_chip_behind(chip_map, k) for k in range(1, chips)]
    if chosen:
        send(total - 2, chosen[0])
    for job in range(total - 1):
        attended = last = emit(job, entered[job], attended, last)
    enter, final, chosen, last = state_step(placement, group, None, None, pair + chip_maps, earlier(total - 1), last)
    send(total - 1, chosen)
    attended = emit(total - 1, enter, attended, last)
    rollout = deliver([sent[head] for head in range(key_heads)])
    return attended, rollout.reshape(1, 1, head_count * value_heads, DK, DV)


def solution(mesh):
    return jax.shard_map(
        shards,
        mesh=mesh,
        in_specs=(
            P(None, "seq", None, "head"),
            P(None, "seq", "head"),
            P(None, "seq", "head"),
            P(None, None, "head"),
            P(None, "head"),
            P(None, "head", "seq"),
            P(None, "head", "seq"),
            P(),
            P(),
            P("seq", None),
        ),
        out_specs=(P(None, "seq", "head"), P("seq", "head", None, None, None)),
        check_vma=False,
    )
```

```python
import functools

import jax
import jax.numpy as jnp
from jax import lax
from jax.experimental import pallas as pl
from jax.experimental.pallas import tpu as pltpu
from jax.sharding import PartitionSpec as P

DK = 128
DV = 128
CONV = 4
BLOCK = 128
TINY = 16
EDGE = 8
EPSILON = 1e-06
VMEM_BYTES = 40 * 1024 * 1024
SMALL_VMEM_BYTES = 8 * 1024 * 1024
F32 = jnp.float32
BF16 = jnp.bfloat16


def far(x):
    return pltpu.with_memory_space_constraint(x, pltpu.HBM)


def dot(a, b):
    return lax.dot_general(a, b, (((1,), (0,)), ((), ())), preferred_element_type=F32)


def silu(x):
    half = 0.5 * x
    return half + half * jnp.tanh(half)


def mixed_rows(pad_ref, taps, rim, first, step, c):
    total = None
    for i in range(CONV):
        start = rim + first + step * (c * BLOCK + i - (CONV - 1))
        stride = None if step == 1 else step
        term = pad_ref[pl.ds(start, BLOCK, stride), :] * taps[i]
        total = term if total is None else total + term
    return silu(total)


def unit_rows(x):
    return x * lax.rsqrt(jnp.sum(x * x, axis=-1, keepdims=True) + EPSILON)


def heads_rows(ref, head, group):
    every = ref[0]
    rows = every[:group]
    for n in range(1, every.shape[0] // group):
        rows = jnp.where(head == n, every[n * group : (n + 1) * group], rows)
    return rows


def gates_of_heads(log_ref, gain_ref, used, head, group):
    log = heads_rows(log_ref, head, group)
    lane = lax.broadcasted_iota(jnp.int32, log.shape, 1)
    valid = lane < used
    cum = jnp.where(valid, log, 0.0)
    gain = jnp.where(valid, heads_rows(gain_ref, head, group), 0.0)
    shift = 1
    while shift < BLOCK:
        cum = cum + jnp.where(lane % BLOCK >= shift, pltpu.roll(cum, shift, 1), 0.0)
        shift *= 2
    return cum, gain


def as_columns(rows, chunks):
    parts = [rows[:, c * BLOCK : (c + 1) * BLOCK] for c in range(chunks)]
    short = BLOCK - 8 * chunks
    if short:
        parts.append(jnp.zeros((short, BLOCK), F32))
    return jnp.concatenate(parts, axis=0).T


def block_bases(parts, chunks):
    rows = jnp.concatenate(parts, axis=0)
    short = 7 - rows.shape[0]
    fill = [jnp.zeros((short, rows.shape[1]), F32)] if short else []
    rows = jnp.concatenate([rows] + fill + [jnp.ones((1, rows.shape[1]), F32)], axis=0)
    return [rows[:, c * BLOCK : (c + 1) * BLOCK] for c in range(chunks)]


def spread_squares(base, group, kinds):
    high = base.astype(BF16).astype(F32)
    middle = (base - high).astype(BF16).astype(F32)
    low = base - high - middle
    parts = [high, middle, low]
    row = lax.broadcasted_iota(jnp.int32, (32, BLOCK), 0)
    which = row % 8
    real = row < 24
    stacked = jnp.concatenate(parts + [jnp.zeros_like(high)], axis=0)
    left = jnp.where(jnp.logical_and(which == 7, real), 1.0, stacked).T.astype(BF16)
    blocks = []
    for h in range(group):
        minus = jnp.concatenate([jnp.broadcast_to(-part[h : h + 1], (8, BLOCK)) for part in parts + [low]], axis=0)
        blocks.append(jnp.where(which == h, 1.0, jnp.where(which == 7, minus, 0.0)))
    for n in range(group, group * kinds):
        blocks.append(jnp.where(which == n, 1.0, 0.0).astype(F32))
    every = dot(left, jnp.concatenate(blocks, axis=1).astype(BF16))
    return [every[:, n * BLOCK : (n + 1) * BLOCK] for n in range(group * kinds)]


def mix(qk_ref, halo_ref, taps_ref, qn_ref, kn_ref, raw_scr, key_heads, chunks):
    kinds = 2 * key_heads
    rim = 2 * EDGE
    taps = taps_ref[...].astype(F32)
    raw_scr[:rim] = halo_ref[0].astype(F32)[:rim]
    raw_scr[rim : rim + qk_ref.shape[1]] = qk_ref[0].astype(F32)
    for c in range(chunks):
        span = slice(c * BLOCK, (c + 1) * BLOCK)
        for kind in range(kinds):
            own = [taps[n : n + 1] for n in range(kind, taps.shape[0], kinds)]
            rows = unit_rows(mixed_rows(raw_scr, own, rim, kind, kinds, c))
            to_ref = kn_ref if kind % 2 else qn_ref
            to_ref[0, span, kind // 2 * DK : (kind // 2 + 1) * DK] = rows.astype(BF16)


def weave(*lists):
    places = []
    for which, entries in enumerate(lists):
        places += [((n + 0.5) / len(entries), which, n) for n in range(len(entries))]
    for _, which, n in sorted(places):
        lists[which][n]()


def prepare_kernel(first, count, head, group, chunks, key_heads, mixes, *refs):
    length_ref, v_ref, halo_ref, v_taps_ref, log_ref, gain_ref, after_ref = refs[:7]
    refs = refs[7:]
    if mixes:
        qk_ref, qk_taps_ref, wu_ref, start_ref, map_ref, token_ref, qn_ref, kn_ref = refs[:8]
        v_pad, m_scr, b_scr, fade_scr, st_scr, a_scr, x_scr, y_scr, raw_scr = refs[8:]
        key_columns = slice(head * DK, (head + 1) * DK)
    else:
        kn_ref, wu_ref, start_ref, map_ref, token_ref = refs[:5]
        v_pad, m_scr, b_scr, fade_scr, st_scr, a_scr, x_scr, y_scr = refs[5:]
        key_columns = slice(0, DK)
    step = pl.program_id(0)
    token_ref[...] = jnp.zeros_like(token_ref)
    used = length_ref[first + jnp.minimum(step, count - 1)] - lax.axis_index("seq") * (chunks * BLOCK)
    units = [(h, c) for c in range(chunks) for h in range(group)]
    slot = step % 2
    live = jnp.logical_and(step < count, used > 0)

    def begin():
        row = lax.broadcasted_iota(jnp.int32, (DV + DK, DK), 0)
        lane = lax.broadcasted_iota(jnp.int32, (DV + DK, DK), 1)
        for h in range(group):
            st_scr[h] = jnp.where(row == lane + DV, 1.0, 0.0).astype(F32)

    def advance(c):
        narrow, moved = {}, {}

        def load(h):
            narrow[h] = st_scr[h].astype(BF16)
            start_ref[0, h, c * (DV + DK) : (c + 1) * (DV + DK), :] = narrow[h]

        def move(h):
            moved[h] = dot(narrow[h], m_scr[1 - slot, c, h])

        def store(h):
            fade = fade_scr[1 - slot, c, h : h + 1, :]
            state = st_scr[h, :DV] * fade + (moved[h][:DV] + b_scr[1 - slot, c, h])
            trans = st_scr[h, DV:] * fade + moved[h][DV:]
            if c < chunks - 1:
                st_scr[h, :DV] = state
                st_scr[h, DV:] = trans
            else:
                map_ref[h, :DV] = state.astype(BF16)
                map_ref[h, DV:] = trans.astype(BF16)

        return [functools.partial(act, h) for act in (load, move, store) for h in range(group)]

    recurrence = [begin]
    for c in range(chunks):
        recurrence += advance(c)

    @pl.when(jnp.logical_not(live))
    def _():
        @pl.when(step > 0)
        def _():
            weave(recurrence)

        @pl.when(step < count)
        def _():
            if mixes:
                qn_ref[...] = jnp.zeros_like(qn_ref)
                kn_ref[...] = jnp.zeros_like(kn_ref)
            wu_ref[...] = jnp.zeros_like(wu_ref)
            fade_scr[slot] = jnp.ones(fade_scr.shape[1:], F32)
            m_scr[slot] = jnp.zeros(m_scr.shape[1:], BF16)
            b_scr[slot] = jnp.zeros(b_scr.shape[1:], F32)

    @pl.when(live)
    def _():
        if mixes:
            mix(qk_ref, halo_ref, qk_taps_ref, qn_ref, kn_ref, raw_scr, key_heads, chunks)
        halo = halo_ref[0].astype(F32)
        for h in range(group):
            columns = slice(h * DV, (h + 1) * DV)
            v_pad[pl.ds(EDGE + h, chunks * BLOCK, group), :] = v_ref[0, :, columns].astype(F32)
        for i in range(CONV - 1):
            for h in range(group):
                source = 2 * EDGE + (i * key_heads + head) * group + h
                to = EDGE + (i - CONV + 1) * group + h
                v_pad[to : to + 1, :] = halo[source : source + 1]
        v_all_taps = v_taps_ref[...].astype(F32)
        v_taps = [[v_all_taps[i : i + 1, h * DV : (h + 1) * DV] for i in range(CONV)] for h in range(group)]

        cum, gain = gates_of_heads(log_ref, gain_ref, used, head, group)
        both_gains = gain * jnp.exp(cum)
        bases = block_bases([-cum], chunks)

        def span(c):
            return slice(c * BLOCK, (c + 1) * BLOCK)

        row = lax.broadcasted_iota(jnp.int32, (BLOCK, BLOCK), 0)
        lane = lax.broadcasted_iota(jnp.int32, (BLOCK, BLOCK), 1)
        above = row < lane
        small_row = lax.broadcasted_iota(jnp.int32, (TINY, BLOCK), 0)
        small_lane = lax.broadcasted_iota(jnp.int32, (TINY, BLOCK), 1)
        part_of = small_lane // TINY
        tiny_eye = jnp.where(small_row == small_lane % TINY, 1.0, 0.0).astype(F32)

        keys = [kn_ref[0, span(c), key_columns] for c in range(chunks)]
        turned = {}

        def front(some):
            ops, kk, later, compact, solved = [], {}, {}, {}, {}
            local = [(h, c) for c in some for h in range(group)]

            def start(c):
                turned[c] = keys[c].T
                kk[c] = dot(keys[c], turned[c])
                later[c] = spread_squares(bases[c], group, 1)

            def mask(h, c):
                r = h * chunks + c
                strict = jnp.where(above, jnp.exp(later[c][h]) * kk[c] * -gain[h : h + 1, span(c)], 0.0)
                a_scr[r] = strict.astype(BF16)
                tiny = strict[0:TINY]
                for b in range(1, BLOCK // TINY):
                    tiny = jnp.where(part_of == b, strict[b * TINY : (b + 1) * TINY], tiny)
                compact[r] = tiny
                solved[r] = tiny_eye

            def eliminate(j, r):
                factor = jnp.take_along_axis(compact[r], part_of * TINY + j, axis=1, mode="promise_in_bounds")
                solved[r] = solved[r] + factor * solved[r][j : j + 1, :]

            def place(r):
                for b in range(BLOCK // TINY):
                    x_scr[r, b * TINY : (b + 1) * TINY, :] = jnp.where(part_of == b, solved[r], 0.0).astype(BF16)

            def scale(h, c):
                top = h * (DK + DV)
                v_wide = mixed_rows(v_pad, v_taps[h], EDGE, h, group, c).astype(BF16).T.astype(F32)
                y_scr[c, top : top + DK, :] = (turned[c].astype(F32) * both_gains[h : h + 1, span(c)]).astype(BF16)
                y_scr[c, top + DK : top + DK + DV, :] = (v_wide * gain[h : h + 1, span(c)]).astype(BF16)

            for c in some:
                ops.append(functools.partial(start, c))
            for h, c in local:
                ops.append(functools.partial(mask, h, c))
            for j in range(TINY - 1, 0, -1):
                for h, c in local:
                    ops.append(functools.partial(eliminate, j, h * chunks + c))
            for h, c in local:
                ops.append(functools.partial(place, h * chunks + c))
            right = []
            for c in some:
                right += [functools.partial(scale, h, c) for h in range(group)]
            return ops, right

        def back(some):
            ops, own, moved = [], {}, {}
            local = [(h, c) for c in some for h in range(group)]

            def reach(size, r):
                half_lane = lax.broadcasted_iota(jnp.int32, (BLOCK // 2, BLOCK), 1)
                half_row = lax.broadcasted_iota(jnp.int32, (BLOCK // 2, BLOCK), 0)
                partner = half_lane // size == 2 * (half_row // size) + 1
                own[r] = jnp.concatenate([x_scr[r, s : s + size, :] for s in range(0, BLOCK, 2 * size)], axis=0)
                moved[r] = jnp.where(partner, dot(own[r], a_scr[r]), 0.0).astype(BF16)

            def join(size, r):
                update = own[r] + dot(moved[r], x_scr[r]).astype(BF16)
                for n, s in enumerate(range(0, BLOCK, 2 * size)):
                    x_scr[r, s : s + size, :] = update[n * size : (n + 1) * size]

            def solve(h, c):
                r = h * chunks + c
                top = h * (DK + DV)
                sums = cum[:, span(c)]
                last = sums[:, BLOCK - 1 : BLOCK]
                tail = jnp.exp(last - sums)
                fade = jnp.broadcast_to(jnp.exp(last), (group, BLOCK))
                rows = dot(y_scr[c, top : top + DK + DV, :], x_scr[r])
                wu_ref[0, r] = rows.astype(BF16)
                y_scr[c, top : top + DK + DV, :] = (rows * tail[h : h + 1]).astype(BF16)
                fade_scr[slot, c, h : h + 1, :] = fade[h : h + 1]

            def finish(c):
                both = dot(y_scr[c], keys[c])
                for h in range(group):
                    top = h * (DK + DV)
                    m_scr[slot, c, h] = (-both[top : top + DK]).astype(BF16)
                    b_scr[slot, c, h] = both[top + DK : top + DK + DV]

            size = TINY
            while size < BLOCK:
                ops += [functools.partial(reach, size, h * chunks + c) for h, c in local]
                ops += [functools.partial(join, size, h * chunks + c) for h, c in local]
                size *= 2
            ops += [functools.partial(solve, h, c) for h, c in local]
            ops += [functools.partial(finish, c) for c in some]
            return ops

        half = chunks // 2
        early, late = range(half), range(half, chunks)
        early_front, early_right = front(early)
        late_front, late_right = front(late)
        cut = len(recurrence) // 3
        weave(early_front, recurrence[:cut], early_right)
        weave(back(early), late_front, late_right)
        weave(back(late), recurrence[cut:])


def prepare(job, lengths, qk_rows, v_in, halo, qk_taps, v_taps, log_decay, write_gain, key_heads, mixed, after):
    head, first, count = job
    tok = v_in.shape[1]
    value_heads = v_in.shape[2] // DV
    group = value_heads // key_heads
    chunks = tok // BLOCK
    rows = group * chunks
    wide = group * DV
    mixes = mixed is None

    def now(i):
        return jnp.minimum(i, count - 1)

    def before(i):
        return jnp.maximum(i - 1, 0)

    def whole_of(i, lengths):
        return (first + now(i), 0, 0)

    operands = [far(v_in), halo, far(v_taps), far(log_decay), far(write_gain), far(after)]
    in_specs = [
        pl.BlockSpec((1, tok, wide), lambda i, lengths: (first + now(i), 0, head)),
        pl.BlockSpec((1,) + halo.shape[1:], whole_of),
        pl.BlockSpec((CONV, wide), lambda i, lengths: (0, head)),
        pl.BlockSpec((1, value_heads, tok), whole_of),
        pl.BlockSpec((1, value_heads, tok), whole_of),
        pl.BlockSpec(memory_space=pltpu.HBM),
    ]
    out_specs = [
        pl.BlockSpec((1, rows, DK + DV, BLOCK), lambda i, lengths: (now(i), 0, 0, 0)),
        pl.BlockSpec((1, group, chunks * (DV + DK), DK), lambda i, lengths: (before(i), 0, 0, 0)),
        pl.BlockSpec((group, DV + DK, DK), lambda i, lengths: (before(i), 0, 0)),
        pl.BlockSpec((8, 128), lambda i, lengths: (0, 0)),
    ]
    out_shape = [
        pltpu.HBM((count, rows, DK + DV, BLOCK), BF16),
        pltpu.HBM((count, group, chunks * (DV + DK), DK), BF16),
        jax.ShapeDtypeStruct((count * group, DV + DK, DK), BF16),
        pltpu.HBM((8, 128), F32),
    ]
    scratch = [
        pltpu.VMEM((tok * group + 2 * EDGE, DV), F32),
        pltpu.VMEM((2, chunks, group, DK, DK), BF16),
        pltpu.VMEM((2, chunks, group, DV, DK), F32),
        pltpu.VMEM((2, chunks, group, BLOCK), F32),
        pltpu.VMEM((group, DV + DK, DK), F32),
        pltpu.VMEM((rows, BLOCK, BLOCK), BF16),
        pltpu.VMEM((rows, BLOCK, BLOCK), BF16),
        pltpu.VMEM((chunks, group * (DK + DV), BLOCK), BF16),
    ]
    if mixes:
        operands += [far(qk_rows), far(qk_taps)]
        in_specs += [
            pl.BlockSpec((1,) + qk_rows.shape[1:], whole_of),
            pl.BlockSpec(qk_taps.shape, lambda i, lengths: (0, 0)),
        ]
        out_specs += [pl.BlockSpec((1, tok, key_heads * DK), lambda i, lengths: (now(i), 0, 0))] * 2
        out_shape += [pltpu.HBM((count, tok, key_heads * DK), BF16)] * 2
        scratch.append(pltpu.VMEM((qk_rows.shape[1] + 3 * EDGE, DK), F32))
    else:
        operands.append(far(mixed))
        in_specs.append(pl.BlockSpec((1, tok, DK), lambda i, lengths: (first + now(i), 0, head)))
    return pl.pallas_call(
        functools.partial(prepare_kernel, first, count, head, group, chunks, key_heads, mixes),
        grid_spec=pltpu.PrefetchScalarGridSpec(
            num_scalar_prefetch=1,
            grid=(count + 1,),
            in_specs=in_specs,
            out_specs=out_specs,
            scratch_shapes=scratch,
        ),
        out_shape=out_shape,
        compiler_params=pltpu.CompilerParams(vmem_limit_bytes=VMEM_BYTES),
        cost_estimate=pl.CostEstimate(flops=5 * 10**9 * count, bytes_accessed=4 * 2**20 * count, transcendentals=10**6),
        name="prepare",
    )(far(lengths), *operands)


def outputs_kernel(
    first, head, group, chunks,
    length_ref, qn_ref, kn_ref, wu_ref, start_ref, log_ref, gain_ref, enter_ref, z_ref, norm_ref, held_ref, after_ref,
    out_ref,
    first_scr, score_scr, seen_scr,
):
    used = length_ref[first + pl.program_id(0)] - lax.axis_index("seq") * (chunks * BLOCK)
    units = [(h, c) for c in range(chunks) for h in range(group)]

    @pl.when(used <= 0)
    def _():
        out_ref[...] = jnp.zeros_like(out_ref)

    @pl.when(used > 0)
    def _():
        cum, gain = gates_of_heads(log_ref, gain_ref, used, head, group)
        faded = jnp.exp(cum)
        columns = as_columns(jnp.concatenate([cum] * (8 // group), axis=0), chunks)
        row = lax.broadcasted_iota(jnp.int32, (BLOCK, BLOCK), 0)
        lane = lax.broadcasted_iota(jnp.int32, (BLOCK, BLOCK), 1)
        upto = row <= lane
        norm_gain = norm_ref[...]

        def span(c):
            return slice(c * BLOCK, (c + 1) * BLOCK)

        for c in range(chunks):
            turned = qn_ref[0, span(c), :].T
            kq = dot(kn_ref[0, span(c), :], turned)
            q_wide = turned.astype(F32)
            for h in range(group):
                r = h * chunks + c
                ratio = jnp.exp(cum[h : h + 1, span(c)] - columns[:, c * 8 + h : c * 8 + h + 1])
                score_scr[r] = jnp.where(upto, ratio * kq, 0.0).astype(BF16)
                seen_scr[r] = q_wide * faded[h : h + 1, span(c)]
                top = c * (DV + DK)
                moved = dot(enter_ref[h], start_ref[0, h, top + DV : top + DV + DK, :])
                first_scr[r] = (moved + start_ref[0, h, top : top + DV, :].astype(F32)).astype(BF16)
        both, raws = {}, {}
        for h, c in units:
            r = h * chunks + c
            both[r] = dot(wu_ref[0, r], score_scr[r])
        for h, c in units:
            r = h * chunks + c
            seen = (seen_scr[r] - both[r][:DK]).astype(BF16)
            raw = dot(first_scr[r], seen) + both[r][DK:]
            mean = jnp.sum(raw * raw, axis=0, keepdims=True) * (1.0 / DV)
            raws[r] = (raw * lax.rsqrt(mean + EPSILON)).astype(BF16)
        for h, c in units:
            scaled = raws[h * chunks + c].T.astype(F32)
            cols = slice(h * DV, (h + 1) * DV)
            gated = scaled * norm_gain * silu(z_ref[0, span(c), cols].astype(F32))
            out_ref[0, span(c), cols] = jnp.where(row + c * BLOCK < used, gated, 0.0).astype(BF16)


def outputs(
    job, piece, lengths, qn, kn, wu, starts, log_decay, write_gain, enter, gate_z, norm_gain, key_heads, held, after,
):
    head, first, _ = job
    begin, count = piece
    prompts, tok, width = gate_z.shape
    rows = wu.shape[1]
    chunks = tok // BLOCK
    group = rows // chunks
    wide = group * DV
    value_heads = key_heads * group
    shift = begin - first
    from_mix = begin if qn.shape[0] == prompts else shift

    def whole_of(i, lengths):
        return (begin + i, 0, 0)

    def wide_of(i, lengths):
        return (begin + i, 0, head)

    def mixed_of(i, lengths):
        return (from_mix + i, 0, head)

    empty = held is None
    return pl.pallas_call(
        functools.partial(outputs_kernel, begin, head, group, chunks),
        grid_spec=pltpu.PrefetchScalarGridSpec(
            num_scalar_prefetch=1,
            grid=(count,),
            in_specs=[
                pl.BlockSpec((1, tok, DK), mixed_of),
                pl.BlockSpec((1, tok, DK), mixed_of),
                pl.BlockSpec((1, rows, DK + DV, BLOCK), lambda i, lengths: (shift + i, 0, 0, 0)),
                pl.BlockSpec((1, group, chunks * (DV + DK), DK), lambda i, lengths: (shift + i, 0, 0, 0)),
                pl.BlockSpec((1, value_heads, tok), whole_of),
                pl.BlockSpec((1, value_heads, tok), whole_of),
                pl.BlockSpec((group, DK, DV), lambda i, lengths: (shift + i, 0, 0)),
                pl.BlockSpec((1, tok, wide), wide_of),
                pl.BlockSpec((1, DV), lambda i, lengths: (0, 0)),
                pl.BlockSpec(memory_space=pltpu.HBM),
                pl.BlockSpec(memory_space=pltpu.HBM),
            ],
            out_specs=pl.BlockSpec((1, tok, wide), wide_of),
            scratch_shapes=[
                pltpu.VMEM((rows, DV, DK), BF16),
                pltpu.VMEM((rows, BLOCK, BLOCK), BF16),
                pltpu.VMEM((rows, BLOCK, DV), F32),
            ],
        ),
        out_shape=pltpu.HBM((prompts, tok, width), BF16),
        input_output_aliases={} if empty else {10: 0},
        compiler_params=pltpu.CompilerParams(vmem_limit_bytes=VMEM_BYTES),
        cost_estimate=pl.CostEstimate(flops=3 * 10**9 * count, bytes_accessed=4 * 2**20 * count, transcendentals=10**6),
        name="outputs",
    )(
        far(lengths), far(qn), far(kn), far(wu), far(starts), far(log_decay), far(write_gain), enter, far(gate_z),
        far(norm_gain.reshape(1, DV)), far(after if empty else held), far(norm_gain.reshape(1, DV) if after is held else after),
    )


def last_rows(qk_rows, v_in, rim):
    prompts, _, width = v_in.shape
    tall = 2 * EDGE
    heads = width // DV

    def kernel(qk_ref, v_ref, out_ref):
        for p in range(prompts):
            out_ref[p, :tall] = qk_ref[p]
            values = v_ref[p].astype(F32)
            rows = [
                values[tall - rim + i : tall - rim + i + 1, h * DV : (h + 1) * DV]
                for i in range(rim)
                for h in range(heads)
            ]
            rows.append(jnp.zeros((tall - rim * heads, DV), F32))
            out_ref[p, tall:] = jnp.concatenate(rows, axis=0).astype(BF16)

    return pl.pallas_call(
        kernel,
        grid=(1,),
        in_specs=[
            pl.BlockSpec((prompts, tall, DK), lambda i: (0, qk_rows.shape[1] // tall - 1, 0)),
            pl.BlockSpec((prompts, tall, width), lambda i: (0, v_in.shape[1] // tall - 1, 0)),
        ],
        out_specs=pl.BlockSpec((prompts, 2 * tall, DK), lambda i: (0, 0, 0)),
        out_shape=jax.ShapeDtypeStruct((prompts, 2 * tall, DK), BF16),
        compiler_params=pltpu.CompilerParams(vmem_limit_bytes=SMALL_VMEM_BYTES),
        name="last_rows",
    )(far(qk_rows), far(v_in))


def own_chip():
    seq = lax.axis_index("seq")
    return seq // 2, seq % 2 == 1


def early_late(own, other, odd):
    return jnp.where(odd, other, own), jnp.where(odd, own, other)


def follow(there, running):
    return dot(running, there[DV:])


def compose_maps(ins, outs):
    own_ref, other_ref = ins
    _, odd = own_chip()
    for n in range(own_ref.shape[0]):
        early, late = early_late(own_ref[n], other_ref[n], odd)
        both = follow(late, early)
        outs[0][n, :DV] = (both[:DV] + late[:DV].astype(F32)).astype(BF16)
        outs[0][n, DV:] = both[DV:].astype(BF16)


def close_maps(ins, outs):
    own_ref, other_ref = ins[:2]
    refs = ins[2:]
    chips = len(refs)
    chip, odd = own_chip()

    def of_chip(j, n):
        value = refs[0][n]
        for k in range(1, chips):
            value = jnp.where((chip + chips - k) % chips == j, refs[k][n], value)
        return value

    every = range(own_ref.shape[0])
    running = [of_chip(0, n)[:DV] for n in every]
    entering = [jnp.zeros_like(running[n]) for n in every]
    for j in range(1, chips):
        entering = [jnp.where(chip == j, running[n], entering[n]) for n in every]
        there = [of_chip(j, n) for n in every]
        running = [(follow(there[n], running[n]) + there[n][:DV].astype(F32)).astype(BF16) for n in every]
    for n in every:
        early, _ = early_late(own_ref[n], other_ref[n], odd)
        second = (follow(early, entering[n]) + early[:DV].astype(F32)).astype(BF16)
        outs[0][n] = jnp.where(odd, second, entering[n])
        outs[1][n] = running[n].T


def chain_maps(ins, outs):
    ins = (ins[0],) + tuple(ins[:0:-1])
    count = len(ins)
    mine = lax.axis_index("seq")
    every = range(ins[0].shape[0])

    def run(at):
        running = [ins[at][n, :DV] for n in every]
        for n in every:
            if at == 0:
                outs[0][n] = jnp.zeros_like(running[n])
        for j in range(1, count):
            there = ins[at ^ j]
            if j == at:
                for n in every:
                    outs[0][n] = running[n]
            moved = [follow(there.at[n], running[n]) for n in every]
            running = [(moved[n] + there[n, :DV].astype(F32)).astype(BF16) for n in every]
        for n in every:
            outs[1][n] = running[n].T

    for at in range(count):
        pl.when(mine == at)(functools.partial(run, at))


def choose_finals(group, placement_ref, finals, outs):
    refs = [(ref, n) for ref in finals for n in range(ref.shape[0] // group)]
    for r in range(placement_ref.shape[1]):
        prompt = placement_ref[0, r]
        for p, (ref, n) in enumerate(refs):
            @pl.when(prompt == p)
            def _(ref=ref, n=n):
                outs[0][r] = ref[n * group : (n + 1) * group]


def state_step(placement, group, compose, chain, close, earlier, after):
    operands, shapes = [placement], []
    steps = []
    if compose is not None:
        steps.append(("compose", len(operands), len(compose), len(shapes)))
        operands += compose
        shapes += [compose[0]]
    if chain is not None or close is not None:
        steps.append(("chain" if close is None else "close", len(operands), len(close or chain), len(shapes)))
        close = close or chain
        operands += close
        shapes += [jax.ShapeDtypeStruct((close[0].shape[0], DK, DV), BF16)] * 2
        if earlier is not None:
            steps.append(("choose", len(operands), len(earlier), len(shapes)))
            operands += earlier
            shapes.append(jax.ShapeDtypeStruct((placement.shape[1], group, DK, DV), BF16))
    out_shape = [jax.ShapeDtypeStruct(x.shape, x.dtype) for x in shapes] + [pltpu.HBM((8, 128), F32)]

    def kernel(*refs):
        refs[-1][...] = jnp.zeros_like(refs[-1])
        ins, outs = refs[: len(operands)], refs[len(operands) + 1 :]
        closed = None
        for kind, at, size, to in steps:
            part = ins[at : at + size]
            if kind == "compose":
                compose_maps(part, outs[to : to + 1])
            elif kind in ("close", "chain"):
                (close_maps if kind == "close" else chain_maps)(part, outs[to : to + 2])
                closed = outs[to + 1]
            else:
                choose_finals(group, ins[0], list(part) + [closed], outs[to:])

    vmem = pl.BlockSpec(memory_space=pltpu.VMEM)
    return pl.pallas_call(
        kernel,
        in_specs=[pl.BlockSpec(memory_space=pltpu.SMEM)]
        + [vmem] * (len(operands) - 1)
        + [pl.BlockSpec(memory_space=pltpu.HBM)],
        out_specs=[vmem] * len(out_shape),
        out_shape=out_shape,
        compiler_params=pltpu.CompilerParams(vmem_limit_bytes=SMALL_VMEM_BYTES),
        cost_estimate=pl.CostEstimate(flops=10**9, bytes_accessed=2**20, transcendentals=0),
        name="state_step",
    )(*operands, far(after))


def deliver(parts):
    count, group = parts[0].shape[:2]

    def kernel(*refs):
        for n, ref in enumerate(refs[:-1]):
            refs[-1][:, n * group : (n + 1) * group] = ref[...].astype(F32)

    return pl.pallas_call(
        kernel,
        grid=(2,),
        in_specs=[pl.BlockSpec((count // 2, group, DK, DV), lambda i: (i, 0, 0, 0))] * len(parts),
        out_specs=pl.BlockSpec((count // 2, group * len(parts), DK, DV), lambda i: (i, 0, 0, 0)),
        out_shape=jax.ShapeDtypeStruct((count, group * len(parts), DK, DV), F32),
        compiler_params=pltpu.CompilerParams(vmem_limit_bytes=VMEM_BYTES),
        name="deliver",
    )(*parts)


def across(block, distance):
    count = lax.axis_size("seq")
    return lax.ppermute(block, "seq", [(i, i ^ distance) for i in range(count)])


def from_chip_behind(block, distance):
    count = lax.axis_size("seq")
    chips = count // 2
    route = [(i, ((i // 2 + distance) % chips) * 2 + i % 2) for i in range(count)]
    return lax.ppermute(block, "seq", route)


def shards(
    qk_in, v_in, gate_z, conv_qk, conv_v, log_decay, write_gain, norm_gain, prompt_lengths, placement,
):
    prompts, tok = qk_in.shape[:2]
    key_heads = qk_in.shape[3] // DK
    value_heads = v_in.shape[2] // DV
    rim = CONV - 1
    seq_count = lax.axis_size("seq")
    head_count = lax.axis_size("head")

    def by_head(x):
        x = x.reshape(x.shape[0], x.shape[1], 2, key_heads, DK)
        return jnp.transpose(x, (0, 1, 3, 2, 4)).reshape(x.shape[0], -1, DK)

    qk_rows = by_head(qk_in)
    qk_taps = by_head(conv_qk[None])[0]
    tails = last_rows(qk_rows, v_in, rim)
    halo = lax.ppermute(tails, "seq", [(i, i + 1) for i in range(seq_count - 1)])
    group = value_heads // key_heads
    chips = seq_count // 2
    half = prompts // 2
    jobs = [(head, 0, prompts) for head in range(key_heads)]
    if key_heads == 1:
        jobs = [(0, 0, half), (0, half, prompts - half)]
    total = len(jobs)
    made, finals, sent = [], [], {}
    attended = None
    last = v_in

    def finish(job, results):
        head = jobs[job][0]
        finals.append(results[1])
        if len(results) > 3:
            sent[head] = lax.all_to_all(results[2], "head", 0, 0)
        return results[0], results[-1]

    def earlier(job):
        same = [n for n in range(total) if jobs[n][0] == jobs[job][0]]
        return [finals[n] for n in same[:-1]] if job == same[-1] else None

    def emit(job, entered, attended, last):
        qn, kn, wu, starts, _ = made[job]
        return outputs(
            jobs[job], jobs[job][1:], prompt_lengths, qn, kn, wu, starts, log_decay, write_gain,
            entered, gate_z, norm_gain, key_heads, attended, last,
        )

    for job in jobs:
        mixed = None if job[0] == 0 else made[0][:2]
        wu, starts, own_map, last, *new = prepare(
            job, prompt_lengths, qk_rows, v_in, halo, qk_taps, conv_v, log_decay, write_gain, key_heads,
            mixed and mixed[1], last,
        )
        moved = [own_map]
        if job == jobs[-1]:
            moved.append(across(own_map, 1))
        else:
            moved += [across(own_map, k) for k in range(seq_count - 1, 0, -1)]
        made.append((*(mixed or new), wu, starts, moved))

    entered = []
    for job in range(total - 1):
        results = state_step(placement, group, None, made[job][4], None, earlier(job), last)
        enter, last = finish(job, results)
        entered.append(enter)
    pair = made[-1][4]
    chip_map, last = state_step(placement, group, pair, None, None, None, last)
    chip_maps = [chip_map] + [from_chip_behind(chip_map, k) for k in range(1, chips)]
    for job in range(total - 1):
        attended = last = emit(job, entered[job], attended, last)
    results = state_step(placement, group, None, None, pair + chip_maps, earlier(total - 1), last)
    enter, last = finish(total - 1, results)
    attended = emit(total - 1, enter, attended, last)
    rollout = deliver([sent[head] for head in range(key_heads)])
    return attended, rollout.reshape(1, 1, head_count * value_heads, DK, DV)


def solution(mesh):
    return jax.shard_map(
        shards,
        mesh=mesh,
        in_specs=(
            P(None, "seq", None, "head"),
            P(None, "seq", "head"),
            P(None, "seq", "head"),
            P(None, None, "head"),
            P(None, "head"),
            P(None, "head", "seq"),
            P(None, "head", "seq"),
            P(),
            P(),
            P("seq", None),
        ),
        out_specs=(P(None, "seq", "head"), P("seq", "head", None, None, None)),
        check_vma=False,
    )
```
